32 devices in a mesh: wide: 8 (over z, x), narrow: 4 (over y, core).
Axes of the slice: x: 2, y: 2, z: 4, core: 2. Of those that a mesh axis runs over, the one named last changes fastest.
Arguments:
- hidden_in: float32 [8192, 768], P(('wide', 'narrow')), may hold values from -6 to 6
- out_cot: float32 [8192, 768], P(('wide', 'narrow')), may hold values from -6 to 6
- lengths: int32 [8], P('wide'), may hold values from 1 to 1024, as said below
- norm_gain: float32 [768], P('narrow'), may hold values from 0.5 to 1.5
- w_zx: float32 [2, 768, 1536], P(None, 'wide', 'narrow'), may hold values from -0.21875 to 0.21875
- w_bc: float32 [768, 256], P('wide'), may hold values from -0.21875 to 0.21875
- w_dt: float32 [768, 24, 2], P('wide', 'narrow'), may hold values from -0.109375 to 0.109375
- conv_x: float32 [4, 1536], P(None, 'narrow'), may hold values from -0.5 to 0.5
- conv_bc: float32 [4, 256], replicated, may hold values from -0.5 to 0.5
- head_params: float32 [5, 24], P(None, 'narrow'), as said below
- out_gain: float32 [1536], P('narrow'), as said below
- w_out: float32 [1536, 768], P('narrow', 'wide'), may hold values from -0.15625 to 0.15625
- left_statistic_gate: float32 [2, 4, 768, 768], P(None, 'narrow', 'wide'), as said below
- stat_right_zx: float32 [2, 1536, 384], P(None, 'narrow'), as said below
- stat_left_out: float32 [1536, 384], P('narrow'), as said below
- stat_right_out: float32 [4, 768, 768], P('narrow', 'wide'), as said below
- inverse_root_left_gate: float32 [2, 4, 768, 768], P(None, 'narrow', 'wide'), as said below
- inverse_root_right_gate: float32 [2, 1536, 384], P(None, 'narrow'), as said below
- root_left_out: float32 [1536, 384], P('narrow'), as said below
- root_right_out: float32 [4, 768, 768], P('narrow', 'wide'), as said below
Outputs:
- block_out: float32 [8192, 768], P(('wide', 'narrow'))
- in_grad: float32 [8192, 768], P(('wide', 'narrow'))
- clip_norm: float32 [], replicated
- grad_zx: float32 [2, 768, 1536], P(None, 'wide', 'narrow')
- new_w_zx: float32 [2, 768, 1536], P(None, 'wide', 'narrow')
- new_stat_left_zx: float32 [2, 4, 768, 768], P(None, 'narrow', 'wide')
- new_stat_right_zx: float32 [2, 1536, 384], P(None, 'narrow')
- grad_out: float32 [1536, 768], P('narrow', 'wide')
- new_w_out: float32 [1536, 768], P('narrow', 'wide')
- new_stat_left_out: float32 [1536, 384], P('narrow')
- new_stat_right_out: float32 [4, 768, 768], P('narrow', 'wide')
- grad_bc: float32 [768, 256], P('wide')
- new_w_bc: float32 [768, 256], P('wide')
- grad_dt: float32 [768, 24, 2], P('wide', 'narrow')
- new_w_dt: float32 [768, 24, 2], P('wide', 'narrow')
- grad_conv_x: float32 [4, 1536], P(None, 'narrow')
- new_conv_x: float32 [4, 1536], P(None, 'narrow')
- grad_conv_bc: float32 [4, 256], replicated
- new_conv_bc: float32 [4, 256], replicated
- grad_head: float32 [5, 24], P(None, 'narrow')
- new_head: float32 [5, 24], P(None, 'narrow')
- grad_out_gain: float32 [1536], P('narrow')
- new_out_gain: float32 [1536], P('narrow')
- grad_norm_gain: float32 [768], P('narrow')
- new_norm_gain: float32 [768], P('narrow')
The draws below stay inside these ranges and needn't reach their ends.
Inputs may be any that keep to these rules, and one draw needn't show every extreme that they name: `lengths`: real tokens of each sequence; the remaining slots of its 1024 are padding. `head_params`: per head: the first two rows are step biases, the next two log rates, the last the diagonal term. `out_gain`: positive gains. `left_statistic_gate`: each D x D matrix is symmetric positive definite. `stat_right_zx`: each 384 x 384 block is symmetric positive definite. `stat_left_out`: each 384 x 384 block is symmetric positive definite. `stat_right_out`: each D x D matrix is symmetric positive definite. `inverse_root_left_gate`: each D x D matrix is symmetric. `inverse_root_right_gate`: each 384 x 384 block is symmetric. `root_left_out`: each 384 x 384 block is symmetric. `root_right_out`: each D x D matrix is symmetric.
All inputs are finite; a program needn't handle non-finite values.
Results may differ from the reference program's by a relative error of at most 0.0003.
Values sent between devices are 32-bit elements; how exact they have to be, the bound alone decides.
A program may use at most 192 MiB of HBM per device.

```python
import math
import jax
import jax.numpy as jnp
from jax import lax

D = 768
HEADS = 24
STATE = 64
CONV = 4
SPAN = 128
SEQ_LEN = 1024
SEQ_DEV = 1
INNER = 1536
BLOCK = 384
SEQS = 8
TOKENS = 8192
N_NARROW = 4


def sym_blocks(key, count, size, scale):
    first, second = jax.random.split(key)
    diag = scale * jnp.exp(jax.random.uniform(first, (count, size), jnp.float32, math.log(1.5), math.log(6.0)))
    noise = jax.random.normal(second, (count, size, size), jnp.float32) * (0.9 * scale / math.sqrt(size))
    sym = 0.5 * (noise + jnp.swapaxes(noise, 1, 2))
    return sym + diag[:, :, None] * jnp.eye(size, dtype=jnp.float32)


def grad_square():
    return 1.0 / (3.0 * D * INNER)


def draw_lengths(key, part):
    key = jax.random.fold_in(key, 5)
    index = jnp.arange(SEQS, dtype=jnp.int32)
    lowest = SEQ_LEN * 3 // 10 + SEQ_LEN * 7 // 10 * index // max(SEQS - 1, 1)
    cut = jax.random.randint(key, (SEQS,), 0, SEQ_LEN // 8 + 1, dtype=jnp.int32)
    length = jnp.maximum(lowest - cut, 1)
    return jnp.where(index == SEQS - 1, SEQ_LEN, length).astype(jnp.int32)


def draw_head_params(key, part):
    key = jax.random.fold_in(key, 7)
    first, second, third = jax.random.split(key, 3)
    step0 = jnp.exp(jax.random.uniform(first, (2, HEADS), jnp.float32, math.log(0.001), math.log(0.1)))
    bias = step0 + jnp.log(-jnp.expm1(-step0))
    rates = jnp.log(jax.random.uniform(second, (2, HEADS), jnp.float32, 1.0, 16.0))
    skip = jax.random.uniform(third, (1, HEADS), jnp.float32, 0.5, 1.5)
    return jnp.concatenate([bias, rates, skip], axis=0)


def draw_out_gain(key, part):
    key = jax.random.fold_in(key, 9)
    place = jnp.arange(INNER, dtype=jnp.float32) / (INNER - 1)
    return (0.5 + 1.5 * place) * jax.random.uniform(key, (INNER,), jnp.float32, 0.8, 1.2)


def draw_left_statistic_gate(key, part):
    key = jax.random.fold_in(key, 11)
    return sym_blocks(key, 2 * (INNER // BLOCK), D, BLOCK * grad_square()).reshape(2, INNER // BLOCK, D, D)


def draw_stat_right_zx(key, part):
    key = jax.random.fold_in(key, 13)
    return sym_blocks(key, 2 * (INNER // BLOCK), BLOCK, D * grad_square()).reshape(2, INNER, BLOCK)


def draw_stat_left_out(key, part):
    key = jax.random.fold_in(key, 17)
    return sym_blocks(key, INNER // BLOCK, BLOCK, D * grad_square()).reshape(INNER, BLOCK)


def draw_stat_right_out(key, part):
    key = jax.random.fold_in(key, 19)
    return sym_blocks(key, INNER // BLOCK, D, BLOCK * grad_square())


def draw_inverse_root_left_gate(key, part):
    key = jax.random.fold_in(key, 23)
    scale = 0.3 * (BLOCK * grad_square()) ** (-0.25)
    return sym_blocks(key, 2 * (INNER // BLOCK), D, scale).reshape(2, INNER // BLOCK, D, D)


def draw_inverse_root_right_gate(key, part):
    key = jax.random.fold_in(key, 29)
    scale = 0.3 * (D * grad_square()) ** (-0.25)
    return sym_blocks(key, 2 * (INNER // BLOCK), BLOCK, scale).reshape(2, INNER, BLOCK)


def draw_root_left_out(key, part):
    key = jax.random.fold_in(key, 31)
    scale = 0.3 * (D * grad_square()) ** (-0.25)
    return sym_blocks(key, INNER // BLOCK, BLOCK, scale).reshape(INNER, BLOCK)


def draw_root_right_out(key, part):
    key = jax.random.fold_in(key, 37)
    scale = 0.3 * (BLOCK * grad_square()) ** (-0.25)
    return sym_blocks(key, INNER // BLOCK, D, scale)


def levels(key, extent, shards, least, largest):
    level, own = 1.0, jax.random.fold_in(key, 6)
    for dim, shards_of in shards:
        draws = jnp.exp(jax.random.uniform(jax.random.fold_in(own, dim), (shards_of,), jnp.float32, least / len(shards), largest / len(shards)))
        level = level * jnp.repeat(draws, extent[dim] // shards_of).reshape([-1 if axis == dim else 1 for axis in range(len(extent))])
    return level


def gaussian(own_key, shape, deviation, most, cuts=(), kind=jnp.bfloat16):
    entries = jax.random.normal(own_key, shape, jnp.float32) * deviation
    if len(cuts) > 0:
        entries = levels(own_key, shape, cuts, -0.22, 0.18) * entries
    return jnp.clip(entries, min=-most, max=most).astype(kind)


def setup_inputs(seed: int = 0) -> dict:
    streams_of = jax.random.split(jax.random.key(seed), 21)
    hidden_in = gaussian(streams_of[0], (TOKENS, D), 1.0, 6.0, ((0, 32),), jnp.float32)
    out_cot = gaussian(streams_of[1], (TOKENS, D), 1.0, 6.0, ((0, 32),), jnp.float32)
    lengths = draw_lengths(jax.random.fold_in(streams_of[20], 71), 0)
    norm_gain = jnp.clip(1.0 + 0.1 * jax.random.normal(streams_of[3], (D,), jnp.float32), 0.5, 1.5)
    w_zx = gaussian(streams_of[4], (2, D, INNER), D ** -0.5, 0.21875, ((1, 8), (2, 4)), jnp.float32)
    w_bc = gaussian(streams_of[5], (D, 4 * STATE), D ** -0.5, 0.21875, ((0, 8),), jnp.float32)
    w_dt = gaussian(streams_of[6], (D, HEADS, 2), (4 * D) ** -0.5, 0.109375, ((0, 8), (1, 4)), jnp.float32)
    conv_x = jnp.clip(jax.random.uniform(streams_of[7], (CONV, INNER), jnp.float32, -0.5, 0.5) * levels(streams_of[7], (CONV, INNER), ((1, 4),), -0.4, 0.0), -0.5, 0.5)
    conv_bc = jnp.clip(jax.random.uniform(streams_of[8], (CONV, 4 * STATE), jnp.float32, -0.5, 0.5), -0.5, 0.5)
    head_params = draw_head_params(jax.random.fold_in(streams_of[20], 71), 0)
    out_gain = draw_out_gain(jax.random.fold_in(streams_of[20], 71), 0)
    w_out = gaussian(streams_of[11], (INNER, D), INNER ** -0.5, 0.15625, ((0, 4), (1, 8)), jnp.float32)
    left_statistic_gate = draw_left_statistic_gate(jax.random.fold_in(streams_of[20], 71), 0)
    stat_right_zx = draw_stat_right_zx(jax.random.fold_in(streams_of[20], 71), 0)
    stat_left_out = draw_stat_left_out(jax.random.fold_in(streams_of[20], 71), 0)
    stat_right_out = draw_stat_right_out(jax.random.fold_in(streams_of[20], 71), 0)
    inverse_root_left_gate = draw_inverse_root_left_gate(jax.random.fold_in(streams_of[20], 71), 0)
    inverse_root_right_gate = draw_inverse_root_right_gate(jax.random.fold_in(streams_of[20], 71), 0)
    root_left_out = draw_root_left_out(jax.random.fold_in(streams_of[20], 71), 0)
    root_right_out = draw_root_right_out(jax.random.fold_in(streams_of[20], 71), 0)
    return {"hidden_in": hidden_in, "out_cot": out_cot, "lengths": lengths, "norm_gain": norm_gain, "w_zx": w_zx, "w_bc": w_bc, "w_dt": w_dt, "conv_x": conv_x, "conv_bc": conv_bc, "head_params": head_params, "out_gain": out_gain, "w_out": w_out, "left_statistic_gate": left_statistic_gate, "stat_right_zx": stat_right_zx, "stat_left_out": stat_left_out, "stat_right_out": stat_right_out, "inverse_root_left_gate": inverse_root_left_gate, "inverse_root_right_gate": inverse_root_right_gate, "root_left_out": root_left_out, "root_right_out": root_right_out}


@jax.custom_vjp
def low(v):
    return lax.optimization_barrier(v.astype(jnp.bfloat16)).astype(jnp.float32)

@jax.custom_vjp
def low_back(v):
    return v

def low_keep(v):
    return (low(v), None)

def low_pass(kept, grad):
    return (grad,)

def back_keep(v):
    return (v, None)

def back_low(kept, grad):
    return (low(grad),)
low.defvjp(low_keep, low_pass)
low_back.defvjp(back_keep, back_low)

def silu(v):
    return v / (1.0 + jnp.exp(-v))

def causal(values, taps):
    count = taps.shape[0]
    length = values.shape[1]
    padded = jnp.pad(values, ((0, 0), (count - 1, 0), (0, 0)))
    total = taps[0] * padded[:, 0:length]
    for j in range(1, count):
        total = total + taps[j] * padded[:, j:j + length]
    return total

def scan_ssd(xh, steps, logs, bmat, cmat, span):
    hyper_parameters = lax.Precision.HIGHEST
    seqs, length, heads, width = xh.shape
    blocks = length // span
    xq = xh.reshape(seqs, blocks, span, heads, width).transpose(0, 1, 3, 2, 4)
    dq = steps.reshape(seqs, blocks, span, heads).transpose(0, 1, 3, 2)
    aq = logs.reshape(seqs, blocks, span, heads).transpose(0, 1, 3, 2)
    bq = bmat.reshape(seqs, blocks, span, -1)
    cq = cmat.reshape(seqs, blocks, span, -1)
    cum = jnp.cumsum(aq, axis=-1)
    lower = jnp.arange(span)[:, None] >= jnp.arange(span)[None, :]
    diff = cum[..., :, None] - cum[..., None, :]
    decay = jnp.where(lower, jnp.exp(jnp.where(lower, diff, 0.0)), 0.0)
    inner = jnp.einsum('sctn,scun->sctu', cq, bq, precision=hyper_parameters)
    weights = inner[:, :, None] * decay * dq[..., None, :]
    y_in = jnp.einsum('schtu,schup->schtp', weights, xq, precision=hyper_parameters)
    tail = jnp.exp(cum[..., -1:] - cum) * dq
    states = jnp.einsum('scun,schu,schup->schnp', bq, tail, xq, precision=hyper_parameters)
    totals = jnp.exp(cum[..., -1])

    def advance(carry, inputs):
        piece, factor = inputs
        return (carry * factor[..., None, None] + piece, carry)
    start = jnp.zeros((seqs, heads, bq.shape[-1], width), jnp.float32)
    _, before = lax.scan(jax.checkpoint(advance), start, (states.transpose(1, 0, 2, 3, 4), totals.transpose(1, 0, 2)))
    before = before.transpose(1, 0, 2, 3, 4)
    y_out = jnp.einsum('sctn,schnp->schtp', cq, before, precision=hyper_parameters) * jnp.exp(cum)[..., None]
    return (y_in + y_out).transpose(0, 1, 3, 2, 4).reshape(seqs, length, heads, width)

def mixer(normed, w_zx, w_bc, w_dt, conv_x, conv_bc, head_params, live, seqs):
    hyper_parameters = lax.Precision.HIGHEST
    tokens = normed.shape[0]
    seq_len = tokens // seqs
    heads = w_dt.shape[1]
    state = w_bc.shape[1] // 4
    gate = jnp.dot(normed, w_zx[0], precision=hyper_parameters)
    xin = jnp.dot(normed, w_zx[1], precision=hyper_parameters)
    bc_pre = jnp.dot(normed, w_bc, precision=hyper_parameters)
    dt_pre = jnp.dot(normed, w_dt.reshape(w_dt.shape[0], heads * 2), precision=hyper_parameters).reshape(tokens, heads, 2)
    xconv = silu(causal(xin.reshape(seqs, seq_len, -1), conv_x)) * live.reshape(seqs, seq_len)[..., None]
    bconv = silu(causal(bc_pre.reshape(seqs, seq_len, -1), conv_bc))
    steps = jax.nn.softplus(dt_pre + head_params[0:2].T)
    logs = -jnp.exp(head_params[2:4].T) * steps
    width = xconv.shape[-1] // heads
    xh = xconv.reshape(seqs, seq_len, heads, width)
    steps = steps.reshape(seqs, seq_len, heads, 2)
    logs = logs.reshape(seqs, seq_len, heads, 2)
    b_fwd = bconv[..., 0:state]
    c_fwd = bconv[..., state:2 * state]
    b_rev = bconv[..., 2 * state:3 * state]
    c_rev = bconv[..., 3 * state:4 * state]
    forward = scan_ssd(xh, steps[..., 0], logs[..., 0], b_fwd, c_fwd, SPAN)
    backward = jnp.flip(scan_ssd(jnp.flip(xh, 1), jnp.flip(steps[..., 1], 1), jnp.flip(logs[..., 1], 1), jnp.flip(b_rev, 1), jnp.flip(c_rev, 1), SPAN), 1)
    fwd_part = jnp.pad(forward[:, :-1], ((0, 0), (1, 0), (0, 0), (0, 0)))
    rev_part = jnp.pad(backward[:, 1:], ((0, 0), (0, 1), (0, 0), (0, 0)))
    mixed = fwd_part + rev_part + head_params[4][:, None] * xh
    return mixed.reshape(tokens, -1) * silu(gate)

def layer(hidden, norm_gain, w_zx, w_bc, w_dt, conv_x, conv_bc, head_params, out_gain, w_out, live, seqs):
    hyper_parameters = lax.Precision.HIGHEST
    inv_rms = lax.rsqrt(lax.optimization_barrier(jnp.mean(hidden * hidden, axis=-1)) + 1e-05)
    normed = hidden * inv_rms[:, None] * norm_gain
    gated = mixer(normed, w_zx, w_bc, w_dt, conv_x, conv_bc, head_params, live, seqs)
    gate_rms = lax.rsqrt(lax.optimization_barrier(jnp.mean(gated * gated, axis=-1)) + 1e-05)
    onorm = gated * gate_rms[:, None] * out_gain
    branch = jnp.dot(onorm, w_out, precision=hyper_parameters)
    return hidden + live[:, None] * branch

def reference(hidden_in, out_cot, lengths, norm_gain, w_zx, w_bc, w_dt, conv_x, conv_bc, head_params, out_gain, w_out, left_statistic_gate, stat_right_zx, stat_left_out, stat_right_out, inverse_root_left_gate, inverse_root_right_gate, root_left_out, root_right_out):
    hyper_parameters = lax.Precision.HIGHEST
    params = (norm_gain, w_zx, w_bc, w_dt, conv_x, conv_bc, head_params, out_gain, w_out)
    groups = SEQS // SEQ_DEV
    group_tokens = SEQ_DEV * SEQ_LEN
    inputs = (hidden_in.reshape(groups, group_tokens, D), out_cot.reshape(groups, group_tokens, D), lengths.reshape(groups, SEQ_DEV))

    def visit(total, item):
        hidden, cot, lens = item
        live = (jnp.arange(SEQ_LEN)[None, :] < lens[:, None]).astype(jnp.float32).reshape(-1)

        def run(h, *weights):
            return layer(h, *weights, live, SEQ_DEV)
        result, back = jax.vjp(run, hidden, *params)
        grads = back(cot)
        total = tuple((a + b for a, b in zip(total, grads[1:])))
        return (total, (result, grads[0]))
    zeros = tuple((jnp.zeros_like(p) for p in params))
    total, (results, dxs) = lax.scan(visit, zeros, inputs)
    block_out = results.reshape(TOKENS, D)
    in_grad = dxs.reshape(TOKENS, D)
    squares = jnp.float32(0.0)
    for g in total:
        squares = squares + jnp.sum(g * g)
    clip_norm = jnp.sqrt(squares)
    factor = 1.0 / jnp.maximum(clip_norm, 1.0)
    g_ng, g_zx, g_bc, g_dt, g_cx, g_cbc, g_head, g_og, g_out = tuple((g * factor for g in total))
    nblk = N_NARROW
    gzb = g_zx.reshape(2, D, nblk, BLOCK)
    left_zx = 0.5 * left_statistic_gate + 0.5 * jnp.einsum('mdkb,mekb->mkde', gzb, gzb, precision=hyper_parameters)
    right_zx = 0.5 * stat_right_zx + 0.5 * jnp.einsum('mdkb,mdkc->mkbc', gzb, gzb, precision=hyper_parameters).reshape(2, INNER, BLOCK)
    update_step_gate = jnp.einsum('mkde,mekb->mdkb', inverse_root_left_gate, gzb, precision=hyper_parameters)
    update_step_gate = jnp.einsum('mdkb,mkbc->mdkc', update_step_gate, inverse_root_right_gate.reshape(2, nblk, BLOCK, BLOCK), precision=hyper_parameters)
    new_zx = w_zx - 0.5 * update_step_gate.reshape(2, D, INNER)
    gob = g_out.reshape(nblk, BLOCK, D)
    left_out = 0.5 * stat_left_out + 0.5 * jnp.einsum('kbd,kcd->kbc', gob, gob, precision=hyper_parameters).reshape(INNER, BLOCK)
    right_out = 0.5 * stat_right_out + 0.5 * jnp.einsum('kbd,kbe->kde', gob, gob, precision=hyper_parameters)
    step_out = jnp.einsum('kbc,kcd->kbd', root_left_out.reshape(nblk, BLOCK, BLOCK), gob, precision=hyper_parameters)
    step_out = jnp.einsum('kbd,ked->kbe', step_out, root_right_out, precision=hyper_parameters)
    new_out = w_out - 0.5 * step_out.reshape(INNER, D)
    rate = 10.0
    return (block_out, in_grad, clip_norm, g_zx, new_zx, left_zx, right_zx, g_out, new_out, left_out, right_out, g_bc, w_bc - rate * g_bc, g_dt, w_dt - rate * g_dt, g_cx, conv_x - rate * g_cx, g_cbc, conv_bc - rate * g_cbc, g_head, head_params - rate * g_head, g_og, out_gain - rate * g_og, g_ng, norm_gain - rate * g_ng)
```

```python
import functools

import jax
import jax.numpy as jnp
from jax import lax
from jax.experimental import pallas as pl
from jax.experimental.pallas import tpu as pltpu
from jax.sharding import PartitionSpec as P

SPAN = 128
WIDTH = 64
HIGH = lax.Precision.HIGH
F32 = jnp.float32
NN = (((1,), (0,)), ((), ()))
NT = (((1,), (1,)), ((), ()))
TN = (((0,), (0,)), ((), ()))
TT = (((0,), (1,)), ((), ()))


def dot(a, b, dims=NN):
    return lax.dot_general(a, b, dims, precision=HIGH, preferred_element_type=F32)


def halves(v):
    hi = v.astype(jnp.bfloat16)
    return hi, (v - hi.astype(F32)).astype(jnp.bfloat16)


def product(a, b, dims=NN):
    (ah, al), (bh, bl) = a, b
    (left,), (right,) = dims[0]
    return lax.dot_general(
        jnp.concatenate([ah, al, ah], axis=left),
        jnp.concatenate([bh, bh, bl], axis=right),
        dims,
        preferred_element_type=F32,
    )


def dot3(a, b, dims=NN):
    return product(halves(a), halves(b), dims)


def sigmoid(v):
    return 1.0 / (1.0 + jnp.exp(-v))


def split3(v):
    hi = v.astype(jnp.bfloat16)
    rest = v - hi.astype(F32)
    mid = rest.astype(jnp.bfloat16)
    lo = (rest - mid.astype(F32)).astype(jnp.bfloat16)
    return jnp.concatenate([hi, mid, lo], axis=0)


def exact_dot(v, ones):
    rows = v.shape[0]
    out = lax.dot_general(split3(v), ones, NN, preferred_element_type=F32)
    return out[0:rows] + out[rows : 2 * rows] + out[2 * rows : 3 * rows]


def iota(shape, axis):
    return lax.broadcasted_iota(jnp.int32, shape, axis)


def shift_right(v, count):
    return jnp.where(iota(v.shape, 1) >= count, pltpu.roll(v, count, axis=1), 0.0)


def shift_left(v, count):
    length = v.shape[1]
    return jnp.where(iota(v.shape, 1) < length - count, pltpu.roll(v, length - count, axis=1), 0.0)


def conv_rows(v, taps):
    count = taps.shape[1]
    total = taps[:, count - 1 : count] * v
    for j in range(count - 1):
        total = total + taps[:, j : j + 1] * shift_right(v, count - 1 - j)
    return total


def pieces(ref, chans, state):
    bc = 2 * chans
    dt = bc + 4 * state
    return ref.at[0:chans], ref.at[chans:bc], ref.at[bc:dt], ref.at[dt : dt + 16]


def convolve(x_ref, bc_ref, live_ref, cx_ref, cbc_ref, xc_ref, dx_act_ref, b_ref, c_ref, dbc_act_ref):
    chans, tokens = xc_ref.shape
    state = c_ref.shape[0] // 2
    live = live_ref[...]

    def conv_x_rows(i, _):
        rows = pl.ds(pl.multiple_of(i * 8, 8), 8)
        u = conv_rows(x_ref[rows, :], cx_ref[rows, :])
        s = sigmoid(u)
        xc_ref[rows, :] = u * s * live
        dx_act_ref[rows, :] = (s + u * s * (1.0 - s)) * live
        return 0

    lax.fori_loop(0, chans // 8, conv_x_rows, 0, unroll=2)

    def conv_bc_rows(i, _, src, dst, dst_row, shift):
        rows = pl.ds(pl.multiple_of(src * state + i * 8, 8), 8)
        out = pl.ds(pl.multiple_of(dst_row + i * 8, 8), 8)
        u = conv_rows(bc_ref[rows, :], cbc_ref[rows, :])
        s = sigmoid(u)
        dbc_act_ref[rows, :] = s + u * s * (1.0 - s)
        v = u * s
        if shift == 1:
            v = shift_right(v, 1)
        if shift == -1:
            v = shift_left(v, 1)
        dst[out, :] = v
        return 0

    for src, dst, row, shift in ((0, b_ref, 0, 0), (1, c_ref, 0, 1), (2, b_ref, state, 0), (3, c_ref, state, -1)):
        lax.fori_loop(
            0,
            state // 8,
            functools.partial(conv_bc_rows, src=src, dst=dst, dst_row=row, shift=shift),
            0,
            unroll=2,
        )


def step_sizes(pre_ref, hp_ref, step_ref, cum_ref, cumex_ref, heads):
    blocks = pre_ref.shape[1] // SPAN
    pre = pre_ref[...] + hp_ref[:, 0:1]
    steps = jnp.maximum(pre, 0.0) + jnp.log1p(jnp.exp(-jnp.abs(pre)))
    step_ref[...] = steps
    logs = -hp_ref[:, 1:2] * steps
    rows16 = iota((16, SPAN), 0)
    lane16 = iota((16, SPAN), 1)
    row_q = iota((SPAN, SPAN), 0)
    lane_q = iota((SPAN, SPAN), 1)
    upto = (row_q <= lane_q).astype(F32).astype(jnp.bfloat16)
    downto = (row_q >= lane_q).astype(F32).astype(jnp.bfloat16)
    both = jnp.concatenate([upto, downto], axis=1)
    for b in range(blocks):
        sums = exact_dot(logs[:, b * SPAN : (b + 1) * SPAN], both)
        cum = jnp.where(rows16 < heads, sums[:, 0:SPAN], sums[:, SPAN : 2 * SPAN])
        ex_f = jnp.where(lane16 >= 1, pltpu.roll(cum, 1, axis=1), 0.0)
        ex_r = jnp.where(lane16 < SPAN - 1, pltpu.roll(cum, SPAN - 1, axis=1), 0.0)
        cum_ref[:, b * SPAN : (b + 1) * SPAN] = cum
        cumex_ref[:, b * SPAN : (b + 1) * SPAN] = jnp.where(rows16 < heads, ex_f, ex_r)


def states(xc_ref, b_ref, step_ref, cum_ref, sloc_ref, hcat_ref, heads):
    blocks = xc_ref.shape[1] // SPAN
    state = b_ref.shape[0] // 2

    def local_states(b, _):
        sl = pl.ds(pl.multiple_of(b * SPAN, SPAN), SPAN)
        bcat = spread(b_ref[:, sl], state)
        tail = tails(cum_ref[:, sl], step_ref[:, sl], heads)
        left = tailed(xc_ref[:, sl], tail, range(heads), heads)
        sloc_ref[b] = dot3(left, bcat, NT)
        return 0

    lax.fori_loop(0, blocks, local_states, 0)

    lane_h = iota((WIDTH, 2 * state), 1)
    for h in range(heads):
        rows = slice(h * WIDTH, (h + 1) * WIDTH)
        carry = jnp.zeros((WIDTH, 2 * state), F32)
        for i in range(blocks):
            r = blocks - 1 - i
            hcat_ref[i, rows, 0:state] = carry[:, 0:state]
            hcat_ref[r, rows, state : 2 * state] = carry[:, state : 2 * state]
            tot_f = jnp.exp(cum_ref[h : h + 1, (i + 1) * SPAN - 1 : (i + 1) * SPAN])
            tot_r = jnp.exp(cum_ref[heads + h : heads + h + 1, r * SPAN : r * SPAN + 1])
            factor = jnp.where(lane_h < state, tot_f, tot_r)
            piece = jnp.where(lane_h < state, sloc_ref[i, rows, :], sloc_ref[r, rows, :])
            carry = carry * factor + piece


def outputs(z_ref, xc_ref, b_ref, c_ref, step_ref, cum_ref, cumex_ref, hcat_ref, hp_ref, y_ref, inner_ref, heads, emit):
    blocks = xc_ref.shape[1] // SPAN
    state = b_ref.shape[0] // 2
    row_q = iota((SPAN, SPAN), 0)
    lane_q = iota((SPAN, SPAN), 1)
    lower = row_q < lane_q
    diag = row_q == lane_q

    def block(b, _):
        sl = pl.ds(pl.multiple_of(b * SPAN, SPAN), SPAN)
        bb, cc = b_ref[:, sl], c_ref[:, sl]
        inner = jnp.where(
            lower, dot3(bb[0:state], cc[0:state], TN), dot3(bb[state:], cc[state:], TN)
        )
        inner_ref[b] = inner
        cum, steps, cumex = cum_ref[:, sl], step_ref[:, sl], cumex_ref[:, sl]
        scale = jnp.exp(cumex)
        cols = columns(cum, steps)
        sums = None
        entering = dot3(hcat_ref[b], spread(cc, state))
        x_parts = halves(xc_ref[:, sl])
        for h in range(heads):
            rows = slice(h * WIDTH, (h + 1) * WIDTH)
            decay = decays(cols, cumex, lower, diag, h, heads)
            mt = jnp.where(diag, hp_ref[h : h + 1, 2:3], inner * decay)
            y = product((x_parts[0][rows], x_parts[1][rows]), halves(mt))
            y = y + entering[rows, 0:SPAN] * scale[h : h + 1]
            y = y + entering[rows, SPAN:] * scale[heads + h : heads + h + 1]
            z = z_ref[rows, sl]
            y_ref[rows, sl] = y
            sums = emit(b, sl, h, rows, y * (z * sigmoid(z)), sums)
        return 0

    lax.fori_loop(0, blocks, block, 0)


def fwd_kernel(
    heads,
    proj_ref,
    live_ref,
    cx_ref,
    cbc_ref,
    hp_ref,
    y_ref,
    xc_ref,
    dx_act_ref,
    b_ref,
    c_ref,
    dbc_act_ref,
    step_ref,
    cum_ref,
    cumex_ref,
    hcat_ref,
    inner_ref,
    gated_ref,
    sq_ref,
    sloc_ref,
):
    z_ref, x_ref, bc_ref, pre_ref = pieces(proj_ref, xc_ref.shape[0], c_ref.shape[0] // 2)
    convolve(x_ref, bc_ref, live_ref, cx_ref, cbc_ref, xc_ref, dx_act_ref, b_ref, c_ref, dbc_act_ref)
    step_sizes(pre_ref, hp_ref, step_ref, cum_ref, cumex_ref, heads)
    states(xc_ref, b_ref, step_ref, cum_ref, sloc_ref, hcat_ref, heads)

    def emit(b, sl, h, rows, gated, total):
        gated_ref[rows, sl] = gated
        part = jnp.sum(gated * gated, axis=0, keepdims=True)
        total = part if total is None else total + part
        if h == heads - 1:
            sq_ref[:, sl] = total
        return total

    outputs(z_ref, xc_ref, b_ref, c_ref, step_ref, cum_ref, cumex_ref, hcat_ref, hp_ref, y_ref, inner_ref, heads, emit)


def spread(bb, state):
    zero = jnp.zeros((state, SPAN), F32)
    top = jnp.concatenate([bb[0:state], zero], axis=1)
    low = jnp.concatenate([zero, bb[state:]], axis=1)
    return jnp.concatenate([top, low], axis=0)


def tails(cum, steps, heads):
    rows = iota((16, SPAN), 0)
    last = jnp.where(rows[:, 0:1] < heads, cum[:, SPAN - 1 : SPAN], cum[:, 0:1])
    return jnp.exp(last - cum) * steps


def tailed(xc, tail, chosen, heads):
    parts = []
    for i, h in enumerate(chosen):
        x = xc[i * WIDTH : (i + 1) * WIDTH]
        parts.append(
            jnp.concatenate([x * tail[h : h + 1], x * tail[heads + h : heads + h + 1]], axis=1)
        )
    return jnp.concatenate(parts, axis=0)


def columns(cum, steps):
    pad = jnp.zeros((SPAN - 32, SPAN), F32)
    return jnp.transpose(jnp.concatenate([cum, steps, pad], axis=0))


def decays(cols, cumex, lower, diag, h, heads):
    f, r = h, heads + h
    arg = jnp.where(
        lower, cumex[f : f + 1] - cols[:, f : f + 1], cumex[r : r + 1] - cols[:, r : r + 1]
    )
    step = jnp.where(lower, cols[:, 16 + f : 17 + f], cols[:, 16 + r : 17 + r])
    return jnp.where(diag, 0.0, jnp.exp(arg) * step)


def gate_back(z_ref, y_ref, don_ref, rms, coef, og_ref, dy_ref, dz_ref, dog_ref, onorm_ref=None):
    chans = y_ref.shape[0]

    def gate_rows(i, _):
        rows = pl.ds(pl.multiple_of(i * 8, 8), 8)
        z, y, don, og = z_ref[rows, :], y_ref[rows, :], don_ref[rows, :], og_ref[rows, :]
        s = sigmoid(z)
        act = z * s
        gated = y * act
        normed = rms * don
        dog_ref[rows, 0:1] = jnp.sum(gated * normed, axis=1, keepdims=True)
        dgated = normed * og - gated * coef
        dy_ref[rows, :] = dgated * act
        dz_ref[rows, :] = dgated * y * (s + act * (1.0 - s))
        if onorm_ref is not None:
            onorm_ref[rows, :] = gated * rms * og
        return 0

    lax.fori_loop(0, chans // 8, gate_rows, 0, unroll=2)


def back_intra(xc_ref, c_ref, inner_ref, step_ref, cum_ref, cumex_ref, hcat_ref, hp_ref, dy_s, dxc_s, dh_s, dc_s, din_s, g_s, cv_s, dd_s, chosen, heads, tick):
    blocks = xc_ref.shape[1] // SPAN
    state = c_ref.shape[0] // 2
    lower = iota((SPAN, SPAN), 0) < iota((SPAN, SPAN), 1)
    diag = iota((SPAN, SPAN), 0) == iota((SPAN, SPAN), 1)
    first = chosen[0] == 0

    def block(b, put):
        sl = pl.ds(pl.multiple_of(b * SPAN, SPAN), SPAN)
        cc = c_ref[:, sl]
        inner = inner_ref[b]
        cumex = cumex_ref[:, sl]
        scale = jnp.exp(cumex)
        cols = columns(cum_ref[:, sl], step_ref[:, sl])
        dinner = jnp.zeros((SPAN, SPAN), F32) if first else din_s[b]
        dcc = jnp.zeros((2 * state, SPAN), F32) if first else dc_s[:, sl]
        for h in chosen:
            f, r = h, heads + h
            rows = slice(h * WIDTH, (h + 1) * WIDTH)
            decay = decays(cols, cumex, lower, diag, h, heads)
            mt = inner * decay
            e_f, e_r = scale[f : f + 1], scale[r : r + 1]
            ce = jnp.concatenate([cc[0:state] * e_f, cc[state:] * e_r], axis=0)
            x = xc_ref[rows, sl]
            dy = dy_s[rows, sl]
            dy_parts = halves(dy)
            left = jnp.concatenate([x, hcat_ref[b, rows, :]], axis=1)
            back = product(halves(left), dy_parts, TN)
            dmt, dce = back[0:SPAN], back[SPAN:]
            dinner = dinner + dmt * decay
            w = dmt * mt
            over_f = jnp.sum(jnp.where(lower, w, 0.0), axis=0, keepdims=True)
            over_r = jnp.sum(jnp.where(lower, 0.0, w), axis=0, keepdims=True)
            prod = dce * ce
            put(g_s, (slice(f, f + 1), sl), over_f + jnp.sum(prod[0:state], axis=0, keepdims=True))
            put(g_s, (slice(r, r + 1), sl), over_r + jnp.sum(prod[state:], axis=0, keepdims=True))
            dcc = dcc + jnp.concatenate([dce[0:state] * e_f, dce[state:] * e_r], axis=0)
            right = jnp.concatenate(
                [jnp.where(lower, mt, 0.0), jnp.where(lower, 0.0, mt), ce], axis=0
            )
            out = product(dy_parts, halves(right), NT)
            dx_f, dx_r = out[:, 0:SPAN], out[:, SPAN : 2 * SPAN]
            put(dh_s, (b, rows, slice(None)), out[:, 2 * SPAN :])
            put(cv_s, (slice(f, f + 1), sl), jnp.sum(x * dx_f, axis=0, keepdims=True))
            put(cv_s, (slice(r, r + 1), sl), jnp.sum(x * dx_r, axis=0, keepdims=True))
            put(dd_s, (slice(h, h + 1), sl), jnp.sum(x * dy, axis=0, keepdims=True))
            put(dxc_s, (rows, sl), dx_f + dx_r + hp_ref[h : h + 1, 2:3] * dy)
        put(din_s, (b,), dinner)
        put(dc_s, (slice(None), sl), dcc)

    two_at_a_time(blocks, block, tick)


def two_at_a_time(blocks, block, tick):
    def body(i, _):
        stores = []
        for b in (2 * i, 2 * i + 1):
            block(b, lambda ref, at, value: stores.append((ref, at, value)))
        for ref, at, value in stores:
            ref[at] = value
        tick(2 * i)
        tick(2 * i + 1)
        return 0

    lax.fori_loop(0, blocks // 2, body, 0)


def back_states(cum_ref, hcat_ref, dh_s, tq_s, state, chosen, heads):
    blocks = hcat_ref.shape[0]
    lane_h = iota((WIDTH, 2 * state), 1)
    lane_1 = iota((1, 2 * state), 1)
    for h in chosen:
        rows = slice(h * WIDTH, (h + 1) * WIDTH)
        carry = jnp.zeros((WIDTH, 2 * state), F32)
        for i in range(blocks):
            f = blocks - 1 - i
            tot_f = jnp.exp(cum_ref[h : h + 1, (f + 1) * SPAN - 1 : (f + 1) * SPAN])
            tot_r = jnp.exp(cum_ref[heads + h : heads + h + 1, i * SPAN : i * SPAN + 1])
            factor = jnp.where(lane_h < state, tot_f, tot_r)
            direct = jnp.where(lane_h < state, dh_s[f, rows, :], dh_s[i, rows, :])
            kept = jnp.where(lane_h < state, hcat_ref[f, rows, :], hcat_ref[i, rows, :])
            scaled = carry * factor
            dots = jnp.sum(scaled * kept, axis=0, keepdims=True)
            q_f = jnp.sum(jnp.where(lane_1 < state, dots, 0.0), axis=1, keepdims=True)
            q_r = jnp.sum(jnp.where(lane_1 < state, 0.0, dots), axis=1, keepdims=True)
            tq_s[f, h : h + 1, :] = jnp.broadcast_to(q_f, (1, SPAN))
            tq_s[i, heads + h : heads + h + 1, :] = jnp.broadcast_to(q_r, (1, SPAN))
            dh_s[f, rows, 0:state] = carry[:, 0:state]
            dh_s[i, rows, state:] = carry[:, state:]
            carry = scaled + direct


def back_inter(xc_ref, b_ref, step_ref, cum_ref, dxc_s, dh_s, db_s, v_s, chosen, heads, tick):
    blocks = xc_ref.shape[1] // SPAN
    state = b_ref.shape[0] // 2
    first = chosen[0] == 0
    group = slice(chosen[0] * WIDTH, (chosen[-1] + 1) * WIDTH)

    def block(b, put):
        sl = pl.ds(pl.multiple_of(b * SPAN, SPAN), SPAN)
        bcat = spread(b_ref[:, sl], state)
        tail = tails(cum_ref[:, sl], step_ref[:, sl], heads)
        xc = xc_ref[group, sl]
        dxc = dxc_s[group, sl]
        dsl = halves(dh_s[b, group, :])
        dleft = product(dsl, halves(bcat))
        dbs = product(dsl, halves(tailed(xc, tail, chosen, heads)), TN)
        db = jnp.concatenate([dbs[0:state, 0:SPAN], dbs[state:, SPAN:]], axis=0)
        put(db_s, (slice(None), sl), db if first else db_s[:, sl] + db)
        parts = []
        for i, h in enumerate(chosen):
            f, r = h, heads + h
            part = slice(i * WIDTH, (i + 1) * WIDTH)
            tx_f = dleft[part, 0:SPAN] * tail[f : f + 1]
            tx_r = dleft[part, SPAN:] * tail[r : r + 1]
            put(v_s, (slice(f, f + 1), sl), jnp.sum(xc[part] * tx_f, axis=0, keepdims=True))
            put(v_s, (slice(r, r + 1), sl), jnp.sum(xc[part] * tx_r, axis=0, keepdims=True))
            parts.append(dxc[part] + tx_f + tx_r)
        put(dxc_s, (group, sl), jnp.concatenate(parts, axis=0))

    two_at_a_time(blocks, block, tick)


def back_logs(b_ref, c_ref, pre_ref, step_ref, hp_ref, ddt_ref, dhp_ref, db_s, dc_s, din_s, g_s, cv_s, v_s, dd_s, tq_s, heads):
    blocks = pre_ref.shape[1] // SPAN
    state = b_ref.shape[0] // 2
    row_q = iota((SPAN, SPAN), 0)
    lane_q = iota((SPAN, SPAN), 1)
    lower = row_q < lane_q
    strict = (row_q > lane_q).astype(F32)
    weak = (row_q >= lane_q).astype(F32)
    strict_t = (row_q < lane_q).astype(F32)
    weak_t = (row_q <= lane_q).astype(F32)
    tri = jnp.concatenate(
        [
            jnp.concatenate([strict, strict_t], axis=1),
            jnp.concatenate([weak, weak_t], axis=1),
            jnp.concatenate([strict_t, strict], axis=1),
        ],
        axis=0,
    ).astype(jnp.bfloat16)
    rows16 = iota((16, SPAN), 0)
    used = rows16 < 2 * heads
    rate = hp_ref[:, 1:2]

    def block(b, carry):
        bias_sum, log_sum, skip_sum = carry
        sl = pl.ds(pl.multiple_of(b * SPAN, SPAN), SPAN)
        dinner = din_s[b]
        both = jnp.concatenate(
            [jnp.where(lower, dinner, 0.0), jnp.where(lower, 0.0, dinner)], axis=0
        )
        dc_s[:, sl] = dc_s[:, sl] + dot3(spread(b_ref[:, sl], state), both)
        db = dot3(c_ref[:, sl], both, NT)
        db_s[0:state, sl] = db_s[0:state, sl] + db[0:state, 0:SPAN]
        db_s[state:, sl] = db_s[state:, sl] + db[state:, SPAN:]
        g = jnp.where(used, g_s[:, sl], 0.0)
        c = jnp.where(used, cv_s[:, sl], 0.0)
        v = jnp.where(used, v_s[:, sl], 0.0)
        steps = step_ref[:, sl]
        sums = exact_dot(jnp.concatenate([g, -c, v], axis=1), tri)
        dlog = jnp.where(rows16 < heads, sums[:, 0:SPAN], sums[:, SPAN:])
        dlog = dlog + jnp.where(used, tq_s[b], 0.0)
        pre = pre_ref[:, sl] + hp_ref[:, 0:1]
        small = steps < 1e-30
        ratio = jnp.where(small, 1.0, sigmoid(pre) / jnp.where(small, 1.0, steps))
        dpre = (c + v) * ratio - rate * dlog * sigmoid(pre)
        ddt_ref[:, sl] = dpre
        skip = jnp.where(rows16 < heads, dd_s[:, sl], 0.0)
        return bias_sum + dpre, log_sum - rate * dlog * steps, skip_sum + skip

    zeros16 = jnp.zeros((16, SPAN), F32)
    bias_sum, log_sum, skip = lax.fori_loop(0, blocks, block, (zeros16, zeros16, zeros16))
    dhp_ref[:, 0:1] = jnp.sum(bias_sum, axis=1, keepdims=True)
    dhp_ref[:, 1:2] = jnp.sum(log_sum, axis=1, keepdims=True)
    dhp_ref[:, 2:3] = jnp.sum(skip, axis=1, keepdims=True)


def conv_back(du, v, taps):
    count = taps.shape[1]
    dv = taps[:, count - 1 : count] * du
    sums = [jnp.sum(du * v, axis=1, keepdims=True)]
    for j in range(count - 2, -1, -1):
        moved = shift_left(du, count - 1 - j)
        dv = dv + taps[:, j : j + 1] * moved
        sums.append(jnp.sum(moved * v, axis=1, keepdims=True))
    return dv, sums[::-1]


def conv_x_back(xin_ref, cx_ref, dx_act_ref, dxc_s, dxin_ref, dcx_ref, start, count):
    def group(i, _):
        rows = pl.ds(pl.multiple_of(start + i * 8, 8), 8)
        dv, sums = conv_back(dxc_s[rows, :] * dx_act_ref[rows, :], xin_ref[rows, :], cx_ref[rows, :])
        dxin_ref[rows, :] = dv
        for j, item in enumerate(sums):
            dcx_ref[rows, j : j + 1] = item
        return 0

    lax.fori_loop(0, count // 8, group, 0, unroll=2)


def conv_bc_back(bc_ref, cbc_ref, dbc_act_ref, db_s, dc_s, dbc_ref, dcbc_ref):
    state = db_s.shape[0] // 2

    def group(i, _, src, grad, grad_row, shift):
        rows = pl.ds(pl.multiple_of(src * state + i * 8, 8), 8)
        from_rows = pl.ds(pl.multiple_of(grad_row + i * 8, 8), 8)
        d = grad[from_rows, :]
        if shift == 1:
            d = shift_left(d, 1)
        if shift == -1:
            d = shift_right(d, 1)
        dv, sums = conv_back(d * dbc_act_ref[rows, :], bc_ref[rows, :], cbc_ref[rows, :])
        dbc_ref[rows, :] = dv
        for j, item in enumerate(sums):
            dcbc_ref[rows, j : j + 1] = item
        return 0

    for src, grad, row, shift in ((0, db_s, 0, 0), (1, dc_s, 0, 1), (2, db_s, state, 0), (3, dc_s, state, -1)):
        lax.fori_loop(
            0,
            state // 8,
            functools.partial(group, src=src, grad=grad, grad_row=row, shift=shift),
            0,
            unroll=2,
        )


def pairs_of(heads):
    return [tuple(range(h, min(h + 2, heads))) for h in range(0, heads, 2)]


def bwd_kernel(
    heads,
    proj_ref,
    y_ref,
    xc_ref,
    dx_act_ref,
    b_ref,
    c_ref,
    dbc_act_ref,
    step_ref,
    cum_ref,
    cumex_ref,
    hcat_ref,
    inner_ref,
    don_ref,
    rms_ref,
    coef_ref,
    og_ref,
    cx_ref,
    cbc_ref,
    hp_ref,
    dproj_ref,
    dcx_ref,
    dcbc_ref,
    dhp_ref,
    dog_ref,
    dy_s,
    dxc_s,
    dh_s,
    db_s,
    dc_s,
    din_s,
    g_s,
    cv_s,
    v_s,
    dd_s,
    tq_s,
):
    chans, state = y_ref.shape[0], b_ref.shape[0] // 2
    z_ref, xin_ref, bc_ref, pre_ref = pieces(proj_ref, chans, state)
    dz_ref, dxin_ref, dbc_ref, ddt_ref = pieces(dproj_ref, chans, state)
    gate_back(z_ref, y_ref, don_ref, rms_ref[...], coef_ref[...], og_ref, dy_s, dz_ref, dog_ref)
    for chosen in pairs_of(heads):
        back_intra(
            xc_ref, c_ref, inner_ref, step_ref, cum_ref, cumex_ref, hcat_ref, hp_ref, dy_s, dxc_s, dh_s, dc_s,
            din_s, g_s, cv_s, dd_s, chosen, heads, lambda b: None,
        )
        back_states(cum_ref, hcat_ref, dh_s, tq_s, state, chosen, heads)
        back_inter(xc_ref, b_ref, step_ref, cum_ref, dxc_s, dh_s, db_s, v_s, chosen, heads, lambda b: None)
    conv_x_back(xin_ref, cx_ref, dx_act_ref, dxc_s, dxin_ref, dcx_ref, 0, chans)
    back_logs(
        b_ref, c_ref, pre_ref, step_ref, hp_ref, ddt_ref, dhp_ref, db_s, dc_s, din_s, g_s, cv_s, v_s, dd_s, tq_s, heads
    )
    conv_bc_back(bc_ref, cbc_ref, dbc_act_ref, db_s, dc_s, dbc_ref, dcbc_ref)


def call(kernel, out_shapes, scratch, flops):
    return pl.pallas_call(
        kernel,
        out_shape=[jax.ShapeDtypeStruct(shape, F32) for shape in out_shapes],
        scratch_shapes=[pltpu.VMEM(shape, F32) for shape in scratch],
        compiler_params=pltpu.CompilerParams(vmem_limit_bytes=56 * 1024 * 1024),
        cost_estimate=pl.CostEstimate(flops=flops, bytes_accessed=20_000_000, transcendentals=0),
    )


def run_fwd(proj, live, cx, cbc, hp, heads):
    tokens = proj.shape[1]
    chans, n4 = cx.shape[0], cbc.shape[0]
    blocks = tokens // SPAN
    full, half, rows = (chans, tokens), (n4 // 2, tokens), (16, tokens)
    return call(
        functools.partial(fwd_kernel, heads),
        [full, full, full, half, half, (n4, tokens), rows, rows, rows, (blocks, chans, n4 // 2), (blocks, SPAN, SPAN), full, (1, tokens)],
        [(blocks, chans, n4 // 2)],
        2_000_000_000,
    )(proj, live, cx, cbc, hp)


def run_bwd(proj, kept, don, rms, coef, og, cx, cbc, hp, heads):
    tokens = proj.shape[1]
    chans, n4 = cx.shape[0], cbc.shape[0]
    blocks = tokens // SPAN
    full, half, rows = (chans, tokens), (n4 // 2, tokens), (16, tokens)
    return call(
        functools.partial(bwd_kernel, heads),
        [proj.shape, (chans, 4), (n4, 4), (16, 3), (chans, 1)],
        [full, full, (blocks, chans, n4 // 2), half, half, (blocks, SPAN, SPAN), rows, rows, rows, rows, (blocks, 16, SPAN)],
        4_000_000_000,
    )(proj, *kept, don, rms, coef, og, cx, cbc, hp)


def square_sum(arrays):
    total = jnp.float32(0.0)
    for item in arrays:
        total = total + jnp.sum(item * item)
    return total


def pad_rows(v):
    return jnp.concatenate([v, jnp.zeros((16 - v.shape[0],) + v.shape[1:], v.dtype)], axis=0)


def local(
    hidden_in,
    out_cot,
    lengths,
    norm_gain,
    w_zx,
    w_bc,
    w_dt,
    conv_x,
    conv_bc,
    head_params,
    out_gain,
    w_out,
    left_statistic_gate,
    stat_right_zx,
    stat_left_out,
    stat_right_out,
    inverse_root_left_gate,
    inverse_root_right_gate,
    root_left_out,
    root_right_out,
):
    rows, chans = w_zx.shape[1], w_zx.shape[2]
    heads = w_dt.shape[1]
    n4 = w_bc.shape[1]
    own_rows, width = hidden_in.shape
    narrow_id, wide_id = lax.axis_index("narrow"), lax.axis_index("wide")

    full_in = lax.all_gather(hidden_in, "narrow", axis=0, tiled=True)
    full_gain = lax.all_gather(norm_gain, "narrow", axis=0, tiled=True)
    dt_cols = jnp.transpose(w_dt, (0, 2, 1)).reshape(rows, 2 * heads)
    own_w = jnp.concatenate(
        [w_zx[0], w_zx[1], w_bc, dt_cols, jnp.zeros((rows, 16 - 2 * heads), F32)], axis=1
    )
    w_in = lax.all_gather(own_w, "wide", axis=0, tiled=True)
    wide_out = lax.all_gather(w_out, "wide", axis=1, tiled=True)

    tokens = full_in.shape[0]
    live = (jnp.arange(tokens) < lengths[0]).astype(F32)
    row_start = narrow_id * own_rows
    live_own = lax.dynamic_slice_in_dim(live, row_start, own_rows, 0)
    dbranch = lax.all_gather(live_own[:, None] * out_cot, "narrow", axis=0, tiled=True)

    inv_rms = lax.rsqrt(jnp.mean(full_in * full_in, axis=-1) + 1e-05)
    normed = full_in * inv_rms[:, None] * full_gain
    proj = dot(w_in, normed, TT)
    cx, cbc = conv_x.T, conv_bc.T
    hp = jnp.concatenate(
        [
            pad_rows(head_params[0:2].reshape(2 * heads, 1)),
            pad_rows(jnp.exp(head_params[2:4]).reshape(2 * heads, 1)),
            pad_rows(head_params[4].reshape(heads, 1)),
        ],
        axis=1,
    )
    *kept, gated, squares = run_fwd(proj, live[None, :], cx, cbc, hp, heads)
    donorm = dot(wide_out, dbranch, NT)
    inner = jnp.sum(gated * (donorm * out_gain[:, None]), axis=0, keepdims=True)
    stats = lax.psum(jnp.concatenate([squares, inner], axis=0), "narrow")
    inner_total = chans * lax.axis_size("narrow")
    rms = lax.rsqrt(stats[0:1] / inner_total + 1e-05)
    coef = rms**3 * stats[1:2] / inner_total
    onorm = gated * rms * out_gain[:, None]
    branch = lax.psum_scatter(dot(onorm, wide_out, TN), "narrow", scatter_dimension=0, tiled=True)
    block_out = hidden_in + live_own[:, None] * branch
    g_out = lax.psum(dot(onorm, dbranch), "wide")

    dproj, d_cx, d_cbc, d_hp, d_og = run_bwd(
        proj, kept, donorm, rms, coef, out_gain[:, None], cx, cbc, hp, heads
    )
    d_normed = dot(dproj, w_in, TT)
    d_w = dot(normed, dproj, TT)
    dnormed = lax.psum_scatter(d_normed, "narrow", scatter_dimension=0, tiled=True)
    own_inv = lax.dynamic_slice_in_dim(inv_rms, row_start, own_rows, 0)[:, None]
    total_dot = jnp.sum(hidden_in * full_gain * dnormed, axis=1, keepdims=True)
    in_grad = out_cot + (
        own_inv * full_gain * dnormed - hidden_in * (own_inv**3 * total_dot / width)
    )
    d_gain = jnp.sum(hidden_in * own_inv * dnormed, axis=0)

    g_zx = lax.psum(d_w[:, 0 : 2 * chans], "wide")
    g_dt, g_cx, g_hp, g_og = lax.psum((d_w[:, 2 * chans + n4 :], d_cx, d_hp, d_og), "wide")
    g_bc, g_cbc, g_gain = lax.psum(
        (d_w[:, 2 * chans : 2 * chans + n4], d_cbc, d_gain), ("wide", "narrow")
    )
    shard = norm_gain.shape[0]
    g_ng = lax.dynamic_slice_in_dim(g_gain, narrow_id * shard, shard, 0)
    g_dt = jnp.transpose(g_dt[:, 0 : 2 * heads].reshape(width, 2, heads), (0, 2, 1))
    g_cx, g_cbc, g_og = g_cx.T, g_cbc.T, g_og[:, 0]
    g_head = jnp.concatenate(
        [
            g_hp[0 : 2 * heads, 0].reshape(2, heads),
            g_hp[0 : 2 * heads, 1].reshape(2, heads),
            g_hp[0:heads, 2].reshape(1, heads),
        ],
        axis=0,
    )
    local_squares = square_sum((g_zx, g_out, g_dt, g_cx, g_head, g_og, g_ng))
    total_squares = lax.psum(local_squares, "narrow") + square_sum((g_bc, g_cbc))
    clip_norm = jnp.sqrt(total_squares)
    factor = 1.0 / jnp.maximum(clip_norm, 1.0)
    c_zx, c_out, c_bc, c_dt = g_zx * factor, g_out * factor, g_bc * factor, g_dt * factor
    c_cx, c_cbc, c_head, c_og, c_ng = (
        g_cx * factor,
        g_cbc * factor,
        g_head * factor,
        g_og * factor,
        g_ng * factor,
    )
    halves = (c_zx[:, 0:chans], c_zx[:, chans:])
    own_zx = lax.dynamic_slice_in_dim(c_zx, wide_id * rows, rows, 0)
    own_halves = (own_zx[:, 0:chans], own_zx[:, chans:])
    left_zx = jnp.stack(
        [
            0.5 * left_statistic_gate[m, 0] + 0.5 * dot(own_halves[m], halves[m], NT)
            for m in range(2)
        ]
    )[:, None]
    right_zx = jnp.stack(
        [0.5 * stat_right_zx[m] + 0.5 * dot(halves[m], halves[m], TN) for m in range(2)]
    )
    new_zx = jnp.stack(
        [
            w_zx[m]
            - 0.5
            * dot(dot(inverse_root_left_gate[m, 0], halves[m]), inverse_root_right_gate[m])
            for m in range(2)
        ]
    )
    cols = w_out.shape[1]
    own_out = lax.dynamic_slice_in_dim(c_out, wide_id * cols, cols, 1)
    left_out = 0.5 * stat_left_out + 0.5 * dot(c_out, c_out, NT)
    right_out = 0.5 * stat_right_out + 0.5 * dot(own_out, c_out, TN)[None]
    new_out = w_out - 0.5 * dot(dot(root_left_out, c_out), root_right_out[0], NT)
    own_bc = lax.dynamic_slice_in_dim(c_bc, wide_id * rows, rows, 0)
    own_dt = lax.dynamic_slice_in_dim(c_dt, wide_id * rows, rows, 0)
    rate = 10.0
    return (
        block_out,
        in_grad,
        clip_norm,
        jnp.stack(own_halves),
        new_zx,
        left_zx,
        right_zx,
        own_out,
        new_out,
        left_out,
        right_out,
        own_bc,
        w_bc - rate * own_bc,
        own_dt,
        w_dt - rate * own_dt,
        c_cx,
        conv_x - rate * c_cx,
        c_cbc,
        conv_bc - rate * c_cbc,
        c_head,
        head_params - rate * c_head,
        c_og,
        out_gain - rate * c_og,
        c_ng,
        norm_gain - rate * c_ng,
    )


MESH = pl.DeviceIdType.MESH
MIB = 1024 * 1024


class Place:
    def __init__(self, wide):
        self.wide = wide
        self.depth = wide // 2
        self.w, self.n = lax.axis_index("wide"), lax.axis_index("narrow")
        self.z, self.x = self.w // 2, self.w % 2
        self.y, self.c = self.n // 2, self.n % 2
        self.core = (self.w, self.y * 2 + 1 - self.c)
        self.row = (self.w, (1 - self.y) * 2 + self.c)
        self.corner = (self.w, (1 - self.y) * 2 + 1 - self.c)
        self.across = (self.z * 2 + 1 - self.x, self.n)

    def group(self):
        return [self.core, self.row, self.corner]

    def along(self, k):
        return ((self.z + k) % self.depth) * 2 + self.x, self.n

    def others(self, k):
        return (self.w + k) % self.wide, self.n


class Links:
    def __init__(self, send, recv):
        self.send, self.recv, self.count, self.started = send, recv, 0, []

    def plan(self, src, dst, device):
        i = self.count
        self.count = i + 1
        item = pltpu.make_async_remote_copy(
            src_ref=src,
            dst_ref=dst,
            send_sem=self.send.at[i],
            recv_sem=self.recv.at[i],
            device_id=device,
            device_id_type=MESH,
        )
        self.started.append(item)
        return item

    def copy(self, src, dst, device):
        item = self.plan(src, dst, device)
        item.start()
        return item

    def release(self, items):
        for item in items:
            item.wait_send()
        self.started = [item for item in self.started if all(item is not done for done in items)]

    def drain(self):
        self.release(list(self.started))


def arrived(copies):
    for item in copies:
        item.wait_recv()


def begin(copies):
    for item in copies:
        item.start()


def greet(devices):
    barrier = pltpu.get_barrier_semaphore()
    for device in devices:
        pl.semaphore_signal(barrier, inc=1, device_id=device, device_id_type=MESH)
    return lambda: pl.semaphore_wait(barrier, len(devices))


def as_row(col):
    return jnp.transpose(jnp.broadcast_to(col, (col.shape[0], 128)))[0:1]


def as_col(row):
    return jnp.transpose(jnp.broadcast_to(row, (128, 128)))[:, 0:1]


def flat(v):
    return v.reshape(-1, v.shape[-1])


class Piece:
    def __init__(self, here, links, part, x_rx, z_rx, full, square):
        self.here, self.part, self.x_rx, self.z_rx = here, part, x_rx, z_rx
        self.full, self.square = full, square
        steps = range(1, here.depth)
        place, column = full.at[here.z, here.x], full.at[:, here.x]
        self.first = links.plan(part.at[:, 1 - here.x], x_rx, here.across)
        self.second = [
            links.plan(x_rx.at[(here.z + k) % here.depth], z_rx.at[k - 1], here.along(k)) for k in steps
        ]
        self.third = [links.plan(place, place, here.along(k)) for k in steps]
        self.fourth = links.plan(column, column, here.across)

    def start(self):
        self.first.start()

    def fold(self):
        self.first.wait_recv()
        for k in range(self.here.depth):
            self.x_rx[k] = self.x_rx[k] + self.part[k, self.here.x]
        begin(self.second)

    def own(self):
        arrived(self.second)
        total = self.x_rx[self.here.z]
        for k in range(1, self.here.depth):
            total = total + self.z_rx[k - 1]
        self.full[self.here.z, self.here.x] = total
        begin(self.third)
        self.square[...] = jnp.broadcast_to(total_square(total), self.square.shape)

    def spread(self):
        arrived(self.third)
        self.fourth.start()

    def finish(self):
        self.fourth.wait_recv()


def total_square(v):
    return jnp.sum(jnp.sum(v * v, axis=0, keepdims=True), axis=1, keepdims=True)


def layer_kernel(
    wide,
    heads,
    shard,
    inner_total,
    length_ref,
    hidden_ref,
    cot_ref,
    gain_ref,
    w_ref,
    wout_ref,
    bcw_ref,
    dtw_ref,
    cx_in,
    cbc_in,
    hp_in,
    og_in,
    block_ref,
    grad_ref,
    gfull,
    bc_own,
    dt_own,
    sv_sum,
    norm_ref,
    hq,
    cq,
    wz_g,
    wx_g,
    wo_g,
    bc_g,
    dt_g,
    gain_g,
    dtt,
    gain_col,
    gain_row,
    turn_s,
    cx_ref,
    cbc_ref,
    hp_ref,
    og_ref,
    live_ref,
    inv_ref,
    proj,
    y_s,
    xc,
    dx_act,
    b_s,
    c_s,
    dbc_act,
    step_s,
    cum_s,
    cumex_s,
    hcat,
    inner_s,
    don,
    onorm,
    dy_s,
    dh_s,
    db_s,
    dc_s,
    din_s,
    g_s,
    cv_s,
    v_s,
    dd_s,
    tq_s,
    cols_s,
    dcbc_s,
    dhp_s,
    dog_s,
    dgain_s,
    stat_own,
    stat_g,
    part,
    x_rx,
    z_rx,
    core_rx,
    row_rx,
    gbc,
    bc_core,
    bc_row,
    bc_mine,
    bc_rx,
    gdt,
    dt_rx,
    shared_g,
    sv_g,
    norm_n,
    norm_w,
    square_s,
    hq_hi,
    hq_lo,
    wt_hi,
    wt_lo,
    send,
    recv,
    stat_send,
    stat_recv,
):
    here = Place(wide)
    links = Links(send, recv)
    w, n, z, x, y, c, depth = here.w, here.n, here.z, here.x, here.y, here.c, here.depth
    group = here.group()
    far = [here.others(k) for k in range(1, wide)]
    own_rows, width = hidden_ref.shape
    chans, tokens = y_s.shape
    state = b_s.shape[0] // 2
    blocks = tokens // SPAN
    parts = tokens // own_rows
    thirds = chans // 128
    z_ref, x_ref, bc_ref, pre_ref = pieces(proj, chans, state)
    met = greet(group + far)
    jobs = [
        Piece(
            here, links, part.at[i if i < 2 * thirds else i - thirds], x_rx.at[i], z_rx.at[i],
            gfull.at[i], square_s.at[i],
        )
        for i in range(3 * thirds)
    ]
    z_jobs, x_jobs, o_jobs = jobs[0:thirds], jobs[thirds : 2 * thirds], jobs[2 * thirds :]

    half = bcw_ref.shape[0] // 2
    wx_g[z, x] = w_ref[1]
    bc_g[z, x, c] = bcw_ref[pl.ds(pl.multiple_of(c * half, 8), half), :]
    dt_g[z, x] = jnp.zeros(dt_g.shape[2:], F32)
    for h in range(heads):
        for i in range(2):
            row = i * heads + h
            dt_g[z, x, row : row + 1, 0 : dtw_ref.shape[2]] = dtw_ref[h, i : i + 1, :]
    line = gain_ref[...].reshape(1, shard)
    gain_g[n] = jnp.zeros(gain_g.shape[1:], F32)
    for i in range((shard + 127) // 128):
        size = min(128, shard - 128 * i)
        gain_g[n, i : i + 1, 0:size] = line[:, 128 * i : 128 * i + size]
    squares = jnp.zeros((1, own_rows), F32)
    for i in range(width // 128):
        turned = jnp.transpose(hidden_ref[:, i * 128 : (i + 1) * 128])
        squares = squares + jnp.sum(turned * turned, axis=0, keepdims=True)
        hq[n, i * 128 : (i + 1) * 128, :] = turned
    inv_ref[...] = lax.rsqrt(squares / width + 1e-05)
    for i in range(width // 128):
        hq[n, i * 128 : (i + 1) * 128, :] = hq[n, i * 128 : (i + 1) * 128, :] * inv_ref[...]
    met()

    def along(ref):
        return [links.copy(ref, ref, here.along(k)) for k in range(1, depth)]

    def exchange(ref):
        return [links.copy(ref, ref, here.row), links.copy(ref, ref, here.core)]

    class Relay:
        def __init__(self, *views):
            self.views = views
            self.direct = [along(view(z)) for view in views]
            self.passed = []

        def begin(self):
            self.passed = [links.copy(view(z), view(z), here.across) for view in self.views]

        def forward(self):
            for k in range(1, depth):
                source = (z + depth - k) % depth
                for view, copies in zip(self.views, self.direct):
                    copies[k - 1].wait_recv()
                    self.passed.append(links.copy(view(source), view(source), here.across))

        def wait(self):
            arrived(self.passed)

    h_copies = exchange(hq.at[n])
    gain_copies = [links.copy(gain_g.at[n], gain_g.at[n], device) for device in group]
    first = Relay(
        lambda i: wx_g.at[i, x], lambda i: bc_g.at[i, x, c], lambda i: dt_g.at[i, x]
    )
    first.begin()

    wz_g[z, x] = w_ref[0]
    wo_g[z, x] = wout_ref[...]
    live_ref[...] = jnp.where(iota((1, tokens), 1) < length_ref[0], 1.0, 0.0)
    live_own = live_ref[:, pl.ds(pl.multiple_of(n * own_rows, 128), own_rows)]
    for i in range(width // 128):
        cq[n, i * 128 : (i + 1) * 128, :] = jnp.transpose(cot_ref[:, i * 128 : (i + 1) * 128]) * live_own
    turn_s[...] = jnp.zeros_like(turn_s)
    for ref, out in ((cx_in, cx_ref), (cbc_in, cbc_ref)):
        for i in range(ref.shape[1] // 128):
            turn_s[0:4, :] = ref[:, i * 128 : (i + 1) * 128]
            out[i * 128 : (i + 1) * 128, :] = jnp.transpose(turn_s[...])[:, 0:4]
    turn_s[...] = jnp.zeros_like(turn_s)
    turn_s[0:1, 0:heads] = hp_in[0:1, :]
    turn_s[0:1, heads : 2 * heads] = hp_in[1:2, :]
    turn_s[1:2, 0:heads] = jnp.exp(hp_in[2:3, :])
    turn_s[1:2, heads : 2 * heads] = jnp.exp(hp_in[3:4, :])
    turn_s[2:3, 0:heads] = hp_in[4:5, :]
    hp_ref[...] = jnp.transpose(turn_s[...])[0:16, 0:3]
    og_line = og_in[...].reshape(1, chans)
    for i in range(thirds):
        og_ref[i * 128 : (i + 1) * 128, :] = as_col(og_line[:, i * 128 : (i + 1) * 128])
    cols_s[...] = jnp.zeros_like(cols_s)
    dcbc_s[...] = jnp.zeros_like(dcbc_s)
    dhp_s[...] = jnp.zeros_like(dhp_s)

    def cut(q):
        hq_hi[q], hq_lo[q] = halves(hq[q])

    cut(n)
    h_copies[1].wait_recv()
    cut(here.core[1])
    first.forward()
    second = Relay(lambda i: wz_g.at[i, x])
    h_copies[0].wait_recv()
    other = here.row[1]
    h_far = links.copy(hq.at[other], hq.at[other], here.core)
    c_copies = exchange(cq.at[n])
    arrived(gain_copies)
    for q in range(parts):
        turned = jnp.transpose(jnp.concatenate([gain_g[q], jnp.zeros((120, 128), F32)], axis=0))
        for i in range((shard + 127) // 128):
            size = min(128, shard - 128 * i)
            start = shard * q + 128 * i
            gain_col[start : start + size, :] = turned[0:size, i : i + 1]
    for i in range(width // 128):
        gain_row[:, i * 128 : (i + 1) * 128] = as_row(gain_col[i * 128 : (i + 1) * 128, :])

    def turn(ref, row, scale=True):
        for i in range(ref.shape[-1] // 128):
            cols = flat(ref[..., i * 128 : (i + 1) * 128])
            if scale:
                cols = cols * gain_col[...]
            for dst, value in zip((wt_hi, wt_lo), halves(jnp.transpose(cols))):
                dst[row + i * 128 : row + (i + 1) * 128, :] = value

    def quarter(q):
        return pl.ds(pl.multiple_of(q * own_rows, 128), own_rows)

    def each_quarter(body):
        def step(q, _):
            body(q)
            return 0

        lax.fori_loop(0, parts, step, 0)

    def rows_of(start, stop):
        return wt_hi[start:stop, :], wt_lo[start:stop, :]

    def project(out_ref, weights):
        def body(q):
            out_ref[:, quarter(q)] = product(weights(), (hq_hi[q], hq_lo[q]))

        each_quarter(body)

    first.wait()
    second.begin()
    bc_core_copy = links.copy(bc_g.at[:, :, c], bc_g.at[:, :, c], here.core)
    turn(wx_g, chans)
    lanes = width // wide
    for i in range(wide):
        dtt[:, i * lanes : (i + 1) * lanes] = dt_g[i // 2, i % 2][:, 0:lanes]
    h_far.wait_recv()
    cut(here.row[1])
    cut(here.corner[1])
    project(x_ref, lambda: rows_of(chans, 2 * chans))
    second.forward()
    third = Relay(lambda i: wo_g.at[i, x])
    third.begin()
    bc_core_copy.wait_recv()
    turn(bc_g, 2 * chans)
    project(bc_ref, lambda: rows_of(2 * chans, 2 * chans + 4 * state))
    project(pre_ref, lambda: halves(dtt[...] * gain_row[...]))
    c_copies[0].wait_recv()
    c_far = links.copy(cq.at[other], cq.at[other], here.core)
    convolve(x_ref, bc_ref, live_ref, cx_ref, cbc_ref, xc, dx_act, b_s, c_s, dbc_act)
    second.wait()
    third.forward()
    step_sizes(pre_ref, hp_ref, step_s, cum_s, cumex_s, heads)
    states(xc, b_s, step_s, cum_s, dh_s, hcat, heads)
    turn(wz_g, 0)
    project(z_ref, lambda: rows_of(0, chans))

    def stat_copy(j, b):
        return pltpu.make_async_remote_copy(
            src_ref=stat_own.at[b],
            dst_ref=stat_g.at[n, b],
            send_sem=stat_send.at[j, b],
            recv_sem=stat_recv.at[j, b],
            device_id=group[j],
            device_id_type=MESH,
        )

    def tell(b, row):
        stats = jnp.broadcast_to(row, (8, SPAN))
        stat_own[b] = stats
        stat_g[n, b] = stats
        for j in range(3):
            stat_copy(j, b).start()

    def told(b):
        for j in range(3):
            stat_copy(j, b).wait_recv()
        total = stat_g[0, b]
        for q in range(1, parts):
            total = total + stat_g[q, b]
        return total[0:1]

    def emit(b, sl, h, rows, gated, sums):
        onorm[rows, sl] = gated
        row = jnp.sum(gated * gated, axis=0, keepdims=True)
        row = row if sums is None else row + sums
        if h == heads - 1:
            tell(b, row)
        return row

    outputs(z_ref, xc, b_s, c_s, step_s, cum_s, cumex_s, hcat, hp_ref, y_s, inner_s, heads, emit)
    rms = jnp.concatenate(
        [lax.rsqrt(told(b) / inner_total + 1e-05) for b in range(blocks)], axis=1
    )

    def scale_rows(i, _):
        rows = pl.ds(pl.multiple_of(i * 8, 8), 8)
        onorm[rows, :] = onorm[rows, :] * rms * og_ref[rows, :]
        return 0

    lax.fori_loop(0, chans // 8, scale_rows, 0, unroll=2)
    c_copies[1].wait_recv()
    c_far.wait_recv()

    def weight_grad(put, right, left=lambda q: (hq_hi[q], hq_lo[q])):
        def body(q):
            put(q, product(left(q), halves(right(q)), NT))

        each_quarter(body)

    block_shape = part.shape[1:]

    def add_to(start, count):
        def put(q, value):
            for i in range(count):
                ref = part.at[start + i]
                piece = value[:, i * 128 : (i + 1) * 128].reshape(block_shape)
                ref[...] = jnp.where(q == 0, piece, ref[...] + piece)

        return put

    def scaled(i):
        part[i] = (flat(part[i]) * gain_col[...]).reshape(block_shape)

    part[...] = jnp.zeros_like(part)
    for start, stop in ((0, 1), (1, thirds)):
        rows = slice(start * 128, stop * 128)
        weight_grad(
            add_to(thirds + start, stop - start),
            lambda q, rows=rows: onorm[rows, quarter(q)],
            lambda q: halves(cq[q]),
        )
        for job in o_jobs[start:stop]:
            job.start()
    third.wait()
    turn(wo_g, 0, False)

    def donorm(q):
        don[:, quarter(q)] = product(rows_of(0, chans), halves(cq[q]))

    each_quarter(donorm)

    def inner_sums(b, _):
        sl = pl.ds(pl.multiple_of(b * SPAN, SPAN), SPAN)
        gate = z_ref[:, sl]
        gated = y_s[:, sl] * (gate * sigmoid(gate))
        tell(blocks + b, jnp.sum(gated * (don[:, sl] * og_ref[...]), axis=0, keepdims=True))
        return 0

    lax.fori_loop(0, blocks, inner_sums, 0)

    links.release(c_copies + [c_far])

    class Return:
        def __init__(self, rx, row_rx, compute, steps=((), (), (), ())):
            self.rx, self.row_rx = rx, row_rx
            first = links.count
            self.cores = [links.plan(cq.at[k * 2 + 1 - c], rx.at[k], here.core) for k in range(2)]
            self.last = links.plan(rx.at[1 - y], row_rx, here.row)

            def body(k, _):
                q = (k % 2) * 2 + (c + 1 + k // 2) % 2
                cq[q] = compute(q)

                @pl.when(k < 2)
                def _():
                    pltpu.make_async_remote_copy(
                        src_ref=cq.at[q],
                        dst_ref=rx.at[k % 2],
                        send_sem=links.send.at[first + k % 2],
                        recv_sem=links.recv.at[first + k % 2],
                        device_id=here.core,
                        device_id_type=MESH,
                    ).start()

                for at, items in enumerate(steps):

                    @pl.when(k == at)
                    def _(items=items):
                        for step in items:
                            step()

                return 0

            lax.fori_loop(0, 4, body, 0)

        def fold(self):
            arrived(self.cores)
            for k in range(2):
                self.rx[k] = self.rx[k] + cq[k * 2 + c]
            self.last.start()

        def total(self):
            self.last.wait_recv()
            return self.rx[y] + self.row_rx[...]

    o0, o1, o2 = o_jobs
    z0, z1, z2 = z_jobs
    x0, x1, x2 = x_jobs
    branch = Return(core_rx.at[0], row_rx.at[0], lambda q: dot3(flat(wo_g[...]), onorm[:, quarter(q)]))
    o0.fold()
    told_inner = jnp.concatenate([told(blocks + b) for b in range(blocks)], axis=1)
    coef = rms**3 * told_inner / inner_total
    gate_back(z_ref, y_s, don, rms, coef, og_ref, dy_s, z_ref, dog_s)
    weight_grad(add_to(0, thirds), lambda q: z_ref[:, quarter(q)])
    for i, job in enumerate(z_jobs):
        scaled(i)
        job.start()
    o1.fold()
    o0.own()

    def x_grad(i):
        links.release([o_jobs[i].first])
        part[thirds + i] = jnp.zeros(block_shape, F32)
        weight_grad(add_to(thirds + i, 1), lambda q: x_ref[i * 128 : (i + 1) * 128, quarter(q)])
        scaled(thirds + i)

    within = [
        {0: [o2.fold], 6: [o1.own, z0.fold]},
        {1: [o2.own, z2.fold], 3: [branch.fold], 5: [o1.spread]},
        {0: [z1.own], 5: [o2.spread], 6: [x1.fold]},
    ]
    between = [
        {6: [o0.spread], 7: [z1.fold]},
        {6: [z0.own, x0.fold]},
        {4: [z2.own]},
    ]

    def ticks(plan):
        def tick(b):
            for at, steps in plan.items():

                @pl.when(b == at)
                def _(steps=steps):
                    for step in steps:
                        step()

        return tick

    for i, chosen in enumerate(pairs_of(heads)):
        back_intra(
            xc, c_s, inner_s, step_s, cum_s, cumex_s, hcat, hp_ref, dy_s, y_s, dh_s, dc_s,
            din_s, g_s, cv_s, dd_s, chosen, heads, ticks(within[i]),
        )
        back_states(cum_s, hcat, dh_s, tq_s, state, chosen, heads)
        back_inter(xc, b_s, step_s, cum_s, y_s, dh_s, db_s, v_s, chosen, heads, ticks(between[i]))
        conv_x_back(x_ref, cx_ref, dx_act, y_s, x_ref, cols_s, i * 128, 128)
        x_grad(i)
        x_jobs[i].start()

    back_logs(
        b_s, c_s, pre_ref, step_s, hp_ref, pre_ref, dhp_s, db_s, dc_s, din_s, g_s, cv_s, v_s, dd_s, tq_s, heads
    )
    z0.spread()
    conv_bc_back(bc_ref, cbc_ref, dbc_act, db_s, dc_s, bc_ref, dcbc_s)
    gbc_shape = gbc.shape

    def add_bc(q, value):
        gbc[...] = jnp.where(q == 0, value.reshape(gbc_shape), gbc[...] + value.reshape(gbc_shape))

    gbc[...] = jnp.zeros_like(gbc)
    weight_grad(add_bc, lambda q: bc_ref[:, quarter(q)])
    gbc[...] = (flat(gbc[...]) * gain_col[...]).reshape(gbc_shape)
    bc_first = links.copy(gbc.at[:, :, 1 - c], bc_core, here.core)
    x0.own()
    x2.fold()
    dt_grad = jnp.zeros((16, width), F32)
    for q in range(parts):
        step = halves(pre_ref[:, q * own_rows : (q + 1) * own_rows])
        dt_grad = dt_grad + product(step, (hq_hi[q], hq_lo[q]), NT)
    dt_grad = dt_grad * gain_row[...]
    gdt[...] = jnp.zeros_like(gdt)
    for i in range(wide):
        gdt[i, :, 0:lanes] = dt_grad[:, i * lanes : (i + 1) * lanes]
    dt_rx[w] = gdt[w]
    dt_copies = [links.copy(gdt.at[device[0]], dt_rx.at[w], device) for device in far]
    dgain_s[...] = jnp.zeros_like(dgain_s)
    bc_first.wait_recv()
    for k in range(2):
        bc_core[:, k] = bc_core[:, k] + gbc[:, k, c]
    for k in range(wide):
        bc_mine[k] = bc_core[k, 1 - y]
    bc_second = links.copy(bc_mine, bc_row, here.row)

    links.release(branch.cores)

    for k in range(parts):
        pieces_of = []
        for ref, start in ((wz_g, 0), (wx_g, chans), (bc_g, 2 * chans)):
            a, b = max(k * own_rows, start), min((k + 1) * own_rows, start + ref.shape[-1])
            if a < b:
                pieces_of.append(flat(ref[..., a - start : b - start]))
        hq_hi[k], hq_lo[k] = halves(jnp.concatenate(pieces_of, axis=1))

    def normed_back(q):
        sl = quarter(q)

        def add(k, value):
            rows = pl.ds(pl.multiple_of(k * own_rows, 8), own_rows)
            return value + product((hq_hi[k], hq_lo[k]), halves(proj[rows, sl]))

        value = lax.fori_loop(0, parts, add, dot3(dtt[...], pre_ref[:, sl], TN))
        dgain_s[...] = dgain_s[...] + jnp.sum(value * hq[q], axis=1, keepdims=True)
        return value

    back = Return(core_rx.at[1], row_rx.at[1], normed_back, ([z1.spread], [], [x1.own], []))
    back.fold()
    small = 128
    shared_g[n] = jnp.zeros(shared_g.shape[1:], F32)
    for i in range(4 * state // 128):
        sl = slice(i * 128, (i + 1) * 128)
        shared_g[n, 0:4, sl] = jnp.transpose(dcbc_s[sl, :])[0:4]
    for i in range(width // 128):
        shared_g[n, 8 + i : 9 + i, 0:128] = as_row(dgain_s[i * 128 : (i + 1) * 128, :])
    shared_copies = [links.copy(shared_g.at[n], shared_g.at[n], device) for device in group]
    bc_second.wait_recv()
    links.release([bc_second])
    for k in range(wide):
        bc_mine[k] = bc_core[k, y] + bc_row[k]
    bc_rx[w] = bc_mine[w]
    bc_copies = [links.copy(bc_mine.at[device[0]], bc_rx.at[w], device) for device in far]
    sv_g[w] = jnp.zeros(sv_g.shape[1:], F32)
    for i in range(thirds):
        sl = slice(i * 128, (i + 1) * 128)
        sv_g[w, 0:4, sl] = jnp.transpose(cols_s[sl, :])[0:4]
        sv_g[w, 4:5, sl] = as_row(dog_s[sl, :])
    sv_g[w, :, chans : chans + small] = dhp_s[...]
    z2.spread()
    arrived(shared_copies)
    total = shared_g[0]
    for q in range(1, parts):
        total = total + shared_g[q]
    sv_g[w, :, chans + small :] = total
    sv_copies = [links.copy(sv_g.at[w], sv_g.at[w], device) for device in far]

    arrived(bc_copies)
    own = bc_rx[0]
    for k in range(1, wide):
        own = own + bc_rx[k]
    bc_own[n] = own
    bc_group = [links.copy(bc_own.at[n], bc_own.at[n], device) for device in group]
    squares = total_square(own)
    arrived(dt_copies)
    own = dt_rx[0]
    for k in range(1, wide):
        own = own + dt_rx[k]
    dt_own[...] = own
    squares = squares + total_square(own)
    arrived(sv_copies)
    own = sv_g[0]
    for k in range(1, wide):
        own = own + sv_g[k]
    sv_sum[...] = own
    x0.spread()
    x2.own()
    for i in range(3 * thirds):
        squares = squares + square_s[i][:, 0:1]
    once = jnp.where(w == 0, 1.0, 0.0)
    squares = squares + once * total_square(own[:, 0 : chans + small])
    squares = squares + jnp.where(n == 0, once, 0.0) * total_square(own[:, chans + small :])
    norm_n[n] = jnp.broadcast_to(squares, (8, 128))
    norm_copies = [links.copy(norm_n.at[n], norm_n.at[n], device) for device in group]

    x1.spread()

    block = branch.total() * live_ref[:, pl.ds(pl.multiple_of(n * own_rows, 128), own_rows)]
    for i in range(width // 128):
        sl = slice(i * 128, (i + 1) * 128)
        block_ref[:, sl] = hidden_ref[:, sl] + jnp.transpose(block[sl, :])
    arrived(norm_copies)
    norm_w[w] = norm_n[0] + norm_n[1] + norm_n[2] + norm_n[3]
    wide_copies = [links.copy(norm_w.at[w], norm_w.at[w], device) for device in far]
    x2.spread()
    dn = back.total() * gain_col[...]
    dots = jnp.sum(dn * hq[n], axis=0, keepdims=True) / width
    for i in range(width // 128):
        sl = slice(i * 128, (i + 1) * 128)
        value = inv_ref[...] * (dn[sl] - hq[n, sl, :] * dots)
        grad_ref[:, sl] = cot_ref[:, sl] + jnp.transpose(value)
    arrived(wide_copies)
    total = norm_w[0]
    for k in range(1, wide):
        total = total + norm_w[k]
    norm_ref[...] = jnp.sqrt(total)
    for job in jobs:
        job.finish()
    arrived(bc_group)
    links.drain()

    def sent(b, _):
        for j in range(3):
            stat_copy(j, b).wait_send()
        return 0

    lax.fori_loop(0, 2 * blocks, sent, 0)


def run_layer(lengths, hidden, cot, gain, w_zx, w_out, w_bc, dtw, cx, cbc, hp, og, heads, shard, wide, narrow):
    own_rows, width = hidden.shape
    tokens = own_rows * narrow
    chans, n4 = cx.shape[1], cbc.shape[1]
    rows = w_zx.shape[1]
    depth, blocks, half, thirds = wide // 2, tokens // SPAN, n4 // 2, chans // 128
    full, bc2, small = (chans, tokens), (half, tokens), (16, tokens)
    quarters = (narrow, width, own_rows)
    weights = (depth, 2, rows, chans)
    piece = (3 * thirds, depth, 2, rows, 128)
    quarter = (width // wide // 4, n4)
    sums = (16, chans + 128 + 256)
    shapes = [
        hidden.shape,
        hidden.shape,
        piece,
        (4,) + quarter,
        (16, 128),
        sums,
        (8, 128),
    ]
    scratch = [
        quarters,
        quarters,
        weights,
        weights,
        weights,
        (depth, 2, 2, rows // 2, n4),
        (depth, 2, 16, 128),
        (narrow, 8, 128),
        (16, width),
        (width, 1),
        (1, width),
        (128, 128),
        (chans, 4),
        (n4, 4),
        (16, 3),
        (chans, 1),
        (1, tokens),
        (1, own_rows),
        (2 * chans + n4 + 16, tokens),
        full,
        full,
        full,
        bc2,
        bc2,
        (n4, tokens),
        small,
        small,
        small,
        (blocks, chans, half),
        (blocks, SPAN, SPAN),
        full,
        full,
        full,
        (blocks, chans, half),
        bc2,
        bc2,
        (blocks, SPAN, SPAN),
        small,
        small,
        small,
        small,
        (blocks, 16, SPAN),
        (chans, 128),
        (n4, 128),
        (16, 128),
        (chans, 1),
        (width, 1),
        (2 * blocks, 8, 128),
        (narrow, 2 * blocks, 8, 128),
        (2 * thirds,) + piece[1:],
        (3 * thirds, depth, rows, 128),
        (3 * thirds, depth - 1, rows, 128),
        (2, 2, width, own_rows),
        (2, width, own_rows),
        (wide, 2, 2) + quarter,
        (wide, 2) + quarter,
        (wide,) + quarter,
        (wide,) + quarter,
        (wide,) + quarter,
        (wide, 16, 128),
        (wide, 16, 128),
        (narrow, 16, 256),
        (wide,) + sums,
        (narrow, 8, 128),
        (wide, 8, 128),
        (3 * thirds, 1, 128),
    ]
    lows = [quarters] * 2 + [(2 * chans + n4, width)] * 2
    copies = 200
    operands = (lengths, hidden, cot, gain, w_zx, w_out, w_bc, dtw, cx, cbc, hp, og)
    return pl.pallas_call(
        functools.partial(layer_kernel, wide, heads, shard, chans * narrow),
        out_shape=[jax.ShapeDtypeStruct(shape, F32) for shape in shapes],
        in_specs=[pl.BlockSpec(memory_space=pltpu.SMEM)]
        + [pl.BlockSpec(memory_space=pltpu.VMEM)] * (len(operands) - 1),
        scratch_shapes=[pltpu.VMEM(shape, F32) for shape in scratch]
        + [pltpu.VMEM(shape, jnp.bfloat16) for shape in lows]
        + [
            pltpu.SemaphoreType.DMA((copies,)),
            pltpu.SemaphoreType.DMA((copies,)),
            pltpu.SemaphoreType.DMA((3, 2 * blocks)),
            pltpu.SemaphoreType.DMA((3, 2 * blocks)),
        ],
        compiler_params=pltpu.CompilerParams(
            vmem_limit_bytes=62 * MIB, collective_id=0, has_side_effects=True
        ),
        cost_estimate=pl.CostEstimate(flops=20_000_000_000, bytes_accessed=20_000_000, transcendentals=0),
    )(*operands)


def finish_kernel(
    wide,
    narrow,
    gfull,
    bc_own,
    dt_own,
    sv,
    norm_ref,
    block_in,
    grad_in,
    stat_l,
    stat_r,
    stat_lo,
    stat_ro,
    root_l,
    root_r,
    root_lo,
    root_ro,
    w_ref,
    wout_ref,
    bcw_ref,
    dtw_ref,
    cx_ref,
    cbc_ref,
    hp_ref,
    og_ref,
    gain_ref,
    block_out,
    in_grad,
    clip,
    g_zx,
    new_zx,
    new_l,
    new_r,
    g_out,
    new_out,
    new_lo,
    new_ro,
    g_bc,
    new_bc,
    g_dt,
    new_dt,
    g_cx,
    new_cx,
    g_cbc,
    new_cbc,
    g_hp,
    new_hp,
    g_og,
    new_og,
    g_ng,
    new_ng,
    g_s,
    l_s,
    r_s,
    lo_s,
    ro_s,
    rl_s,
    rr_s,
    rlo_s,
    rro_s,
    in_sem,
    out_sem,
):
    rate = 10.0
    chans = w_ref.shape[2]
    thirds = chans // 128
    place = lax.axis_index("wide")
    z, x = place // 2, place % 2
    factor = 1.0 / jnp.maximum(norm_ref[0:1, 0:1], 1.0)
    fetches, results = [], []

    def fetch(src, dst):
        item = pltpu.make_async_copy(src, dst, in_sem.at[len(fetches)])
        item.start()
        fetches.append(item)
        return item

    def result(src, dst):
        item = pltpu.make_async_copy(src, dst, out_sem.at[len(results)])
        item.start()
        results.append(item)

    waits = []
    for m in (2, 0, 1):
        gs = g_s.at[m * thirds : (m + 1) * thirds]
        whole_m = fetch(gfull.at[m * thirds : (m + 1) * thirds], gs)
        if m == 2:
            others = [(root_ro, rro_s), (root_lo, rlo_s), (stat_ro, ro_s), (stat_lo, lo_s)]
        else:
            others = [(root_l.at[m], rl_s.at[m]), (root_r.at[m], rr_s.at[m])]
            others += [(stat_l.at[m], l_s.at[m]), (stat_r.at[m], r_s.at[m])]
        waits.append([whole_m] + [fetch(*pair) for pair in others])
    block_out[...] = block_in[...]
    in_grad[...] = grad_in[...]
    clip[...] = norm_ref[0:1, 0:1]

    def both(m):
        for item in waits[(1, 2, 0)[m]]:
            item.wait()
        parts = [flat(g_s[m * thirds + i]) for i in range(thirds)]
        mine = [g_s[m * thirds + i, z, x] for i in range(thirds)]
        return jnp.concatenate(mine, axis=1) * factor, halves(jnp.concatenate(parts, axis=1) * factor)

    own, full = both(2)
    g_out[...] = own
    ro_s[...] = 0.5 * ro_s[...] + 0.5 * product(halves(own), full, NT)
    result(ro_s, new_ro)
    lo_s[...] = 0.5 * lo_s[...] + 0.5 * product(full, full, TN)
    result(lo_s, new_lo)
    new_out[...] = wout_ref[...] - 0.5 * dot3(product(halves(rro_s[...]), full), rlo_s[...], NT)
    for m in range(2):
        own, full = both(m)
        g_zx[m] = own
        l_s[m] = 0.5 * l_s[m] + 0.5 * product(halves(own), full, NT)
        result(l_s.at[m], new_l.at[m])
        r_s[m] = 0.5 * r_s[m] + 0.5 * product(full, full, TN)
        result(r_s.at[m], new_r.at[m])
        new_zx[m] = w_ref[m] - 0.5 * dot3(product(halves(rl_s[m]), full), rr_s[m])

    grad = flat(bc_own[...]) * factor
    g_bc[...] = grad
    new_bc[...] = bcw_ref[...] - rate * grad
    heads, _, rows = dtw_ref.shape
    for h in range(heads):
        for i in range(2):
            row = i * heads + h
            grad = dt_own[row : row + 1, 0:rows] * factor
            g_dt[h, i : i + 1, :] = grad
            new_dt[h, i : i + 1, :] = dtw_ref[h, i : i + 1, :] - rate * grad
    sums = sv[...] * factor
    grad = sums[0:4, 0:chans]
    g_cx[...] = grad
    new_cx[...] = cx_ref[...] - rate * grad
    grad = sums[4:5, 0:chans]
    g_og[...] = grad.reshape(chans)
    new_og[...] = og_ref[...] - rate * g_og[...]
    n4 = cbc_ref.shape[1]
    last = chans + 128
    grad = sums[0:4, last : last + n4]
    g_cbc[...] = grad
    new_cbc[...] = cbc_ref[...] - rate * grad
    turned = jnp.transpose(
        jnp.concatenate([sums[:, chans:last], jnp.zeros((112, 128), F32)], axis=0)
    )
    for i, (row, start) in enumerate(((0, 0), (0, heads), (1, 0), (1, heads), (2, 0))):
        grad = turned[row : row + 1, start : start + heads]
        g_hp[i : i + 1, :] = grad
        new_hp[i : i + 1, :] = hp_ref[i : i + 1, :] - rate * grad
    shard = gain_ref.shape[0]
    count = narrow * shard // 128
    line = jnp.concatenate([sums[8 + i : 9 + i, last : last + 128] for i in range(count)], axis=1)
    grad = jnp.zeros((1, shard), F32)
    for q in range(narrow):
        piece = line[:, q * shard : (q + 1) * shard]
        grad = jnp.where(lax.axis_index("narrow") == q, piece, grad)
    g_ng[...] = grad.reshape(shard)
    new_ng[...] = gain_ref[...] - rate * g_ng[...]
    for item in results:
        item.wait()


def run_finish(partials, stats, roots, params, tokens_shape, wide, narrow):
    stat_l, stat_r, stat_lo, stat_ro = stats
    w_zx, w_out, w_bc, w_dt, cx, cbc, hp, og, gain = params
    like = [w_zx, w_zx, stat_l, stat_r, w_out, w_out, stat_lo, stat_ro]
    like += [item for item in (w_bc, w_dt, cx, cbc, hp, og, gain) for _ in range(2)]
    shapes = [tokens_shape, tokens_shape, (1, 1)] + [item.shape for item in like]
    far, near = pl.BlockSpec(memory_space=pl.ANY), pl.BlockSpec(memory_space=pltpu.VMEM)
    gfull = partials[0]
    kept = [gfull, stat_l, stat_r, stat_lo, stat_ro, *roots]
    return pl.pallas_call(
        functools.partial(finish_kernel, wide, narrow),
        out_shape=[jax.ShapeDtypeStruct(shape, F32) for shape in shapes],
        in_specs=[far] + [near] * 6 + [far] * 8 + [near] * len(params),
        out_specs=[near] * 5 + [far] * 2 + [near] * 2 + [far] * 2 + [near] * (len(shapes) - 11),
        scratch_shapes=[pltpu.VMEM(item.shape, F32) for item in kept]
        + [pltpu.SemaphoreType.DMA((15,)), pltpu.SemaphoreType.DMA((6,))],
        compiler_params=pltpu.CompilerParams(vmem_limit_bytes=56 * MIB),
        cost_estimate=pl.CostEstimate(flops=4_000_000_000, bytes_accessed=20_000_000, transcendentals=0),
    )(*partials, *stats, *roots, *params)


def fast_local(
    wide,
    narrow,
    hidden_in,
    out_cot,
    lengths,
    norm_gain,
    w_zx,
    w_bc,
    w_dt,
    conv_x,
    conv_bc,
    head_params,
    out_gain,
    w_out,
    left_statistic_gate,
    stat_right_zx,
    stat_left_out,
    stat_right_out,
    inverse_root_left_gate,
    inverse_root_right_gate,
    root_left_out,
    root_right_out,
):
    heads, shard = w_dt.shape[1], norm_gain.shape[0]
    out_rows, dt_rows = w_out.T, jnp.transpose(w_dt, (1, 2, 0))
    block, grad, *partials = run_layer(
        lengths,
        hidden_in,
        out_cot,
        norm_gain,
        w_zx,
        out_rows,
        w_bc,
        dt_rows,
        conv_x,
        conv_bc,
        head_params,
        out_gain,
        heads,
        shard,
        wide,
        narrow,
    )
    (
        block_out,
        in_grad,
        clip,
        g_zx,
        new_zx,
        new_l,
        new_r,
        g_out,
        new_out,
        new_lo,
        new_ro,
        g_bc,
        new_bc,
        g_dt,
        new_dt,
        *rest,
    ) = run_finish(
        (*partials, block, grad),
        (left_statistic_gate[:, 0], stat_right_zx, stat_left_out, stat_right_out[0]),
        (inverse_root_left_gate[:, 0], inverse_root_right_gate, root_left_out, root_right_out[0]),
        (w_zx, out_rows, w_bc, dt_rows, conv_x, conv_bc, head_params, out_gain, norm_gain),
        hidden_in.shape,
        wide,
        narrow,
    )
    return (
        block_out,
        in_grad,
        clip.reshape(()),
        g_zx,
        new_zx,
        new_l[:, None],
        new_r,
        g_out.T,
        new_out.T,
        new_lo,
        new_ro[None],
        g_bc,
        new_bc,
        jnp.transpose(g_dt, (2, 0, 1)),
        jnp.transpose(new_dt, (2, 0, 1)),
        *rest,
    )


def solution(mesh):
    wide, narrow = mesh.shape["wide"], mesh.shape["narrow"]
    body = functools.partial(fast_local, wide, narrow) if (wide, narrow) == (8, 4) else local
    return jax.shard_map(
        body,
        mesh=mesh,
        in_specs=(
            P(("wide", "narrow"), None),
            P(("wide", "narrow"), None),
            P("wide"),
            P("narrow"),
            P(None, "wide", "narrow"),
            P("wide", None),
            P("wide", "narrow", None),
            P(None, "narrow"),
            P(),
            P(None, "narrow"),
            P("narrow"),
            P("narrow", "wide"),
            P(None, "narrow", "wide", None),
            P(None, "narrow", None),
            P("narrow", None),
            P("narrow", "wide", None),
            P(None, "narrow", "wide", None),
            P(None, "narrow", None),
            P("narrow", None),
            P("narrow", "wide", None),
        ),
        out_specs=(
            P(("wide", "narrow"), None),
            P(("wide", "narrow"), None),
            P(),
            P(None, "wide", "narrow"),
            P(None, "wide", "narrow"),
            P(None, "narrow", "wide", None),
            P(None, "narrow", None),
            P("narrow", "wide"),
            P("narrow", "wide"),
            P("narrow", None),
            P("narrow", "wide", None),
            P("wide", None),
            P("wide", None),
            P("wide", "narrow", None),
            P("wide", "narrow", None),
            P(None, "narrow"),
            P(None, "narrow"),
            P(),
            P(),
            P(None, "narrow"),
            P(None, "narrow"),
            P("narrow"),
            P("narrow"),
            P("narrow"),
            P("narrow"),
        ),
        check_vma=False,
    )
```

```python
import functools

import jax
import jax.numpy as jnp
from jax import lax
from jax.experimental import pallas as pl
from jax.experimental.pallas import tpu as pltpu
from jax.sharding import PartitionSpec as P

SPAN = 128
WIDTH = 64
HIGH = lax.Precision.HIGH
F32 = jnp.float32
NN = (((1,), (0,)), ((), ()))
NT = (((1,), (1,)), ((), ()))
TN = (((0,), (0,)), ((), ()))
TT = (((0,), (1,)), ((), ()))


def dot(a, b, dims=NN):
    return lax.dot_general(a, b, dims, precision=HIGH, preferred_element_type=F32)


def halves(v):
    hi = v.astype(jnp.bfloat16)
    return hi, (v - hi.astype(F32)).astype(jnp.bfloat16)


def product(a, b, dims=NN):
    (ah, al), (bh, bl) = a, b
    (left,), (right,) = dims[0]
    rows, depth = ah.shape[1 - left], ah.shape[left]

    def times(u, v):
        return lax.dot_general(u, v, dims, preferred_element_type=F32)

    if depth < 128:
        return times(
            jnp.concatenate([ah, al, ah], axis=left), jnp.concatenate([bh, bh, bl], axis=right)
        )
    if depth == 128:
        top = jnp.concatenate([ah, ah], axis=left)
        low = jnp.concatenate([al, jnp.zeros_like(al)], axis=left)
        out = times(jnp.concatenate([top, low], axis=1 - left), jnp.concatenate([bh, bl], axis=right))
        return out[0:rows] + out[rows:]
    out = times(jnp.concatenate([ah, al], axis=1 - left), bh)
    return out[0:rows] + out[rows:] + times(ah, bl)


def dot3(a, b, dims=NN):
    return product(halves(a), halves(b), dims)


def sigmoid(v):
    return 1.0 / (1.0 + jnp.exp(-v))


def split3(v):
    hi = v.astype(jnp.bfloat16)
    rest = v - hi.astype(F32)
    mid = rest.astype(jnp.bfloat16)
    lo = (rest - mid.astype(F32)).astype(jnp.bfloat16)
    return jnp.concatenate([hi, mid, lo], axis=0)


def exact_dot(v, ones):
    rows = v.shape[0]
    out = lax.dot_general(split3(v), ones, NN, preferred_element_type=F32)
    return out[0:rows] + out[rows : 2 * rows] + out[2 * rows : 3 * rows]


def iota(shape, axis):
    return lax.broadcasted_iota(jnp.int32, shape, axis)


def shift_right(v, count):
    return jnp.where(iota(v.shape, 1) >= count, pltpu.roll(v, count, axis=1), 0.0)


def shift_left(v, count):
    length = v.shape[1]
    return jnp.where(iota(v.shape, 1) < length - count, pltpu.roll(v, length - count, axis=1), 0.0)


def conv_rows(v, taps):
    count = taps.shape[1]
    total = taps[:, count - 1 : count] * v
    for j in range(count - 1):
        total = total + taps[:, j : j + 1] * shift_right(v, count - 1 - j)
    return total


def pieces(ref, chans, state):
    bc = 2 * chans
    dt = bc + 4 * state
    return ref.at[0:chans], ref.at[chans:bc], ref.at[bc:dt], ref.at[dt : dt + 16]


def convolve(x_ref, bc_ref, live_ref, cx_ref, cbc_ref, xc_ref, dx_act_ref, b_ref, c_ref, dbc_act_ref):
    chans, tokens = xc_ref.shape
    state = c_ref.shape[0] // 2
    live = live_ref[...]

    def conv_x_rows(i, _):
        rows = pl.ds(pl.multiple_of(i * 8, 8), 8)
        u = conv_rows(x_ref[rows, :], cx_ref[rows, :])
        s = sigmoid(u)
        xc_ref[rows, :] = u * s * live
        dx_act_ref[rows, :] = (s + u * s * (1.0 - s)) * live
        return 0

    lax.fori_loop(0, chans // 8, conv_x_rows, 0, unroll=2)

    def conv_bc_rows(i, _, src, dst, dst_row, shift):
        rows = pl.ds(pl.multiple_of(src * state + i * 8, 8), 8)
        out = pl.ds(pl.multiple_of(dst_row + i * 8, 8), 8)
        u = conv_rows(bc_ref[rows, :], cbc_ref[rows, :])
        s = sigmoid(u)
        dbc_act_ref[rows, :] = s + u * s * (1.0 - s)
        v = u * s
        if shift == 1:
            v = shift_right(v, 1)
        if shift == -1:
            v = shift_left(v, 1)
        dst[out, :] = v
        return 0

    for src, dst, row, shift in ((0, b_ref, 0, 0), (1, c_ref, 0, 1), (2, b_ref, state, 0), (3, c_ref, state, -1)):
        lax.fori_loop(
            0,
            state // 8,
            functools.partial(conv_bc_rows, src=src, dst=dst, dst_row=row, shift=shift),
            0,
            unroll=2,
        )


def step_sizes(pre_ref, hp_ref, step_ref, cum_ref, cumex_ref, heads):
    blocks = pre_ref.shape[1] // SPAN
    pre = pre_ref[...] + hp_ref[:, 0:1]
    steps = jnp.maximum(pre, 0.0) + jnp.log1p(jnp.exp(-jnp.abs(pre)))
    step_ref[...] = steps
    logs = -hp_ref[:, 1:2] * steps
    rows16 = iota((16, SPAN), 0)
    lane16 = iota((16, SPAN), 1)
    row_q = iota((SPAN, SPAN), 0)
    lane_q = iota((SPAN, SPAN), 1)
    upto = (row_q <= lane_q).astype(F32).astype(jnp.bfloat16)
    downto = (row_q >= lane_q).astype(F32).astype(jnp.bfloat16)
    both = jnp.concatenate([upto, downto], axis=1)
    for b in range(blocks):
        sums = exact_dot(logs[:, b * SPAN : (b + 1) * SPAN], both)
        cum = jnp.where(rows16 < heads, sums[:, 0:SPAN], sums[:, SPAN : 2 * SPAN])
        ex_f = jnp.where(lane16 >= 1, pltpu.roll(cum, 1, axis=1), 0.0)
        ex_r = jnp.where(lane16 < SPAN - 1, pltpu.roll(cum, SPAN - 1, axis=1), 0.0)
        cum_ref[:, b * SPAN : (b + 1) * SPAN] = cum
        cumex_ref[:, b * SPAN : (b + 1) * SPAN] = jnp.where(rows16 < heads, ex_f, ex_r)


def states(xc_ref, b_ref, step_ref, cum_ref, sloc_ref, hcat_ref, heads):
    blocks = xc_ref.shape[1] // SPAN
    state = b_ref.shape[0] // 2

    def local_states(b, _):
        sl = pl.ds(pl.multiple_of(b * SPAN, SPAN), SPAN)
        bcat = spread(b_ref[:, sl], state)
        tail = tails(cum_ref[:, sl], step_ref[:, sl], heads)
        left = tailed(xc_ref[:, sl], tail, range(heads), heads)
        sloc_ref[b] = dot3(left, bcat, NT)
        return 0

    lax.fori_loop(0, blocks, local_states, 0)

    lane_h = iota((WIDTH, 2 * state), 1)
    for h in range(heads):
        rows = slice(h * WIDTH, (h + 1) * WIDTH)
        carry = jnp.zeros((WIDTH, 2 * state), F32)
        for i in range(blocks):
            r = blocks - 1 - i
            hcat_ref[i, rows, 0:state] = carry[:, 0:state]
            hcat_ref[r, rows, state : 2 * state] = carry[:, state : 2 * state]
            tot_f = jnp.exp(cum_ref[h : h + 1, (i + 1) * SPAN - 1 : (i + 1) * SPAN])
            tot_r = jnp.exp(cum_ref[heads + h : heads + h + 1, r * SPAN : r * SPAN + 1])
            factor = jnp.where(lane_h < state, tot_f, tot_r)
            piece = jnp.where(lane_h < state, sloc_ref[i, rows, :], sloc_ref[r, rows, :])
            carry = carry * factor + piece


def outputs(z_ref, xc_ref, b_ref, c_ref, step_ref, cum_ref, cumex_ref, hcat_ref, hp_ref, y_ref, inner_ref, heads, emit):
    blocks = xc_ref.shape[1] // SPAN
    state = b_ref.shape[0] // 2
    row_q = iota((SPAN, SPAN), 0)
    lane_q = iota((SPAN, SPAN), 1)
    lower = row_q < lane_q
    diag = row_q == lane_q

    def block(b, _):
        sl = pl.ds(pl.multiple_of(b * SPAN, SPAN), SPAN)
        bb, cc = b_ref[:, sl], c_ref[:, sl]
        inner = jnp.where(
            lower, dot3(bb[0:state], cc[0:state], TN), dot3(bb[state:], cc[state:], TN)
        )
        inner_ref[b] = inner
        cum, steps, cumex = cum_ref[:, sl], step_ref[:, sl], cumex_ref[:, sl]
        scale = jnp.exp(cumex)
        cols = columns(cum, steps)
        sums = None
        entering = dot3(hcat_ref[b], spread(cc, state))
        x_parts = halves(xc_ref[:, sl])
        for h in range(heads):
            rows = slice(h * WIDTH, (h + 1) * WIDTH)
            decay = decays(cols, cumex, lower, diag, h, heads)
            mt = jnp.where(diag, hp_ref[h : h + 1, 2:3], inner * decay)
            y = product((x_parts[0][rows], x_parts[1][rows]), halves(mt))
            y = y + entering[rows, 0:SPAN] * scale[h : h + 1]
            y = y + entering[rows, SPAN:] * scale[heads + h : heads + h + 1]
            z = z_ref[rows, sl]
            y_ref[rows, sl] = y
            sums = emit(b, sl, h, rows, y * (z * sigmoid(z)), sums)
        return 0

    lax.fori_loop(0, blocks, block, 0)


def fwd_kernel(
    heads,
    proj_ref,
    live_ref,
    cx_ref,
    cbc_ref,
    hp_ref,
    y_ref,
    xc_ref,
    dx_act_ref,
    b_ref,
    c_ref,
    dbc_act_ref,
    step_ref,
    cum_ref,
    cumex_ref,
    hcat_ref,
    inner_ref,
    gated_ref,
    sq_ref,
    sloc_ref,
):
    z_ref, x_ref, bc_ref, pre_ref = pieces(proj_ref, xc_ref.shape[0], c_ref.shape[0] // 2)
    convolve(x_ref, bc_ref, live_ref, cx_ref, cbc_ref, xc_ref, dx_act_ref, b_ref, c_ref, dbc_act_ref)
    step_sizes(pre_ref, hp_ref, step_ref, cum_ref, cumex_ref, heads)
    states(xc_ref, b_ref, step_ref, cum_ref, sloc_ref, hcat_ref, heads)

    def emit(b, sl, h, rows, gated, total):
        gated_ref[rows, sl] = gated
        part = jnp.sum(gated * gated, axis=0, keepdims=True)
        total = part if total is None else total + part
        if h == heads - 1:
            sq_ref[:, sl] = total
        return total

    outputs(z_ref, xc_ref, b_ref, c_ref, step_ref, cum_ref, cumex_ref, hcat_ref, hp_ref, y_ref, inner_ref, heads, emit)


def spread(bb, state):
    zero = jnp.zeros((state, SPAN), F32)
    top = jnp.concatenate([bb[0:state], zero], axis=1)
    low = jnp.concatenate([zero, bb[state:]], axis=1)
    return jnp.concatenate([top, low], axis=0)


def tails(cum, steps, heads):
    rows = iota((16, SPAN), 0)
    last = jnp.where(rows[:, 0:1] < heads, cum[:, SPAN - 1 : SPAN], cum[:, 0:1])
    return jnp.exp(last - cum) * steps


def tailed(xc, tail, chosen, heads):
    parts = []
    for i, h in enumerate(chosen):
        x = xc[i * WIDTH : (i + 1) * WIDTH]
        parts.append(
            jnp.concatenate([x * tail[h : h + 1], x * tail[heads + h : heads + h + 1]], axis=1)
        )
    return jnp.concatenate(parts, axis=0)


def columns(cum, steps):
    pad = jnp.zeros((SPAN - 32, SPAN), F32)
    return jnp.transpose(jnp.concatenate([cum, steps, pad], axis=0))


def decays(cols, cumex, lower, diag, h, heads):
    f, r = h, heads + h
    arg = jnp.where(
        lower, cumex[f : f + 1] - cols[:, f : f + 1], cumex[r : r + 1] - cols[:, r : r + 1]
    )
    step = jnp.where(lower, cols[:, 16 + f : 17 + f], cols[:, 16 + r : 17 + r])
    return jnp.where(diag, 0.0, jnp.exp(arg) * step)


def gate_back(z_ref, y_ref, don_ref, rms, coef, og_ref, dy_ref, dz_ref, dog_ref, onorm_ref=None):
    chans = y_ref.shape[0]

    def gate_rows(i, _):
        rows = pl.ds(pl.multiple_of(i * 8, 8), 8)
        z, y, don, og = z_ref[rows, :], y_ref[rows, :], don_ref[rows, :], og_ref[rows, :]
        s = sigmoid(z)
        act = z * s
        gated = y * act
        normed = rms * don
        dog_ref[rows, 0:1] = jnp.sum(gated * normed, axis=1, keepdims=True)
        dgated = normed * og - gated * coef
        dy_ref[rows, :] = dgated * act
        dz_ref[rows, :] = dgated * y * (s + act * (1.0 - s))
        if onorm_ref is not None:
            onorm_ref[rows, :] = gated * rms * og
        return 0

    lax.fori_loop(0, chans // 8, gate_rows, 0, unroll=2)


def back_intra(xc_ref, c_ref, inner_ref, step_ref, cum_ref, cumex_ref, hcat_ref, hp_ref, dy_s, dxc_s, dh_s, dc_s, din_s, g_s, cv_s, dd_s, chosen, heads, tick):
    blocks = xc_ref.shape[1] // SPAN
    state = c_ref.shape[0] // 2
    lower = iota((SPAN, SPAN), 0) < iota((SPAN, SPAN), 1)
    diag = iota((SPAN, SPAN), 0) == iota((SPAN, SPAN), 1)
    first = chosen[0] == 0

    def block(b, put):
        sl = pl.ds(pl.multiple_of(b * SPAN, SPAN), SPAN)
        cc = c_ref[:, sl]
        inner = inner_ref[b]
        cumex = cumex_ref[:, sl]
        scale = jnp.exp(cumex)
        cols = columns(cum_ref[:, sl], step_ref[:, sl])
        dinner = jnp.zeros((SPAN, SPAN), F32) if first else din_s[b]
        dcc = jnp.zeros((2 * state, SPAN), F32) if first else dc_s[:, sl]
        for h in chosen:
            f, r = h, heads + h
            rows = slice(h * WIDTH, (h + 1) * WIDTH)
            decay = decays(cols, cumex, lower, diag, h, heads)
            mt = inner * decay
            e_f, e_r = scale[f : f + 1], scale[r : r + 1]
            ce = jnp.concatenate([cc[0:state] * e_f, cc[state:] * e_r], axis=0)
            x = xc_ref[rows, sl]
            dy = dy_s[rows, sl]
            dy_parts = halves(dy)
            left = jnp.concatenate([x, hcat_ref[b, rows, :]], axis=1)
            back = product(halves(left), dy_parts, TN)
            dmt, dce = back[0:SPAN], back[SPAN:]
            dinner = dinner + dmt * decay
            w = dmt * mt
            over_f = jnp.sum(jnp.where(lower, w, 0.0), axis=0, keepdims=True)
            over_r = jnp.sum(jnp.where(lower, 0.0, w), axis=0, keepdims=True)
            prod = dce * ce
            put(g_s, (slice(f, f + 1), sl), over_f + jnp.sum(prod[0:state], axis=0, keepdims=True))
            put(g_s, (slice(r, r + 1), sl), over_r + jnp.sum(prod[state:], axis=0, keepdims=True))
            dcc = dcc + jnp.concatenate([dce[0:state] * e_f, dce[state:] * e_r], axis=0)
            right = jnp.concatenate(
                [jnp.where(lower, mt, 0.0), jnp.where(lower, 0.0, mt), ce], axis=0
            )
            out = product(dy_parts, halves(right), NT)
            dx_f, dx_r = out[:, 0:SPAN], out[:, SPAN : 2 * SPAN]
            put(dh_s, (b, rows, slice(None)), out[:, 2 * SPAN :])
            put(cv_s, (slice(f, f + 1), sl), jnp.sum(x * dx_f, axis=0, keepdims=True))
            put(cv_s, (slice(r, r + 1), sl), jnp.sum(x * dx_r, axis=0, keepdims=True))
            put(dd_s, (slice(h, h + 1), sl), jnp.sum(x * dy, axis=0, keepdims=True))
            put(dxc_s, (rows, sl), dx_f + dx_r + hp_ref[h : h + 1, 2:3] * dy)
        put(din_s, (b,), dinner)
        put(dc_s, (slice(None), sl), dcc)

    two_at_a_time(blocks, block, tick)


def two_at_a_time(blocks, block, tick):
    def body(i, _):
        stores = []
        for b in (2 * i, 2 * i + 1):
            block(b, lambda ref, at, value: stores.append((ref, at, value)))
        for ref, at, value in stores:
            ref[at] = value
        tick(2 * i)
        tick(2 * i + 1)
        return 0

    lax.fori_loop(0, blocks // 2, body, 0)


def back_states(cum_ref, hcat_ref, dh_s, tq_s, state, chosen, heads):
    blocks = hcat_ref.shape[0]
    lane_h = iota((WIDTH, 2 * state), 1)
    lane_1 = iota((1, 2 * state), 1)
    for h in chosen:
        rows = slice(h * WIDTH, (h + 1) * WIDTH)
        carry = jnp.zeros((WIDTH, 2 * state), F32)
        for i in range(blocks):
            f = blocks - 1 - i
            tot_f = jnp.exp(cum_ref[h : h + 1, (f + 1) * SPAN - 1 : (f + 1) * SPAN])
            tot_r = jnp.exp(cum_ref[heads + h : heads + h + 1, i * SPAN : i * SPAN + 1])
            factor = jnp.where(lane_h < state, tot_f, tot_r)
            direct = jnp.where(lane_h < state, dh_s[f, rows, :], dh_s[i, rows, :])
            kept = jnp.where(lane_h < state, hcat_ref[f, rows, :], hcat_ref[i, rows, :])
            scaled = carry * factor
            dots = jnp.sum(scaled * kept, axis=0, keepdims=True)
            q_f = jnp.sum(jnp.where(lane_1 < state, dots, 0.0), axis=1, keepdims=True)
            q_r = jnp.sum(jnp.where(lane_1 < state, 0.0, dots), axis=1, keepdims=True)
            tq_s[f, h : h + 1, :] = jnp.broadcast_to(q_f, (1, SPAN))
            tq_s[i, heads + h : heads + h + 1, :] = jnp.broadcast_to(q_r, (1, SPAN))
            dh_s[f, rows, 0:state] = carry[:, 0:state]
            dh_s[i, rows, state:] = carry[:, state:]
            carry = scaled + direct


def back_inter(xc_ref, b_ref, step_ref, cum_ref, dxc_s, dh_s, db_s, v_s, chosen, heads, tick):
    blocks = xc_ref.shape[1] // SPAN
    state = b_ref.shape[0] // 2
    first = chosen[0] == 0
    group = slice(chosen[0] * WIDTH, (chosen[-1] + 1) * WIDTH)

    def block(b, put):
        sl = pl.ds(pl.multiple_of(b * SPAN, SPAN), SPAN)
        bcat = spread(b_ref[:, sl], state)
        tail = tails(cum_ref[:, sl], step_ref[:, sl], heads)
        xc = xc_ref[group, sl]
        dxc = dxc_s[group, sl]
        dsl = halves(dh_s[b, group, :])
        dleft = product(dsl, halves(bcat))
        dbs = product(dsl, halves(tailed(xc, tail, chosen, heads)), TN)
        db = jnp.concatenate([dbs[0:state, 0:SPAN], dbs[state:, SPAN:]], axis=0)
        put(db_s, (slice(None), sl), db if first else db_s[:, sl] + db)
        parts = []
        for i, h in enumerate(chosen):
            f, r = h, heads + h
            part = slice(i * WIDTH, (i + 1) * WIDTH)
            tx_f = dleft[part, 0:SPAN] * tail[f : f + 1]
            tx_r = dleft[part, SPAN:] * tail[r : r + 1]
            put(v_s, (slice(f, f + 1), sl), jnp.sum(xc[part] * tx_f, axis=0, keepdims=True))
            put(v_s, (slice(r, r + 1), sl), jnp.sum(xc[part] * tx_r, axis=0, keepdims=True))
            parts.append(dxc[part] + tx_f + tx_r)
        put(dxc_s, (group, sl), jnp.concatenate(parts, axis=0))

    two_at_a_time(blocks, block, tick)


def back_logs(b_ref, c_ref, pre_ref, step_ref, hp_ref, ddt_ref, dhp_ref, db_s, dc_s, din_s, g_s, cv_s, v_s, dd_s, tq_s, heads):
    blocks = pre_ref.shape[1] // SPAN
    state = b_ref.shape[0] // 2
    row_q = iota((SPAN, SPAN), 0)
    lane_q = iota((SPAN, SPAN), 1)
    lower = row_q < lane_q
    strict = (row_q > lane_q).astype(F32)
    weak = (row_q >= lane_q).astype(F32)
    strict_t = (row_q < lane_q).astype(F32)
    weak_t = (row_q <= lane_q).astype(F32)
    tri = jnp.concatenate(
        [
            jnp.concatenate([strict, strict_t], axis=1),
            jnp.concatenate([weak, weak_t], axis=1),
            jnp.concatenate([strict_t, strict], axis=1),
        ],
        axis=0,
    ).astype(jnp.bfloat16)
    rows16 = iota((16, SPAN), 0)
    used = rows16 < 2 * heads
    rate = hp_ref[:, 1:2]

    def block(b, carry):
        bias_sum, log_sum, skip_sum = carry
        sl = pl.ds(pl.multiple_of(b * SPAN, SPAN), SPAN)
        dinner = din_s[b]
        both = jnp.concatenate(
            [jnp.where(lower, dinner, 0.0), jnp.where(lower, 0.0, dinner)], axis=0
        )
        dc_s[:, sl] = dc_s[:, sl] + dot3(spread(b_ref[:, sl], state), both)
        db = dot3(c_ref[:, sl], both, NT)
        db_s[0:state, sl] = db_s[0:state, sl] + db[0:state, 0:SPAN]
        db_s[state:, sl] = db_s[state:, sl] + db[state:, SPAN:]
        g = jnp.where(used, g_s[:, sl], 0.0)
        c = jnp.where(used, cv_s[:, sl], 0.0)
        v = jnp.where(used, v_s[:, sl], 0.0)
        steps = step_ref[:, sl]
        sums = exact_dot(jnp.concatenate([g, -c, v], axis=1), tri)
        dlog = jnp.where(rows16 < heads, sums[:, 0:SPAN], sums[:, SPAN:])
        dlog = dlog + jnp.where(used, tq_s[b], 0.0)
        pre = pre_ref[:, sl] + hp_ref[:, 0:1]
        small = steps < 1e-30
        ratio = jnp.where(small, 1.0, sigmoid(pre) / jnp.where(small, 1.0, steps))
        dpre = (c + v) * ratio - rate * dlog * sigmoid(pre)
        ddt_ref[:, sl] = dpre
        skip = jnp.where(rows16 < heads, dd_s[:, sl], 0.0)
        return bias_sum + dpre, log_sum - rate * dlog * steps, skip_sum + skip

    zeros16 = jnp.zeros((16, SPAN), F32)
    bias_sum, log_sum, skip = lax.fori_loop(0, blocks, block, (zeros16, zeros16, zeros16))
    dhp_ref[:, 0:1] = jnp.sum(bias_sum, axis=1, keepdims=True)
    dhp_ref[:, 1:2] = jnp.sum(log_sum, axis=1, keepdims=True)
    dhp_ref[:, 2:3] = jnp.sum(skip, axis=1, keepdims=True)


def conv_back(du, v, taps):
    count = taps.shape[1]
    dv = taps[:, count - 1 : count] * du
    sums = [jnp.sum(du * v, axis=1, keepdims=True)]
    for j in range(count - 2, -1, -1):
        moved = shift_left(du, count - 1 - j)
        dv = dv + taps[:, j : j + 1] * moved
        sums.append(jnp.sum(moved * v, axis=1, keepdims=True))
    return dv, sums[::-1]


def conv_x_back(xin_ref, cx_ref, dx_act_ref, dxc_s, dxin_ref, dcx_ref, start, count):
    def group(i, _):
        rows = pl.ds(pl.multiple_of(start + i * 8, 8), 8)
        dv, sums = conv_back(dxc_s[rows, :] * dx_act_ref[rows, :], xin_ref[rows, :], cx_ref[rows, :])
        dxin_ref[rows, :] = dv
        for j, item in enumerate(sums):
            dcx_ref[rows, j : j + 1] = item
        return 0

    lax.fori_loop(0, count // 8, group, 0, unroll=2)


def conv_bc_back(bc_ref, cbc_ref, dbc_act_ref, db_s, dc_s, dbc_ref, dcbc_ref):
    state = db_s.shape[0] // 2

    def group(i, _, src, grad, grad_row, shift):
        rows = pl.ds(pl.multiple_of(src * state + i * 8, 8), 8)
        from_rows = pl.ds(pl.multiple_of(grad_row + i * 8, 8), 8)
        d = grad[from_rows, :]
        if shift == 1:
            d = shift_left(d, 1)
        if shift == -1:
            d = shift_right(d, 1)
        dv, sums = conv_back(d * dbc_act_ref[rows, :], bc_ref[rows, :], cbc_ref[rows, :])
        dbc_ref[rows, :] = dv
        for j, item in enumerate(sums):
            dcbc_ref[rows, j : j + 1] = item
        return 0

    for src, grad, row, shift in ((0, db_s, 0, 0), (1, dc_s, 0, 1), (2, db_s, state, 0), (3, dc_s, state, -1)):
        lax.fori_loop(
            0,
            state // 8,
            functools.partial(group, src=src, grad=grad, grad_row=row, shift=shift),
            0,
            unroll=2,
        )


def pairs_of(heads):
    return [tuple(range(h, min(h + 2, heads))) for h in range(0, heads, 2)]


def bwd_kernel(
    heads,
    proj_ref,
    y_ref,
    xc_ref,
    dx_act_ref,
    b_ref,
    c_ref,
    dbc_act_ref,
    step_ref,
    cum_ref,
    cumex_ref,
    hcat_ref,
    inner_ref,
    don_ref,
    rms_ref,
    coef_ref,
    og_ref,
    cx_ref,
    cbc_ref,
    hp_ref,
    dproj_ref,
    dcx_ref,
    dcbc_ref,
    dhp_ref,
    dog_ref,
    dy_s,
    dxc_s,
    dh_s,
    db_s,
    dc_s,
    din_s,
    g_s,
    cv_s,
    v_s,
    dd_s,
    tq_s,
):
    chans, state = y_ref.shape[0], b_ref.shape[0] // 2
    z_ref, xin_ref, bc_ref, pre_ref = pieces(proj_ref, chans, state)
    dz_ref, dxin_ref, dbc_ref, ddt_ref = pieces(dproj_ref, chans, state)
    gate_back(z_ref, y_ref, don_ref, rms_ref[...], coef_ref[...], og_ref, dy_s, dz_ref, dog_ref)
    for chosen in pairs_of(heads):
        back_intra(
            xc_ref, c_ref, inner_ref, step_ref, cum_ref, cumex_ref, hcat_ref, hp_ref, dy_s, dxc_s, dh_s, dc_s,
            din_s, g_s, cv_s, dd_s, chosen, heads, lambda b: None,
        )
        back_states(cum_ref, hcat_ref, dh_s, tq_s, state, chosen, heads)
        back_inter(xc_ref, b_ref, step_ref, cum_ref, dxc_s, dh_s, db_s, v_s, chosen, heads, lambda b: None)
    conv_x_back(xin_ref, cx_ref, dx_act_ref, dxc_s, dxin_ref, dcx_ref, 0, chans)
    back_logs(
        b_ref, c_ref, pre_ref, step_ref, hp_ref, ddt_ref, dhp_ref, db_s, dc_s, din_s, g_s, cv_s, v_s, dd_s, tq_s, heads
    )
    conv_bc_back(bc_ref, cbc_ref, dbc_act_ref, db_s, dc_s, dbc_ref, dcbc_ref)


def call(kernel, out_shapes, scratch, flops):
    return pl.pallas_call(
        kernel,
        out_shape=[jax.ShapeDtypeStruct(shape, F32) for shape in out_shapes],
        scratch_shapes=[pltpu.VMEM(shape, F32) for shape in scratch],
        compiler_params=pltpu.CompilerParams(vmem_limit_bytes=56 * 1024 * 1024),
        cost_estimate=pl.CostEstimate(flops=flops, bytes_accessed=20_000_000, transcendentals=0),
    )


def run_fwd(proj, live, cx, cbc, hp, heads):
    tokens = proj.shape[1]
    chans, n4 = cx.shape[0], cbc.shape[0]
    blocks = tokens // SPAN
    full, half, rows = (chans, tokens), (n4 // 2, tokens), (16, tokens)
    return call(
        functools.partial(fwd_kernel, heads),
        [full, full, full, half, half, (n4, tokens), rows, rows, rows, (blocks, chans, n4 // 2), (blocks, SPAN, SPAN), full, (1, tokens)],
        [(blocks, chans, n4 // 2)],
        2_000_000_000,
    )(proj, live, cx, cbc, hp)


def run_bwd(proj, kept, don, rms, coef, og, cx, cbc, hp, heads):
    tokens = proj.shape[1]
    chans, n4 = cx.shape[0], cbc.shape[0]
    blocks = tokens // SPAN
    full, half, rows = (chans, tokens), (n4 // 2, tokens), (16, tokens)
    return call(
        functools.partial(bwd_kernel, heads),
        [proj.shape, (chans, 4), (n4, 4), (16, 3), (chans, 1)],
        [full, full, (blocks, chans, n4 // 2), half, half, (blocks, SPAN, SPAN), rows, rows, rows, rows, (blocks, 16, SPAN)],
        4_000_000_000,
    )(proj, *kept, don, rms, coef, og, cx, cbc, hp)


def square_sum(arrays):
    total = jnp.float32(0.0)
    for item in arrays:
        total = total + jnp.sum(item * item)
    return total


def pad_rows(v):
    return jnp.concatenate([v, jnp.zeros((16 - v.shape[0],) + v.shape[1:], v.dtype)], axis=0)


def local(
    hidden_in,
    out_cot,
    lengths,
    norm_gain,
    w_zx,
    w_bc,
    w_dt,
    conv_x,
    conv_bc,
    head_params,
    out_gain,
    w_out,
    left_statistic_gate,
    stat_right_zx,
    stat_left_out,
    stat_right_out,
    inverse_root_left_gate,
    inverse_root_right_gate,
    root_left_out,
    root_right_out,
):
    rows, chans = w_zx.shape[1], w_zx.shape[2]
    heads = w_dt.shape[1]
    n4 = w_bc.shape[1]
    own_rows, width = hidden_in.shape
    narrow_id, wide_id = lax.axis_index("narrow"), lax.axis_index("wide")

    full_in = lax.all_gather(hidden_in, "narrow", axis=0, tiled=True)
    full_gain = lax.all_gather(norm_gain, "narrow", axis=0, tiled=True)
    dt_cols = jnp.transpose(w_dt, (0, 2, 1)).reshape(rows, 2 * heads)
    own_w = jnp.concatenate(
        [w_zx[0], w_zx[1], w_bc, dt_cols, jnp.zeros((rows, 16 - 2 * heads), F32)], axis=1
    )
    w_in = lax.all_gather(own_w, "wide", axis=0, tiled=True)
    wide_out = lax.all_gather(w_out, "wide", axis=1, tiled=True)

    tokens = full_in.shape[0]
    live = (jnp.arange(tokens) < lengths[0]).astype(F32)
    row_start = narrow_id * own_rows
    live_own = lax.dynamic_slice_in_dim(live, row_start, own_rows, 0)
    dbranch = lax.all_gather(live_own[:, None] * out_cot, "narrow", axis=0, tiled=True)

    inv_rms = lax.rsqrt(jnp.mean(full_in * full_in, axis=-1) + 1e-05)
    normed = full_in * inv_rms[:, None] * full_gain
    proj = dot(w_in, normed, TT)
    cx, cbc = conv_x.T, conv_bc.T
    hp = jnp.concatenate(
        [
            pad_rows(head_params[0:2].reshape(2 * heads, 1)),
            pad_rows(jnp.exp(head_params[2:4]).reshape(2 * heads, 1)),
            pad_rows(head_params[4].reshape(heads, 1)),
        ],
        axis=1,
    )
    *kept, gated, squares = run_fwd(proj, live[None, :], cx, cbc, hp, heads)
    donorm = dot(wide_out, dbranch, NT)
    inner = jnp.sum(gated * (donorm * out_gain[:, None]), axis=0, keepdims=True)
    stats = lax.psum(jnp.concatenate([squares, inner], axis=0), "narrow")
    inner_total = chans * lax.axis_size("narrow")
    rms = lax.rsqrt(stats[0:1] / inner_total + 1e-05)
    coef = rms**3 * stats[1:2] / inner_total
    onorm = gated * rms * out_gain[:, None]
    branch = lax.psum_scatter(dot(onorm, wide_out, TN), "narrow", scatter_dimension=0, tiled=True)
    block_out = hidden_in + live_own[:, None] * branch
    g_out = lax.psum(dot(onorm, dbranch), "wide")

    dproj, d_cx, d_cbc, d_hp, d_og = run_bwd(
        proj, kept, donorm, rms, coef, out_gain[:, None], cx, cbc, hp, heads
    )
    d_normed = dot(dproj, w_in, TT)
    d_w = dot(normed, dproj, TT)
    dnormed = lax.psum_scatter(d_normed, "narrow", scatter_dimension=0, tiled=True)
    own_inv = lax.dynamic_slice_in_dim(inv_rms, row_start, own_rows, 0)[:, None]
    total_dot = jnp.sum(hidden_in * full_gain * dnormed, axis=1, keepdims=True)
    in_grad = out_cot + (
        own_inv * full_gain * dnormed - hidden_in * (own_inv**3 * total_dot / width)
    )
    d_gain = jnp.sum(hidden_in * own_inv * dnormed, axis=0)

    g_zx = lax.psum(d_w[:, 0 : 2 * chans], "wide")
    g_dt, g_cx, g_hp, g_og = lax.psum((d_w[:, 2 * chans + n4 :], d_cx, d_hp, d_og), "wide")
    g_bc, g_cbc, g_gain = lax.psum(
        (d_w[:, 2 * chans : 2 * chans + n4], d_cbc, d_gain), ("wide", "narrow")
    )
    shard = norm_gain.shape[0]
    g_ng = lax.dynamic_slice_in_dim(g_gain, narrow_id * shard, shard, 0)
    g_dt = jnp.transpose(g_dt[:, 0 : 2 * heads].reshape(width, 2, heads), (0, 2, 1))
    g_cx, g_cbc, g_og = g_cx.T, g_cbc.T, g_og[:, 0]
    g_head = jnp.concatenate(
        [
            g_hp[0 : 2 * heads, 0].reshape(2, heads),
            g_hp[0 : 2 * heads, 1].reshape(2, heads),
            g_hp[0:heads, 2].reshape(1, heads),
        ],
        axis=0,
    )
    local_squares = square_sum((g_zx, g_out, g_dt, g_cx, g_head, g_og, g_ng))
    total_squares = lax.psum(local_squares, "narrow") + square_sum((g_bc, g_cbc))
    clip_norm = jnp.sqrt(total_squares)
    factor = 1.0 / jnp.maximum(clip_norm, 1.0)
    c_zx, c_out, c_bc, c_dt = g_zx * factor, g_out * factor, g_bc * factor, g_dt * factor
    c_cx, c_cbc, c_head, c_og, c_ng = (
        g_cx * factor,
        g_cbc * factor,
        g_head * factor,
        g_og * factor,
        g_ng * factor,
    )
    halves = (c_zx[:, 0:chans], c_zx[:, chans:])
    own_zx = lax.dynamic_slice_in_dim(c_zx, wide_id * rows, rows, 0)
    own_halves = (own_zx[:, 0:chans], own_zx[:, chans:])
    left_zx = jnp.stack(
        [
            0.5 * left_statistic_gate[m, 0] + 0.5 * dot(own_halves[m], halves[m], NT)
            for m in range(2)
        ]
    )[:, None]
    right_zx = jnp.stack(
        [0.5 * stat_right_zx[m] + 0.5 * dot(halves[m], halves[m], TN) for m in range(2)]
    )
    new_zx = jnp.stack(
        [
            w_zx[m]
            - 0.5
            * dot(dot(inverse_root_left_gate[m, 0], halves[m]), inverse_root_right_gate[m])
            for m in range(2)
        ]
    )
    cols = w_out.shape[1]
    own_out = lax.dynamic_slice_in_dim(c_out, wide_id * cols, cols, 1)
    left_out = 0.5 * stat_left_out + 0.5 * dot(c_out, c_out, NT)
    right_out = 0.5 * stat_right_out + 0.5 * dot(own_out, c_out, TN)[None]
    new_out = w_out - 0.5 * dot(dot(root_left_out, c_out), root_right_out[0], NT)
    own_bc = lax.dynamic_slice_in_dim(c_bc, wide_id * rows, rows, 0)
    own_dt = lax.dynamic_slice_in_dim(c_dt, wide_id * rows, rows, 0)
    rate = 10.0
    return (
        block_out,
        in_grad,
        clip_norm,
        jnp.stack(own_halves),
        new_zx,
        left_zx,
        right_zx,
        own_out,
        new_out,
        left_out,
        right_out,
        own_bc,
        w_bc - rate * own_bc,
        own_dt,
        w_dt - rate * own_dt,
        c_cx,
        conv_x - rate * c_cx,
        c_cbc,
        conv_bc - rate * c_cbc,
        c_head,
        head_params - rate * c_head,
        c_og,
        out_gain - rate * c_og,
        c_ng,
        norm_gain - rate * c_ng,
    )


MESH = pl.DeviceIdType.MESH
MIB = 1024 * 1024


class Place:
    def __init__(self, wide):
        self.wide = wide
        self.depth = wide // 2
        self.w, self.n = lax.axis_index("wide"), lax.axis_index("narrow")
        self.z, self.x = self.w // 2, self.w % 2
        self.y, self.c = self.n // 2, self.n % 2
        self.core = (self.w, self.y * 2 + 1 - self.c)
        self.row = (self.w, (1 - self.y) * 2 + self.c)
        self.corner = (self.w, (1 - self.y) * 2 + 1 - self.c)
        self.across = (self.z * 2 + 1 - self.x, self.n)

    def group(self):
        return [self.core, self.row, self.corner]

    def along(self, k):
        return ((self.z + k) % self.depth) * 2 + self.x, self.n

    def others(self, k):
        return (self.w + k) % self.wide, self.n


class Links:
    def __init__(self, send, recv):
        self.send, self.recv, self.count, self.started = send, recv, 0, []

    def plan(self, src, dst, device):
        i = self.count
        self.count = i + 1
        item = pltpu.make_async_remote_copy(
            src_ref=src,
            dst_ref=dst,
            send_sem=self.send.at[i],
            recv_sem=self.recv.at[i],
            device_id=device,
            device_id_type=MESH,
        )
        self.started.append(item)
        return item

    def copy(self, src, dst, device):
        item = self.plan(src, dst, device)
        item.start()
        return item

    def release(self, items):
        for item in items:
            item.wait_send()
        self.started = [item for item in self.started if all(item is not done for done in items)]

    def drain(self):
        self.release(list(self.started))


def arrived(copies):
    for item in copies:
        item.wait_recv()


def begin(copies):
    for item in copies:
        item.start()


def greet(devices):
    barrier = pltpu.get_barrier_semaphore()
    for device in devices:
        pl.semaphore_signal(barrier, inc=1, device_id=device, device_id_type=MESH)
    return lambda: pl.semaphore_wait(barrier, len(devices))


def as_row(col):
    return jnp.transpose(jnp.broadcast_to(col, (col.shape[0], 128)))[0:1]


def as_col(row):
    return jnp.transpose(jnp.broadcast_to(row, (128, 128)))[:, 0:1]


def flat(v):
    return v.reshape(-1, v.shape[-1])


class Piece:
    def __init__(self, here, links, part, x_rx, z_rx, full, square):
        self.here, self.part, self.x_rx, self.z_rx = here, part, x_rx, z_rx
        self.full, self.square = full, square
        steps = range(1, here.depth)
        place, column = full.at[here.z, here.x], full.at[:, here.x]
        self.first = links.plan(part.at[:, 1 - here.x], x_rx, here.across)
        self.second = [
            links.plan(x_rx.at[(here.z + k) % here.depth], z_rx.at[k - 1], here.along(k)) for k in steps
        ]
        self.third = [links.plan(place, place, here.along(k)) for k in steps]
        self.fourth = links.plan(column, column, here.across)

    def start(self):
        self.first.start()

    def fold(self):
        self.first.wait_recv()
        for k in range(self.here.depth):
            self.x_rx[k] = self.x_rx[k] + self.part[k, self.here.x]
        begin(self.second)

    def own(self):
        arrived(self.second)
        total = self.x_rx[self.here.z]
        for k in range(1, self.here.depth):
            total = total + self.z_rx[k - 1]
        self.full[self.here.z, self.here.x] = total
        begin(self.third)
        self.square[...] = jnp.broadcast_to(total_square(total), self.square.shape)

    def spread(self):
        arrived(self.third)
        self.fourth.start()

    def finish(self):
        self.fourth.wait_recv()


def total_square(v):
    return jnp.sum(jnp.sum(v * v, axis=0, keepdims=True), axis=1, keepdims=True)


def layer_kernel(
    wide,
    heads,
    shard,
    inner_total,
    length_ref,
    hidden_ref,
    cot_ref,
    gain_ref,
    w_ref,
    wout_ref,
    bcw_ref,
    dtw_ref,
    cx_in,
    cbc_in,
    hp_in,
    og_in,
    block_ref,
    grad_ref,
    gfull,
    bc_own,
    dt_own,
    sv_sum,
    norm_ref,
    hq,
    cq,
    wz_g,
    wx_g,
    wo_g,
    bc_g,
    dt_g,
    gain_g,
    dtt,
    gain_col,
    gain_row,
    turn_s,
    cx_ref,
    cbc_ref,
    hp_ref,
    og_ref,
    live_ref,
    inv_ref,
    proj,
    y_s,
    xc,
    dx_act,
    b_s,
    c_s,
    dbc_act,
    step_s,
    cum_s,
    cumex_s,
    hcat,
    inner_s,
    don,
    onorm,
    dy_s,
    dh_s,
    db_s,
    dc_s,
    din_s,
    g_s,
    cv_s,
    v_s,
    dd_s,
    tq_s,
    cols_s,
    dcbc_s,
    dhp_s,
    dog_s,
    dgain_s,
    stat_own,
    stat_g,
    part,
    x_rx,
    z_rx,
    core_rx,
    row_rx,
    gbc,
    bc_core,
    bc_row,
    bc_mine,
    bc_rx,
    gdt,
    dt_rx,
    shared_g,
    sv_g,
    norm_n,
    norm_w,
    square_s,
    hq_hi,
    hq_lo,
    wt_hi,
    wt_lo,
    send,
    recv,
    stat_send,
    stat_recv,
):
    here = Place(wide)
    links = Links(send, recv)
    w, n, z, x, y, c, depth = here.w, here.n, here.z, here.x, here.y, here.c, here.depth
    group = here.group()
    far = [here.others(k) for k in range(1, wide)]
    own_rows, width = hidden_ref.shape
    chans, tokens = y_s.shape
    state = b_s.shape[0] // 2
    blocks = tokens // SPAN
    parts = tokens // own_rows
    thirds = chans // 128
    z_ref, x_ref, bc_ref, pre_ref = pieces(proj, chans, state)
    met = greet(group + far)
    jobs = [
        Piece(
            here, links, part.at[i if i < 2 * thirds else i - thirds], x_rx.at[i], z_rx.at[i],
            gfull.at[i], square_s.at[i],
        )
        for i in range(3 * thirds)
    ]
    z_jobs, x_jobs, o_jobs = jobs[0:thirds], jobs[thirds : 2 * thirds], jobs[2 * thirds :]

    half = bcw_ref.shape[0] // 2
    wx_g[z, x] = w_ref[1]
    bc_g[z, x, c] = bcw_ref[pl.ds(pl.multiple_of(c * half, 8), half), :]
    dt_g[z, x] = jnp.zeros(dt_g.shape[2:], F32)
    for h in range(heads):
        for i in range(2):
            row = i * heads + h
            dt_g[z, x, row : row + 1, 0 : dtw_ref.shape[2]] = dtw_ref[h, i : i + 1, :]
    line = gain_ref[...].reshape(1, shard)
    gain_g[n] = jnp.zeros(gain_g.shape[1:], F32)
    for i in range((shard + 127) // 128):
        size = min(128, shard - 128 * i)
        gain_g[n, i : i + 1, 0:size] = line[:, 128 * i : 128 * i + size]
    squares = jnp.zeros((1, own_rows), F32)
    for i in range(width // 128):
        turned = jnp.transpose(hidden_ref[:, i * 128 : (i + 1) * 128])
        squares = squares + jnp.sum(turned * turned, axis=0, keepdims=True)
        hq[n, i * 128 : (i + 1) * 128, :] = turned
    inv_ref[...] = lax.rsqrt(squares / width + 1e-05)
    for i in range(width // 128):
        hq[n, i * 128 : (i + 1) * 128, :] = hq[n, i * 128 : (i + 1) * 128, :] * inv_ref[...]
    met()

    def along(ref):
        return [links.copy(ref, ref, here.along(k)) for k in range(1, depth)]

    def exchange(ref):
        return [links.copy(ref, ref, here.row), links.copy(ref, ref, here.core)]

    class Relay:
        def __init__(self, *views):
            self.views = views
            self.direct = [along(view(z)) for view in views]
            self.passed = []

        def begin(self):
            self.passed = [links.copy(view(z), view(z), here.across) for view in self.views]

        def forward(self):
            for k in range(1, depth):
                source = (z + depth - k) % depth
                for view, copies in zip(self.views, self.direct):
                    copies[k - 1].wait_recv()
                    self.passed.append(links.copy(view(source), view(source), here.across))

        def wait(self):
            arrived(self.passed)

    h_copies = exchange(hq.at[n])
    gain_copies = [links.copy(gain_g.at[n], gain_g.at[n], device) for device in group]
    early = Relay(lambda i: bc_g.at[i, x, c], lambda i: dt_g.at[i, x])
    early.begin()
    first = Relay(lambda i: wx_g.at[i, x])
    first.begin()

    wz_g[z, x] = w_ref[0]
    wo_g[z, x] = wout_ref[...]
    live_ref[...] = jnp.where(iota((1, tokens), 1) < length_ref[0], 1.0, 0.0)
    live_own = live_ref[:, pl.ds(pl.multiple_of(n * own_rows, 128), own_rows)]
    for i in range(width // 128):
        cq[n, i * 128 : (i + 1) * 128, :] = jnp.transpose(cot_ref[:, i * 128 : (i + 1) * 128]) * live_own
    turn_s[...] = jnp.zeros_like(turn_s)
    for ref, out in ((cx_in, cx_ref), (cbc_in, cbc_ref)):
        for i in range(ref.shape[1] // 128):
            turn_s[0:4, :] = ref[:, i * 128 : (i + 1) * 128]
            out[i * 128 : (i + 1) * 128, :] = jnp.transpose(turn_s[...])[:, 0:4]
    turn_s[...] = jnp.zeros_like(turn_s)
    turn_s[0:1, 0:heads] = hp_in[0:1, :]
    turn_s[0:1, heads : 2 * heads] = hp_in[1:2, :]
    turn_s[1:2, 0:heads] = jnp.exp(hp_in[2:3, :])
    turn_s[1:2, heads : 2 * heads] = jnp.exp(hp_in[3:4, :])
    turn_s[2:3, 0:heads] = hp_in[4:5, :]
    hp_ref[...] = jnp.transpose(turn_s[...])[0:16, 0:3]
    og_line = og_in[...].reshape(1, chans)
    for i in range(thirds):
        og_ref[i * 128 : (i + 1) * 128, :] = as_col(og_line[:, i * 128 : (i + 1) * 128])
    cols_s[...] = jnp.zeros_like(cols_s)
    dcbc_s[...] = jnp.zeros_like(dcbc_s)
    dhp_s[...] = jnp.zeros_like(dhp_s)

    def cut(q):
        hq_hi[q], hq_lo[q] = halves(hq[q])

    cut(n)
    h_copies[1].wait_recv()
    cut(here.core[1])
    early.forward()
    first.forward()
    second = Relay(lambda i: wz_g.at[i, x])
    h_copies[0].wait_recv()
    other = here.row[1]
    h_far = links.copy(hq.at[other], hq.at[other], here.core)
    c_copies = exchange(cq.at[n])
    arrived(gain_copies)
    for q in range(parts):
        turned = jnp.transpose(jnp.concatenate([gain_g[q], jnp.zeros((120, 128), F32)], axis=0))
        for i in range((shard + 127) // 128):
            size = min(128, shard - 128 * i)
            start = shard * q + 128 * i
            gain_col[start : start + size, :] = turned[0:size, i : i + 1]
    for i in range(width // 128):
        gain_row[:, i * 128 : (i + 1) * 128] = as_row(gain_col[i * 128 : (i + 1) * 128, :])

    def turn(ref, row, scale=True):
        for i in range(ref.shape[-1] // 128):
            cols = flat(ref[..., i * 128 : (i + 1) * 128])
            if scale:
                cols = cols * gain_col[...]
            for dst, value in zip((wt_hi, wt_lo), halves(jnp.transpose(cols))):
                dst[row + i * 128 : row + (i + 1) * 128, :] = value

    def quarter(q):
        return pl.ds(pl.multiple_of(q * own_rows, 128), own_rows)

    def each_quarter(body):
        def step(q, _):
            body(q)
            return 0

        lax.fori_loop(0, parts, step, 0)

    def rows_of(start, stop):
        return wt_hi[start:stop, :], wt_lo[start:stop, :]

    def project(out_ref, weights):
        def body(q):
            out_ref[:, quarter(q)] = product(weights(), (hq_hi[q], hq_lo[q]))

        each_quarter(body)

    early.wait()
    bc_core_copy = links.copy(bc_g.at[:, :, c], bc_g.at[:, :, c], here.core)
    lanes = width // wide
    for i in range(wide):
        dtt[:, i * lanes : (i + 1) * lanes] = dt_g[i // 2, i % 2][:, 0:lanes]
    last = 2 * chans + 4 * state
    wt_hi[last:, :], wt_lo[last:, :] = halves(dtt[...] * gain_row[...])
    bc_core_copy.wait_recv()
    turn(bc_g, 2 * chans)
    first.wait()
    second.begin()
    turn(wx_g, chans)
    h_far.wait_recv()
    cut(here.row[1])
    cut(here.corner[1])
    project(proj.at[chans:], lambda: rows_of(chans, last + 16))
    second.forward()
    third = Relay(lambda i: wo_g.at[i, x])
    third.begin()
    c_copies[0].wait_recv()
    c_far = links.copy(cq.at[other], cq.at[other], here.core)
    convolve(x_ref, bc_ref, live_ref, cx_ref, cbc_ref, xc, dx_act, b_s, c_s, dbc_act)
    second.wait()
    third.forward()
    step_sizes(pre_ref, hp_ref, step_s, cum_s, cumex_s, heads)
    states(xc, b_s, step_s, cum_s, dh_s, hcat, heads)
    turn(wz_g, 0)
    project(z_ref, lambda: rows_of(0, chans))

    def stat_copy(j, b):
        return pltpu.make_async_remote_copy(
            src_ref=stat_own.at[b],
            dst_ref=stat_g.at[n, b],
            send_sem=stat_send.at[j, b],
            recv_sem=stat_recv.at[j, b],
            device_id=group[j],
            device_id_type=MESH,
        )

    def tell(b, row):
        stats = jnp.broadcast_to(row, (8, SPAN))
        stat_own[b] = stats
        stat_g[n, b] = stats
        for j in range(3):
            stat_copy(j, b).start()

    def told(b):
        for j in range(3):
            stat_copy(j, b).wait_recv()
        total = stat_g[0, b]
        for q in range(1, parts):
            total = total + stat_g[q, b]
        return total[0:1]

    def emit(b, sl, h, rows, gated, sums):
        onorm[rows, sl] = gated
        row = jnp.sum(gated * gated, axis=0, keepdims=True)
        row = row if sums is None else row + sums
        if h == heads - 1:
            tell(b, row)
        return row

    outputs(z_ref, xc, b_s, c_s, step_s, cum_s, cumex_s, hcat, hp_ref, y_s, inner_s, heads, emit)
    rms = jnp.concatenate(
        [lax.rsqrt(told(b) / inner_total + 1e-05) for b in range(blocks)], axis=1
    )

    def scale_rows(i, _):
        rows = pl.ds(pl.multiple_of(i * 8, 8), 8)
        onorm[rows, :] = onorm[rows, :] * rms * og_ref[rows, :]
        return 0

    lax.fori_loop(0, chans // 8, scale_rows, 0, unroll=2)
    c_copies[1].wait_recv()
    c_far.wait_recv()

    def weight_grad(put, right, left=lambda q: (hq_hi[q], hq_lo[q])):
        def body(q):
            put(q, product(left(q), halves(right(q)), NT))

        each_quarter(body)

    block_shape = part.shape[1:]

    def add_to(start, count):
        def put(q, value):
            for i in range(count):
                ref = part.at[start + i]
                piece = value[:, i * 128 : (i + 1) * 128].reshape(block_shape)
                ref[...] = jnp.where(q == 0, piece, ref[...] + piece)

        return put

    def scaled(i):
        part[i] = (flat(part[i]) * gain_col[...]).reshape(block_shape)

    part[...] = jnp.zeros_like(part)
    for start, stop in ((0, 1), (1, thirds)):
        rows = slice(start * 128, stop * 128)
        weight_grad(
            add_to(thirds + start, stop - start),
            lambda q, rows=rows: onorm[rows, quarter(q)],
            lambda q: halves(cq[q]),
        )
        for job in o_jobs[start:stop]:
            job.start()
    third.wait()
    turn(wo_g, 0, False)

    def donorm(q):
        don[:, quarter(q)] = product(rows_of(0, chans), halves(cq[q]))

    each_quarter(donorm)

    def inner_sums(b, _):
        sl = pl.ds(pl.multiple_of(b * SPAN, SPAN), SPAN)
        gate = z_ref[:, sl]
        gated = y_s[:, sl] * (gate * sigmoid(gate))
        tell(blocks + b, jnp.sum(gated * (don[:, sl] * og_ref[...]), axis=0, keepdims=True))
        return 0

    lax.fori_loop(0, blocks, inner_sums, 0)

    links.release(c_copies + [c_far])

    class Return:
        def __init__(self, rx, row_rx, compute, steps=((), (), (), ())):
            self.rx, self.row_rx = rx, row_rx
            first = links.count
            self.cores = [links.plan(cq.at[k * 2 + 1 - c], rx.at[k], here.core) for k in range(2)]
            self.last = links.plan(rx.at[1 - y], row_rx, here.row)

            def body(k, _):
                q = (k % 2) * 2 + (c + 1 + k // 2) % 2
                cq[q] = compute(q)

                @pl.when(k < 2)
                def _():
                    pltpu.make_async_remote_copy(
                        src_ref=cq.at[q],
                        dst_ref=rx.at[k % 2],
                        send_sem=links.send.at[first + k % 2],
                        recv_sem=links.recv.at[first + k % 2],
                        device_id=here.core,
                        device_id_type=MESH,
                    ).start()

                for at, items in enumerate(steps):

                    @pl.when(k == at)
                    def _(items=items):
                        for step in items:
                            step()

                return 0

            lax.fori_loop(0, 4, body, 0)

        def fold(self):
            arrived(self.cores)
            for k in range(2):
                self.rx[k] = self.rx[k] + cq[k * 2 + c]
            self.last.start()

        def total(self):
            self.last.wait_recv()
            return self.rx[y] + self.row_rx[...]

    o0, o1, o2 = o_jobs
    z0, z1, z2 = z_jobs
    x0, x1, x2 = x_jobs
    branch = Return(core_rx.at[0], row_rx.at[0], lambda q: dot3(flat(wo_g[...]), onorm[:, quarter(q)]))
    o0.fold()
    told_inner = jnp.concatenate([told(blocks + b) for b in range(blocks)], axis=1)
    coef = rms**3 * told_inner / inner_total
    gate_back(z_ref, y_s, don, rms, coef, og_ref, dy_s, z_ref, dog_s)
    weight_grad(add_to(0, thirds), lambda q: z_ref[:, quarter(q)])
    for i, job in enumerate(z_jobs):
        scaled(i)
        job.start()
    o1.fold()
    o0.own()

    def x_grad(i):
        links.release([o_jobs[i].first])
        part[thirds + i] = jnp.zeros(block_shape, F32)
        weight_grad(add_to(thirds + i, 1), lambda q: x_ref[i * 128 : (i + 1) * 128, quarter(q)])
        scaled(thirds + i)

    within = [
        {0: [o2.fold], 6: [o1.own, z0.fold]},
        {1: [o2.own, z2.fold], 3: [branch.fold], 5: [o1.spread]},
        {0: [z1.own], 5: [o2.spread], 6: [x1.fold]},
    ]
    between = [
        {6: [o0.spread], 7: [z1.fold]},
        {6: [z0.own, x0.fold]},
        {4: [z2.own]},
    ]

    def ticks(plan):
        def tick(b):
            for at, steps in plan.items():

                @pl.when(b == at)
                def _(steps=steps):
                    for step in steps:
                        step()

        return tick

    for i, chosen in enumerate(pairs_of(heads)):
        back_intra(
            xc, c_s, inner_s, step_s, cum_s, cumex_s, hcat, hp_ref, dy_s, y_s, dh_s, dc_s,
            din_s, g_s, cv_s, dd_s, chosen, heads, ticks(within[i]),
        )
        back_states(cum_s, hcat, dh_s, tq_s, state, chosen, heads)
        back_inter(xc, b_s, step_s, cum_s, y_s, dh_s, db_s, v_s, chosen, heads, ticks(between[i]))
        conv_x_back(x_ref, cx_ref, dx_act, y_s, x_ref, cols_s, i * 128, 128)
        x_grad(i)
        x_jobs[i].start()

    back_logs(
        b_s, c_s, pre_ref, step_s, hp_ref, pre_ref, dhp_s, db_s, dc_s, din_s, g_s, cv_s, v_s, dd_s, tq_s, heads
    )
    z0.spread()
    conv_bc_back(bc_ref, cbc_ref, dbc_act, db_s, dc_s, bc_ref, dcbc_s)
    gbc_shape = gbc.shape

    def add_bc(q, value):
        gbc[...] = jnp.where(q == 0, value.reshape(gbc_shape), gbc[...] + value.reshape(gbc_shape))

    gbc[...] = jnp.zeros_like(gbc)
    weight_grad(add_bc, lambda q: bc_ref[:, quarter(q)])
    gbc[...] = (flat(gbc[...]) * gain_col[...]).reshape(gbc_shape)
    bc_first = links.copy(gbc.at[:, :, 1 - c], bc_core, here.core)
    x0.own()
    x2.fold()
    dt_grad = jnp.zeros((16, width), F32)
    for q in range(parts):
        step = halves(pre_ref[:, q * own_rows : (q + 1) * own_rows])
        dt_grad = dt_grad + product(step, (hq_hi[q], hq_lo[q]), NT)
    dt_grad = dt_grad * gain_row[...]
    gdt[...] = jnp.zeros_like(gdt)
    for i in range(wide):
        gdt[i, :, 0:lanes] = dt_grad[:, i * lanes : (i + 1) * lanes]
    dt_rx[w] = gdt[w]
    dt_copies = [links.copy(gdt.at[device[0]], dt_rx.at[w], device) for device in far]
    dgain_s[...] = jnp.zeros_like(dgain_s)
    bc_first.wait_recv()
    for k in range(2):
        bc_core[:, k] = bc_core[:, k] + gbc[:, k, c]
    for k in range(wide):
        bc_mine[k] = bc_core[k, 1 - y]
    bc_second = links.copy(bc_mine, bc_row, here.row)

    links.release(branch.cores)

    for k in range(parts):
        pieces_of = []
        for ref, start in ((wz_g, 0), (wx_g, chans), (bc_g, 2 * chans)):
            a, b = max(k * own_rows, start), min((k + 1) * own_rows, start + ref.shape[-1])
            if a < b:
                pieces_of.append(flat(ref[..., a - start : b - start]))
        hq_hi[k], hq_lo[k] = halves(jnp.concatenate(pieces_of, axis=1))

    def normed_back(q):
        sl = quarter(q)

        def add(k, value):
            rows = pl.ds(pl.multiple_of(k * own_rows, 8), own_rows)
            return value + product((hq_hi[k], hq_lo[k]), halves(proj[rows, sl]))

        value = lax.fori_loop(0, parts, add, dot3(dtt[...], pre_ref[:, sl], TN))
        dgain_s[...] = dgain_s[...] + jnp.sum(value * hq[q], axis=1, keepdims=True)
        return value

    back = Return(core_rx.at[1], row_rx.at[1], normed_back, ([z1.spread], [], [x1.own], []))
    back.fold()
    small = 128
    shared_g[n] = jnp.zeros(shared_g.shape[1:], F32)
    for i in range(4 * state // 128):
        sl = slice(i * 128, (i + 1) * 128)
        shared_g[n, 0:4, sl] = jnp.transpose(dcbc_s[sl, :])[0:4]
    for i in range(width // 128):
        shared_g[n, 8 + i : 9 + i, 0:128] = as_row(dgain_s[i * 128 : (i + 1) * 128, :])
    shared_copies = [links.copy(shared_g.at[n], shared_g.at[n], device) for device in group]
    bc_second.wait_recv()
    links.release([bc_second])
    for k in range(wide):
        bc_mine[k] = bc_core[k, y] + bc_row[k]
    bc_rx[w] = bc_mine[w]
    bc_copies = [links.copy(bc_mine.at[device[0]], bc_rx.at[w], device) for device in far]
    sv_g[w] = jnp.zeros(sv_g.shape[1:], F32)
    for i in range(thirds):
        sl = slice(i * 128, (i + 1) * 128)
        sv_g[w, 0:4, sl] = jnp.transpose(cols_s[sl, :])[0:4]
        sv_g[w, 4:5, sl] = as_row(dog_s[sl, :])
    sv_g[w, :, chans : chans + small] = dhp_s[...]
    z2.spread()
    arrived(shared_copies)
    total = shared_g[0]
    for q in range(1, parts):
        total = total + shared_g[q]
    sv_g[w, :, chans + small :] = total
    sv_copies = [links.copy(sv_g.at[w], sv_g.at[w], device) for device in far]

    arrived(bc_copies)
    own = bc_rx[0]
    for k in range(1, wide):
        own = own + bc_rx[k]
    bc_own[n] = own
    bc_group = [links.copy(bc_own.at[n], bc_own.at[n], device) for device in group]
    squares = total_square(own)
    arrived(dt_copies)
    own = dt_rx[0]
    for k in range(1, wide):
        own = own + dt_rx[k]
    dt_own[...] = own
    squares = squares + total_square(own)
    arrived(sv_copies)
    own = sv_g[0]
    for k in range(1, wide):
        own = own + sv_g[k]
    sv_sum[...] = own
    x0.spread()
    x2.own()
    for i in range(3 * thirds):
        squares = squares + square_s[i][:, 0:1]
    once = jnp.where(w == 0, 1.0, 0.0)
    squares = squares + once * total_square(own[:, 0 : chans + small])
    squares = squares + jnp.where(n == 0, once, 0.0) * total_square(own[:, chans + small :])
    norm_n[n] = jnp.broadcast_to(squares, (8, 128))
    norm_copies = [links.copy(norm_n.at[n], norm_n.at[n], device) for device in group]

    x1.spread()

    block = branch.total() * live_ref[:, pl.ds(pl.multiple_of(n * own_rows, 128), own_rows)]
    for i in range(width // 128):
        sl = slice(i * 128, (i + 1) * 128)
        block_ref[:, sl] = hidden_ref[:, sl] + jnp.transpose(block[sl, :])
    arrived(norm_copies)
    norm_w[w] = norm_n[0] + norm_n[1] + norm_n[2] + norm_n[3]
    wide_copies = [links.copy(norm_w.at[w], norm_w.at[w], device) for device in far]
    x2.spread()
    dn = back.total() * gain_col[...]
    dots = jnp.sum(dn * hq[n], axis=0, keepdims=True) / width
    for i in range(width // 128):
        sl = slice(i * 128, (i + 1) * 128)
        value = inv_ref[...] * (dn[sl] - hq[n, sl, :] * dots)
        grad_ref[:, sl] = cot_ref[:, sl] + jnp.transpose(value)
    arrived(wide_copies)
    total = norm_w[0]
    for k in range(1, wide):
        total = total + norm_w[k]
    norm_ref[...] = jnp.sqrt(total)
    for job in jobs:
        job.finish()
    arrived(bc_group)
    links.drain()

    def sent(b, _):
        for j in range(3):
            stat_copy(j, b).wait_send()
        return 0

    lax.fori_loop(0, 2 * blocks, sent, 0)


def run_layer(lengths, hidden, cot, gain, w_zx, w_out, w_bc, dtw, cx, cbc, hp, og, heads, shard, wide, narrow):
    own_rows, width = hidden.shape
    tokens = own_rows * narrow
    chans, n4 = cx.shape[1], cbc.shape[1]
    rows = w_zx.shape[1]
    depth, blocks, half, thirds = wide // 2, tokens // SPAN, n4 // 2, chans // 128
    full, bc2, small = (chans, tokens), (half, tokens), (16, tokens)
    quarters = (narrow, width, own_rows)
    weights = (depth, 2, rows, chans)
    piece = (3 * thirds, depth, 2, rows, 128)
    quarter = (width // wide // 4, n4)
    sums = (16, chans + 128 + 256)
    shapes = [
        hidden.shape,
        hidden.shape,
        piece,
        (4,) + quarter,
        (16, 128),
        sums,
        (8, 128),
    ]
    scratch = [
        quarters,
        quarters,
        weights,
        weights,
        weights,
        (depth, 2, 2, rows // 2, n4),
        (depth, 2, 16, 128),
        (narrow, 8, 128),
        (16, width),
        (width, 1),
        (1, width),
        (128, 128),
        (chans, 4),
        (n4, 4),
        (16, 3),
        (chans, 1),
        (1, tokens),
        (1, own_rows),
        (2 * chans + n4 + 16, tokens),
        full,
        full,
        full,
        bc2,
        bc2,
        (n4, tokens),
        small,
        small,
        small,
        (blocks, chans, half),
        (blocks, SPAN, SPAN),
        full,
        full,
        full,
        (blocks, chans, half),
        bc2,
        bc2,
        (blocks, SPAN, SPAN),
        small,
        small,
        small,
        small,
        (blocks, 16, SPAN),
        (chans, 128),
        (n4, 128),
        (16, 128),
        (chans, 1),
        (width, 1),
        (2 * blocks, 8, 128),
        (narrow, 2 * blocks, 8, 128),
        (2 * thirds,) + piece[1:],
        (3 * thirds, depth, rows, 128),
        (3 * thirds, depth - 1, rows, 128),
        (2, 2, width, own_rows),
        (2, width, own_rows),
        (wide, 2, 2) + quarter,
        (wide, 2) + quarter,
        (wide,) + quarter,
        (wide,) + quarter,
        (wide,) + quarter,
        (wide, 16, 128),
        (wide, 16, 128),
        (narrow, 16, 256),
        (wide,) + sums,
        (narrow, 8, 128),
        (wide, 8, 128),
        (3 * thirds, 1, 128),
    ]
    lows = [quarters] * 2 + [(2 * chans + n4 + 16, width)] * 2
    copies = 200
    operands = (lengths, hidden, cot, gain, w_zx, w_out, w_bc, dtw, cx, cbc, hp, og)
    return pl.pallas_call(
        functools.partial(layer_kernel, wide, heads, shard, chans * narrow),
        out_shape=[jax.ShapeDtypeStruct(shape, F32) for shape in shapes],
        in_specs=[pl.BlockSpec(memory_space=pltpu.SMEM)]
        + [pl.BlockSpec(memory_space=pltpu.VMEM)] * (len(operands) - 1),
        scratch_shapes=[pltpu.VMEM(shape, F32) for shape in scratch]
        + [pltpu.VMEM(shape, jnp.bfloat16) for shape in lows]
        + [
            pltpu.SemaphoreType.DMA((copies,)),
            pltpu.SemaphoreType.DMA((copies,)),
            pltpu.SemaphoreType.DMA((3, 2 * blocks)),
            pltpu.SemaphoreType.DMA((3, 2 * blocks)),
        ],
        compiler_params=pltpu.CompilerParams(
            vmem_limit_bytes=62 * MIB, collective_id=0, has_side_effects=True
        ),
        cost_estimate=pl.CostEstimate(flops=20_000_000_000, bytes_accessed=20_000_000, transcendentals=0),
    )(*operands)


def finish_kernel(
    wide,
    narrow,
    gfull,
    bc_own,
    dt_own,
    sv,
    norm_ref,
    block_in,
    grad_in,
    stat_l,
    stat_r,
    stat_lo,
    stat_ro,
    root_l,
    root_r,
    root_lo,
    root_ro,
    w_ref,
    wout_ref,
    bcw_ref,
    dtw_ref,
    cx_ref,
    cbc_ref,
    hp_ref,
    og_ref,
    gain_ref,
    block_out,
    in_grad,
    clip,
    g_zx,
    new_zx,
    new_l,
    new_r,
    g_out,
    new_out,
    new_lo,
    new_ro,
    g_bc,
    new_bc,
    g_dt,
    new_dt,
    g_cx,
    new_cx,
    g_cbc,
    new_cbc,
    g_hp,
    new_hp,
    g_og,
    new_og,
    g_ng,
    new_ng,
    g_s,
    l_s,
    r_s,
    lo_s,
    ro_s,
    rl_s,
    rr_s,
    rlo_s,
    rro_s,
    in_sem,
    out_sem,
):
    rate = 10.0
    chans = w_ref.shape[2]
    thirds = chans // 128
    place = lax.axis_index("wide")
    z, x = place // 2, place % 2
    factor = 1.0 / jnp.maximum(norm_ref[0:1, 0:1], 1.0)
    fetches, results = [], []

    def fetch(src, dst):
        item = pltpu.make_async_copy(src, dst, in_sem.at[len(fetches)])
        item.start()
        fetches.append(item)
        return item

    def result(src, dst):
        item = pltpu.make_async_copy(src, dst, out_sem.at[len(results)])
        item.start()
        results.append(item)

    waits = []
    for m in (2, 0, 1):
        gs = g_s.at[m * thirds : (m + 1) * thirds]
        whole_m = fetch(gfull.at[m * thirds : (m + 1) * thirds], gs)
        if m == 2:
            others = [(root_ro, rro_s), (root_lo, rlo_s), (stat_ro, ro_s), (stat_lo, lo_s)]
        else:
            others = [(root_l.at[m], rl_s.at[m]), (root_r.at[m], rr_s.at[m])]
            others += [(stat_l.at[m], l_s.at[m]), (stat_r.at[m], r_s.at[m])]
        waits.append([whole_m] + [fetch(*pair) for pair in others])
    block_out[...] = block_in[...]
    in_grad[...] = grad_in[...]
    clip[...] = norm_ref[0:1, 0:1]

    def both(m):
        for item in waits[(1, 2, 0)[m]]:
            item.wait()
        parts = [flat(g_s[m * thirds + i]) for i in range(thirds)]
        mine = [g_s[m * thirds + i, z, x] for i in range(thirds)]
        return jnp.concatenate(mine, axis=1) * factor, halves(jnp.concatenate(parts, axis=1) * factor)

    own, full = both(2)
    g_out[...] = own
    ro_s[...] = 0.5 * ro_s[...] + 0.5 * product(halves(own), full, NT)
    result(ro_s, new_ro)
    lo_s[...] = 0.5 * lo_s[...] + 0.5 * product(full, full, TN)
    result(lo_s, new_lo)
    new_out[...] = wout_ref[...] - 0.5 * dot3(product(halves(rro_s[...]), full), rlo_s[...], NT)
    for m in range(2):
        own, full = both(m)
        g_zx[m] = own
        l_s[m] = 0.5 * l_s[m] + 0.5 * product(halves(own), full, NT)
        result(l_s.at[m], new_l.at[m])
        r_s[m] = 0.5 * r_s[m] + 0.5 * product(full, full, TN)
        result(r_s.at[m], new_r.at[m])
        new_zx[m] = w_ref[m] - 0.5 * dot3(product(halves(rl_s[m]), full), rr_s[m])

    grad = flat(bc_own[...]) * factor
    g_bc[...] = grad
    new_bc[...] = bcw_ref[...] - rate * grad
    heads, _, rows = dtw_ref.shape
    for h in range(heads):
        for i in range(2):
            row = i * heads + h
            grad = dt_own[row : row + 1, 0:rows] * factor
            g_dt[h, i : i + 1, :] = grad
            new_dt[h, i : i + 1, :] = dtw_ref[h, i : i + 1, :] - rate * grad
    sums = sv[...] * factor
    grad = sums[0:4, 0:chans]
    g_cx[...] = grad
    new_cx[...] = cx_ref[...] - rate * grad
    grad = sums[4:5, 0:chans]
    g_og[...] = grad.reshape(chans)
    new_og[...] = og_ref[...] - rate * g_og[...]
    n4 = cbc_ref.shape[1]
    last = chans + 128
    grad = sums[0:4, last : last + n4]
    g_cbc[...] = grad
    new_cbc[...] = cbc_ref[...] - rate * grad
    turned = jnp.transpose(
        jnp.concatenate([sums[:, chans:last], jnp.zeros((112, 128), F32)], axis=0)
    )
    for i, (row, start) in enumerate(((0, 0), (0, heads), (1, 0), (1, heads), (2, 0))):
        grad = turned[row : row + 1, start : start + heads]
        g_hp[i : i + 1, :] = grad
        new_hp[i : i + 1, :] = hp_ref[i : i + 1, :] - rate * grad
    shard = gain_ref.shape[0]
    count = narrow * shard // 128
    line = jnp.concatenate([sums[8 + i : 9 + i, last : last + 128] for i in range(count)], axis=1)
    grad = jnp.zeros((1, shard), F32)
    for q in range(narrow):
        piece = line[:, q * shard : (q + 1) * shard]
        grad = jnp.where(lax.axis_index("narrow") == q, piece, grad)
    g_ng[...] = grad.reshape(shard)
    new_ng[...] = gain_ref[...] - rate * g_ng[...]
    for item in results:
        item.wait()


def run_finish(partials, stats, roots, params, tokens_shape, wide, narrow):
    stat_l, stat_r, stat_lo, stat_ro = stats
    w_zx, w_out, w_bc, w_dt, cx, cbc, hp, og, gain = params
    like = [w_zx, w_zx, stat_l, stat_r, w_out, w_out, stat_lo, stat_ro]
    like += [item for item in (w_bc, w_dt, cx, cbc, hp, og, gain) for _ in range(2)]
    shapes = [tokens_shape, tokens_shape, (1, 1)] + [item.shape for item in like]
    far, near = pl.BlockSpec(memory_space=pl.ANY), pl.BlockSpec(memory_space=pltpu.VMEM)
    gfull = partials[0]
    kept = [gfull, stat_l, stat_r, stat_lo, stat_ro, *roots]
    return pl.pallas_call(
        functools.partial(finish_kernel, wide, narrow),
        out_shape=[jax.ShapeDtypeStruct(shape, F32) for shape in shapes],
        in_specs=[far] + [near] * 6 + [far] * 8 + [near] * len(params),
        out_specs=[near] * 5 + [far] * 2 + [near] * 2 + [far] * 2 + [near] * (len(shapes) - 11),
        scratch_shapes=[pltpu.VMEM(item.shape, F32) for item in kept]
        + [pltpu.SemaphoreType.DMA((15,)), pltpu.SemaphoreType.DMA((6,))],
        compiler_params=pltpu.CompilerParams(vmem_limit_bytes=56 * MIB),
        cost_estimate=pl.CostEstimate(flops=4_000_000_000, bytes_accessed=20_000_000, transcendentals=0),
    )(*partials, *stats, *roots, *params)


def fast_local(
    wide,
    narrow,
    hidden_in,
    out_cot,
    lengths,
    norm_gain,
    w_zx,
    w_bc,
    w_dt,
    conv_x,
    conv_bc,
    head_params,
    out_gain,
    w_out,
    left_statistic_gate,
    stat_right_zx,
    stat_left_out,
    stat_right_out,
    inverse_root_left_gate,
    inverse_root_right_gate,
    root_left_out,
    root_right_out,
):
    heads, shard = w_dt.shape[1], norm_gain.shape[0]
    out_rows, dt_rows = w_out.T, jnp.transpose(w_dt, (1, 2, 0))
    block, grad, *partials = run_layer(
        lengths,
        hidden_in,
        out_cot,
        norm_gain,
        w_zx,
        out_rows,
        w_bc,
        dt_rows,
        conv_x,
        conv_bc,
        head_params,
        out_gain,
        heads,
        shard,
        wide,
        narrow,
    )
    (
        block_out,
        in_grad,
        clip,
        g_zx,
        new_zx,
        new_l,
        new_r,
        g_out,
        new_out,
        new_lo,
        new_ro,
        g_bc,
        new_bc,
        g_dt,
        new_dt,
        *rest,
    ) = run_finish(
        (*partials, block, grad),
        (left_statistic_gate[:, 0], stat_right_zx, stat_left_out, stat_right_out[0]),
        (inverse_root_left_gate[:, 0], inverse_root_right_gate, root_left_out, root_right_out[0]),
        (w_zx, out_rows, w_bc, dt_rows, conv_x, conv_bc, head_params, out_gain, norm_gain),
        hidden_in.shape,
        wide,
        narrow,
    )
    return (
        block_out,
        in_grad,
        clip.reshape(()),
        g_zx,
        new_zx,
        new_l[:, None],
        new_r,
        g_out.T,
        new_out.T,
        new_lo,
        new_ro[None],
        g_bc,
        new_bc,
        jnp.transpose(g_dt, (2, 0, 1)),
        jnp.transpose(new_dt, (2, 0, 1)),
        *rest,
    )


def solution(mesh):
    wide, narrow = mesh.shape["wide"], mesh.shape["narrow"]
    body = functools.partial(fast_local, wide, narrow) if (wide, narrow) == (8, 4) else local
    return jax.shard_map(
        body,
        mesh=mesh,
        in_specs=(
            P(("wide", "narrow"), None),
            P(("wide", "narrow"), None),
            P("wide"),
            P("narrow"),
            P(None, "wide", "narrow"),
            P("wide", None),
            P("wide", "narrow", None),
            P(None, "narrow"),
            P(),
            P(None, "narrow"),
            P("narrow"),
            P("narrow", "wide"),
            P(None, "narrow", "wide", None),
            P(None, "narrow", None),
            P("narrow", None),
            P("narrow", "wide", None),
            P(None, "narrow", "wide", None),
            P(None, "narrow", None),
            P("narrow", None),
            P("narrow", "wide", None),
        ),
        out_specs=(
            P(("wide", "narrow"), None),
            P(("wide", "narrow"), None),
            P(),
            P(None, "wide", "narrow"),
            P(None, "wide", "narrow"),
            P(None, "narrow", "wide", None),
            P(None, "narrow", None),
            P("narrow", "wide"),
            P("narrow", "wide"),
            P("narrow", None),
            P("narrow", "wide", None),
            P("wide", None),
            P("wide", None),
            P("wide", "narrow", None),
            P("wide", "narrow", None),
            P(None, "narrow"),
            P(None, "narrow"),
            P(),
            P(),
            P(None, "narrow"),
            P(None, "narrow"),
            P("narrow"),
            P("narrow"),
            P("narrow"),
            P("narrow"),
        ),
        check_vma=False,
    )
```

```python
import functools
import math

import jax
import jax.numpy as jnp
from jax import lax
from jax.experimental import pallas as pl
from jax.experimental.pallas import tpu as pltpu
from jax.sharding import PartitionSpec as P

SPAN = 128
WIDTH = 64
HIGH = lax.Precision.HIGH
F32 = jnp.float32
NN = (((1,), (0,)), ((), ()))
NT = (((1,), (1,)), ((), ()))
TN = (((0,), (0,)), ((), ()))
TT = (((0,), (1,)), ((), ()))


def dot(a, b, dims=NN):
    return lax.dot_general(a, b, dims, precision=HIGH, preferred_element_type=F32)


def halves(v):
    hi = v.astype(jnp.bfloat16)
    return hi, (v - hi.astype(F32)).astype(jnp.bfloat16)


def product(a, b, dims=NN):
    (ah, al), (bh, bl) = a, b
    (left,), (right,) = dims[0]
    rows, depth = ah.shape[1 - left], ah.shape[left]

    def times(u, v):
        return lax.dot_general(u, v, dims, preferred_element_type=F32)

    if depth < 128:
        return times(
            jnp.concatenate([ah, al, ah], axis=left), jnp.concatenate([bh, bh, bl], axis=right)
        )
    if depth == 128:
        top = jnp.concatenate([ah, ah], axis=left)
        low = jnp.concatenate([al, jnp.zeros_like(al)], axis=left)
        out = times(jnp.concatenate([top, low], axis=1 - left), jnp.concatenate([bh, bl], axis=right))
        return out[0:rows] + out[rows:]
    out = times(jnp.concatenate([ah, al], axis=1 - left), bh)
    return out[0:rows] + out[rows:] + times(ah, bl)


def dot3(a, b, dims=NN):
    return product(halves(a), halves(b), dims)


def sigmoid(v):
    return 1.0 / (1.0 + jnp.exp(-v))


def split3(v):
    hi = v.astype(jnp.bfloat16)
    rest = v - hi.astype(F32)
    mid = rest.astype(jnp.bfloat16)
    lo = (rest - mid.astype(F32)).astype(jnp.bfloat16)
    return jnp.concatenate([hi, mid, lo], axis=0)


def exact_dot(v, ones):
    rows = v.shape[0]
    out = lax.dot_general(split3(v), ones, NN, preferred_element_type=F32)
    return out[0:rows] + out[rows : 2 * rows] + out[2 * rows : 3 * rows]


def iota(shape, axis):
    return lax.broadcasted_iota(jnp.int32, shape, axis)


def shift_right(v, count):
    return jnp.where(iota(v.shape, 1) >= count, pltpu.roll(v, count, axis=1), 0.0)


def shift_left(v, count):
    length = v.shape[1]
    return jnp.where(iota(v.shape, 1) < length - count, pltpu.roll(v, length - count, axis=1), 0.0)


def conv_rows(v, taps):
    count = taps.shape[1]
    total = taps[:, count - 1 : count] * v
    for j in range(count - 1):
        total = total + taps[:, j : j + 1] * shift_right(v, count - 1 - j)
    return total


def pieces(ref, chans, state):
    bc = 2 * chans
    dt = bc + 4 * state
    return ref.at[0:chans], ref.at[chans:bc], ref.at[bc:dt], ref.at[dt : dt + 16]


def convolve(x_ref, bc_ref, live_ref, cx_ref, cbc_ref, xc_ref, dx_act_ref, b_ref, c_ref, dbc_act_ref):
    chans, tokens = xc_ref.shape
    state = c_ref.shape[0] // 2
    live = live_ref[...]

    def conv_x_rows(i, _):
        rows = pl.ds(pl.multiple_of(i * 8, 8), 8)
        u = conv_rows(x_ref[rows, :], cx_ref[rows, :])
        s = sigmoid(u)
        xc_ref[rows, :] = u * s * live
        dx_act_ref[rows, :] = (s + u * s * (1.0 - s)) * live
        return 0

    lax.fori_loop(0, chans // 8, conv_x_rows, 0, unroll=2)

    def conv_bc_rows(i, _, src, dst, dst_row, shift):
        rows = pl.ds(pl.multiple_of(src * state + i * 8, 8), 8)
        out = pl.ds(pl.multiple_of(dst_row + i * 8, 8), 8)
        u = conv_rows(bc_ref[rows, :], cbc_ref[rows, :])
        s = sigmoid(u)
        dbc_act_ref[rows, :] = s + u * s * (1.0 - s)
        v = u * s
        if shift == 1:
            v = shift_right(v, 1)
        if shift == -1:
            v = shift_left(v, 1)
        dst[out, :] = v
        return 0

    for src, dst, row, shift in ((0, b_ref, 0, 0), (1, c_ref, 0, 1), (2, b_ref, state, 0), (3, c_ref, state, -1)):
        lax.fori_loop(
            0,
            state // 8,
            functools.partial(conv_bc_rows, src=src, dst=dst, dst_row=row, shift=shift),
            0,
            unroll=2,
        )


def step_sizes(pre_ref, hp_ref, step_ref, cum_ref, cumex_ref, heads):
    blocks = pre_ref.shape[1] // SPAN
    pre = pre_ref[...] + hp_ref[:, 0:1]
    steps = jnp.maximum(pre, 0.0) + jnp.log1p(jnp.exp(-jnp.abs(pre)))
    step_ref[...] = steps
    logs = -hp_ref[:, 1:2] * steps
    rows16 = iota((16, SPAN), 0)
    lane16 = iota((16, SPAN), 1)
    row_q = iota((SPAN, SPAN), 0)
    lane_q = iota((SPAN, SPAN), 1)
    upto = (row_q <= lane_q).astype(F32).astype(jnp.bfloat16)
    downto = (row_q >= lane_q).astype(F32).astype(jnp.bfloat16)
    both = jnp.concatenate([upto, downto], axis=1)
    for b in range(blocks):
        sums = exact_dot(logs[:, b * SPAN : (b + 1) * SPAN], both)
        cum = jnp.where(rows16 < heads, sums[:, 0:SPAN], sums[:, SPAN : 2 * SPAN])
        ex_f = jnp.where(lane16 >= 1, pltpu.roll(cum, 1, axis=1), 0.0)
        ex_r = jnp.where(lane16 < SPAN - 1, pltpu.roll(cum, SPAN - 1, axis=1), 0.0)
        cum_ref[:, b * SPAN : (b + 1) * SPAN] = cum
        cumex_ref[:, b * SPAN : (b + 1) * SPAN] = jnp.where(rows16 < heads, ex_f, ex_r)


def states(xc_ref, b_ref, step_ref, cum_ref, sloc_ref, hcat_ref, heads):
    blocks = xc_ref.shape[1] // SPAN
    state = b_ref.shape[0] // 2

    def local_states(b, _):
        sl = pl.ds(pl.multiple_of(b * SPAN, SPAN), SPAN)
        bcat = spread(b_ref[:, sl], state)
        tail = tails(cum_ref[:, sl], step_ref[:, sl], heads)
        left = tailed(xc_ref[:, sl], tail, range(heads), heads)
        sloc_ref[b] = dot3(left, bcat, NT)
        return 0

    lax.fori_loop(0, blocks, local_states, 0)

    lane_h = iota((WIDTH, 2 * state), 1)
    for h in range(heads):
        rows = slice(h * WIDTH, (h + 1) * WIDTH)
        carry = jnp.zeros((WIDTH, 2 * state), F32)
        for i in range(blocks):
            r = blocks - 1 - i
            hcat_ref[i, rows, 0:state] = carry[:, 0:state]
            hcat_ref[r, rows, state : 2 * state] = carry[:, state : 2 * state]
            tot_f = jnp.exp(cum_ref[h : h + 1, (i + 1) * SPAN - 1 : (i + 1) * SPAN])
            tot_r = jnp.exp(cum_ref[heads + h : heads + h + 1, r * SPAN : r * SPAN + 1])
            factor = jnp.where(lane_h < state, tot_f, tot_r)
            piece = jnp.where(lane_h < state, sloc_ref[i, rows, :], sloc_ref[r, rows, :])
            carry = carry * factor + piece


def outputs(z_ref, xc_ref, b_ref, c_ref, step_ref, cum_ref, cumex_ref, hcat_ref, hp_ref, y_ref, inner_ref, heads, emit):
    blocks = xc_ref.shape[1] // SPAN
    state = b_ref.shape[0] // 2
    row_q = iota((SPAN, SPAN), 0)
    lane_q = iota((SPAN, SPAN), 1)
    lower = row_q < lane_q
    diag = row_q == lane_q

    def block(b, _):
        sl = pl.ds(pl.multiple_of(b * SPAN, SPAN), SPAN)
        bb, cc = b_ref[:, sl], c_ref[:, sl]
        inner = jnp.where(
            lower, dot3(bb[0:state], cc[0:state], TN), dot3(bb[state:], cc[state:], TN)
        )
        inner_ref[b] = inner
        cum, steps, cumex = cum_ref[:, sl], step_ref[:, sl], cumex_ref[:, sl]
        scale = jnp.exp(cumex)
        cols = columns(cum, steps)
        sums = None
        entering = dot3(hcat_ref[b], spread(cc, state))
        x_parts = halves(xc_ref[:, sl])
        for h in range(heads):
            rows = slice(h * WIDTH, (h + 1) * WIDTH)
            decay = decays(cols, cumex, lower, diag, h, heads)
            mt = jnp.where(diag, hp_ref[h : h + 1, 2:3], inner * decay)
            y = product((x_parts[0][rows], x_parts[1][rows]), halves(mt))
            y = y + entering[rows, 0:SPAN] * scale[h : h + 1]
            y = y + entering[rows, SPAN:] * scale[heads + h : heads + h + 1]
            z = z_ref[rows, sl]
            y_ref[rows, sl] = y
            sums = emit(b, sl, h, rows, y * (z * sigmoid(z)), sums)
        return 0

    lax.fori_loop(0, blocks, block, 0)


def fwd_kernel(
    heads,
    proj_ref,
    live_ref,
    cx_ref,
    cbc_ref,
    hp_ref,
    y_ref,
    xc_ref,
    dx_act_ref,
    b_ref,
    c_ref,
    dbc_act_ref,
    step_ref,
    cum_ref,
    cumex_ref,
    hcat_ref,
    inner_ref,
    gated_ref,
    sq_ref,
    sloc_ref,
):
    z_ref, x_ref, bc_ref, pre_ref = pieces(proj_ref, xc_ref.shape[0], c_ref.shape[0] // 2)
    convolve(x_ref, bc_ref, live_ref, cx_ref, cbc_ref, xc_ref, dx_act_ref, b_ref, c_ref, dbc_act_ref)
    step_sizes(pre_ref, hp_ref, step_ref, cum_ref, cumex_ref, heads)
    states(xc_ref, b_ref, step_ref, cum_ref, sloc_ref, hcat_ref, heads)

    def emit(b, sl, h, rows, gated, total):
        gated_ref[rows, sl] = gated
        part = jnp.sum(gated * gated, axis=0, keepdims=True)
        total = part if total is None else total + part
        if h == heads - 1:
            sq_ref[:, sl] = total
        return total

    outputs(z_ref, xc_ref, b_ref, c_ref, step_ref, cum_ref, cumex_ref, hcat_ref, hp_ref, y_ref, inner_ref, heads, emit)


def spread(bb, state):
    zero = jnp.zeros((state, SPAN), F32)
    top = jnp.concatenate([bb[0:state], zero], axis=1)
    low = jnp.concatenate([zero, bb[state:]], axis=1)
    return jnp.concatenate([top, low], axis=0)


def tails(cum, steps, heads):
    rows = iota((16, SPAN), 0)
    last = jnp.where(rows[:, 0:1] < heads, cum[:, SPAN - 1 : SPAN], cum[:, 0:1])
    return jnp.exp(last - cum) * steps


def tailed(xc, tail, chosen, heads):
    parts = []
    for i, h in enumerate(chosen):
        x = xc[i * WIDTH : (i + 1) * WIDTH]
        parts.append(
            jnp.concatenate([x * tail[h : h + 1], x * tail[heads + h : heads + h + 1]], axis=1)
        )
    return jnp.concatenate(parts, axis=0)


def columns(cum, steps):
    pad = jnp.zeros((SPAN - 32, SPAN), F32)
    return jnp.transpose(jnp.concatenate([cum, steps, pad], axis=0))


def decays(cols, cumex, lower, diag, h, heads):
    f, r = h, heads + h
    arg = jnp.where(
        lower, cumex[f : f + 1] - cols[:, f : f + 1], cumex[r : r + 1] - cols[:, r : r + 1]
    )
    step = jnp.where(lower, cols[:, 16 + f : 17 + f], cols[:, 16 + r : 17 + r])
    return jnp.where(diag, 0.0, jnp.exp(arg) * step)


def gate_back(z_ref, y_ref, don_ref, rms, coef, og_ref, dy_ref, dz_ref, dog_ref, onorm_ref=None):
    chans = y_ref.shape[0]

    def gate_rows(i, _):
        rows = pl.ds(pl.multiple_of(i * 8, 8), 8)
        z, y, don, og = z_ref[rows, :], y_ref[rows, :], don_ref[rows, :], og_ref[rows, :]
        s = sigmoid(z)
        act = z * s
        gated = y * act
        normed = rms * don
        dog_ref[rows, 0:1] = jnp.sum(gated * normed, axis=1, keepdims=True)
        dgated = normed * og - gated * coef
        dy_ref[rows, :] = dgated * act
        dz_ref[rows, :] = dgated * y * (s + act * (1.0 - s))
        if onorm_ref is not None:
            onorm_ref[rows, :] = gated * rms * og
        return 0

    lax.fori_loop(0, chans // 8, gate_rows, 0, unroll=2)


def back_intra(xc_ref, c_ref, inner_ref, step_ref, cum_ref, cumex_ref, hcat_ref, hp_ref, dy_s, dxc_s, dh_s, dc_s, din_s, g_s, cv_s, dd_s, chosen, heads, tick):
    blocks = xc_ref.shape[1] // SPAN
    state = c_ref.shape[0] // 2
    lower = iota((SPAN, SPAN), 0) < iota((SPAN, SPAN), 1)
    diag = iota((SPAN, SPAN), 0) == iota((SPAN, SPAN), 1)
    first = chosen[0] == 0

    def block(b, put):
        sl = pl.ds(pl.multiple_of(b * SPAN, SPAN), SPAN)
        cc = c_ref[:, sl]
        inner = inner_ref[b]
        cumex = cumex_ref[:, sl]
        scale = jnp.exp(cumex)
        cols = columns(cum_ref[:, sl], step_ref[:, sl])
        dinner = jnp.zeros((SPAN, SPAN), F32) if first else din_s[b]
        dcc = jnp.zeros((2 * state, SPAN), F32) if first else dc_s[:, sl]
        for h in chosen:
            f, r = h, heads + h
            rows = slice(h * WIDTH, (h + 1) * WIDTH)
            decay = decays(cols, cumex, lower, diag, h, heads)
            mt = inner * decay
            e_f, e_r = scale[f : f + 1], scale[r : r + 1]
            ce = jnp.concatenate([cc[0:state] * e_f, cc[state:] * e_r], axis=0)
            x = xc_ref[rows, sl]
            dy = dy_s[rows, sl]
            dy_parts = halves(dy)
            left = jnp.concatenate([x, hcat_ref[b, rows, :]], axis=1)
            back = product(halves(left), dy_parts, TN)
            dmt, dce = back[0:SPAN], back[SPAN:]
            dinner = dinner + dmt * decay
            w = dmt * mt
            over_f = jnp.sum(jnp.where(lower, w, 0.0), axis=0, keepdims=True)
            over_r = jnp.sum(jnp.where(lower, 0.0, w), axis=0, keepdims=True)
            prod = dce * ce
            put(g_s, (slice(f, f + 1), sl), over_f + jnp.sum(prod[0:state], axis=0, keepdims=True))
            put(g_s, (slice(r, r + 1), sl), over_r + jnp.sum(prod[state:], axis=0, keepdims=True))
            dcc = dcc + jnp.concatenate([dce[0:state] * e_f, dce[state:] * e_r], axis=0)
            right = jnp.concatenate(
                [jnp.where(lower, mt, 0.0), jnp.where(lower, 0.0, mt), ce], axis=0
            )
            out = product(dy_parts, halves(right), NT)
            dx_f, dx_r = out[:, 0:SPAN], out[:, SPAN : 2 * SPAN]
            put(dh_s, (b, rows, slice(None)), out[:, 2 * SPAN :])
            put(cv_s, (slice(f, f + 1), sl), jnp.sum(x * dx_f, axis=0, keepdims=True))
            put(cv_s, (slice(r, r + 1), sl), jnp.sum(x * dx_r, axis=0, keepdims=True))
            put(dd_s, (slice(h, h + 1), sl), jnp.sum(x * dy, axis=0, keepdims=True))
            put(dxc_s, (rows, sl), dx_f + dx_r + hp_ref[h : h + 1, 2:3] * dy)
        put(din_s, (b,), dinner)
        put(dc_s, (slice(None), sl), dcc)

    two_at_a_time(blocks, block, tick)


def two_at_a_time(blocks, block, tick):
    def body(i, _):
        stores = []
        for b in (2 * i, 2 * i + 1):
            block(b, lambda ref, at, value: stores.append((ref, at, value)))
        for ref, at, value in stores:
            ref[at] = value
        tick(2 * i)
        tick(2 * i + 1)
        return 0

    lax.fori_loop(0, blocks // 2, body, 0)


def back_states(cum_ref, hcat_ref, dh_s, tq_s, state, chosen, heads):
    blocks = hcat_ref.shape[0]
    lane_h = iota((WIDTH, 2 * state), 1)
    lane_1 = iota((1, 2 * state), 1)
    for h in chosen:
        rows = slice(h * WIDTH, (h + 1) * WIDTH)
        carry = jnp.zeros((WIDTH, 2 * state), F32)
        for i in range(blocks):
            f = blocks - 1 - i
            tot_f = jnp.exp(cum_ref[h : h + 1, (f + 1) * SPAN - 1 : (f + 1) * SPAN])
            tot_r = jnp.exp(cum_ref[heads + h : heads + h + 1, i * SPAN : i * SPAN + 1])
            factor = jnp.where(lane_h < state, tot_f, tot_r)
            direct = jnp.where(lane_h < state, dh_s[f, rows, :], dh_s[i, rows, :])
            kept = jnp.where(lane_h < state, hcat_ref[f, rows, :], hcat_ref[i, rows, :])
            scaled = carry * factor
            dots = jnp.sum(scaled * kept, axis=0, keepdims=True)
            q_f = jnp.sum(jnp.where(lane_1 < state, dots, 0.0), axis=1, keepdims=True)
            q_r = jnp.sum(jnp.where(lane_1 < state, 0.0, dots), axis=1, keepdims=True)
            tq_s[f, h : h + 1, :] = jnp.broadcast_to(q_f, (1, SPAN))
            tq_s[i, heads + h : heads + h + 1, :] = jnp.broadcast_to(q_r, (1, SPAN))
            dh_s[f, rows, 0:state] = carry[:, 0:state]
            dh_s[i, rows, state:] = carry[:, state:]
            carry = scaled + direct


def back_inter(xc_ref, b_ref, step_ref, cum_ref, dxc_s, dh_s, db_s, v_s, chosen, heads, tick):
    blocks = xc_ref.shape[1] // SPAN
    state = b_ref.shape[0] // 2
    first = chosen[0] == 0
    group = slice(chosen[0] * WIDTH, (chosen[-1] + 1) * WIDTH)

    def block(b, put):
        sl = pl.ds(pl.multiple_of(b * SPAN, SPAN), SPAN)
        bcat = spread(b_ref[:, sl], state)
        tail = tails(cum_ref[:, sl], step_ref[:, sl], heads)
        xc = xc_ref[group, sl]
        dxc = dxc_s[group, sl]
        dsl = halves(dh_s[b, group, :])
        dleft = product(dsl, halves(bcat))
        dbs = product(dsl, halves(tailed(xc, tail, chosen, heads)), TN)
        db = jnp.concatenate([dbs[0:state, 0:SPAN], dbs[state:, SPAN:]], axis=0)
        put(db_s, (slice(None), sl), db if first else db_s[:, sl] + db)
        parts = []
        for i, h in enumerate(chosen):
            f, r = h, heads + h
            part = slice(i * WIDTH, (i + 1) * WIDTH)
            tx_f = dleft[part, 0:SPAN] * tail[f : f + 1]
            tx_r = dleft[part, SPAN:] * tail[r : r + 1]
            put(v_s, (slice(f, f + 1), sl), jnp.sum(xc[part] * tx_f, axis=0, keepdims=True))
            put(v_s, (slice(r, r + 1), sl), jnp.sum(xc[part] * tx_r, axis=0, keepdims=True))
            parts.append(dxc[part] + tx_f + tx_r)
        put(dxc_s, (group, sl), jnp.concatenate(parts, axis=0))

    two_at_a_time(blocks, block, tick)


def back_logs(b_ref, c_ref, pre_ref, step_ref, hp_ref, ddt_ref, dhp_ref, db_s, dc_s, din_s, g_s, cv_s, v_s, dd_s, tq_s, heads):
    blocks = pre_ref.shape[1] // SPAN
    state = b_ref.shape[0] // 2
    row_q = iota((SPAN, SPAN), 0)
    lane_q = iota((SPAN, SPAN), 1)
    lower = row_q < lane_q
    strict = (row_q > lane_q).astype(F32)
    weak = (row_q >= lane_q).astype(F32)
    strict_t = (row_q < lane_q).astype(F32)
    weak_t = (row_q <= lane_q).astype(F32)
    tri = jnp.concatenate(
        [
            jnp.concatenate([strict, strict_t], axis=1),
            jnp.concatenate([weak, weak_t], axis=1),
            jnp.concatenate([strict_t, strict], axis=1),
        ],
        axis=0,
    ).astype(jnp.bfloat16)
    rows16 = iota((16, SPAN), 0)
    used = rows16 < 2 * heads
    rate = hp_ref[:, 1:2]

    def block(b, carry):
        bias_sum, log_sum, skip_sum = carry
        sl = pl.ds(pl.multiple_of(b * SPAN, SPAN), SPAN)
        dinner = din_s[b]
        both = jnp.concatenate(
            [jnp.where(lower, dinner, 0.0), jnp.where(lower, 0.0, dinner)], axis=0
        )
        dc_s[:, sl] = dc_s[:, sl] + dot3(spread(b_ref[:, sl], state), both)
        db = dot3(c_ref[:, sl], both, NT)
        db_s[0:state, sl] = db_s[0:state, sl] + db[0:state, 0:SPAN]
        db_s[state:, sl] = db_s[state:, sl] + db[state:, SPAN:]
        g = jnp.where(used, g_s[:, sl], 0.0)
        c = jnp.where(used, cv_s[:, sl], 0.0)
        v = jnp.where(used, v_s[:, sl], 0.0)
        steps = step_ref[:, sl]
        sums = exact_dot(jnp.concatenate([g, -c, v], axis=1), tri)
        dlog = jnp.where(rows16 < heads, sums[:, 0:SPAN], sums[:, SPAN:])
        dlog = dlog + jnp.where(used, tq_s[b], 0.0)
        pre = pre_ref[:, sl] + hp_ref[:, 0:1]
        small = steps < 1e-30
        ratio = jnp.where(small, 1.0, sigmoid(pre) / jnp.where(small, 1.0, steps))
        dpre = (c + v) * ratio - rate * dlog * sigmoid(pre)
        ddt_ref[:, sl] = dpre
        skip = jnp.where(rows16 < heads, dd_s[:, sl], 0.0)
        return bias_sum + dpre, log_sum - rate * dlog * steps, skip_sum + skip

    zeros16 = jnp.zeros((16, SPAN), F32)
    bias_sum, log_sum, skip = lax.fori_loop(0, blocks, block, (zeros16, zeros16, zeros16))
    dhp_ref[:, 0:1] = jnp.sum(bias_sum, axis=1, keepdims=True)
    dhp_ref[:, 1:2] = jnp.sum(log_sum, axis=1, keepdims=True)
    dhp_ref[:, 2:3] = jnp.sum(skip, axis=1, keepdims=True)


def conv_back(du, v, taps):
    count = taps.shape[1]
    dv = taps[:, count - 1 : count] * du
    sums = [jnp.sum(du * v, axis=1, keepdims=True)]
    for j in range(count - 2, -1, -1):
        moved = shift_left(du, count - 1 - j)
        dv = dv + taps[:, j : j + 1] * moved
        sums.append(jnp.sum(moved * v, axis=1, keepdims=True))
    return dv, sums[::-1]


def conv_x_back(xin_ref, cx_ref, dx_act_ref, dxc_s, dxin_ref, dcx_ref, start, count):
    def group(i, _):
        rows = pl.ds(pl.multiple_of(start + i * 8, 8), 8)
        dv, sums = conv_back(dxc_s[rows, :] * dx_act_ref[rows, :], xin_ref[rows, :], cx_ref[rows, :])
        dxin_ref[rows, :] = dv
        for j, item in enumerate(sums):
            dcx_ref[rows, j : j + 1] = item
        return 0

    lax.fori_loop(0, count // 8, group, 0, unroll=2)


def conv_bc_back(bc_ref, cbc_ref, dbc_act_ref, db_s, dc_s, dbc_ref, dcbc_ref):
    state = db_s.shape[0] // 2

    def group(i, _, src, grad, grad_row, shift):
        rows = pl.ds(pl.multiple_of(src * state + i * 8, 8), 8)
        from_rows = pl.ds(pl.multiple_of(grad_row + i * 8, 8), 8)
        d = grad[from_rows, :]
        if shift == 1:
            d = shift_left(d, 1)
        if shift == -1:
            d = shift_right(d, 1)
        dv, sums = conv_back(d * dbc_act_ref[rows, :], bc_ref[rows, :], cbc_ref[rows, :])
        dbc_ref[rows, :] = dv
        for j, item in enumerate(sums):
            dcbc_ref[rows, j : j + 1] = item
        return 0

    for src, grad, row, shift in ((0, db_s, 0, 0), (1, dc_s, 0, 1), (2, db_s, state, 0), (3, dc_s, state, -1)):
        lax.fori_loop(
            0,
            state // 8,
            functools.partial(group, src=src, grad=grad, grad_row=row, shift=shift),
            0,
            unroll=2,
        )


def pairs_of(heads):
    return [tuple(range(h, min(h + 2, heads))) for h in range(0, heads, 2)]


def bwd_kernel(
    heads,
    proj_ref,
    y_ref,
    xc_ref,
    dx_act_ref,
    b_ref,
    c_ref,
    dbc_act_ref,
    step_ref,
    cum_ref,
    cumex_ref,
    hcat_ref,
    inner_ref,
    don_ref,
    rms_ref,
    coef_ref,
    og_ref,
    cx_ref,
    cbc_ref,
    hp_ref,
    dproj_ref,
    dcx_ref,
    dcbc_ref,
    dhp_ref,
    dog_ref,
    dy_s,
    dxc_s,
    dh_s,
    db_s,
    dc_s,
    din_s,
    g_s,
    cv_s,
    v_s,
    dd_s,
    tq_s,
):
    chans, state = y_ref.shape[0], b_ref.shape[0] // 2
    z_ref, xin_ref, bc_ref, pre_ref = pieces(proj_ref, chans, state)
    dz_ref, dxin_ref, dbc_ref, ddt_ref = pieces(dproj_ref, chans, state)
    gate_back(z_ref, y_ref, don_ref, rms_ref[...], coef_ref[...], og_ref, dy_s, dz_ref, dog_ref)
    for chosen in pairs_of(heads):
        back_intra(
            xc_ref, c_ref, inner_ref, step_ref, cum_ref, cumex_ref, hcat_ref, hp_ref, dy_s, dxc_s, dh_s, dc_s,
            din_s, g_s, cv_s, dd_s, chosen, heads, lambda b: None,
        )
        back_states(cum_ref, hcat_ref, dh_s, tq_s, state, chosen, heads)
        back_inter(xc_ref, b_ref, step_ref, cum_ref, dxc_s, dh_s, db_s, v_s, chosen, heads, lambda b: None)
    conv_x_back(xin_ref, cx_ref, dx_act_ref, dxc_s, dxin_ref, dcx_ref, 0, chans)
    back_logs(
        b_ref, c_ref, pre_ref, step_ref, hp_ref, ddt_ref, dhp_ref, db_s, dc_s, din_s, g_s, cv_s, v_s, dd_s, tq_s, heads
    )
    conv_bc_back(bc_ref, cbc_ref, dbc_act_ref, db_s, dc_s, dbc_ref, dcbc_ref)


def call(kernel, out_shapes, scratch, flops):
    return pl.pallas_call(
        kernel,
        out_shape=[jax.ShapeDtypeStruct(shape, F32) for shape in out_shapes],
        scratch_shapes=[pltpu.VMEM(shape, F32) for shape in scratch],
        compiler_params=pltpu.CompilerParams(vmem_limit_bytes=56 * 1024 * 1024),
        cost_estimate=pl.CostEstimate(flops=flops, bytes_accessed=20_000_000, transcendentals=0),
    )


def run_fwd(proj, live, cx, cbc, hp, heads):
    tokens = proj.shape[1]
    chans, n4 = cx.shape[0], cbc.shape[0]
    blocks = tokens // SPAN
    full, half, rows = (chans, tokens), (n4 // 2, tokens), (16, tokens)
    return call(
        functools.partial(fwd_kernel, heads),
        [full, full, full, half, half, (n4, tokens), rows, rows, rows, (blocks, chans, n4 // 2), (blocks, SPAN, SPAN), full, (1, tokens)],
        [(blocks, chans, n4 // 2)],
        2_000_000_000,
    )(proj, live, cx, cbc, hp)


def run_bwd(proj, kept, don, rms, coef, og, cx, cbc, hp, heads):
    tokens = proj.shape[1]
    chans, n4 = cx.shape[0], cbc.shape[0]
    blocks = tokens // SPAN
    full, half, rows = (chans, tokens), (n4 // 2, tokens), (16, tokens)
    return call(
        functools.partial(bwd_kernel, heads),
        [proj.shape, (chans, 4), (n4, 4), (16, 3), (chans, 1)],
        [full, full, (blocks, chans, n4 // 2), half, half, (blocks, SPAN, SPAN), rows, rows, rows, rows, (blocks, 16, SPAN)],
        4_000_000_000,
    )(proj, *kept, don, rms, coef, og, cx, cbc, hp)


def square_sum(arrays):
    total = jnp.float32(0.0)
    for item in arrays:
        total = total + jnp.sum(item * item)
    return total


def pad_rows(v):
    return jnp.concatenate([v, jnp.zeros((16 - v.shape[0],) + v.shape[1:], v.dtype)], axis=0)


def local(
    hidden_in,
    out_cot,
    lengths,
    norm_gain,
    w_zx,
    w_bc,
    w_dt,
    conv_x,
    conv_bc,
    head_params,
    out_gain,
    w_out,
    left_statistic_gate,
    stat_right_zx,
    stat_left_out,
    stat_right_out,
    inverse_root_left_gate,
    inverse_root_right_gate,
    root_left_out,
    root_right_out,
):
    rows, chans = w_zx.shape[1], w_zx.shape[2]
    heads = w_dt.shape[1]
    n4 = w_bc.shape[1]
    own_rows, width = hidden_in.shape
    narrow_id, wide_id = lax.axis_index("narrow"), lax.axis_index("wide")

    full_in = lax.all_gather(hidden_in, "narrow", axis=0, tiled=True)
    full_gain = lax.all_gather(norm_gain, "narrow", axis=0, tiled=True)
    dt_cols = jnp.transpose(w_dt, (0, 2, 1)).reshape(rows, 2 * heads)
    own_w = jnp.concatenate(
        [w_zx[0], w_zx[1], w_bc, dt_cols, jnp.zeros((rows, 16 - 2 * heads), F32)], axis=1
    )
    w_in = lax.all_gather(own_w, "wide", axis=0, tiled=True)
    wide_out = lax.all_gather(w_out, "wide", axis=1, tiled=True)

    tokens = full_in.shape[0]
    live = (jnp.arange(tokens) < lengths[0]).astype(F32)
    row_start = narrow_id * own_rows
    live_own = lax.dynamic_slice_in_dim(live, row_start, own_rows, 0)
    dbranch = lax.all_gather(live_own[:, None] * out_cot, "narrow", axis=0, tiled=True)

    inv_rms = lax.rsqrt(jnp.mean(full_in * full_in, axis=-1) + 1e-05)
    normed = full_in * inv_rms[:, None] * full_gain
    proj = dot(w_in, normed, TT)
    cx, cbc = conv_x.T, conv_bc.T
    hp = jnp.concatenate(
        [
            pad_rows(head_params[0:2].reshape(2 * heads, 1)),
            pad_rows(jnp.exp(head_params[2:4]).reshape(2 * heads, 1)),
            pad_rows(head_params[4].reshape(heads, 1)),
        ],
        axis=1,
    )
    *kept, gated, squares = run_fwd(proj, live[None, :], cx, cbc, hp, heads)
    donorm = dot(wide_out, dbranch, NT)
    inner = jnp.sum(gated * (donorm * out_gain[:, None]), axis=0, keepdims=True)
    stats = lax.psum(jnp.concatenate([squares, inner], axis=0), "narrow")
    inner_total = chans * lax.axis_size("narrow")
    rms = lax.rsqrt(stats[0:1] / inner_total + 1e-05)
    coef = rms**3 * stats[1:2] / inner_total
    onorm = gated * rms * out_gain[:, None]
    branch = lax.psum_scatter(dot(onorm, wide_out, TN), "narrow", scatter_dimension=0, tiled=True)
    block_out = hidden_in + live_own[:, None] * branch
    g_out = lax.psum(dot(onorm, dbranch), "wide")

    dproj, d_cx, d_cbc, d_hp, d_og = run_bwd(
        proj, kept, donorm, rms, coef, out_gain[:, None], cx, cbc, hp, heads
    )
    d_normed = dot(dproj, w_in, TT)
    d_w = dot(normed, dproj, TT)
    dnormed = lax.psum_scatter(d_normed, "narrow", scatter_dimension=0, tiled=True)
    own_inv = lax.dynamic_slice_in_dim(inv_rms, row_start, own_rows, 0)[:, None]
    total_dot = jnp.sum(hidden_in * full_gain * dnormed, axis=1, keepdims=True)
    in_grad = out_cot + (
        own_inv * full_gain * dnormed - hidden_in * (own_inv**3 * total_dot / width)
    )
    d_gain = jnp.sum(hidden_in * own_inv * dnormed, axis=0)

    g_zx = lax.psum(d_w[:, 0 : 2 * chans], "wide")
    g_dt, g_cx, g_hp, g_og = lax.psum((d_w[:, 2 * chans + n4 :], d_cx, d_hp, d_og), "wide")
    g_bc, g_cbc, g_gain = lax.psum(
        (d_w[:, 2 * chans : 2 * chans + n4], d_cbc, d_gain), ("wide", "narrow")
    )
    shard = norm_gain.shape[0]
    g_ng = lax.dynamic_slice_in_dim(g_gain, narrow_id * shard, shard, 0)
    g_dt = jnp.transpose(g_dt[:, 0 : 2 * heads].reshape(width, 2, heads), (0, 2, 1))
    g_cx, g_cbc, g_og = g_cx.T, g_cbc.T, g_og[:, 0]
    g_head = jnp.concatenate(
        [
            g_hp[0 : 2 * heads, 0].reshape(2, heads),
            g_hp[0 : 2 * heads, 1].reshape(2, heads),
            g_hp[0:heads, 2].reshape(1, heads),
        ],
        axis=0,
    )
    local_squares = square_sum((g_zx, g_out, g_dt, g_cx, g_head, g_og, g_ng))
    total_squares = lax.psum(local_squares, "narrow") + square_sum((g_bc, g_cbc))
    clip_norm = jnp.sqrt(total_squares)
    factor = 1.0 / jnp.maximum(clip_norm, 1.0)
    c_zx, c_out, c_bc, c_dt = g_zx * factor, g_out * factor, g_bc * factor, g_dt * factor
    c_cx, c_cbc, c_head, c_og, c_ng = (
        g_cx * factor,
        g_cbc * factor,
        g_head * factor,
        g_og * factor,
        g_ng * factor,
    )
    halves = (c_zx[:, 0:chans], c_zx[:, chans:])
    own_zx = lax.dynamic_slice_in_dim(c_zx, wide_id * rows, rows, 0)
    own_halves = (own_zx[:, 0:chans], own_zx[:, chans:])
    left_zx = jnp.stack(
        [
            0.5 * left_statistic_gate[m, 0] + 0.5 * dot(own_halves[m], halves[m], NT)
            for m in range(2)
        ]
    )[:, None]
    right_zx = jnp.stack(
        [0.5 * stat_right_zx[m] + 0.5 * dot(halves[m], halves[m], TN) for m in range(2)]
    )
    new_zx = jnp.stack(
        [
            w_zx[m]
            - 0.5
            * dot(dot(inverse_root_left_gate[m, 0], halves[m]), inverse_root_right_gate[m])
            for m in range(2)
        ]
    )
    cols = w_out.shape[1]
    own_out = lax.dynamic_slice_in_dim(c_out, wide_id * cols, cols, 1)
    left_out = 0.5 * stat_left_out + 0.5 * dot(c_out, c_out, NT)
    right_out = 0.5 * stat_right_out + 0.5 * dot(own_out, c_out, TN)[None]
    new_out = w_out - 0.5 * dot(dot(root_left_out, c_out), root_right_out[0], NT)
    own_bc = lax.dynamic_slice_in_dim(c_bc, wide_id * rows, rows, 0)
    own_dt = lax.dynamic_slice_in_dim(c_dt, wide_id * rows, rows, 0)
    rate = 10.0
    return (
        block_out,
        in_grad,
        clip_norm,
        jnp.stack(own_halves),
        new_zx,
        left_zx,
        right_zx,
        own_out,
        new_out,
        left_out,
        right_out,
        own_bc,
        w_bc - rate * own_bc,
        own_dt,
        w_dt - rate * own_dt,
        c_cx,
        conv_x - rate * c_cx,
        c_cbc,
        conv_bc - rate * c_cbc,
        c_head,
        head_params - rate * c_head,
        c_og,
        out_gain - rate * c_og,
        c_ng,
        norm_gain - rate * c_ng,
    )


MESH = pl.DeviceIdType.MESH
MIB = 1024 * 1024


class Place:
    def __init__(self, wide):
        self.wide = wide
        self.depth = wide // 2
        self.w, self.n = lax.axis_index("wide"), lax.axis_index("narrow")
        self.z, self.x = self.w // 2, self.w % 2
        self.y, self.c = self.n // 2, self.n % 2
        self.core = (self.w, self.y * 2 + 1 - self.c)
        self.row = (self.w, (1 - self.y) * 2 + self.c)
        self.corner = (self.w, (1 - self.y) * 2 + 1 - self.c)
        self.across = (self.z * 2 + 1 - self.x, self.n)

    def group(self):
        return [self.core, self.row, self.corner]

    def along(self, k):
        return ((self.z + k) % self.depth) * 2 + self.x, self.n

    def others(self, k):
        return (self.w + k) % self.wide, self.n


class Copy:
    def __init__(self, src, dst, send, recv, device):
        def piece(u, v):
            return pltpu.make_async_remote_copy(
                src_ref=u, dst_ref=v, send_sem=send, recv_sem=recv, device_id=device, device_id_type=MESH
            )

        shape = src.shape
        unit = 8 if len(shape) == 2 else 1
        count = max(1, round(4 * math.prod(shape) / 49152))
        while shape[0] % (count * unit):
            count -= 1
        size = shape[0] // count
        self.whole = piece(src, dst)
        self.pieces = [
            piece(src.at[i * size : (i + 1) * size], dst.at[i * size : (i + 1) * size]) for i in range(count)
        ]

    def start(self):
        for item in self.pieces:
            item.start()

    def wait_recv(self):
        self.whole.wait_recv()

    def wait_send(self):
        self.whole.wait_send()


class Links:
    def __init__(self, send, recv):
        self.send, self.recv, self.count, self.started = send, recv, 0, []

    def plan(self, src, dst, device):
        i = self.count
        self.count = i + 1
        item = Copy(src, dst, self.send.at[i], self.recv.at[i], device)
        self.started.append(item)
        return item

    def copy(self, src, dst, device):
        item = self.plan(src, dst, device)
        item.start()
        return item

    def release(self, items):
        for item in items:
            item.wait_send()
        self.started = [item for item in self.started if all(item is not done for done in items)]

    def drain(self):
        self.release(list(self.started))


def arrived(copies):
    for item in copies:
        item.wait_recv()


def begin(copies):
    for item in copies:
        item.start()


def greet(devices):
    barrier = pltpu.get_barrier_semaphore()
    for device in devices:
        pl.semaphore_signal(barrier, inc=1, device_id=device, device_id_type=MESH)
    return lambda: pl.semaphore_wait(barrier, len(devices))


def as_row(col):
    return jnp.transpose(jnp.broadcast_to(col, (col.shape[0], 128)))[0:1]


def as_col(row):
    return jnp.transpose(jnp.broadcast_to(row, (128, 128)))[:, 0:1]


def flat(v):
    return v.reshape(-1, v.shape[-1])


class Piece:
    def __init__(self, here, links, part, x_rx, z_rx, full, square):
        self.here, self.part, self.x_rx, self.z_rx = here, part, x_rx, z_rx
        self.full, self.square = full, square
        steps = range(1, here.depth)
        place, column = full.at[here.z, here.x], full.at[:, here.x]
        self.first = links.plan(part.at[:, 1 - here.x], x_rx, here.across)
        self.second = [
            links.plan(x_rx.at[(here.z + k) % here.depth], z_rx.at[k - 1], here.along(k)) for k in steps
        ]
        self.third = [links.plan(place, place, here.along(k)) for k in steps]
        self.fourth = links.plan(column, column, here.across)

    def start(self):
        self.first.start()

    def fold(self):
        self.first.wait_recv()
        for k in range(self.here.depth):
            self.x_rx[k] = self.x_rx[k] + self.part[k, self.here.x]
        begin(self.second)

    def own(self):
        arrived(self.second)
        total = self.x_rx[self.here.z]
        for k in range(1, self.here.depth):
            total = total + self.z_rx[k - 1]
        self.full[self.here.z, self.here.x] = total
        begin(self.third)
        self.square[...] = jnp.broadcast_to(total_square(total), self.square.shape)

    def spread(self):
        arrived(self.third)
        self.fourth.start()

    def finish(self):
        self.fourth.wait_recv()


def total_square(v):
    return jnp.sum(jnp.sum(v * v, axis=0, keepdims=True), axis=1, keepdims=True)


def layer_kernel(
    wide,
    heads,
    shard,
    inner_total,
    length_ref,
    hidden_ref,
    cot_ref,
    gain_ref,
    w_ref,
    wout_ref,
    bcw_ref,
    dtw_ref,
    cx_in,
    cbc_in,
    hp_in,
    og_in,
    block_ref,
    grad_ref,
    gfull,
    bc_own,
    dt_own,
    sv_sum,
    norm_ref,
    hq,
    cq,
    wz_g,
    wx_g,
    wo_g,
    bc_g,
    dt_g,
    gain_g,
    dtt,
    gain_col,
    gain_row,
    turn_s,
    cx_ref,
    cbc_ref,
    hp_ref,
    og_ref,
    live_ref,
    inv_ref,
    proj,
    y_s,
    xc,
    dx_act,
    b_s,
    c_s,
    dbc_act,
    step_s,
    cum_s,
    cumex_s,
    hcat,
    inner_s,
    don,
    onorm,
    dy_s,
    dh_s,
    db_s,
    dc_s,
    din_s,
    g_s,
    cv_s,
    v_s,
    dd_s,
    tq_s,
    cols_s,
    dcbc_s,
    dhp_s,
    dog_s,
    dgain_s,
    stat_own,
    stat_g,
    part,
    x_rx,
    z_rx,
    core_rx,
    row_rx,
    gbc,
    bc_core,
    bc_row,
    bc_mine,
    bc_rx,
    gdt,
    dt_rx,
    shared_g,
    sv_g,
    norm_n,
    norm_w,
    square_s,
    hq_hi,
    hq_lo,
    wt_hi,
    wt_lo,
    send,
    recv,
    stat_send,
    stat_recv,
):
    here = Place(wide)
    links = Links(send, recv)
    w, n, z, x, y, c, depth = here.w, here.n, here.z, here.x, here.y, here.c, here.depth
    group = here.group()
    far = [here.others(k) for k in range(1, wide)]
    own_rows, width = hidden_ref.shape
    chans, tokens = y_s.shape
    state = b_s.shape[0] // 2
    blocks = tokens // SPAN
    parts = tokens // own_rows
    thirds = chans // 128
    z_ref, x_ref, bc_ref, pre_ref = pieces(proj, chans, state)
    met = greet(group + far)
    jobs = [
        Piece(
            here, links, part.at[i if i < 2 * thirds else i - thirds], x_rx.at[i], z_rx.at[i],
            gfull.at[i], square_s.at[i],
        )
        for i in range(3 * thirds)
    ]
    z_jobs, x_jobs, o_jobs = jobs[0:thirds], jobs[thirds : 2 * thirds], jobs[2 * thirds :]

    half = bcw_ref.shape[0] // 2
    wx_g[z, x] = w_ref[1]
    bc_g[z, x, c] = bcw_ref[pl.ds(pl.multiple_of(c * half, 8), half), :]
    dt_g[z, x] = jnp.zeros(dt_g.shape[2:], F32)
    for h in range(heads):
        for i in range(2):
            row = i * heads + h
            dt_g[z, x, row : row + 1, 0 : dtw_ref.shape[2]] = dtw_ref[h, i : i + 1, :]
    line = gain_ref[...].reshape(1, shard)
    gain_g[n] = jnp.zeros(gain_g.shape[1:], F32)
    for i in range((shard + 127) // 128):
        size = min(128, shard - 128 * i)
        gain_g[n, i : i + 1, 0:size] = line[:, 128 * i : 128 * i + size]
    squares = jnp.zeros((1, own_rows), F32)
    for i in range(width // 128):
        turned = jnp.transpose(hidden_ref[:, i * 128 : (i + 1) * 128])
        squares = squares + jnp.sum(turned * turned, axis=0, keepdims=True)
        hq[n, i * 128 : (i + 1) * 128, :] = turned
    inv_ref[...] = lax.rsqrt(squares / width + 1e-05)
    for i in range(width // 128):
        hq[n, i * 128 : (i + 1) * 128, :] = hq[n, i * 128 : (i + 1) * 128, :] * inv_ref[...]
    met()

    def along(ref):
        return [links.copy(ref, ref, here.along(k)) for k in range(1, depth)]

    def exchange(ref):
        return [links.copy(ref, ref, here.row), links.copy(ref, ref, here.core)]

    class Relay:
        def __init__(self, *views):
            self.views = views
            self.direct = [along(view(z)) for view in views]
            self.passed = []

        def begin(self):
            self.passed = [links.copy(view(z), view(z), here.across) for view in self.views]

        def forward(self):
            for k in range(1, depth):
                source = (z + depth - k) % depth
                for view, copies in zip(self.views, self.direct):
                    copies[k - 1].wait_recv()
                    self.passed.append(links.copy(view(source), view(source), here.across))

        def wait(self):
            arrived(self.passed)

    h_copies = exchange(hq.at[n])
    gain_copies = [links.copy(gain_g.at[n], gain_g.at[n], device) for device in group]
    early = Relay(lambda i: bc_g.at[i, x, c], lambda i: dt_g.at[i, x])
    early.begin()
    first = Relay(lambda i: wx_g.at[i, x])
    first.begin()

    wz_g[z, x] = w_ref[0]
    wo_g[z, x] = wout_ref[...]
    live_ref[...] = jnp.where(iota((1, tokens), 1) < length_ref[0], 1.0, 0.0)
    live_own = live_ref[:, pl.ds(pl.multiple_of(n * own_rows, 128), own_rows)]
    for i in range(width // 128):
        cq[n, i * 128 : (i + 1) * 128, :] = jnp.transpose(cot_ref[:, i * 128 : (i + 1) * 128]) * live_own
    turn_s[...] = jnp.zeros_like(turn_s)
    for ref, out in ((cx_in, cx_ref), (cbc_in, cbc_ref)):
        for i in range(ref.shape[1] // 128):
            turn_s[0:4, :] = ref[:, i * 128 : (i + 1) * 128]
            out[i * 128 : (i + 1) * 128, :] = jnp.transpose(turn_s[...])[:, 0:4]
    turn_s[...] = jnp.zeros_like(turn_s)
    turn_s[0:1, 0:heads] = hp_in[0:1, :]
    turn_s[0:1, heads : 2 * heads] = hp_in[1:2, :]
    turn_s[1:2, 0:heads] = jnp.exp(hp_in[2:3, :])
    turn_s[1:2, heads : 2 * heads] = jnp.exp(hp_in[3:4, :])
    turn_s[2:3, 0:heads] = hp_in[4:5, :]
    hp_ref[...] = jnp.transpose(turn_s[...])[0:16, 0:3]
    og_line = og_in[...].reshape(1, chans)
    for i in range(thirds):
        og_ref[i * 128 : (i + 1) * 128, :] = as_col(og_line[:, i * 128 : (i + 1) * 128])
    cols_s[...] = jnp.zeros_like(cols_s)
    dcbc_s[...] = jnp.zeros_like(dcbc_s)
    dhp_s[...] = jnp.zeros_like(dhp_s)

    def cut(q):
        hq_hi[q], hq_lo[q] = halves(hq[q])

    cut(n)
    h_copies[1].wait_recv()
    cut(here.core[1])
    early.forward()
    first.forward()
    second = Relay(lambda i: wz_g.at[i, x])
    h_copies[0].wait_recv()
    other = here.row[1]
    h_far = links.copy(hq.at[other], hq.at[other], here.core)
    c_copies = exchange(cq.at[n])
    arrived(gain_copies)
    for q in range(parts):
        turned = jnp.transpose(jnp.concatenate([gain_g[q], jnp.zeros((120, 128), F32)], axis=0))
        for i in range((shard + 127) // 128):
            size = min(128, shard - 128 * i)
            start = shard * q + 128 * i
            gain_col[start : start + size, :] = turned[0:size, i : i + 1]
    for i in range(width // 128):
        gain_row[:, i * 128 : (i + 1) * 128] = as_row(gain_col[i * 128 : (i + 1) * 128, :])

    def turn(ref, row, scale=True):
        for i in range(ref.shape[-1] // 128):
            cols = flat(ref[..., i * 128 : (i + 1) * 128])
            if scale:
                cols = cols * gain_col[...]
            for dst, value in zip((wt_hi, wt_lo), halves(jnp.transpose(cols))):
                dst[row + i * 128 : row + (i + 1) * 128, :] = value

    def quarter(q):
        return pl.ds(pl.multiple_of(q * own_rows, 128), own_rows)

    def each_quarter(body):
        def step(q, _):
            body(q)
            return 0

        lax.fori_loop(0, parts, step, 0)

    def rows_of(start, stop):
        return wt_hi[start:stop, :], wt_lo[start:stop, :]

    def project(out_ref, weights):
        def body(q):
            out_ref[:, quarter(q)] = product(weights(), (hq_hi[q], hq_lo[q]))

        each_quarter(body)

    early.wait()
    bc_core_copy = links.copy(bc_g.at[:, :, c], bc_g.at[:, :, c], here.core)
    lanes = width // wide
    for i in range(wide):
        dtt[:, i * lanes : (i + 1) * lanes] = dt_g[i // 2, i % 2][:, 0:lanes]
    last = 2 * chans + 4 * state
    wt_hi[last:, :], wt_lo[last:, :] = halves(dtt[...] * gain_row[...])
    bc_core_copy.wait_recv()
    turn(bc_g, 2 * chans)
    first.wait()
    second.begin()
    turn(wx_g, chans)
    h_far.wait_recv()
    cut(here.row[1])
    cut(here.corner[1])
    project(proj.at[chans:], lambda: rows_of(chans, last + 16))
    second.forward()
    third = Relay(lambda i: wo_g.at[i, x])
    third.begin()
    c_copies[0].wait_recv()
    c_far = links.copy(cq.at[other], cq.at[other], here.core)
    convolve(x_ref, bc_ref, live_ref, cx_ref, cbc_ref, xc, dx_act, b_s, c_s, dbc_act)
    second.wait()
    third.forward()
    step_sizes(pre_ref, hp_ref, step_s, cum_s, cumex_s, heads)
    states(xc, b_s, step_s, cum_s, dh_s, hcat, heads)
    turn(wz_g, 0)
    project(z_ref, lambda: rows_of(0, chans))

    def stat_copy(j, b):
        return pltpu.make_async_remote_copy(
            src_ref=stat_own.at[b],
            dst_ref=stat_g.at[n, b],
            send_sem=stat_send.at[j, b],
            recv_sem=stat_recv.at[j, b],
            device_id=group[j],
            device_id_type=MESH,
        )

    def tell(b, row):
        stats = jnp.broadcast_to(row, (8, SPAN))
        stat_own[b] = stats
        stat_g[n, b] = stats
        for j in range(3):
            stat_copy(j, b).start()

    def told(b):
        for j in range(3):
            stat_copy(j, b).wait_recv()
        total = stat_g[0, b]
        for q in range(1, parts):
            total = total + stat_g[q, b]
        return total[0:1]

    def emit(b, sl, h, rows, gated, sums):
        onorm[rows, sl] = gated
        row = jnp.sum(gated * gated, axis=0, keepdims=True)
        row = row if sums is None else row + sums
        if h == heads - 1:
            tell(b, row)
        return row

    outputs(z_ref, xc, b_s, c_s, step_s, cum_s, cumex_s, hcat, hp_ref, y_s, inner_s, heads, emit)
    rms = jnp.concatenate(
        [lax.rsqrt(told(b) / inner_total + 1e-05) for b in range(blocks)], axis=1
    )

    def scale_rows(i, _):
        rows = pl.ds(pl.multiple_of(i * 8, 8), 8)
        onorm[rows, :] = onorm[rows, :] * rms * og_ref[rows, :]
        return 0

    lax.fori_loop(0, chans // 8, scale_rows, 0, unroll=2)
    c_copies[1].wait_recv()
    c_far.wait_recv()

    def weight_grad(put, right, left=lambda q: (hq_hi[q], hq_lo[q])):
        def body(q):
            put(q, product(left(q), halves(right(q)), NT))

        each_quarter(body)

    block_shape = part.shape[1:]

    def add_to(start, count):
        def put(q, value):
            for i in range(count):
                ref = part.at[start + i]
                piece = value[:, i * 128 : (i + 1) * 128].reshape(block_shape)
                ref[...] = jnp.where(q == 0, piece, ref[...] + piece)

        return put

    def scaled(i):
        part[i] = (flat(part[i]) * gain_col[...]).reshape(block_shape)

    part[...] = jnp.zeros_like(part)
    for start, stop in ((0, 1), (1, thirds)):
        rows = slice(start * 128, stop * 128)
        weight_grad(
            add_to(thirds + start, stop - start),
            lambda q, rows=rows: onorm[rows, quarter(q)],
            lambda q: halves(cq[q]),
        )
        for job in o_jobs[start:stop]:
            job.start()
    third.wait()
    turn(wo_g, 0, False)

    def donorm(q):
        don[:, quarter(q)] = product(rows_of(0, chans), halves(cq[q]))

    each_quarter(donorm)

    def inner_sums(b, _):
        sl = pl.ds(pl.multiple_of(b * SPAN, SPAN), SPAN)
        gate = z_ref[:, sl]
        gated = y_s[:, sl] * (gate * sigmoid(gate))
        tell(blocks + b, jnp.sum(gated * (don[:, sl] * og_ref[...]), axis=0, keepdims=True))
        return 0

    lax.fori_loop(0, blocks, inner_sums, 0)

    links.release(c_copies + [c_far])

    class Return:
        def __init__(self, rx, row_rx, compute, steps=((), (), (), ())):
            self.rx, self.row_rx = rx, row_rx
            first = links.count
            self.cores = [links.plan(cq.at[k * 2 + 1 - c], rx.at[k], here.core) for k in range(2)]
            self.last = links.plan(rx.at[1 - y], row_rx, here.row)

            def body(k, _):
                q = (k % 2) * 2 + (c + 1 + k // 2) % 2
                cq[q] = compute(q)

                @pl.when(k < 2)
                def _():
                    i = first + k % 2
                    Copy(cq.at[q], rx.at[k % 2], links.send.at[i], links.recv.at[i], here.core).start()

                for at, items in enumerate(steps):

                    @pl.when(k == at)
                    def _(items=items):
                        for step in items:
                            step()

                return 0

            lax.fori_loop(0, 4, body, 0)

        def fold(self):
            arrived(self.cores)
            for k in range(2):
                self.rx[k] = self.rx[k] + cq[k * 2 + c]
            self.last.start()

        def total(self):
            self.last.wait_recv()
            return self.rx[y] + self.row_rx[...]

    o0, o1, o2 = o_jobs
    z0, z1, z2 = z_jobs
    x0, x1, x2 = x_jobs
    branch = Return(core_rx.at[0], row_rx.at[0], lambda q: dot3(flat(wo_g[...]), onorm[:, quarter(q)]))
    o0.fold()
    told_inner = jnp.concatenate([told(blocks + b) for b in range(blocks)], axis=1)
    coef = rms**3 * told_inner / inner_total
    gate_back(z_ref, y_s, don, rms, coef, og_ref, dy_s, z_ref, dog_s)
    weight_grad(add_to(0, thirds), lambda q: z_ref[:, quarter(q)])
    for i, job in enumerate(z_jobs):
        scaled(i)
        job.start()
    o1.fold()
    o0.own()

    def x_grad(i):
        links.release([o_jobs[i].first])
        part[thirds + i] = jnp.zeros(block_shape, F32)
        weight_grad(add_to(thirds + i, 1), lambda q: x_ref[i * 128 : (i + 1) * 128, quarter(q)])
        scaled(thirds + i)

    within = [
        {0: [o2.fold], 6: [o1.own, z0.fold]},
        {1: [o2.own, z2.fold], 3: [branch.fold], 5: [o1.spread]},
        {0: [z1.own], 5: [o2.spread], 6: [x1.fold]},
    ]
    between = [
        {6: [o0.spread], 7: [z1.fold]},
        {6: [z0.own, x0.fold]},
        {4: [z2.own]},
    ]

    def ticks(plan):
        def tick(b):
            for at, steps in plan.items():

                @pl.when(b == at)
                def _(steps=steps):
                    for step in steps:
                        step()

        return tick

    for i, chosen in enumerate(pairs_of(heads)):
        back_intra(
            xc, c_s, inner_s, step_s, cum_s, cumex_s, hcat, hp_ref, dy_s, y_s, dh_s, dc_s,
            din_s, g_s, cv_s, dd_s, chosen, heads, ticks(within[i]),
        )
        back_states(cum_s, hcat, dh_s, tq_s, state, chosen, heads)
        back_inter(xc, b_s, step_s, cum_s, y_s, dh_s, db_s, v_s, chosen, heads, ticks(between[i]))
        conv_x_back(x_ref, cx_ref, dx_act, y_s, x_ref, cols_s, i * 128, 128)
        x_grad(i)
        x_jobs[i].start()

    back_logs(
        b_s, c_s, pre_ref, step_s, hp_ref, pre_ref, dhp_s, db_s, dc_s, din_s, g_s, cv_s, v_s, dd_s, tq_s, heads
    )
    z0.spread()
    conv_bc_back(bc_ref, cbc_ref, dbc_act, db_s, dc_s, bc_ref, dcbc_s)
    gbc_shape = gbc.shape

    def add_bc(q, value):
        gbc[...] = jnp.where(q == 0, value.reshape(gbc_shape), gbc[...] + value.reshape(gbc_shape))

    gbc[...] = jnp.zeros_like(gbc)
    weight_grad(add_bc, lambda q: bc_ref[:, quarter(q)])
    gbc[...] = (flat(gbc[...]) * gain_col[...]).reshape(gbc_shape)
    bc_first = links.copy(gbc.at[:, :, 1 - c], bc_core, here.core)
    x0.own()
    x2.fold()
    dt_grad = jnp.zeros((16, width), F32)
    for q in range(parts):
        step = halves(pre_ref[:, q * own_rows : (q + 1) * own_rows])
        dt_grad = dt_grad + product(step, (hq_hi[q], hq_lo[q]), NT)
    dt_grad = dt_grad * gain_row[...]
    gdt[...] = jnp.zeros_like(gdt)
    for i in range(wide):
        gdt[i, :, 0:lanes] = dt_grad[:, i * lanes : (i + 1) * lanes]
    dt_rx[w] = gdt[w]
    dt_copies = [links.copy(gdt.at[device[0]], dt_rx.at[w], device) for device in far]
    dgain_s[...] = jnp.zeros_like(dgain_s)
    bc_first.wait_recv()
    for k in range(2):
        bc_core[:, k] = bc_core[:, k] + gbc[:, k, c]
    for k in range(wide):
        bc_mine[k] = bc_core[k, 1 - y]
    bc_second = links.copy(bc_mine, bc_row, here.row)

    links.release(branch.cores)

    for k in range(parts):
        pieces_of = []
        for ref, start in ((wz_g, 0), (wx_g, chans), (bc_g, 2 * chans)):
            a, b = max(k * own_rows, start), min((k + 1) * own_rows, start + ref.shape[-1])
            if a < b:
                pieces_of.append(flat(ref[..., a - start : b - start]))
        hq_hi[k], hq_lo[k] = halves(jnp.concatenate(pieces_of, axis=1))

    def normed_back(q):
        sl = quarter(q)

        def add(k, value):
            rows = pl.ds(pl.multiple_of(k * own_rows, 8), own_rows)
            return value + product((hq_hi[k], hq_lo[k]), halves(proj[rows, sl]))

        value = lax.fori_loop(0, parts, add, dot3(dtt[...], pre_ref[:, sl], TN))
        dgain_s[...] = dgain_s[...] + jnp.sum(value * hq[q], axis=1, keepdims=True)
        return value

    back = Return(core_rx.at[1], row_rx.at[1], normed_back, ([z1.spread], [], [x1.own], []))
    back.fold()
    small = 128
    shared_g[n] = jnp.zeros(shared_g.shape[1:], F32)
    for i in range(4 * state // 128):
        sl = slice(i * 128, (i + 1) * 128)
        shared_g[n, 0:4, sl] = jnp.transpose(dcbc_s[sl, :])[0:4]
    for i in range(width // 128):
        shared_g[n, 8 + i : 9 + i, 0:128] = as_row(dgain_s[i * 128 : (i + 1) * 128, :])
    shared_copies = [links.copy(shared_g.at[n], shared_g.at[n], device) for device in group]
    bc_second.wait_recv()
    links.release([bc_second])
    for k in range(wide):
        bc_mine[k] = bc_core[k, y] + bc_row[k]
    bc_rx[w] = bc_mine[w]
    bc_copies = [links.copy(bc_mine.at[device[0]], bc_rx.at[w], device) for device in far]
    sv_g[w] = jnp.zeros(sv_g.shape[1:], F32)
    for i in range(thirds):
        sl = slice(i * 128, (i + 1) * 128)
        sv_g[w, 0:4, sl] = jnp.transpose(cols_s[sl, :])[0:4]
        sv_g[w, 4:5, sl] = as_row(dog_s[sl, :])
    sv_g[w, :, chans : chans + small] = dhp_s[...]
    z2.spread()
    arrived(shared_copies)
    total = shared_g[0]
    for q in range(1, parts):
        total = total + shared_g[q]
    sv_g[w, :, chans + small :] = total
    sv_copies = [links.copy(sv_g.at[w], sv_g.at[w], device) for device in far]

    arrived(bc_copies)
    own = bc_rx[0]
    for k in range(1, wide):
        own = own + bc_rx[k]
    bc_own[n] = own
    bc_group = [links.copy(bc_own.at[n], bc_own.at[n], device) for device in group]
    squares = total_square(own)
    arrived(dt_copies)
    own = dt_rx[0]
    for k in range(1, wide):
        own = own + dt_rx[k]
    dt_own[...] = own
    squares = squares + total_square(own)
    arrived(sv_copies)
    own = sv_g[0]
    for k in range(1, wide):
        own = own + sv_g[k]
    sv_sum[...] = own
    x0.spread()
    x2.own()
    for i in range(3 * thirds):
        squares = squares + square_s[i][:, 0:1]
    once = jnp.where(w == 0, 1.0, 0.0)
    squares = squares + once * total_square(own[:, 0 : chans + small])
    squares = squares + jnp.where(n == 0, once, 0.0) * total_square(own[:, chans + small :])
    norm_n[n] = jnp.broadcast_to(squares, (8, 128))
    norm_copies = [links.copy(norm_n.at[n], norm_n.at[n], device) for device in group]

    x1.spread()

    block = branch.total() * live_ref[:, pl.ds(pl.multiple_of(n * own_rows, 128), own_rows)]
    for i in range(width // 128):
        sl = slice(i * 128, (i + 1) * 128)
        block_ref[:, sl] = hidden_ref[:, sl] + jnp.transpose(block[sl, :])
    arrived(norm_copies)
    norm_w[w] = norm_n[0] + norm_n[1] + norm_n[2] + norm_n[3]
    wide_copies = [links.copy(norm_w.at[w], norm_w.at[w], device) for device in far]
    x2.spread()
    dn = back.total() * gain_col[...]
    dots = jnp.sum(dn * hq[n], axis=0, keepdims=True) / width
    for i in range(width // 128):
        sl = slice(i * 128, (i + 1) * 128)
        value = inv_ref[...] * (dn[sl] - hq[n, sl, :] * dots)
        grad_ref[:, sl] = cot_ref[:, sl] + jnp.transpose(value)
    arrived(wide_copies)
    total = norm_w[0]
    for k in range(1, wide):
        total = total + norm_w[k]
    norm_ref[...] = jnp.sqrt(total)
    for job in jobs:
        job.finish()
    arrived(bc_group)
    links.drain()

    def sent(b, _):
        for j in range(3):
            stat_copy(j, b).wait_send()
        return 0

    lax.fori_loop(0, 2 * blocks, sent, 0)


def run_layer(lengths, hidden, cot, gain, w_zx, w_out, w_bc, dtw, cx, cbc, hp, og, heads, shard, wide, narrow):
    own_rows, width = hidden.shape
    tokens = own_rows * narrow
    chans, n4 = cx.shape[1], cbc.shape[1]
    rows = w_zx.shape[1]
    depth, blocks, half, thirds = wide // 2, tokens // SPAN, n4 // 2, chans // 128
    full, bc2, small = (chans, tokens), (half, tokens), (16, tokens)
    quarters = (narrow, width, own_rows)
    weights = (depth, 2, rows, chans)
    piece = (3 * thirds, depth, 2, rows, 128)
    quarter = (width // wide // 4, n4)
    sums = (16, chans + 128 + 256)
    shapes = [
        hidden.shape,
        hidden.shape,
        piece,
        (4,) + quarter,
        (16, 128),
        sums,
        (8, 128),
    ]
    scratch = [
        quarters,
        quarters,
        weights,
        weights,
        weights,
        (depth, 2, 2, rows // 2, n4),
        (depth, 2, 16, 128),
        (narrow, 8, 128),
        (16, width),
        (width, 1),
        (1, width),
        (128, 128),
        (chans, 4),
        (n4, 4),
        (16, 3),
        (chans, 1),
        (1, tokens),
        (1, own_rows),
        (2 * chans + n4 + 16, tokens),
        full,
        full,
        full,
        bc2,
        bc2,
        (n4, tokens),
        small,
        small,
        small,
        (blocks, chans, half),
        (blocks, SPAN, SPAN),
        full,
        full,
        full,
        (blocks, chans, half),
        bc2,
        bc2,
        (blocks, SPAN, SPAN),
        small,
        small,
        small,
        small,
        (blocks, 16, SPAN),
        (chans, 128),
        (n4, 128),
        (16, 128),
        (chans, 1),
        (width, 1),
        (2 * blocks, 8, 128),
        (narrow, 2 * blocks, 8, 128),
        (2 * thirds,) + piece[1:],
        (3 * thirds, depth, rows, 128),
        (3 * thirds, depth - 1, rows, 128),
        (2, 2, width, own_rows),
        (2, width, own_rows),
        (wide, 2, 2) + quarter,
        (wide, 2) + quarter,
        (wide,) + quarter,
        (wide,) + quarter,
        (wide,) + quarter,
        (wide, 16, 128),
        (wide, 16, 128),
        (narrow, 16, 256),
        (wide,) + sums,
        (narrow, 8, 128),
        (wide, 8, 128),
        (3 * thirds, 1, 128),
    ]
    lows = [quarters] * 2 + [(2 * chans + n4 + 16, width)] * 2
    copies = 200
    operands = (lengths, hidden, cot, gain, w_zx, w_out, w_bc, dtw, cx, cbc, hp, og)
    return pl.pallas_call(
        functools.partial(layer_kernel, wide, heads, shard, chans * narrow),
        out_shape=[jax.ShapeDtypeStruct(shape, F32) for shape in shapes],
        in_specs=[pl.BlockSpec(memory_space=pltpu.SMEM)]
        + [pl.BlockSpec(memory_space=pltpu.VMEM)] * (len(operands) - 1),
        scratch_shapes=[pltpu.VMEM(shape, F32) for shape in scratch]
        + [pltpu.VMEM(shape, jnp.bfloat16) for shape in lows]
        + [
            pltpu.SemaphoreType.DMA((copies,)),
            pltpu.SemaphoreType.DMA((copies,)),
            pltpu.SemaphoreType.DMA((3, 2 * blocks)),
            pltpu.SemaphoreType.DMA((3, 2 * blocks)),
        ],
        compiler_params=pltpu.CompilerParams(
            vmem_limit_bytes=62 * MIB, collective_id=0, has_side_effects=True
        ),
        cost_estimate=pl.CostEstimate(flops=20_000_000_000, bytes_accessed=20_000_000, transcendentals=0),
    )(*operands)


def finish_kernel(
    wide,
    narrow,
    gfull,
    bc_own,
    dt_own,
    sv,
    norm_ref,
    block_in,
    grad_in,
    stat_l,
    stat_r,
    stat_lo,
    stat_ro,
    root_l,
    root_r,
    root_lo,
    root_ro,
    w_ref,
    wout_ref,
    bcw_ref,
    dtw_ref,
    cx_ref,
    cbc_ref,
    hp_ref,
    og_ref,
    gain_ref,
    block_out,
    in_grad,
    clip,
    g_zx,
    new_zx,
    new_l,
    new_r,
    g_out,
    new_out,
    new_lo,
    new_ro,
    g_bc,
    new_bc,
    g_dt,
    new_dt,
    g_cx,
    new_cx,
    g_cbc,
    new_cbc,
    g_hp,
    new_hp,
    g_og,
    new_og,
    g_ng,
    new_ng,
    g_s,
    l_s,
    r_s,
    lo_s,
    ro_s,
    rl_s,
    rr_s,
    rlo_s,
    rro_s,
    in_sem,
    out_sem,
):
    rate = 10.0
    chans = w_ref.shape[2]
    thirds = chans // 128
    place = lax.axis_index("wide")
    z, x = place // 2, place % 2
    factor = 1.0 / jnp.maximum(norm_ref[0:1, 0:1], 1.0)
    fetches, results = [], []

    def fetch(src, dst):
        item = pltpu.make_async_copy(src, dst, in_sem.at[len(fetches)])
        item.start()
        fetches.append(item)
        return item

    def result(src, dst):
        item = pltpu.make_async_copy(src, dst, out_sem.at[len(results)])
        item.start()
        results.append(item)

    waits = []
    for m in (2, 0, 1):
        gs = g_s.at[m * thirds : (m + 1) * thirds]
        whole_m = fetch(gfull.at[m * thirds : (m + 1) * thirds], gs)
        if m == 2:
            others = [(root_ro, rro_s), (root_lo, rlo_s), (stat_ro, ro_s), (stat_lo, lo_s)]
        else:
            others = [(root_l.at[m], rl_s.at[m]), (root_r.at[m], rr_s.at[m])]
            others += [(stat_l.at[m], l_s.at[m]), (stat_r.at[m], r_s.at[m])]
        waits.append([whole_m] + [fetch(*pair) for pair in others])
    block_out[...] = block_in[...]
    in_grad[...] = grad_in[...]
    clip[...] = norm_ref[0:1, 0:1]

    def both(m):
        for item in waits[(1, 2, 0)[m]]:
            item.wait()
        parts = [flat(g_s[m * thirds + i]) for i in range(thirds)]
        mine = [g_s[m * thirds + i, z, x] for i in range(thirds)]
        return jnp.concatenate(mine, axis=1) * factor, halves(jnp.concatenate(parts, axis=1) * factor)

    own, full = both(2)
    g_out[...] = own
    ro_s[...] = 0.5 * ro_s[...] + 0.5 * product(halves(own), full, NT)
    result(ro_s, new_ro)
    lo_s[...] = 0.5 * lo_s[...] + 0.5 * product(full, full, TN)
    result(lo_s, new_lo)
    new_out[...] = wout_ref[...] - 0.5 * dot3(product(halves(rro_s[...]), full), rlo_s[...], NT)
    for m in range(2):
        own, full = both(m)
        g_zx[m] = own
        l_s[m] = 0.5 * l_s[m] + 0.5 * product(halves(own), full, NT)
        result(l_s.at[m], new_l.at[m])
        r_s[m] = 0.5 * r_s[m] + 0.5 * product(full, full, TN)
        result(r_s.at[m], new_r.at[m])
        new_zx[m] = w_ref[m] - 0.5 * dot3(product(halves(rl_s[m]), full), rr_s[m])

    grad = flat(bc_own[...]) * factor
    g_bc[...] = grad
    new_bc[...] = bcw_ref[...] - rate * grad
    heads, _, rows = dtw_ref.shape
    for h in range(heads):
        for i in range(2):
            row = i * heads + h
            grad = dt_own[row : row + 1, 0:rows] * factor
            g_dt[h, i : i + 1, :] = grad
            new_dt[h, i : i + 1, :] = dtw_ref[h, i : i + 1, :] - rate * grad
    sums = sv[...] * factor
    grad = sums[0:4, 0:chans]
    g_cx[...] = grad
    new_cx[...] = cx_ref[...] - rate * grad
    grad = sums[4:5, 0:chans]
    g_og[...] = grad.reshape(chans)
    new_og[...] = og_ref[...] - rate * g_og[...]
    n4 = cbc_ref.shape[1]
    last = chans + 128
    grad = sums[0:4, last : last + n4]
    g_cbc[...] = grad
    new_cbc[...] = cbc_ref[...] - rate * grad
    turned = jnp.transpose(
        jnp.concatenate([sums[:, chans:last], jnp.zeros((112, 128), F32)], axis=0)
    )
    for i, (row, start) in enumerate(((0, 0), (0, heads), (1, 0), (1, heads), (2, 0))):
        grad = turned[row : row + 1, start : start + heads]
        g_hp[i : i + 1, :] = grad
        new_hp[i : i + 1, :] = hp_ref[i : i + 1, :] - rate * grad
    shard = gain_ref.shape[0]
    count = narrow * shard // 128
    line = jnp.concatenate([sums[8 + i : 9 + i, last : last + 128] for i in range(count)], axis=1)
    grad = jnp.zeros((1, shard), F32)
    for q in range(narrow):
        piece = line[:, q * shard : (q + 1) * shard]
        grad = jnp.where(lax.axis_index("narrow") == q, piece, grad)
    g_ng[...] = grad.reshape(shard)
    new_ng[...] = gain_ref[...] - rate * g_ng[...]
    for item in results:
        item.wait()


def run_finish(partials, stats, roots, params, tokens_shape, wide, narrow):
    stat_l, stat_r, stat_lo, stat_ro = stats
    w_zx, w_out, w_bc, w_dt, cx, cbc, hp, og, gain = params
    like = [w_zx, w_zx, stat_l, stat_r, w_out, w_out, stat_lo, stat_ro]
    like += [item for item in (w_bc, w_dt, cx, cbc, hp, og, gain) for _ in range(2)]
    shapes = [tokens_shape, tokens_shape, (1, 1)] + [item.shape for item in like]
    far, near = pl.BlockSpec(memory_space=pl.ANY), pl.BlockSpec(memory_space=pltpu.VMEM)
    gfull = partials[0]
    kept = [gfull, stat_l, stat_r, stat_lo, stat_ro, *roots]
    return pl.pallas_call(
        functools.partial(finish_kernel, wide, narrow),
        out_shape=[jax.ShapeDtypeStruct(shape, F32) for shape in shapes],
        in_specs=[far] + [near] * 6 + [far] * 8 + [near] * len(params),
        out_specs=[near] * 5 + [far] * 2 + [near] * 2 + [far] * 2 + [near] * (len(shapes) - 11),
        scratch_shapes=[pltpu.VMEM(item.shape, F32) for item in kept]
        + [pltpu.SemaphoreType.DMA((15,)), pltpu.SemaphoreType.DMA((6,))],
        compiler_params=pltpu.CompilerParams(vmem_limit_bytes=56 * MIB),
        cost_estimate=pl.CostEstimate(flops=4_000_000_000, bytes_accessed=20_000_000, transcendentals=0),
    )(*partials, *stats, *roots, *params)


def fast_local(
    wide,
    narrow,
    hidden_in,
    out_cot,
    lengths,
    norm_gain,
    w_zx,
    w_bc,
    w_dt,
    conv_x,
    conv_bc,
    head_params,
    out_gain,
    w_out,
    left_statistic_gate,
    stat_right_zx,
    stat_left_out,
    stat_right_out,
    inverse_root_left_gate,
    inverse_root_right_gate,
    root_left_out,
    root_right_out,
):
    heads, shard = w_dt.shape[1], norm_gain.shape[0]
    out_rows, dt_rows = w_out.T, jnp.transpose(w_dt, (1, 2, 0))
    block, grad, *partials = run_layer(
        lengths,
        hidden_in,
        out_cot,
        norm_gain,
        w_zx,
        out_rows,
        w_bc,
        dt_rows,
        conv_x,
        conv_bc,
        head_params,
        out_gain,
        heads,
        shard,
        wide,
        narrow,
    )
    (
        block_out,
        in_grad,
        clip,
        g_zx,
        new_zx,
        new_l,
        new_r,
        g_out,
        new_out,
        new_lo,
        new_ro,
        g_bc,
        new_bc,
        g_dt,
        new_dt,
        *rest,
    ) = run_finish(
        (*partials, block, grad),
        (left_statistic_gate[:, 0], stat_right_zx, stat_left_out, stat_right_out[0]),
        (inverse_root_left_gate[:, 0], inverse_root_right_gate, root_left_out, root_right_out[0]),
        (w_zx, out_rows, w_bc, dt_rows, conv_x, conv_bc, head_params, out_gain, norm_gain),
        hidden_in.shape,
        wide,
        narrow,
    )
    return (
        block_out,
        in_grad,
        clip.reshape(()),
        g_zx,
        new_zx,
        new_l[:, None],
        new_r,
        g_out.T,
        new_out.T,
        new_lo,
        new_ro[None],
        g_bc,
        new_bc,
        jnp.transpose(g_dt, (2, 0, 1)),
        jnp.transpose(new_dt, (2, 0, 1)),
        *rest,
    )


def solution(mesh):
    wide, narrow = mesh.shape["wide"], mesh.shape["narrow"]
    body = functools.partial(fast_local, wide, narrow) if (wide, narrow) == (8, 4) else local
    return jax.shard_map(
        body,
        mesh=mesh,
        in_specs=(
            P(("wide", "narrow"), None),
            P(("wide", "narrow"), None),
            P("wide"),
            P("narrow"),
            P(None, "wide", "narrow"),
            P("wide", None),
            P("wide", "narrow", None),
            P(None, "narrow"),
            P(),
            P(None, "narrow"),
            P("narrow"),
            P("narrow", "wide"),
            P(None, "narrow", "wide", None),
            P(None, "narrow", None),
            P("narrow", None),
            P("narrow", "wide", None),
            P(None, "narrow", "wide", None),
            P(None, "narrow", None),
            P("narrow", None),
            P("narrow", "wide", None),
        ),
        out_specs=(
            P(("wide", "narrow"), None),
            P(("wide", "narrow"), None),
            P(),
            P(None, "wide", "narrow"),
            P(None, "wide", "narrow"),
            P(None, "narrow", "wide", None),
            P(None, "narrow", None),
            P("narrow", "wide"),
            P("narrow", "wide"),
            P("narrow", None),
            P("narrow", "wide", None),
            P("wide", None),
            P("wide", None),
            P("wide", "narrow", None),
            P("wide", "narrow", None),
            P(None, "narrow"),
            P(None, "narrow"),
            P(),
            P(),
            P(None, "narrow"),
            P(None, "narrow"),
            P("narrow"),
            P("narrow"),
            P("narrow"),
            P("narrow"),
        ),
        check_vma=False,
    )
```

```python
import functools

import jax
import jax.numpy as jnp
from jax import lax
from jax.experimental import pallas as pl
from jax.experimental.pallas import tpu as pltpu
from jax.sharding import PartitionSpec as P

SPAN = 128
WIDTH = 64
HIGH = lax.Precision.HIGH
F32 = jnp.float32
NN = (((1,), (0,)), ((), ()))
NT = (((1,), (1,)), ((), ()))
TN = (((0,), (0,)), ((), ()))
TT = (((0,), (1,)), ((), ()))


def dot(a, b, dims=NN):
    return lax.dot_general(a, b, dims, precision=HIGH, preferred_element_type=F32)


def halves(v):
    hi = v.astype(jnp.bfloat16)
    return hi, (v - hi.astype(F32)).astype(jnp.bfloat16)


def product(a, b, dims=NN):
    (ah, al), (bh, bl) = a, b
    (left,), (right,) = dims[0]
    rows, depth = ah.shape[1 - left], ah.shape[left]

    def times(u, v):
        return lax.dot_general(u, v, dims, preferred_element_type=F32)

    if depth < 128:
        return times(
            jnp.concatenate([ah, al, ah], axis=left), jnp.concatenate([bh, bh, bl], axis=right)
        )
    if depth == 128:
        top = jnp.concatenate([ah, ah], axis=left)
        low = jnp.concatenate([al, jnp.zeros_like(al)], axis=left)
        out = times(jnp.concatenate([top, low], axis=1 - left), jnp.concatenate([bh, bl], axis=right))
        return out[0:rows] + out[rows:]
    out = times(jnp.concatenate([ah, al], axis=1 - left), bh)
    return out[0:rows] + out[rows:] + times(ah, bl)


def dot3(a, b, dims=NN):
    return product(halves(a), halves(b), dims)


def sigmoid(v):
    return 1.0 / (1.0 + jnp.exp(-v))


def split3(v):
    hi = v.astype(jnp.bfloat16)
    rest = v - hi.astype(F32)
    mid = rest.astype(jnp.bfloat16)
    lo = (rest - mid.astype(F32)).astype(jnp.bfloat16)
    return jnp.concatenate([hi, mid, lo], axis=0)


def exact_dot(v, ones):
    rows = v.shape[0]
    out = lax.dot_general(split3(v), ones, NN, preferred_element_type=F32)
    return out[0:rows] + out[rows : 2 * rows] + out[2 * rows : 3 * rows]


def iota(shape, axis):
    return lax.broadcasted_iota(jnp.int32, shape, axis)


def shift_right(v, count):
    return jnp.where(iota(v.shape, 1) >= count, pltpu.roll(v, count, axis=1), 0.0)


def shift_left(v, count):
    length = v.shape[1]
    return jnp.where(iota(v.shape, 1) < length - count, pltpu.roll(v, length - count, axis=1), 0.0)


def conv_rows(v, taps):
    count = taps.shape[1]
    total = taps[:, count - 1 : count] * v
    for j in range(count - 1):
        total = total + taps[:, j : j + 1] * shift_right(v, count - 1 - j)
    return total


def pieces(ref, chans, state):
    bc = 2 * chans
    dt = bc + 4 * state
    return ref.at[0:chans], ref.at[chans:bc], ref.at[bc:dt], ref.at[dt : dt + 16]


def convolve(x_ref, bc_ref, live_ref, cx_ref, cbc_ref, xc_ref, dx_act_ref, b_ref, c_ref, dbc_act_ref):
    chans, tokens = xc_ref.shape
    state = c_ref.shape[0] // 2
    live = live_ref[...]

    def conv_x_rows(i, _):
        rows = pl.ds(pl.multiple_of(i * 8, 8), 8)
        u = conv_rows(x_ref[rows, :], cx_ref[rows, :])
        s = sigmoid(u)
        xc_ref[rows, :] = u * s * live
        dx_act_ref[rows, :] = (s + u * s * (1.0 - s)) * live
        return 0

    lax.fori_loop(0, chans // 8, conv_x_rows, 0, unroll=2)

    def conv_bc_rows(i, _, src, dst, dst_row, shift):
        rows = pl.ds(pl.multiple_of(src * state + i * 8, 8), 8)
        out = pl.ds(pl.multiple_of(dst_row + i * 8, 8), 8)
        u = conv_rows(bc_ref[rows, :], cbc_ref[rows, :])
        s = sigmoid(u)
        dbc_act_ref[rows, :] = s + u * s * (1.0 - s)
        v = u * s
        if shift == 1:
            v = shift_right(v, 1)
        if shift == -1:
            v = shift_left(v, 1)
        dst[out, :] = v
        return 0

    for src, dst, row, shift in ((0, b_ref, 0, 0), (1, c_ref, 0, 1), (2, b_ref, state, 0), (3, c_ref, state, -1)):
        lax.fori_loop(
            0,
            state // 8,
            functools.partial(conv_bc_rows, src=src, dst=dst, dst_row=row, shift=shift),
            0,
            unroll=2,
        )


def step_sizes(pre_ref, hp_ref, step_ref, cum_ref, cumex_ref, heads):
    blocks = pre_ref.shape[1] // SPAN
    pre = pre_ref[...] + hp_ref[:, 0:1]
    steps = jnp.maximum(pre, 0.0) + jnp.log1p(jnp.exp(-jnp.abs(pre)))
    step_ref[...] = steps
    logs = -hp_ref[:, 1:2] * steps
    rows16 = iota((16, SPAN), 0)
    lane16 = iota((16, SPAN), 1)
    row_q = iota((SPAN, SPAN), 0)
    lane_q = iota((SPAN, SPAN), 1)
    upto = (row_q <= lane_q).astype(F32).astype(jnp.bfloat16)
    downto = (row_q >= lane_q).astype(F32).astype(jnp.bfloat16)
    both = jnp.concatenate([upto, downto], axis=1)
    for b in range(blocks):
        sums = exact_dot(logs[:, b * SPAN : (b + 1) * SPAN], both)
        cum = jnp.where(rows16 < heads, sums[:, 0:SPAN], sums[:, SPAN : 2 * SPAN])
        ex_f = jnp.where(lane16 >= 1, pltpu.roll(cum, 1, axis=1), 0.0)
        ex_r = jnp.where(lane16 < SPAN - 1, pltpu.roll(cum, SPAN - 1, axis=1), 0.0)
        cum_ref[:, b * SPAN : (b + 1) * SPAN] = cum
        cumex_ref[:, b * SPAN : (b + 1) * SPAN] = jnp.where(rows16 < heads, ex_f, ex_r)


def states(xc_ref, b_ref, step_ref, cum_ref, sloc_ref, hcat_ref, heads):
    blocks = xc_ref.shape[1] // SPAN
    state = b_ref.shape[0] // 2

    def local_states(b, _):
        sl = pl.ds(pl.multiple_of(b * SPAN, SPAN), SPAN)
        bcat = spread(b_ref[:, sl], state)
        tail = tails(cum_ref[:, sl], step_ref[:, sl], heads)
        left = tailed(xc_ref[:, sl], tail, range(heads), heads)
        sloc_ref[b] = dot3(left, bcat, NT)
        return 0

    lax.fori_loop(0, blocks, local_states, 0)

    lane_h = iota((WIDTH, 2 * state), 1)
    for h in range(heads):
        rows = slice(h * WIDTH, (h + 1) * WIDTH)
        carry = jnp.zeros((WIDTH, 2 * state), F32)
        for i in range(blocks):
            r = blocks - 1 - i
            hcat_ref[i, rows, 0:state] = carry[:, 0:state]
            hcat_ref[r, rows, state : 2 * state] = carry[:, state : 2 * state]
            tot_f = jnp.exp(cum_ref[h : h + 1, (i + 1) * SPAN - 1 : (i + 1) * SPAN])
            tot_r = jnp.exp(cum_ref[heads + h : heads + h + 1, r * SPAN : r * SPAN + 1])
            factor = jnp.where(lane_h < state, tot_f, tot_r)
            piece = jnp.where(lane_h < state, sloc_ref[i, rows, :], sloc_ref[r, rows, :])
            carry = carry * factor + piece


def outputs(z_ref, xc_ref, b_ref, c_ref, step_ref, cum_ref, cumex_ref, hcat_ref, hp_ref, y_ref, inner_ref, heads, emit):
    blocks = xc_ref.shape[1] // SPAN
    state = b_ref.shape[0] // 2
    row_q = iota((SPAN, SPAN), 0)
    lane_q = iota((SPAN, SPAN), 1)
    lower = row_q < lane_q
    diag = row_q == lane_q

    def block(b, _):
        sl = pl.ds(pl.multiple_of(b * SPAN, SPAN), SPAN)
        bb, cc = b_ref[:, sl], c_ref[:, sl]
        inner = jnp.where(
            lower, dot3(bb[0:state], cc[0:state], TN), dot3(bb[state:], cc[state:], TN)
        )
        inner_ref[b] = inner
        cum, steps, cumex = cum_ref[:, sl], step_ref[:, sl], cumex_ref[:, sl]
        scale = jnp.exp(cumex)
        cols = columns(cum, steps)
        sums = None
        entering = dot3(hcat_ref[b], spread(cc, state))
        x_parts = halves(xc_ref[:, sl])
        for h in range(heads):
            rows = slice(h * WIDTH, (h + 1) * WIDTH)
            decay = decays(cols, cumex, lower, diag, h, heads)
            mt = jnp.where(diag, hp_ref[h : h + 1, 2:3], inner * decay)
            y = product((x_parts[0][rows], x_parts[1][rows]), halves(mt))
            y = y + entering[rows, 0:SPAN] * scale[h : h + 1]
            y = y + entering[rows, SPAN:] * scale[heads + h : heads + h + 1]
            z = z_ref[rows, sl]
            y_ref[rows, sl] = y
            sums = emit(b, sl, h, rows, y * (z * sigmoid(z)), sums)
        return 0

    lax.fori_loop(0, blocks, block, 0)


def fwd_kernel(
    heads,
    proj_ref,
    live_ref,
    cx_ref,
    cbc_ref,
    hp_ref,
    y_ref,
    xc_ref,
    dx_act_ref,
    b_ref,
    c_ref,
    dbc_act_ref,
    step_ref,
    cum_ref,
    cumex_ref,
    hcat_ref,
    inner_ref,
    gated_ref,
    sq_ref,
    sloc_ref,
):
    z_ref, x_ref, bc_ref, pre_ref = pieces(proj_ref, xc_ref.shape[0], c_ref.shape[0] // 2)
    convolve(x_ref, bc_ref, live_ref, cx_ref, cbc_ref, xc_ref, dx_act_ref, b_ref, c_ref, dbc_act_ref)
    step_sizes(pre_ref, hp_ref, step_ref, cum_ref, cumex_ref, heads)
    states(xc_ref, b_ref, step_ref, cum_ref, sloc_ref, hcat_ref, heads)

    def emit(b, sl, h, rows, gated, total):
        gated_ref[rows, sl] = gated
        part = jnp.sum(gated * gated, axis=0, keepdims=True)
        total = part if total is None else total + part
        if h == heads - 1:
            sq_ref[:, sl] = total
        return total

    outputs(z_ref, xc_ref, b_ref, c_ref, step_ref, cum_ref, cumex_ref, hcat_ref, hp_ref, y_ref, inner_ref, heads, emit)


def spread(bb, state):
    zero = jnp.zeros((state, SPAN), F32)
    top = jnp.concatenate([bb[0:state], zero], axis=1)
    low = jnp.concatenate([zero, bb[state:]], axis=1)
    return jnp.concatenate([top, low], axis=0)


def tails(cum, steps, heads):
    rows = iota((16, SPAN), 0)
    last = jnp.where(rows[:, 0:1] < heads, cum[:, SPAN - 1 : SPAN], cum[:, 0:1])
    return jnp.exp(last - cum) * steps


def tailed(xc, tail, chosen, heads):
    parts = []
    for i, h in enumerate(chosen):
        x = xc[i * WIDTH : (i + 1) * WIDTH]
        parts.append(
            jnp.concatenate([x * tail[h : h + 1], x * tail[heads + h : heads + h + 1]], axis=1)
        )
    return jnp.concatenate(parts, axis=0)


def columns(cum, steps):
    pad = jnp.zeros((SPAN - 32, SPAN), F32)
    return jnp.transpose(jnp.concatenate([cum, steps, pad], axis=0))


def decays(cols, cumex, lower, diag, h, heads):
    f, r = h, heads + h
    arg = jnp.where(
        lower, cumex[f : f + 1] - cols[:, f : f + 1], cumex[r : r + 1] - cols[:, r : r + 1]
    )
    step = jnp.where(lower, cols[:, 16 + f : 17 + f], cols[:, 16 + r : 17 + r])
    return jnp.where(diag, 0.0, jnp.exp(arg) * step)


def gate_back(z_ref, y_ref, don_ref, rms, coef, og_ref, dy_ref, dz_ref, dog_ref, onorm_ref=None):
    chans = y_ref.shape[0]

    def gate_rows(i, _):
        rows = pl.ds(pl.multiple_of(i * 8, 8), 8)
        z, y, don, og = z_ref[rows, :], y_ref[rows, :], don_ref[rows, :], og_ref[rows, :]
        s = sigmoid(z)
        act = z * s
        gated = y * act
        normed = rms * don
        dog_ref[rows, 0:1] = jnp.sum(gated * normed, axis=1, keepdims=True)
        dgated = normed * og - gated * coef
        dy_ref[rows, :] = dgated * act
        dz_ref[rows, :] = dgated * y * (s + act * (1.0 - s))
        if onorm_ref is not None:
            onorm_ref[rows, :] = gated * rms * og
        return 0

    lax.fori_loop(0, chans // 8, gate_rows, 0, unroll=2)


def back_intra(xc_ref, c_ref, inner_ref, step_ref, cum_ref, cumex_ref, hcat_ref, hp_ref, dy_s, dxc_s, dh_s, dc_s, din_s, g_s, cv_s, dd_s, chosen, heads, tick):
    blocks = xc_ref.shape[1] // SPAN
    state = c_ref.shape[0] // 2
    lower = iota((SPAN, SPAN), 0) < iota((SPAN, SPAN), 1)
    diag = iota((SPAN, SPAN), 0) == iota((SPAN, SPAN), 1)
    first = chosen[0] == 0

    def block(b, put):
        sl = pl.ds(pl.multiple_of(b * SPAN, SPAN), SPAN)
        cc = c_ref[:, sl]
        inner = inner_ref[b]
        cumex = cumex_ref[:, sl]
        scale = jnp.exp(cumex)
        cols = columns(cum_ref[:, sl], step_ref[:, sl])
        dinner = jnp.zeros((SPAN, SPAN), F32) if first else din_s[b]
        dcc = jnp.zeros((2 * state, SPAN), F32) if first else dc_s[:, sl]
        for h in chosen:
            f, r = h, heads + h
            rows = slice(h * WIDTH, (h + 1) * WIDTH)
            decay = decays(cols, cumex, lower, diag, h, heads)
            mt = inner * decay
            e_f, e_r = scale[f : f + 1], scale[r : r + 1]
            ce = jnp.concatenate([cc[0:state] * e_f, cc[state:] * e_r], axis=0)
            x = xc_ref[rows, sl]
            dy = dy_s[rows, sl]
            dy_parts = halves(dy)
            left = jnp.concatenate([x, hcat_ref[b, rows, :]], axis=1)
            back = product(halves(left), dy_parts, TN)
            dmt, dce = back[0:SPAN], back[SPAN:]
            dinner = dinner + dmt * decay
            w = dmt * mt
            over_f = jnp.sum(jnp.where(lower, w, 0.0), axis=0, keepdims=True)
            over_r = jnp.sum(jnp.where(lower, 0.0, w), axis=0, keepdims=True)
            prod = dce * ce
            put(g_s, (slice(f, f + 1), sl), over_f + jnp.sum(prod[0:state], axis=0, keepdims=True))
            put(g_s, (slice(r, r + 1), sl), over_r + jnp.sum(prod[state:], axis=0, keepdims=True))
            dcc = dcc + jnp.concatenate([dce[0:state] * e_f, dce[state:] * e_r], axis=0)
            right = jnp.concatenate(
                [jnp.where(lower, mt, 0.0), jnp.where(lower, 0.0, mt), ce], axis=0
            )
            out = product(dy_parts, halves(right), NT)
            dx_f, dx_r = out[:, 0:SPAN], out[:, SPAN : 2 * SPAN]
            put(dh_s, (b, rows, slice(None)), out[:, 2 * SPAN :])
            put(cv_s, (slice(f, f + 1), sl), jnp.sum(x * dx_f, axis=0, keepdims=True))
            put(cv_s, (slice(r, r + 1), sl), jnp.sum(x * dx_r, axis=0, keepdims=True))
            put(dd_s, (slice(h, h + 1), sl), jnp.sum(x * dy, axis=0, keepdims=True))
            put(dxc_s, (rows, sl), dx_f + dx_r + hp_ref[h : h + 1, 2:3] * dy)
        put(din_s, (b,), dinner)
        put(dc_s, (slice(None), sl), dcc)

    two_at_a_time(blocks, block, tick)


def two_at_a_time(blocks, block, tick):
    def body(i, _):
        stores = []
        for b in (2 * i, 2 * i + 1):
            block(b, lambda ref, at, value: stores.append((ref, at, value)))
        for ref, at, value in stores:
            ref[at] = value
        tick(2 * i)
        tick(2 * i + 1)
        return 0

    lax.fori_loop(0, blocks // 2, body, 0)


def back_states(cum_ref, hcat_ref, dh_s, tq_s, state, chosen, heads):
    blocks = hcat_ref.shape[0]
    lane_h = iota((WIDTH, 2 * state), 1)
    lane_1 = iota((1, 2 * state), 1)
    for h in chosen:
        rows = slice(h * WIDTH, (h + 1) * WIDTH)
        carry = jnp.zeros((WIDTH, 2 * state), F32)
        for i in range(blocks):
            f = blocks - 1 - i
            tot_f = jnp.exp(cum_ref[h : h + 1, (f + 1) * SPAN - 1 : (f + 1) * SPAN])
            tot_r = jnp.exp(cum_ref[heads + h : heads + h + 1, i * SPAN : i * SPAN + 1])
            factor = jnp.where(lane_h < state, tot_f, tot_r)
            direct = jnp.where(lane_h < state, dh_s[f, rows, :], dh_s[i, rows, :])
            kept = jnp.where(lane_h < state, hcat_ref[f, rows, :], hcat_ref[i, rows, :])
            scaled = carry * factor
            dots = jnp.sum(scaled * kept, axis=0, keepdims=True)
            q_f = jnp.sum(jnp.where(lane_1 < state, dots, 0.0), axis=1, keepdims=True)
            q_r = jnp.sum(jnp.where(lane_1 < state, 0.0, dots), axis=1, keepdims=True)
            tq_s[f, h : h + 1, :] = jnp.broadcast_to(q_f, (1, SPAN))
            tq_s[i, heads + h : heads + h + 1, :] = jnp.broadcast_to(q_r, (1, SPAN))
            dh_s[f, rows, 0:state] = carry[:, 0:state]
            dh_s[i, rows, state:] = carry[:, state:]
            carry = scaled + direct


def back_inter(xc_ref, b_ref, step_ref, cum_ref, dxc_s, dh_s, db_s, v_s, chosen, heads, tick):
    blocks = xc_ref.shape[1] // SPAN
    state = b_ref.shape[0] // 2
    first = chosen[0] == 0
    group = slice(chosen[0] * WIDTH, (chosen[-1] + 1) * WIDTH)

    def block(b, put):
        sl = pl.ds(pl.multiple_of(b * SPAN, SPAN), SPAN)
        bcat = spread(b_ref[:, sl], state)
        tail = tails(cum_ref[:, sl], step_ref[:, sl], heads)
        xc = xc_ref[group, sl]
        dxc = dxc_s[group, sl]
        dsl = halves(dh_s[b, group, :])
        dleft = product(dsl, halves(bcat))
        dbs = product(dsl, halves(tailed(xc, tail, chosen, heads)), TN)
        db = jnp.concatenate([dbs[0:state, 0:SPAN], dbs[state:, SPAN:]], axis=0)
        put(db_s, (slice(None), sl), db if first else db_s[:, sl] + db)
        parts = []
        for i, h in enumerate(chosen):
            f, r = h, heads + h
            part = slice(i * WIDTH, (i + 1) * WIDTH)
            tx_f = dleft[part, 0:SPAN] * tail[f : f + 1]
            tx_r = dleft[part, SPAN:] * tail[r : r + 1]
            put(v_s, (slice(f, f + 1), sl), jnp.sum(xc[part] * tx_f, axis=0, keepdims=True))
            put(v_s, (slice(r, r + 1), sl), jnp.sum(xc[part] * tx_r, axis=0, keepdims=True))
            parts.append(dxc[part] + tx_f + tx_r)
        put(dxc_s, (group, sl), jnp.concatenate(parts, axis=0))

    two_at_a_time(blocks, block, tick)


def back_logs(b_ref, c_ref, pre_ref, step_ref, hp_ref, ddt_ref, dhp_ref, db_s, dc_s, din_s, g_s, cv_s, v_s, dd_s, tq_s, heads):
    blocks = pre_ref.shape[1] // SPAN
    state = b_ref.shape[0] // 2
    row_q = iota((SPAN, SPAN), 0)
    lane_q = iota((SPAN, SPAN), 1)
    lower = row_q < lane_q
    strict = (row_q > lane_q).astype(F32)
    weak = (row_q >= lane_q).astype(F32)
    strict_t = (row_q < lane_q).astype(F32)
    weak_t = (row_q <= lane_q).astype(F32)
    tri = jnp.concatenate(
        [
            jnp.concatenate([strict, strict_t], axis=1),
            jnp.concatenate([weak, weak_t], axis=1),
            jnp.concatenate([strict_t, strict], axis=1),
        ],
        axis=0,
    ).astype(jnp.bfloat16)
    rows16 = iota((16, SPAN), 0)
    used = rows16 < 2 * heads
    rate = hp_ref[:, 1:2]

    def block(b, carry):
        bias_sum, log_sum, skip_sum = carry
        sl = pl.ds(pl.multiple_of(b * SPAN, SPAN), SPAN)
        dinner = din_s[b]
        both = jnp.concatenate(
            [jnp.where(lower, dinner, 0.0), jnp.where(lower, 0.0, dinner)], axis=0
        )
        dc_s[:, sl] = dc_s[:, sl] + dot3(spread(b_ref[:, sl], state), both)
        db = dot3(c_ref[:, sl], both, NT)
        db_s[0:state, sl] = db_s[0:state, sl] + db[0:state, 0:SPAN]
        db_s[state:, sl] = db_s[state:, sl] + db[state:, SPAN:]
        g = jnp.where(used, g_s[:, sl], 0.0)
        c = jnp.where(used, cv_s[:, sl], 0.0)
        v = jnp.where(used, v_s[:, sl], 0.0)
        steps = step_ref[:, sl]
        sums = exact_dot(jnp.concatenate([g, -c, v], axis=1), tri)
        dlog = jnp.where(rows16 < heads, sums[:, 0:SPAN], sums[:, SPAN:])
        dlog = dlog + jnp.where(used, tq_s[b], 0.0)
        pre = pre_ref[:, sl] + hp_ref[:, 0:1]
        small = steps < 1e-30
        ratio = jnp.where(small, 1.0, sigmoid(pre) / jnp.where(small, 1.0, steps))
        dpre = (c + v) * ratio - rate * dlog * sigmoid(pre)
        ddt_ref[:, sl] = dpre
        skip = jnp.where(rows16 < heads, dd_s[:, sl], 0.0)
        return bias_sum + dpre, log_sum - rate * dlog * steps, skip_sum + skip

    zeros16 = jnp.zeros((16, SPAN), F32)
    bias_sum, log_sum, skip = lax.fori_loop(0, blocks, block, (zeros16, zeros16, zeros16))
    dhp_ref[:, 0:1] = jnp.sum(bias_sum, axis=1, keepdims=True)
    dhp_ref[:, 1:2] = jnp.sum(log_sum, axis=1, keepdims=True)
    dhp_ref[:, 2:3] = jnp.sum(skip, axis=1, keepdims=True)


def conv_back(du, v, taps):
    count = taps.shape[1]
    dv = taps[:, count - 1 : count] * du
    sums = [jnp.sum(du * v, axis=1, keepdims=True)]
    for j in range(count - 2, -1, -1):
        moved = shift_left(du, count - 1 - j)
        dv = dv + taps[:, j : j + 1] * moved
        sums.append(jnp.sum(moved * v, axis=1, keepdims=True))
    return dv, sums[::-1]


def conv_x_back(xin_ref, cx_ref, dx_act_ref, dxc_s, dxin_ref, dcx_ref, start, count):
    def group(i, _):
        rows = pl.ds(pl.multiple_of(start + i * 8, 8), 8)
        dv, sums = conv_back(dxc_s[rows, :] * dx_act_ref[rows, :], xin_ref[rows, :], cx_ref[rows, :])
        dxin_ref[rows, :] = dv
        for j, item in enumerate(sums):
            dcx_ref[rows, j : j + 1] = item
        return 0

    lax.fori_loop(0, count // 8, group, 0, unroll=2)


def conv_bc_back(bc_ref, cbc_ref, dbc_act_ref, db_s, dc_s, dbc_ref, dcbc_ref):
    state = db_s.shape[0] // 2

    def group(i, _, src, grad, grad_row, shift):
        rows = pl.ds(pl.multiple_of(src * state + i * 8, 8), 8)
        from_rows = pl.ds(pl.multiple_of(grad_row + i * 8, 8), 8)
        d = grad[from_rows, :]
        if shift == 1:
            d = shift_left(d, 1)
        if shift == -1:
            d = shift_right(d, 1)
        dv, sums = conv_back(d * dbc_act_ref[rows, :], bc_ref[rows, :], cbc_ref[rows, :])
        dbc_ref[rows, :] = dv
        for j, item in enumerate(sums):
            dcbc_ref[rows, j : j + 1] = item
        return 0

    for src, grad, row, shift in ((0, db_s, 0, 0), (1, dc_s, 0, 1), (2, db_s, state, 0), (3, dc_s, state, -1)):
        lax.fori_loop(
            0,
            state // 8,
            functools.partial(group, src=src, grad=grad, grad_row=row, shift=shift),
            0,
            unroll=2,
        )


def pairs_of(heads):
    return [tuple(range(h, min(h + 2, heads))) for h in range(0, heads, 2)]


def bwd_kernel(
    heads,
    proj_ref,
    y_ref,
    xc_ref,
    dx_act_ref,
    b_ref,
    c_ref,
    dbc_act_ref,
    step_ref,
    cum_ref,
    cumex_ref,
    hcat_ref,
    inner_ref,
    don_ref,
    rms_ref,
    coef_ref,
    og_ref,
    cx_ref,
    cbc_ref,
    hp_ref,
    dproj_ref,
    dcx_ref,
    dcbc_ref,
    dhp_ref,
    dog_ref,
    dy_s,
    dxc_s,
    dh_s,
    db_s,
    dc_s,
    din_s,
    g_s,
    cv_s,
    v_s,
    dd_s,
    tq_s,
):
    chans, state = y_ref.shape[0], b_ref.shape[0] // 2
    z_ref, xin_ref, bc_ref, pre_ref = pieces(proj_ref, chans, state)
    dz_ref, dxin_ref, dbc_ref, ddt_ref = pieces(dproj_ref, chans, state)
    gate_back(z_ref, y_ref, don_ref, rms_ref[...], coef_ref[...], og_ref, dy_s, dz_ref, dog_ref)
    for chosen in pairs_of(heads):
        back_intra(
            xc_ref, c_ref, inner_ref, step_ref, cum_ref, cumex_ref, hcat_ref, hp_ref, dy_s, dxc_s, dh_s, dc_s,
            din_s, g_s, cv_s, dd_s, chosen, heads, lambda b: None,
        )
        back_states(cum_ref, hcat_ref, dh_s, tq_s, state, chosen, heads)
        back_inter(xc_ref, b_ref, step_ref, cum_ref, dxc_s, dh_s, db_s, v_s, chosen, heads, lambda b: None)
    conv_x_back(xin_ref, cx_ref, dx_act_ref, dxc_s, dxin_ref, dcx_ref, 0, chans)
    back_logs(
        b_ref, c_ref, pre_ref, step_ref, hp_ref, ddt_ref, dhp_ref, db_s, dc_s, din_s, g_s, cv_s, v_s, dd_s, tq_s, heads
    )
    conv_bc_back(bc_ref, cbc_ref, dbc_act_ref, db_s, dc_s, dbc_ref, dcbc_ref)


def call(kernel, out_shapes, scratch, flops):
    return pl.pallas_call(
        kernel,
        out_shape=[jax.ShapeDtypeStruct(shape, F32) for shape in out_shapes],
        scratch_shapes=[pltpu.VMEM(shape, F32) for shape in scratch],
        compiler_params=pltpu.CompilerParams(vmem_limit_bytes=56 * 1024 * 1024),
        cost_estimate=pl.CostEstimate(flops=flops, bytes_accessed=20_000_000, transcendentals=0),
    )


def run_fwd(proj, live, cx, cbc, hp, heads):
    tokens = proj.shape[1]
    chans, n4 = cx.shape[0], cbc.shape[0]
    blocks = tokens // SPAN
    full, half, rows = (chans, tokens), (n4 // 2, tokens), (16, tokens)
    return call(
        functools.partial(fwd_kernel, heads),
        [full, full, full, half, half, (n4, tokens), rows, rows, rows, (blocks, chans, n4 // 2), (blocks, SPAN, SPAN), full, (1, tokens)],
        [(blocks, chans, n4 // 2)],
        2_000_000_000,
    )(proj, live, cx, cbc, hp)


def run_bwd(proj, kept, don, rms, coef, og, cx, cbc, hp, heads):
    tokens = proj.shape[1]
    chans, n4 = cx.shape[0], cbc.shape[0]
    blocks = tokens // SPAN
    full, half, rows = (chans, tokens), (n4 // 2, tokens), (16, tokens)
    return call(
        functools.partial(bwd_kernel, heads),
        [proj.shape, (chans, 4), (n4, 4), (16, 3), (chans, 1)],
        [full, full, (blocks, chans, n4 // 2), half, half, (blocks, SPAN, SPAN), rows, rows, rows, rows, (blocks, 16, SPAN)],
        4_000_000_000,
    )(proj, *kept, don, rms, coef, og, cx, cbc, hp)


def square_sum(arrays):
    total = jnp.float32(0.0)
    for item in arrays:
        total = total + jnp.sum(item * item)
    return total


def pad_rows(v):
    return jnp.concatenate([v, jnp.zeros((16 - v.shape[0],) + v.shape[1:], v.dtype)], axis=0)


def local(
    hidden_in,
    out_cot,
    lengths,
    norm_gain,
    w_zx,
    w_bc,
    w_dt,
    conv_x,
    conv_bc,
    head_params,
    out_gain,
    w_out,
    left_statistic_gate,
    stat_right_zx,
    stat_left_out,
    stat_right_out,
    inverse_root_left_gate,
    inverse_root_right_gate,
    root_left_out,
    root_right_out,
):
    rows, chans = w_zx.shape[1], w_zx.shape[2]
    heads = w_dt.shape[1]
    n4 = w_bc.shape[1]
    own_rows, width = hidden_in.shape
    narrow_id, wide_id = lax.axis_index("narrow"), lax.axis_index("wide")

    full_in = lax.all_gather(hidden_in, "narrow", axis=0, tiled=True)
    full_gain = lax.all_gather(norm_gain, "narrow", axis=0, tiled=True)
    dt_cols = jnp.transpose(w_dt, (0, 2, 1)).reshape(rows, 2 * heads)
    own_w = jnp.concatenate(
        [w_zx[0], w_zx[1], w_bc, dt_cols, jnp.zeros((rows, 16 - 2 * heads), F32)], axis=1
    )
    w_in = lax.all_gather(own_w, "wide", axis=0, tiled=True)
    wide_out = lax.all_gather(w_out, "wide", axis=1, tiled=True)

    tokens = full_in.shape[0]
    live = (jnp.arange(tokens) < lengths[0]).astype(F32)
    row_start = narrow_id * own_rows
    live_own = lax.dynamic_slice_in_dim(live, row_start, own_rows, 0)
    dbranch = lax.all_gather(live_own[:, None] * out_cot, "narrow", axis=0, tiled=True)

    inv_rms = lax.rsqrt(jnp.mean(full_in * full_in, axis=-1) + 1e-05)
    normed = full_in * inv_rms[:, None] * full_gain
    proj = dot(w_in, normed, TT)
    cx, cbc = conv_x.T, conv_bc.T
    hp = jnp.concatenate(
        [
            pad_rows(head_params[0:2].reshape(2 * heads, 1)),
            pad_rows(jnp.exp(head_params[2:4]).reshape(2 * heads, 1)),
            pad_rows(head_params[4].reshape(heads, 1)),
        ],
        axis=1,
    )
    *kept, gated, squares = run_fwd(proj, live[None, :], cx, cbc, hp, heads)
    donorm = dot(wide_out, dbranch, NT)
    inner = jnp.sum(gated * (donorm * out_gain[:, None]), axis=0, keepdims=True)
    stats = lax.psum(jnp.concatenate([squares, inner], axis=0), "narrow")
    inner_total = chans * lax.axis_size("narrow")
    rms = lax.rsqrt(stats[0:1] / inner_total + 1e-05)
    coef = rms**3 * stats[1:2] / inner_total
    onorm = gated * rms * out_gain[:, None]
    branch = lax.psum_scatter(dot(onorm, wide_out, TN), "narrow", scatter_dimension=0, tiled=True)
    block_out = hidden_in + live_own[:, None] * branch
    g_out = lax.psum(dot(onorm, dbranch), "wide")

    dproj, d_cx, d_cbc, d_hp, d_og = run_bwd(
        proj, kept, donorm, rms, coef, out_gain[:, None], cx, cbc, hp, heads
    )
    d_normed = dot(dproj, w_in, TT)
    d_w = dot(normed, dproj, TT)
    dnormed = lax.psum_scatter(d_normed, "narrow", scatter_dimension=0, tiled=True)
    own_inv = lax.dynamic_slice_in_dim(inv_rms, row_start, own_rows, 0)[:, None]
    total_dot = jnp.sum(hidden_in * full_gain * dnormed, axis=1, keepdims=True)
    in_grad = out_cot + (
        own_inv * full_gain * dnormed - hidden_in * (own_inv**3 * total_dot / width)
    )
    d_gain = jnp.sum(hidden_in * own_inv * dnormed, axis=0)

    g_zx = lax.psum(d_w[:, 0 : 2 * chans], "wide")
    g_dt, g_cx, g_hp, g_og = lax.psum((d_w[:, 2 * chans + n4 :], d_cx, d_hp, d_og), "wide")
    g_bc, g_cbc, g_gain = lax.psum(
        (d_w[:, 2 * chans : 2 * chans + n4], d_cbc, d_gain), ("wide", "narrow")
    )
    shard = norm_gain.shape[0]
    g_ng = lax.dynamic_slice_in_dim(g_gain, narrow_id * shard, shard, 0)
    g_dt = jnp.transpose(g_dt[:, 0 : 2 * heads].reshape(width, 2, heads), (0, 2, 1))
    g_cx, g_cbc, g_og = g_cx.T, g_cbc.T, g_og[:, 0]
    g_head = jnp.concatenate(
        [
            g_hp[0 : 2 * heads, 0].reshape(2, heads),
            g_hp[0 : 2 * heads, 1].reshape(2, heads),
            g_hp[0:heads, 2].reshape(1, heads),
        ],
        axis=0,
    )
    local_squares = square_sum((g_zx, g_out, g_dt, g_cx, g_head, g_og, g_ng))
    total_squares = lax.psum(local_squares, "narrow") + square_sum((g_bc, g_cbc))
    clip_norm = jnp.sqrt(total_squares)
    factor = 1.0 / jnp.maximum(clip_norm, 1.0)
    c_zx, c_out, c_bc, c_dt = g_zx * factor, g_out * factor, g_bc * factor, g_dt * factor
    c_cx, c_cbc, c_head, c_og, c_ng = (
        g_cx * factor,
        g_cbc * factor,
        g_head * factor,
        g_og * factor,
        g_ng * factor,
    )
    halves = (c_zx[:, 0:chans], c_zx[:, chans:])
    own_zx = lax.dynamic_slice_in_dim(c_zx, wide_id * rows, rows, 0)
    own_halves = (own_zx[:, 0:chans], own_zx[:, chans:])
    left_zx = jnp.stack(
        [
            0.5 * left_statistic_gate[m, 0] + 0.5 * dot(own_halves[m], halves[m], NT)
            for m in range(2)
        ]
    )[:, None]
    right_zx = jnp.stack(
        [0.5 * stat_right_zx[m] + 0.5 * dot(halves[m], halves[m], TN) for m in range(2)]
    )
    new_zx = jnp.stack(
        [
            w_zx[m]
            - 0.5
            * dot(dot(inverse_root_left_gate[m, 0], halves[m]), inverse_root_right_gate[m])
            for m in range(2)
        ]
    )
    cols = w_out.shape[1]
    own_out = lax.dynamic_slice_in_dim(c_out, wide_id * cols, cols, 1)
    left_out = 0.5 * stat_left_out + 0.5 * dot(c_out, c_out, NT)
    right_out = 0.5 * stat_right_out + 0.5 * dot(own_out, c_out, TN)[None]
    new_out = w_out - 0.5 * dot(dot(root_left_out, c_out), root_right_out[0], NT)
    own_bc = lax.dynamic_slice_in_dim(c_bc, wide_id * rows, rows, 0)
    own_dt = lax.dynamic_slice_in_dim(c_dt, wide_id * rows, rows, 0)
    rate = 10.0
    return (
        block_out,
        in_grad,
        clip_norm,
        jnp.stack(own_halves),
        new_zx,
        left_zx,
        right_zx,
        own_out,
        new_out,
        left_out,
        right_out,
        own_bc,
        w_bc - rate * own_bc,
        own_dt,
        w_dt - rate * own_dt,
        c_cx,
        conv_x - rate * c_cx,
        c_cbc,
        conv_bc - rate * c_cbc,
        c_head,
        head_params - rate * c_head,
        c_og,
        out_gain - rate * c_og,
        c_ng,
        norm_gain - rate * c_ng,
    )


MESH = pl.DeviceIdType.MESH
MIB = 1024 * 1024


class Place:
    def __init__(self, wide):
        self.wide = wide
        self.depth = wide // 2
        self.w, self.n = lax.axis_index("wide"), lax.axis_index("narrow")
        self.z, self.x = self.w // 2, self.w % 2
        self.y, self.c = self.n // 2, self.n % 2
        self.core = (self.w, self.y * 2 + 1 - self.c)
        self.row = (self.w, (1 - self.y) * 2 + self.c)
        self.corner = (self.w, (1 - self.y) * 2 + 1 - self.c)
        self.across = (self.z * 2 + 1 - self.x, self.n)

    def group(self):
        return [self.core, self.row, self.corner]

    def along(self, k):
        return ((self.z + k) % self.depth) * 2 + self.x, self.n

    def others(self, k):
        return (self.w + k) % self.wide, self.n


class Links:
    def __init__(self, send, recv):
        self.send, self.recv, self.count, self.started = send, recv, 0, []

    def plan(self, src, dst, device):
        i = self.count
        self.count = i + 1
        item = pltpu.make_async_remote_copy(
            src_ref=src,
            dst_ref=dst,
            send_sem=self.send.at[i],
            recv_sem=self.recv.at[i],
            device_id=device,
            device_id_type=MESH,
        )
        self.started.append(item)
        return item

    def copy(self, src, dst, device):
        item = self.plan(src, dst, device)
        item.start()
        return item

    def release(self, items):
        for item in items:
            item.wait_send()
        self.started = [item for item in self.started if all(item is not done for done in items)]

    def drain(self):
        self.release(list(self.started))


def arrived(copies):
    for item in copies:
        item.wait_recv()


def begin(copies):
    for item in copies:
        item.start()


def greet(devices):
    barrier = pltpu.get_barrier_semaphore()
    for device in devices:
        pl.semaphore_signal(barrier, inc=1, device_id=device, device_id_type=MESH)
    return lambda: pl.semaphore_wait(barrier, len(devices))


def as_row(col):
    return jnp.transpose(jnp.broadcast_to(col, (col.shape[0], 128)))[0:1]


def as_col(row):
    return jnp.transpose(jnp.broadcast_to(row, (128, 128)))[:, 0:1]


def flat(v):
    return v.reshape(-1, v.shape[-1])


class Piece:
    def __init__(self, here, links, part, x_rx, z_rx, full, square):
        self.here, self.part, self.x_rx, self.z_rx = here, part, x_rx, z_rx
        self.full, self.square = full, square
        steps = range(1, here.depth)
        place, column = full.at[here.z, here.x], full.at[:, here.x]
        self.first = links.plan(part.at[:, 1 - here.x], x_rx, here.across)
        self.second = [
            links.plan(x_rx.at[(here.z + k) % here.depth], z_rx.at[k - 1], here.along(k)) for k in steps
        ]
        self.third = [links.plan(place, place, here.along(k)) for k in steps]
        self.fourth = links.plan(column, column, here.across)

    def start(self):
        self.first.start()

    def fold(self):
        self.first.wait_recv()
        for k in range(self.here.depth):
            self.x_rx[k] = self.x_rx[k] + self.part[k, self.here.x]
        begin(self.second)

    def own(self):
        arrived(self.second)
        total = self.x_rx[self.here.z]
        for k in range(1, self.here.depth):
            total = total + self.z_rx[k - 1]
        self.full[self.here.z, self.here.x] = total
        begin(self.third)
        self.square[...] = jnp.broadcast_to(total_square(total), self.square.shape)

    def spread(self):
        arrived(self.third)
        self.fourth.start()

    def finish(self):
        self.fourth.wait_recv()


def total_square(v):
    return jnp.sum(jnp.sum(v * v, axis=0, keepdims=True), axis=1, keepdims=True)


def layer_kernel(
    wide,
    heads,
    shard,
    inner_total,
    length_ref,
    hidden_ref,
    cot_ref,
    gain_ref,
    w_ref,
    wout_ref,
    bcw_ref,
    dtw_ref,
    cx_in,
    cbc_in,
    hp_in,
    og_in,
    block_ref,
    grad_ref,
    gfull,
    bc_own,
    dt_own,
    sv_sum,
    norm_ref,
    hq,
    cq,
    wz_g,
    wx_g,
    wo_g,
    bc_g,
    dt_g,
    gain_g,
    dtt,
    gain_col,
    gain_row,
    turn_s,
    cx_ref,
    cbc_ref,
    hp_ref,
    og_ref,
    live_ref,
    inv_ref,
    proj,
    y_s,
    xc,
    dx_act,
    b_s,
    c_s,
    dbc_act,
    step_s,
    cum_s,
    cumex_s,
    hcat,
    inner_s,
    don,
    onorm,
    dy_s,
    dh_s,
    db_s,
    dc_s,
    din_s,
    g_s,
    cv_s,
    v_s,
    dd_s,
    tq_s,
    cols_s,
    dcbc_s,
    dhp_s,
    dog_s,
    dgain_s,
    stat_own,
    stat_g,
    part,
    x_rx,
    z_rx,
    core_rx,
    row_rx,
    gbc,
    bc_core,
    bc_row,
    bc_mine,
    bc_rx,
    gdt,
    dt_rx,
    shared_g,
    sv_g,
    norm_n,
    norm_w,
    square_s,
    hq_hi,
    hq_lo,
    wt_hi,
    wt_lo,
    send,
    recv,
    stat_send,
    stat_recv,
):
    here = Place(wide)
    links = Links(send, recv)
    w, n, z, x, y, c, depth = here.w, here.n, here.z, here.x, here.y, here.c, here.depth
    group = here.group()
    far = [here.others(k) for k in range(1, wide)]
    own_rows, width = hidden_ref.shape
    chans, tokens = y_s.shape
    state = b_s.shape[0] // 2
    blocks = tokens // SPAN
    parts = tokens // own_rows
    thirds = chans // 128
    z_ref, x_ref, bc_ref, pre_ref = pieces(proj, chans, state)
    met = greet(group + far)
    jobs = [
        Piece(
            here, links, part.at[i if i < 2 * thirds else i - thirds], x_rx.at[i], z_rx.at[i],
            gfull.at[i], square_s.at[i],
        )
        for i in range(3 * thirds)
    ]
    z_jobs, x_jobs, o_jobs = jobs[0:thirds], jobs[thirds : 2 * thirds], jobs[2 * thirds :]

    half = bcw_ref.shape[0] // 2
    wx_g[z, x] = w_ref[1]
    bc_g[z, x, c] = bcw_ref[pl.ds(pl.multiple_of(c * half, 8), half), :]
    dt_g[z, x] = jnp.zeros(dt_g.shape[2:], F32)
    for h in range(heads):
        for i in range(2):
            row = i * heads + h
            dt_g[z, x, row : row + 1, 0 : dtw_ref.shape[2]] = dtw_ref[h, i : i + 1, :]
    line = gain_ref[...].reshape(1, shard)
    gain_g[n] = jnp.zeros(gain_g.shape[1:], F32)
    for i in range((shard + 127) // 128):
        size = min(128, shard - 128 * i)
        gain_g[n, i : i + 1, 0:size] = line[:, 128 * i : 128 * i + size]
    squares = jnp.zeros((1, own_rows), F32)
    for i in range(width // 128):
        turned = jnp.transpose(hidden_ref[:, i * 128 : (i + 1) * 128])
        squares = squares + jnp.sum(turned * turned, axis=0, keepdims=True)
        hq[n, i * 128 : (i + 1) * 128, :] = turned
    inv_ref[...] = lax.rsqrt(squares / width + 1e-05)
    for i in range(width // 128):
        hq[n, i * 128 : (i + 1) * 128, :] = hq[n, i * 128 : (i + 1) * 128, :] * inv_ref[...]
    met()

    def along(ref):
        return [links.copy(ref, ref, here.along(k)) for k in range(1, depth)]

    def exchange(ref):
        return [links.copy(ref, ref, here.row), links.copy(ref, ref, here.core)]

    class Relay:
        def __init__(self, *views):
            self.views = views
            self.direct = [along(view(z)) for view in views]
            self.passed = []

        def begin(self):
            self.passed = [links.copy(view(z), view(z), here.across) for view in self.views]

        def forward(self, steps=tuple(range(1, depth))):
            for k in steps:
                source = (z + depth - k) % depth
                for view, copies in zip(self.views, self.direct):
                    copies[k - 1].wait_recv()
                    self.passed.append(links.copy(view(source), view(source), here.across))

        def wait(self):
            arrived(self.passed)

    h_copies = exchange(hq.at[n])
    gain_copies = [links.copy(gain_g.at[n], gain_g.at[n], device) for device in group]
    early = Relay(lambda i: bc_g.at[i, x, c], lambda i: dt_g.at[i, x])
    early.begin()
    first = Relay(lambda i: wx_g.at[i, x])
    first.begin()

    wz_g[z, x] = w_ref[0]
    wo_g[z, x] = wout_ref[...]
    live_ref[...] = jnp.where(iota((1, tokens), 1) < length_ref[0], 1.0, 0.0)
    live_own = live_ref[:, pl.ds(pl.multiple_of(n * own_rows, 128), own_rows)]
    for i in range(width // 128):
        cq[n, i * 128 : (i + 1) * 128, :] = jnp.transpose(cot_ref[:, i * 128 : (i + 1) * 128]) * live_own
    turn_s[...] = jnp.zeros_like(turn_s)
    for ref, out in ((cx_in, cx_ref), (cbc_in, cbc_ref)):
        for i in range(ref.shape[1] // 128):
            turn_s[0:4, :] = ref[:, i * 128 : (i + 1) * 128]
            out[i * 128 : (i + 1) * 128, :] = jnp.transpose(turn_s[...])[:, 0:4]
    turn_s[...] = jnp.zeros_like(turn_s)
    turn_s[0:1, 0:heads] = hp_in[0:1, :]
    turn_s[0:1, heads : 2 * heads] = hp_in[1:2, :]
    turn_s[1:2, 0:heads] = jnp.exp(hp_in[2:3, :])
    turn_s[1:2, heads : 2 * heads] = jnp.exp(hp_in[3:4, :])
    turn_s[2:3, 0:heads] = hp_in[4:5, :]
    hp_ref[...] = jnp.transpose(turn_s[...])[0:16, 0:3]
    og_line = og_in[...].reshape(1, chans)
    for i in range(thirds):
        og_ref[i * 128 : (i + 1) * 128, :] = as_col(og_line[:, i * 128 : (i + 1) * 128])
    cols_s[...] = jnp.zeros_like(cols_s)
    dcbc_s[...] = jnp.zeros_like(dcbc_s)
    dhp_s[...] = jnp.zeros_like(dhp_s)

    def cut(q):
        hq_hi[q], hq_lo[q] = halves(hq[q])

    cut(n)
    h_copies[1].wait_recv()
    cut(here.core[1])
    early.forward()
    first.forward()
    second = Relay(lambda i: wz_g.at[i, x])
    h_copies[0].wait_recv()
    other = here.row[1]
    h_far = links.copy(hq.at[other], hq.at[other], here.core)
    c_copies = exchange(cq.at[n])
    arrived(gain_copies)
    for q in range(parts):
        turned = jnp.transpose(jnp.concatenate([gain_g[q], jnp.zeros((120, 128), F32)], axis=0))
        for i in range((shard + 127) // 128):
            size = min(128, shard - 128 * i)
            start = shard * q + 128 * i
            gain_col[start : start + size, :] = turned[0:size, i : i + 1]
    for i in range(width // 128):
        gain_row[:, i * 128 : (i + 1) * 128] = as_row(gain_col[i * 128 : (i + 1) * 128, :])

    def turn(ref, row, scale=True):
        for i in range(ref.shape[-1] // 128):
            cols = flat(ref[..., i * 128 : (i + 1) * 128])
            if scale:
                cols = cols * gain_col[...]
            for dst, value in zip((wt_hi, wt_lo), halves(jnp.transpose(cols))):
                dst[row + i * 128 : row + (i + 1) * 128, :] = value

    def quarter(q):
        return pl.ds(pl.multiple_of(q * own_rows, 128), own_rows)

    def each_quarter(body):
        def step(q, _):
            body(q)
            return 0

        lax.fori_loop(0, parts, step, 0)

    def rows_of(start, stop):
        return wt_hi[start:stop, :], wt_lo[start:stop, :]

    def project(out_ref, weights):
        def body(q):
            out_ref[:, quarter(q)] = product(weights(), (hq_hi[q], hq_lo[q]))

        each_quarter(body)

    early.wait()
    bc_core_copy = links.copy(bc_g.at[:, :, c], bc_g.at[:, :, c], here.core)
    lanes = width // wide
    for i in range(wide):
        dtt[:, i * lanes : (i + 1) * lanes] = dt_g[i // 2, i % 2][:, 0:lanes]
    last = 2 * chans + 4 * state
    wt_hi[last:, :], wt_lo[last:, :] = halves(dtt[...] * gain_row[...])
    bc_core_copy.wait_recv()
    turn(bc_g, 2 * chans)
    first.wait()
    second.begin()
    second.forward((1,))
    turn(wx_g, chans)
    second.forward((2,))
    h_far.wait_recv()
    cut(here.row[1])
    cut(here.corner[1])
    project(proj.at[chans:], lambda: rows_of(chans, last + 16))
    second.forward((3,))
    third = Relay(lambda i: wo_g.at[i, x])
    third.begin()
    c_copies[0].wait_recv()
    c_far = links.copy(cq.at[other], cq.at[other], here.core)
    convolve(x_ref, bc_ref, live_ref, cx_ref, cbc_ref, xc, dx_act, b_s, c_s, dbc_act)
    step_sizes(pre_ref, hp_ref, step_s, cum_s, cumex_s, heads)
    states(xc, b_s, step_s, cum_s, dh_s, hcat, heads)
    second.wait()
    turn(wz_g, 0)
    project(z_ref, lambda: rows_of(0, chans))
    third.forward()

    def stat_copy(j, b):
        return pltpu.make_async_remote_copy(
            src_ref=stat_own.at[b],
            dst_ref=stat_g.at[n, b],
            send_sem=stat_send.at[j, b],
            recv_sem=stat_recv.at[j, b],
            device_id=group[j],
            device_id_type=MESH,
        )

    def tell(b, row):
        stats = jnp.broadcast_to(row, (8, SPAN))
        stat_own[b] = stats
        stat_g[n, b] = stats
        for j in range(3):
            stat_copy(j, b).start()

    def told(b):
        for j in range(3):
            stat_copy(j, b).wait_recv()
        total = stat_g[0, b]
        for q in range(1, parts):
            total = total + stat_g[q, b]
        return total[0:1]

    def emit(b, sl, h, rows, gated, sums):
        onorm[rows, sl] = gated
        row = jnp.sum(gated * gated, axis=0, keepdims=True)
        row = row if sums is None else row + sums
        if h == heads - 1:
            tell(b, row)
        return row

    outputs(z_ref, xc, b_s, c_s, step_s, cum_s, cumex_s, hcat, hp_ref, y_s, inner_s, heads, emit)
    rms = jnp.concatenate(
        [lax.rsqrt(told(b) / inner_total + 1e-05) for b in range(blocks)], axis=1
    )

    def scale_rows(i, _):
        rows = pl.ds(pl.multiple_of(i * 8, 8), 8)
        onorm[rows, :] = onorm[rows, :] * rms * og_ref[rows, :]
        return 0

    lax.fori_loop(0, chans // 8, scale_rows, 0, unroll=2)
    c_copies[1].wait_recv()
    c_far.wait_recv()

    def weight_grad(put, right, left=lambda q: (hq_hi[q], hq_lo[q])):
        def body(q):
            put(q, product(left(q), halves(right(q)), NT))

        each_quarter(body)

    block_shape = part.shape[1:]

    def add_to(start, count):
        def put(q, value):
            for i in range(count):
                ref = part.at[start + i]
                piece = value[:, i * 128 : (i + 1) * 128].reshape(block_shape)
                ref[...] = jnp.where(q == 0, piece, ref[...] + piece)

        return put

    def scaled(i):
        part[i] = (flat(part[i]) * gain_col[...]).reshape(block_shape)

    part[...] = jnp.zeros_like(part)
    for start, stop in ((0, 1), (1, thirds)):
        rows = slice(start * 128, stop * 128)
        weight_grad(
            add_to(thirds + start, stop - start),
            lambda q, rows=rows: onorm[rows, quarter(q)],
            lambda q: halves(cq[q]),
        )
        for job in o_jobs[start:stop]:
            job.start()
    third.wait()
    turn(wo_g, 0, False)

    def donorm(q):
        don[:, quarter(q)] = product(rows_of(0, chans), halves(cq[q]))

    each_quarter(donorm)

    def inner_sums(b, _):
        sl = pl.ds(pl.multiple_of(b * SPAN, SPAN), SPAN)
        gate = z_ref[:, sl]
        gated = y_s[:, sl] * (gate * sigmoid(gate))
        tell(blocks + b, jnp.sum(gated * (don[:, sl] * og_ref[...]), axis=0, keepdims=True))
        return 0

    lax.fori_loop(0, blocks, inner_sums, 0)

    links.release(c_copies + [c_far])

    class Return:
        def __init__(self, rx, row_rx, compute, steps=((), (), (), ())):
            self.rx, self.row_rx = rx, row_rx
            first = links.count
            self.cores = [links.plan(cq.at[k * 2 + 1 - c], rx.at[k], here.core) for k in range(2)]
            self.last = links.plan(rx.at[1 - y], row_rx, here.row)

            def body(k, _):
                q = (k % 2) * 2 + (c + 1 + k // 2) % 2
                cq[q] = compute(q)

                @pl.when(k < 2)
                def _():
                    pltpu.make_async_remote_copy(
                        src_ref=cq.at[q],
                        dst_ref=rx.at[k % 2],
                        send_sem=links.send.at[first + k % 2],
                        recv_sem=links.recv.at[first + k % 2],
                        device_id=here.core,
                        device_id_type=MESH,
                    ).start()

                for at, items in enumerate(steps):

                    @pl.when(k == at)
                    def _(items=items):
                        for step in items:
                            step()

                return 0

            lax.fori_loop(0, 4, body, 0)

        def fold(self):
            arrived(self.cores)
            for k in range(2):
                self.rx[k] = self.rx[k] + cq[k * 2 + c]
            self.last.start()

        def total(self):
            self.last.wait_recv()
            return self.rx[y] + self.row_rx[...]

    o0, o1, o2 = o_jobs
    z0, z1, z2 = z_jobs
    x0, x1, x2 = x_jobs
    branch = Return(core_rx.at[0], row_rx.at[0], lambda q: dot3(flat(wo_g[...]), onorm[:, quarter(q)]))
    o0.fold()
    told_inner = jnp.concatenate([told(blocks + b) for b in range(blocks)], axis=1)
    coef = rms**3 * told_inner / inner_total
    gate_back(z_ref, y_s, don, rms, coef, og_ref, dy_s, z_ref, dog_s)
    weight_grad(add_to(0, thirds), lambda q: z_ref[:, quarter(q)])
    for i, job in enumerate(z_jobs):
        scaled(i)
        job.start()
    o1.fold()
    o0.own()

    def x_grad(i):
        links.release([o_jobs[i].first])
        part[thirds + i] = jnp.zeros(block_shape, F32)
        weight_grad(add_to(thirds + i, 1), lambda q: x_ref[i * 128 : (i + 1) * 128, quarter(q)])
        scaled(thirds + i)

    within = [
        {0: [o2.fold], 6: [o1.own, z0.fold]},
        {1: [o2.own, z2.fold], 3: [branch.fold], 5: [o1.spread]},
        {0: [z1.own], 5: [o2.spread], 6: [x1.fold]},
    ]
    between = [
        {6: [o0.spread], 7: [z1.fold]},
        {6: [z0.own, x0.fold]},
        {4: [z2.own]},
    ]

    def ticks(plan):
        def tick(b):
            for at, steps in plan.items():

                @pl.when(b == at)
                def _(steps=steps):
                    for step in steps:
                        step()

        return tick

    for i, chosen in enumerate(pairs_of(heads)):
        back_intra(
            xc, c_s, inner_s, step_s, cum_s, cumex_s, hcat, hp_ref, dy_s, y_s, dh_s, dc_s,
            din_s, g_s, cv_s, dd_s, chosen, heads, ticks(within[i]),
        )
        back_states(cum_s, hcat, dh_s, tq_s, state, chosen, heads)
        back_inter(xc, b_s, step_s, cum_s, y_s, dh_s, db_s, v_s, chosen, heads, ticks(between[i]))
        conv_x_back(x_ref, cx_ref, dx_act, y_s, x_ref, cols_s, i * 128, 128)
        x_grad(i)
        x_jobs[i].start()

    back_logs(
        b_s, c_s, pre_ref, step_s, hp_ref, pre_ref, dhp_s, db_s, dc_s, din_s, g_s, cv_s, v_s, dd_s, tq_s, heads
    )
    z0.spread()
    conv_bc_back(bc_ref, cbc_ref, dbc_act, db_s, dc_s, bc_ref, dcbc_s)
    gbc_shape = gbc.shape

    def add_bc(q, value):
        gbc[...] = jnp.where(q == 0, value.reshape(gbc_shape), gbc[...] + value.reshape(gbc_shape))

    gbc[...] = jnp.zeros_like(gbc)
    weight_grad(add_bc, lambda q: bc_ref[:, quarter(q)])
    gbc[...] = (flat(gbc[...]) * gain_col[...]).reshape(gbc_shape)
    bc_first = links.copy(gbc.at[:, :, 1 - c], bc_core, here.core)
    x0.own()
    x2.fold()
    dt_grad = jnp.zeros((16, width), F32)
    for q in range(parts):
        step = halves(pre_ref[:, q * own_rows : (q + 1) * own_rows])
        dt_grad = dt_grad + product(step, (hq_hi[q], hq_lo[q]), NT)
    dt_grad = dt_grad * gain_row[...]
    gdt[...] = jnp.zeros_like(gdt)
    for i in range(wide):
        gdt[i, :, 0:lanes] = dt_grad[:, i * lanes : (i + 1) * lanes]
    dt_rx[w] = gdt[w]
    dt_copies = [links.copy(gdt.at[device[0]], dt_rx.at[w], device) for device in far]
    dgain_s[...] = jnp.zeros_like(dgain_s)
    bc_first.wait_recv()
    for k in range(2):
        bc_core[:, k] = bc_core[:, k] + gbc[:, k, c]
    for k in range(wide):
        bc_mine[k] = bc_core[k, 1 - y]
    bc_second = links.copy(bc_mine, bc_row, here.row)

    links.release(branch.cores)

    for k in range(parts):
        pieces_of = []
        for ref, start in ((wz_g, 0), (wx_g, chans), (bc_g, 2 * chans)):
            a, b = max(k * own_rows, start), min((k + 1) * own_rows, start + ref.shape[-1])
            if a < b:
                pieces_of.append(flat(ref[..., a - start : b - start]))
        hq_hi[k], hq_lo[k] = halves(jnp.concatenate(pieces_of, axis=1))

    def normed_back(q):
        sl = quarter(q)

        def add(k, value):
            rows = pl.ds(pl.multiple_of(k * own_rows, 8), own_rows)
            return value + product((hq_hi[k], hq_lo[k]), halves(proj[rows, sl]))

        value = lax.fori_loop(0, parts, add, dot3(dtt[...], pre_ref[:, sl], TN))
        dgain_s[...] = dgain_s[...] + jnp.sum(value * hq[q], axis=1, keepdims=True)
        return value

    back = Return(core_rx.at[1], row_rx.at[1], normed_back, ([z1.spread], [], [x1.own], []))
    back.fold()
    small = 128
    shared_g[n] = jnp.zeros(shared_g.shape[1:], F32)
    for i in range(4 * state // 128):
        sl = slice(i * 128, (i + 1) * 128)
        shared_g[n, 0:4, sl] = jnp.transpose(dcbc_s[sl, :])[0:4]
    for i in range(width // 128):
        shared_g[n, 8 + i : 9 + i, 0:128] = as_row(dgain_s[i * 128 : (i + 1) * 128, :])
    shared_copies = [links.copy(shared_g.at[n], shared_g.at[n], device) for device in group]
    bc_second.wait_recv()
    links.release([bc_second])
    for k in range(wide):
        bc_mine[k] = bc_core[k, y] + bc_row[k]
    bc_rx[w] = bc_mine[w]
    bc_copies = [links.copy(bc_mine.at[device[0]], bc_rx.at[w], device) for device in far]
    sv_g[w] = jnp.zeros(sv_g.shape[1:], F32)
    for i in range(thirds):
        sl = slice(i * 128, (i + 1) * 128)
        sv_g[w, 0:4, sl] = jnp.transpose(cols_s[sl, :])[0:4]
        sv_g[w, 4:5, sl] = as_row(dog_s[sl, :])
    sv_g[w, :, chans : chans + small] = dhp_s[...]
    z2.spread()
    arrived(shared_copies)
    total = shared_g[0]
    for q in range(1, parts):
        total = total + shared_g[q]
    sv_g[w, :, chans + small :] = total
    sv_copies = [links.copy(sv_g.at[w], sv_g.at[w], device) for device in far]

    arrived(bc_copies)
    own = bc_rx[0]
    for k in range(1, wide):
        own = own + bc_rx[k]
    bc_own[n] = own
    bc_group = [links.copy(bc_own.at[n], bc_own.at[n], device) for device in group]
    squares = total_square(own)
    arrived(dt_copies)
    own = dt_rx[0]
    for k in range(1, wide):
        own = own + dt_rx[k]
    dt_own[...] = own
    squares = squares + total_square(own)
    arrived(sv_copies)
    own = sv_g[0]
    for k in range(1, wide):
        own = own + sv_g[k]
    sv_sum[...] = own
    x0.spread()
    x2.own()
    for i in range(3 * thirds):
        squares = squares + square_s[i][:, 0:1]
    once = jnp.where(w == 0, 1.0, 0.0)
    squares = squares + once * total_square(own[:, 0 : chans + small])
    squares = squares + jnp.where(n == 0, once, 0.0) * total_square(own[:, chans + small :])
    norm_n[n] = jnp.broadcast_to(squares, (8, 128))
    norm_copies = [links.copy(norm_n.at[n], norm_n.at[n], device) for device in group]

    x1.spread()

    block = branch.total() * live_ref[:, pl.ds(pl.multiple_of(n * own_rows, 128), own_rows)]
    for i in range(width // 128):
        sl = slice(i * 128, (i + 1) * 128)
        block_ref[:, sl] = hidden_ref[:, sl] + jnp.transpose(block[sl, :])
    arrived(norm_copies)
    norm_w[w] = norm_n[0] + norm_n[1] + norm_n[2] + norm_n[3]
    wide_copies = [links.copy(norm_w.at[w], norm_w.at[w], device) for device in far]
    x2.spread()
    dn = back.total() * gain_col[...]
    dots = jnp.sum(dn * hq[n], axis=0, keepdims=True) / width
    for i in range(width // 128):
        sl = slice(i * 128, (i + 1) * 128)
        value = inv_ref[...] * (dn[sl] - hq[n, sl, :] * dots)
        grad_ref[:, sl] = cot_ref[:, sl] + jnp.transpose(value)
    arrived(wide_copies)
    total = norm_w[0]
    for k in range(1, wide):
        total = total + norm_w[k]
    norm_ref[...] = jnp.sqrt(total)
    for job in jobs:
        job.finish()
    arrived(bc_group)
    links.drain()

    def sent(b, _):
        for j in range(3):
            stat_copy(j, b).wait_send()
        return 0

    lax.fori_loop(0, 2 * blocks, sent, 0)


def run_layer(lengths, hidden, cot, gain, w_zx, w_out, w_bc, dtw, cx, cbc, hp, og, heads, shard, wide, narrow):
    own_rows, width = hidden.shape
    tokens = own_rows * narrow
    chans, n4 = cx.shape[1], cbc.shape[1]
    rows = w_zx.shape[1]
    depth, blocks, half, thirds = wide // 2, tokens // SPAN, n4 // 2, chans // 128
    full, bc2, small = (chans, tokens), (half, tokens), (16, tokens)
    quarters = (narrow, width, own_rows)
    weights = (depth, 2, rows, chans)
    piece = (3 * thirds, depth, 2, rows, 128)
    quarter = (width // wide // 4, n4)
    sums = (16, chans + 128 + 256)
    shapes = [
        hidden.shape,
        hidden.shape,
        piece,
        (4,) + quarter,
        (16, 128),
        sums,
        (8, 128),
    ]
    scratch = [
        quarters,
        quarters,
        weights,
        weights,
        weights,
        (depth, 2, 2, rows // 2, n4),
        (depth, 2, 16, 128),
        (narrow, 8, 128),
        (16, width),
        (width, 1),
        (1, width),
        (128, 128),
        (chans, 4),
        (n4, 4),
        (16, 3),
        (chans, 1),
        (1, tokens),
        (1, own_rows),
        (2 * chans + n4 + 16, tokens),
        full,
        full,
        full,
        bc2,
        bc2,
        (n4, tokens),
        small,
        small,
        small,
        (blocks, chans, half),
        (blocks, SPAN, SPAN),
        full,
        full,
        full,
        (blocks, chans, half),
        bc2,
        bc2,
        (blocks, SPAN, SPAN),
        small,
        small,
        small,
        small,
        (blocks, 16, SPAN),
        (chans, 128),
        (n4, 128),
        (16, 128),
        (chans, 1),
        (width, 1),
        (2 * blocks, 8, 128),
        (narrow, 2 * blocks, 8, 128),
        (2 * thirds,) + piece[1:],
        (3 * thirds, depth, rows, 128),
        (3 * thirds, depth - 1, rows, 128),
        (2, 2, width, own_rows),
        (2, width, own_rows),
        (wide, 2, 2) + quarter,
        (wide, 2) + quarter,
        (wide,) + quarter,
        (wide,) + quarter,
        (wide,) + quarter,
        (wide, 16, 128),
        (wide, 16, 128),
        (narrow, 16, 256),
        (wide,) + sums,
        (narrow, 8, 128),
        (wide, 8, 128),
        (3 * thirds, 1, 128),
    ]
    lows = [quarters] * 2 + [(2 * chans + n4 + 16, width)] * 2
    copies = 200
    operands = (lengths, hidden, cot, gain, w_zx, w_out, w_bc, dtw, cx, cbc, hp, og)
    return pl.pallas_call(
        functools.partial(layer_kernel, wide, heads, shard, chans * narrow),
        out_shape=[jax.ShapeDtypeStruct(shape, F32) for shape in shapes],
        in_specs=[pl.BlockSpec(memory_space=pltpu.SMEM)]
        + [pl.BlockSpec(memory_space=pltpu.VMEM)] * (len(operands) - 1),
        scratch_shapes=[pltpu.VMEM(shape, F32) for shape in scratch]
        + [pltpu.VMEM(shape, jnp.bfloat16) for shape in lows]
        + [
            pltpu.SemaphoreType.DMA((copies,)),
            pltpu.SemaphoreType.DMA((copies,)),
            pltpu.SemaphoreType.DMA((3, 2 * blocks)),
            pltpu.SemaphoreType.DMA((3, 2 * blocks)),
        ],
        compiler_params=pltpu.CompilerParams(
            vmem_limit_bytes=62 * MIB, collective_id=0, has_side_effects=True
        ),
        cost_estimate=pl.CostEstimate(flops=20_000_000_000, bytes_accessed=20_000_000, transcendentals=0),
    )(*operands)


def finish_kernel(
    wide,
    narrow,
    gfull,
    bc_own,
    dt_own,
    sv,
    norm_ref,
    block_in,
    grad_in,
    stat_l,
    stat_r,
    stat_lo,
    stat_ro,
    root_l,
    root_r,
    root_lo,
    root_ro,
    w_ref,
    wout_ref,
    bcw_ref,
    dtw_ref,
    cx_ref,
    cbc_ref,
    hp_ref,
    og_ref,
    gain_ref,
    block_out,
    in_grad,
    clip,
    g_zx,
    new_zx,
    new_l,
    new_r,
    g_out,
    new_out,
    new_lo,
    new_ro,
    g_bc,
    new_bc,
    g_dt,
    new_dt,
    g_cx,
    new_cx,
    g_cbc,
    new_cbc,
    g_hp,
    new_hp,
    g_og,
    new_og,
    g_ng,
    new_ng,
    g_s,
    l_s,
    r_s,
    lo_s,
    ro_s,
    rl_s,
    rr_s,
    rlo_s,
    rro_s,
    in_sem,
    out_sem,
):
    rate = 10.0
    chans = w_ref.shape[2]
    thirds = chans // 128
    place = lax.axis_index("wide")
    z, x = place // 2, place % 2
    factor = 1.0 / jnp.maximum(norm_ref[0:1, 0:1], 1.0)
    fetches, results = [], []

    def fetch(src, dst):
        item = pltpu.make_async_copy(src, dst, in_sem.at[len(fetches)])
        item.start()
        fetches.append(item)
        return item

    def result(src, dst):
        item = pltpu.make_async_copy(src, dst, out_sem.at[len(results)])
        item.start()
        results.append(item)

    waits = []
    for m in (2, 0, 1):
        gs = g_s.at[m * thirds : (m + 1) * thirds]
        whole_m = fetch(gfull.at[m * thirds : (m + 1) * thirds], gs)
        if m == 2:
            others = [(root_ro, rro_s), (root_lo, rlo_s), (stat_ro, ro_s), (stat_lo, lo_s)]
        else:
            others = [(root_l.at[m], rl_s.at[m]), (root_r.at[m], rr_s.at[m])]
            others += [(stat_l.at[m], l_s.at[m]), (stat_r.at[m], r_s.at[m])]
        waits.append([whole_m] + [fetch(*pair) for pair in others])
    block_out[...] = block_in[...]
    in_grad[...] = grad_in[...]
    clip[...] = norm_ref[0:1, 0:1]

    def both(m):
        for item in waits[(1, 2, 0)[m]]:
            item.wait()
        parts = [flat(g_s[m * thirds + i]) for i in range(thirds)]
        mine = [g_s[m * thirds + i, z, x] for i in range(thirds)]
        return jnp.concatenate(mine, axis=1) * factor, halves(jnp.concatenate(parts, axis=1) * factor)

    own, full = both(2)
    g_out[...] = own
    ro_s[...] = 0.5 * ro_s[...] + 0.5 * product(halves(own), full, NT)
    result(ro_s, new_ro)
    lo_s[...] = 0.5 * lo_s[...] + 0.5 * product(full, full, TN)
    result(lo_s, new_lo)
    new_out[...] = wout_ref[...] - 0.5 * dot3(product(halves(rro_s[...]), full), rlo_s[...], NT)
    for m in range(2):
        own, full = both(m)
        g_zx[m] = own
        l_s[m] = 0.5 * l_s[m] + 0.5 * product(halves(own), full, NT)
        result(l_s.at[m], new_l.at[m])
        r_s[m] = 0.5 * r_s[m] + 0.5 * product(full, full, TN)
        result(r_s.at[m], new_r.at[m])
        new_zx[m] = w_ref[m] - 0.5 * dot3(product(halves(rl_s[m]), full), rr_s[m])

    grad = flat(bc_own[...]) * factor
    g_bc[...] = grad
    new_bc[...] = bcw_ref[...] - rate * grad
    heads, _, rows = dtw_ref.shape
    for h in range(heads):
        for i in range(2):
            row = i * heads + h
            grad = dt_own[row : row + 1, 0:rows] * factor
            g_dt[h, i : i + 1, :] = grad
            new_dt[h, i : i + 1, :] = dtw_ref[h, i : i + 1, :] - rate * grad
    sums = sv[...] * factor
    grad = sums[0:4, 0:chans]
    g_cx[...] = grad
    new_cx[...] = cx_ref[...] - rate * grad
    grad = sums[4:5, 0:chans]
    g_og[...] = grad.reshape(chans)
    new_og[...] = og_ref[...] - rate * g_og[...]
    n4 = cbc_ref.shape[1]
    last = chans + 128
    grad = sums[0:4, last : last + n4]
    g_cbc[...] = grad
    new_cbc[...] = cbc_ref[...] - rate * grad
    turned = jnp.transpose(
        jnp.concatenate([sums[:, chans:last], jnp.zeros((112, 128), F32)], axis=0)
    )
    for i, (row, start) in enumerate(((0, 0), (0, heads), (1, 0), (1, heads), (2, 0))):
        grad = turned[row : row + 1, start : start + heads]
        g_hp[i : i + 1, :] = grad
        new_hp[i : i + 1, :] = hp_ref[i : i + 1, :] - rate * grad
    shard = gain_ref.shape[0]
    count = narrow * shard // 128
    line = jnp.concatenate([sums[8 + i : 9 + i, last : last + 128] for i in range(count)], axis=1)
    grad = jnp.zeros((1, shard), F32)
    for q in range(narrow):
        piece = line[:, q * shard : (q + 1) * shard]
        grad = jnp.where(lax.axis_index("narrow") == q, piece, grad)
    g_ng[...] = grad.reshape(shard)
    new_ng[...] = gain_ref[...] - rate * g_ng[...]
    for item in results:
        item.wait()


def run_finish(partials, stats, roots, params, tokens_shape, wide, narrow):
    stat_l, stat_r, stat_lo, stat_ro = stats
    w_zx, w_out, w_bc, w_dt, cx, cbc, hp, og, gain = params
    like = [w_zx, w_zx, stat_l, stat_r, w_out, w_out, stat_lo, stat_ro]
    like += [item for item in (w_bc, w_dt, cx, cbc, hp, og, gain) for _ in range(2)]
    shapes = [tokens_shape, tokens_shape, (1, 1)] + [item.shape for item in like]
    far, near = pl.BlockSpec(memory_space=pl.ANY), pl.BlockSpec(memory_space=pltpu.VMEM)
    gfull = partials[0]
    kept = [gfull, stat_l, stat_r, stat_lo, stat_ro, *roots]
    return pl.pallas_call(
        functools.partial(finish_kernel, wide, narrow),
        out_shape=[jax.ShapeDtypeStruct(shape, F32) for shape in shapes],
        in_specs=[far] + [near] * 6 + [far] * 8 + [near] * len(params),
        out_specs=[near] * 5 + [far] * 2 + [near] * 2 + [far] * 2 + [near] * (len(shapes) - 11),
        scratch_shapes=[pltpu.VMEM(item.shape, F32) for item in kept]
        + [pltpu.SemaphoreType.DMA((15,)), pltpu.SemaphoreType.DMA((6,))],
        compiler_params=pltpu.CompilerParams(vmem_limit_bytes=56 * MIB),
        cost_estimate=pl.CostEstimate(flops=4_000_000_000, bytes_accessed=20_000_000, transcendentals=0),
    )(*partials, *stats, *roots, *params)


def fast_local(
    wide,
    narrow,
    hidden_in,
    out_cot,
    lengths,
    norm_gain,
    w_zx,
    w_bc,
    w_dt,
    conv_x,
    conv_bc,
    head_params,
    out_gain,
    w_out,
    left_statistic_gate,
    stat_right_zx,
    stat_left_out,
    stat_right_out,
    inverse_root_left_gate,
    inverse_root_right_gate,
    root_left_out,
    root_right_out,
):
    heads, shard = w_dt.shape[1], norm_gain.shape[0]
    out_rows, dt_rows = w_out.T, jnp.transpose(w_dt, (1, 2, 0))
    block, grad, *partials = run_layer(
        lengths,
        hidden_in,
        out_cot,
        norm_gain,
        w_zx,
        out_rows,
        w_bc,
        dt_rows,
        conv_x,
        conv_bc,
        head_params,
        out_gain,
        heads,
        shard,
        wide,
        narrow,
    )
    (
        block_out,
        in_grad,
        clip,
        g_zx,
        new_zx,
        new_l,
        new_r,
        g_out,
        new_out,
        new_lo,
        new_ro,
        g_bc,
        new_bc,
        g_dt,
        new_dt,
        *rest,
    ) = run_finish(
        (*partials, block, grad),
        (left_statistic_gate[:, 0], stat_right_zx, stat_left_out, stat_right_out[0]),
        (inverse_root_left_gate[:, 0], inverse_root_right_gate, root_left_out, root_right_out[0]),
        (w_zx, out_rows, w_bc, dt_rows, conv_x, conv_bc, head_params, out_gain, norm_gain),
        hidden_in.shape,
        wide,
        narrow,
    )
    return (
        block_out,
        in_grad,
        clip.reshape(()),
        g_zx,
        new_zx,
        new_l[:, None],
        new_r,
        g_out.T,
        new_out.T,
        new_lo,
        new_ro[None],
        g_bc,
        new_bc,
        jnp.transpose(g_dt, (2, 0, 1)),
        jnp.transpose(new_dt, (2, 0, 1)),
        *rest,
    )


def solution(mesh):
    wide, narrow = mesh.shape["wide"], mesh.shape["narrow"]
    body = functools.partial(fast_local, wide, narrow) if (wide, narrow) == (8, 4) else local
    return jax.shard_map(
        body,
        mesh=mesh,
        in_specs=(
            P(("wide", "narrow"), None),
            P(("wide", "narrow"), None),
            P("wide"),
            P("narrow"),
            P(None, "wide", "narrow"),
            P("wide", None),
            P("wide", "narrow", None),
            P(None, "narrow"),
            P(),
            P(None, "narrow"),
            P("narrow"),
            P("narrow", "wide"),
            P(None, "narrow", "wide", None),
            P(None, "narrow", None),
            P("narrow", None),
            P("narrow", "wide", None),
            P(None, "narrow", "wide", None),
            P(None, "narrow", None),
            P("narrow", None),
            P("narrow", "wide", None),
        ),
        out_specs=(
            P(("wide", "narrow"), None),
            P(("wide", "narrow"), None),
            P(),
            P(None, "wide", "narrow"),
            P(None, "wide", "narrow"),
            P(None, "narrow", "wide", None),
            P(None, "narrow", None),
            P("narrow", "wide"),
            P("narrow", "wide"),
            P("narrow", None),
            P("narrow", "wide", None),
            P("wide", None),
            P("wide", None),
            P("wide", "narrow", None),
            P("wide", "narrow", None),
            P(None, "narrow"),
            P(None, "narrow"),
            P(),
            P(),
            P(None, "narrow"),
            P(None, "narrow"),
            P("narrow"),
            P("narrow"),
            P("narrow"),
            P("narrow"),
        ),
        check_vma=False,
    )
```

```python
import functools

import jax
import jax.numpy as jnp
from jax import lax
from jax.experimental import pallas as pl
from jax.experimental.pallas import tpu as pltpu
from jax.sharding import PartitionSpec as P

SPAN = 128
WIDTH = 64
HIGH = lax.Precision.HIGH
F32 = jnp.float32
NN = (((1,), (0,)), ((), ()))
NT = (((1,), (1,)), ((), ()))
TN = (((0,), (0,)), ((), ()))
TT = (((0,), (1,)), ((), ()))


def dot(a, b, dims=NN):
    return lax.dot_general(a, b, dims, precision=HIGH, preferred_element_type=F32)


def halves(v):
    hi = v.astype(jnp.bfloat16)
    return hi, (v - hi.astype(F32)).astype(jnp.bfloat16)


def product(a, b, dims=NN):
    (ah, al), (bh, bl) = a, b
    (left,), (right,) = dims[0]
    rows, depth = ah.shape[1 - left], ah.shape[left]

    def times(u, v):
        return lax.dot_general(u, v, dims, preferred_element_type=F32)

    if depth < 128:
        return times(
            jnp.concatenate([ah, al, ah], axis=left), jnp.concatenate([bh, bh, bl], axis=right)
        )
    if depth == 128:
        top = jnp.concatenate([ah, ah], axis=left)
        low = jnp.concatenate([al, jnp.zeros_like(al)], axis=left)
        out = times(jnp.concatenate([top, low], axis=1 - left), jnp.concatenate([bh, bl], axis=right))
        return out[0:rows] + out[rows:]
    out = times(jnp.concatenate([ah, al], axis=1 - left), bh)
    return out[0:rows] + out[rows:] + times(ah, bl)


def dot3(a, b, dims=NN):
    return product(halves(a), halves(b), dims)


def sigmoid(v):
    return 1.0 / (1.0 + jnp.exp(-v))


def split3(v):
    hi = v.astype(jnp.bfloat16)
    rest = v - hi.astype(F32)
    mid = rest.astype(jnp.bfloat16)
    lo = (rest - mid.astype(F32)).astype(jnp.bfloat16)
    return jnp.concatenate([hi, mid, lo], axis=0)


def exact_dot(v, ones):
    rows = v.shape[0]
    out = lax.dot_general(split3(v), ones, NN, preferred_element_type=F32)
    return out[0:rows] + out[rows : 2 * rows] + out[2 * rows : 3 * rows]


def iota(shape, axis):
    return lax.broadcasted_iota(jnp.int32, shape, axis)


def shift_right(v, count):
    return jnp.where(iota(v.shape, 1) >= count, pltpu.roll(v, count, axis=1), 0.0)


def shift_left(v, count):
    length = v.shape[1]
    return jnp.where(iota(v.shape, 1) < length - count, pltpu.roll(v, length - count, axis=1), 0.0)


def conv_rows(v, taps):
    count = taps.shape[1]
    total = taps[:, count - 1 : count] * v
    for j in range(count - 1):
        total = total + taps[:, j : j + 1] * shift_right(v, count - 1 - j)
    return total


def pieces(ref, chans, state):
    bc = 2 * chans
    dt = bc + 4 * state
    return ref.at[0:chans], ref.at[chans:bc], ref.at[bc:dt], ref.at[dt : dt + 16]


def convolve(x_ref, bc_ref, live_ref, cx_ref, cbc_ref, xc_ref, dx_act_ref, b_ref, c_ref, dbc_act_ref):
    chans, tokens = xc_ref.shape
    state = c_ref.shape[0] // 2
    live = live_ref[...]

    def conv_x_rows(i, _):
        rows = pl.ds(pl.multiple_of(i * 8, 8), 8)
        u = conv_rows(x_ref[rows, :], cx_ref[rows, :])
        s = sigmoid(u)
        xc_ref[rows, :] = u * s * live
        dx_act_ref[rows, :] = (s + u * s * (1.0 - s)) * live
        return 0

    lax.fori_loop(0, chans // 8, conv_x_rows, 0, unroll=2)

    def conv_bc_rows(i, _, src, dst, dst_row, shift):
        rows = pl.ds(pl.multiple_of(src * state + i * 8, 8), 8)
        out = pl.ds(pl.multiple_of(dst_row + i * 8, 8), 8)
        u = conv_rows(bc_ref[rows, :], cbc_ref[rows, :])
        s = sigmoid(u)
        dbc_act_ref[rows, :] = s + u * s * (1.0 - s)
        v = u * s
        if shift == 1:
            v = shift_right(v, 1)
        if shift == -1:
            v = shift_left(v, 1)
        dst[out, :] = v
        return 0

    for src, dst, row, shift in ((0, b_ref, 0, 0), (1, c_ref, 0, 1), (2, b_ref, state, 0), (3, c_ref, state, -1)):
        lax.fori_loop(
            0,
            state // 8,
            functools.partial(conv_bc_rows, src=src, dst=dst, dst_row=row, shift=shift),
            0,
            unroll=2,
        )


def step_sizes(pre_ref, hp_ref, step_ref, cum_ref, cumex_ref, heads):
    blocks = pre_ref.shape[1] // SPAN
    pre = pre_ref[...] + hp_ref[:, 0:1]
    steps = jnp.maximum(pre, 0.0) + jnp.log1p(jnp.exp(-jnp.abs(pre)))
    step_ref[...] = steps
    logs = -hp_ref[:, 1:2] * steps
    rows16 = iota((16, SPAN), 0)
    lane16 = iota((16, SPAN), 1)
    row_q = iota((SPAN, SPAN), 0)
    lane_q = iota((SPAN, SPAN), 1)
    upto = (row_q <= lane_q).astype(F32).astype(jnp.bfloat16)
    downto = (row_q >= lane_q).astype(F32).astype(jnp.bfloat16)
    both = jnp.concatenate([upto, downto], axis=1)
    for b in range(blocks):
        sums = exact_dot(logs[:, b * SPAN : (b + 1) * SPAN], both)
        cum = jnp.where(rows16 < heads, sums[:, 0:SPAN], sums[:, SPAN : 2 * SPAN])
        ex_f = jnp.where(lane16 >= 1, pltpu.roll(cum, 1, axis=1), 0.0)
        ex_r = jnp.where(lane16 < SPAN - 1, pltpu.roll(cum, SPAN - 1, axis=1), 0.0)
        cum_ref[:, b * SPAN : (b + 1) * SPAN] = cum
        cumex_ref[:, b * SPAN : (b + 1) * SPAN] = jnp.where(rows16 < heads, ex_f, ex_r)


def states(xc_ref, b_ref, step_ref, cum_ref, sloc_ref, hcat_ref, heads):
    blocks = xc_ref.shape[1] // SPAN
    state = b_ref.shape[0] // 2

    def local_states(b, _):
        sl = pl.ds(pl.multiple_of(b * SPAN, SPAN), SPAN)
        bcat = spread(b_ref[:, sl], state)
        tail = tails(cum_ref[:, sl], step_ref[:, sl], heads)
        left = tailed(xc_ref[:, sl], tail, range(heads), heads)
        sloc_ref[b] = dot3(left, bcat, NT)
        return 0

    lax.fori_loop(0, blocks, local_states, 0)

    lane_h = iota((WIDTH, 2 * state), 1)
    for h in range(heads):
        rows = slice(h * WIDTH, (h + 1) * WIDTH)
        carry = jnp.zeros((WIDTH, 2 * state), F32)
        for i in range(blocks):
            r = blocks - 1 - i
            hcat_ref[i, rows, 0:state] = carry[:, 0:state]
            hcat_ref[r, rows, state : 2 * state] = carry[:, state : 2 * state]
            tot_f = jnp.exp(cum_ref[h : h + 1, (i + 1) * SPAN - 1 : (i + 1) * SPAN])
            tot_r = jnp.exp(cum_ref[heads + h : heads + h + 1, r * SPAN : r * SPAN + 1])
            factor = jnp.where(lane_h < state, tot_f, tot_r)
            piece = jnp.where(lane_h < state, sloc_ref[i, rows, :], sloc_ref[r, rows, :])
            carry = carry * factor + piece


def outputs(z_ref, xc_ref, b_ref, c_ref, step_ref, cum_ref, cumex_ref, hcat_ref, hp_ref, y_ref, inner_ref, heads, emit):
    blocks = xc_ref.shape[1] // SPAN
    state = b_ref.shape[0] // 2
    row_q = iota((SPAN, SPAN), 0)
    lane_q = iota((SPAN, SPAN), 1)
    lower = row_q < lane_q
    diag = row_q == lane_q

    def block(b, _):
        sl = pl.ds(pl.multiple_of(b * SPAN, SPAN), SPAN)
        bb, cc = b_ref[:, sl], c_ref[:, sl]
        inner = jnp.where(
            lower, dot3(bb[0:state], cc[0:state], TN), dot3(bb[state:], cc[state:], TN)
        )
        inner_ref[b] = inner
        cum, steps, cumex = cum_ref[:, sl], step_ref[:, sl], cumex_ref[:, sl]
        scale = jnp.exp(cumex)
        cols = columns(cum, steps)
        sums = None
        entering = dot3(hcat_ref[b], spread(cc, state))
        x_parts = halves(xc_ref[:, sl])
        for h in range(heads):
            rows = slice(h * WIDTH, (h + 1) * WIDTH)
            decay = decays(cols, cumex, lower, diag, h, heads)
            mt = jnp.where(diag, hp_ref[h : h + 1, 2:3], inner * decay)
            y = product((x_parts[0][rows], x_parts[1][rows]), halves(mt))
            y = y + entering[rows, 0:SPAN] * scale[h : h + 1]
            y = y + entering[rows, SPAN:] * scale[heads + h : heads + h + 1]
            z = z_ref[rows, sl]
            y_ref[rows, sl] = y
            sums = emit(b, sl, h, rows, y * (z * sigmoid(z)), sums)
        return 0

    lax.fori_loop(0, blocks, block, 0)


def fwd_kernel(
    heads,
    proj_ref,
    live_ref,
    cx_ref,
    cbc_ref,
    hp_ref,
    y_ref,
    xc_ref,
    dx_act_ref,
    b_ref,
    c_ref,
    dbc_act_ref,
    step_ref,
    cum_ref,
    cumex_ref,
    hcat_ref,
    inner_ref,
    gated_ref,
    sq_ref,
    sloc_ref,
):
    z_ref, x_ref, bc_ref, pre_ref = pieces(proj_ref, xc_ref.shape[0], c_ref.shape[0] // 2)
    convolve(x_ref, bc_ref, live_ref, cx_ref, cbc_ref, xc_ref, dx_act_ref, b_ref, c_ref, dbc_act_ref)
    step_sizes(pre_ref, hp_ref, step_ref, cum_ref, cumex_ref, heads)
    states(xc_ref, b_ref, step_ref, cum_ref, sloc_ref, hcat_ref, heads)

    def emit(b, sl, h, rows, gated, total):
        gated_ref[rows, sl] = gated
        part = jnp.sum(gated * gated, axis=0, keepdims=True)
        total = part if total is None else total + part
        if h == heads - 1:
            sq_ref[:, sl] = total
        return total

    outputs(z_ref, xc_ref, b_ref, c_ref, step_ref, cum_ref, cumex_ref, hcat_ref, hp_ref, y_ref, inner_ref, heads, emit)


def spread(bb, state):
    zero = jnp.zeros((state, SPAN), F32)
    top = jnp.concatenate([bb[0:state], zero], axis=1)
    low = jnp.concatenate([zero, bb[state:]], axis=1)
    return jnp.concatenate([top, low], axis=0)


def tails(cum, steps, heads):
    rows = iota((16, SPAN), 0)
    last = jnp.where(rows[:, 0:1] < heads, cum[:, SPAN - 1 : SPAN], cum[:, 0:1])
    return jnp.exp(last - cum) * steps


def tailed(xc, tail, chosen, heads):
    parts = []
    for i, h in enumerate(chosen):
        x = xc[i * WIDTH : (i + 1) * WIDTH]
        parts.append(
            jnp.concatenate([x * tail[h : h + 1], x * tail[heads + h : heads + h + 1]], axis=1)
        )
    return jnp.concatenate(parts, axis=0)


def columns(cum, steps):
    pad = jnp.zeros((SPAN - 32, SPAN), F32)
    return jnp.transpose(jnp.concatenate([cum, steps, pad], axis=0))


def decays(cols, cumex, lower, diag, h, heads):
    f, r = h, heads + h
    arg = jnp.where(
        lower, cumex[f : f + 1] - cols[:, f : f + 1], cumex[r : r + 1] - cols[:, r : r + 1]
    )
    step = jnp.where(lower, cols[:, 16 + f : 17 + f], cols[:, 16 + r : 17 + r])
    return jnp.where(diag, 0.0, jnp.exp(arg) * step)


def gate_back(z_ref, y_ref, don_ref, rms, coef, og_ref, dy_ref, dz_ref, dog_ref, onorm_ref=None):
    chans = y_ref.shape[0]

    def gate_rows(i, _):
        rows = pl.ds(pl.multiple_of(i * 8, 8), 8)
        z, y, don, og = z_ref[rows, :], y_ref[rows, :], don_ref[rows, :], og_ref[rows, :]
        s = sigmoid(z)
        act = z * s
        gated = y * act
        normed = rms * don
        dog_ref[rows, 0:1] = jnp.sum(gated * normed, axis=1, keepdims=True)
        dgated = normed * og - gated * coef
        dy_ref[rows, :] = dgated * act
        dz_ref[rows, :] = dgated * y * (s + act * (1.0 - s))
        if onorm_ref is not None:
            onorm_ref[rows, :] = gated * rms * og
        return 0

    lax.fori_loop(0, chans // 8, gate_rows, 0, unroll=2)


def back_intra(xc_ref, c_ref, inner_ref, step_ref, cum_ref, cumex_ref, hcat_ref, hp_ref, dy_s, dxc_s, dh_s, dc_s, din_s, g_s, cv_s, dd_s, chosen, heads, tick):
    blocks = xc_ref.shape[1] // SPAN
    state = c_ref.shape[0] // 2
    lower = iota((SPAN, SPAN), 0) < iota((SPAN, SPAN), 1)
    diag = iota((SPAN, SPAN), 0) == iota((SPAN, SPAN), 1)
    first = chosen[0] == 0

    def block(b, put):
        sl = pl.ds(pl.multiple_of(b * SPAN, SPAN), SPAN)
        cc = c_ref[:, sl]
        inner = inner_ref[b]
        cumex = cumex_ref[:, sl]
        scale = jnp.exp(cumex)
        cols = columns(cum_ref[:, sl], step_ref[:, sl])
        dinner = jnp.zeros((SPAN, SPAN), F32) if first else din_s[b]
        dcc = jnp.zeros((2 * state, SPAN), F32) if first else dc_s[:, sl]
        for h in chosen:
            f, r = h, heads + h
            rows = slice(h * WIDTH, (h + 1) * WIDTH)
            decay = decays(cols, cumex, lower, diag, h, heads)
            mt = inner * decay
            e_f, e_r = scale[f : f + 1], scale[r : r + 1]
            ce = jnp.concatenate([cc[0:state] * e_f, cc[state:] * e_r], axis=0)
            x = xc_ref[rows, sl]
            dy = dy_s[rows, sl]
            dy_parts = halves(dy)
            left = jnp.concatenate([x, hcat_ref[b, rows, :]], axis=1)
            back = product(halves(left), dy_parts, TN)
            dmt, dce = back[0:SPAN], back[SPAN:]
            dinner = dinner + dmt * decay
            w = dmt * mt
            over_f = jnp.sum(jnp.where(lower, w, 0.0), axis=0, keepdims=True)
            over_r = jnp.sum(jnp.where(lower, 0.0, w), axis=0, keepdims=True)
            prod = dce * ce
            put(g_s, (slice(f, f + 1), sl), over_f + jnp.sum(prod[0:state], axis=0, keepdims=True))
            put(g_s, (slice(r, r + 1), sl), over_r + jnp.sum(prod[state:], axis=0, keepdims=True))
            dcc = dcc + jnp.concatenate([dce[0:state] * e_f, dce[state:] * e_r], axis=0)
            right = jnp.concatenate(
                [jnp.where(lower, mt, 0.0), jnp.where(lower, 0.0, mt), ce], axis=0
            )
            out = product(dy_parts, halves(right), NT)
            dx_f, dx_r = out[:, 0:SPAN], out[:, SPAN : 2 * SPAN]
            put(dh_s, (b, rows, slice(None)), out[:, 2 * SPAN :])
            put(cv_s, (slice(f, f + 1), sl), jnp.sum(x * dx_f, axis=0, keepdims=True))
            put(cv_s, (slice(r, r + 1), sl), jnp.sum(x * dx_r, axis=0, keepdims=True))
            put(dd_s, (slice(h, h + 1), sl), jnp.sum(x * dy, axis=0, keepdims=True))
            put(dxc_s, (rows, sl), dx_f + dx_r + hp_ref[h : h + 1, 2:3] * dy)
        put(din_s, (b,), dinner)
        put(dc_s, (slice(None), sl), dcc)

    two_at_a_time(blocks, block, tick)


def two_at_a_time(blocks, block, tick):
    def body(i, _):
        stores = []
        for b in (2 * i, 2 * i + 1):
            block(b, lambda ref, at, value: stores.append((ref, at, value)))
        for ref, at, value in stores:
            ref[at] = value
        tick(2 * i)
        tick(2 * i + 1)
        return 0

    lax.fori_loop(0, blocks // 2, body, 0)


def back_states(cum_ref, hcat_ref, dh_s, tq_s, state, chosen, heads):
    blocks = hcat_ref.shape[0]
    lane_h = iota((WIDTH, 2 * state), 1)
    lane_1 = iota((1, 2 * state), 1)
    for h in chosen:
        rows = slice(h * WIDTH, (h + 1) * WIDTH)
        carry = jnp.zeros((WIDTH, 2 * state), F32)
        for i in range(blocks):
            f = blocks - 1 - i
            tot_f = jnp.exp(cum_ref[h : h + 1, (f + 1) * SPAN - 1 : (f + 1) * SPAN])
            tot_r = jnp.exp(cum_ref[heads + h : heads + h + 1, i * SPAN : i * SPAN + 1])
            factor = jnp.where(lane_h < state, tot_f, tot_r)
            direct = jnp.where(lane_h < state, dh_s[f, rows, :], dh_s[i, rows, :])
            kept = jnp.where(lane_h < state, hcat_ref[f, rows, :], hcat_ref[i, rows, :])
            scaled = carry * factor
            dots = jnp.sum(scaled * kept, axis=0, keepdims=True)
            q_f = jnp.sum(jnp.where(lane_1 < state, dots, 0.0), axis=1, keepdims=True)
            q_r = jnp.sum(jnp.where(lane_1 < state, 0.0, dots), axis=1, keepdims=True)
            tq_s[f, h : h + 1, :] = jnp.broadcast_to(q_f, (1, SPAN))
            tq_s[i, heads + h : heads + h + 1, :] = jnp.broadcast_to(q_r, (1, SPAN))
            dh_s[f, rows, 0:state] = carry[:, 0:state]
            dh_s[i, rows, state:] = carry[:, state:]
            carry = scaled + direct


def back_inter(xc_ref, b_ref, step_ref, cum_ref, dxc_s, dh_s, db_s, v_s, chosen, heads, tick):
    blocks = xc_ref.shape[1] // SPAN
    state = b_ref.shape[0] // 2
    first = chosen[0] == 0
    group = slice(chosen[0] * WIDTH, (chosen[-1] + 1) * WIDTH)

    def block(b, put):
        sl = pl.ds(pl.multiple_of(b * SPAN, SPAN), SPAN)
        bcat = spread(b_ref[:, sl], state)
        tail = tails(cum_ref[:, sl], step_ref[:, sl], heads)
        xc = xc_ref[group, sl]
        dxc = dxc_s[group, sl]
        dsl = halves(dh_s[b, group, :])
        dleft = product(dsl, halves(bcat))
        dbs = product(dsl, halves(tailed(xc, tail, chosen, heads)), TN)
        db = jnp.concatenate([dbs[0:state, 0:SPAN], dbs[state:, SPAN:]], axis=0)
        put(db_s, (slice(None), sl), db if first else db_s[:, sl] + db)
        parts = []
        for i, h in enumerate(chosen):
            f, r = h, heads + h
            part = slice(i * WIDTH, (i + 1) * WIDTH)
            tx_f = dleft[part, 0:SPAN] * tail[f : f + 1]
            tx_r = dleft[part, SPAN:] * tail[r : r + 1]
            put(v_s, (slice(f, f + 1), sl), jnp.sum(xc[part] * tx_f, axis=0, keepdims=True))
            put(v_s, (slice(r, r + 1), sl), jnp.sum(xc[part] * tx_r, axis=0, keepdims=True))
            parts.append(dxc[part] + tx_f + tx_r)
        put(dxc_s, (group, sl), jnp.concatenate(parts, axis=0))

    two_at_a_time(blocks, block, tick)


def back_logs(b_ref, c_ref, pre_ref, step_ref, hp_ref, ddt_ref, dhp_ref, db_s, dc_s, din_s, g_s, cv_s, v_s, dd_s, tq_s, heads):
    blocks = pre_ref.shape[1] // SPAN
    state = b_ref.shape[0] // 2
    row_q = iota((SPAN, SPAN), 0)
    lane_q = iota((SPAN, SPAN), 1)
    lower = row_q < lane_q
    strict = (row_q > lane_q).astype(F32)
    weak = (row_q >= lane_q).astype(F32)
    strict_t = (row_q < lane_q).astype(F32)
    weak_t = (row_q <= lane_q).astype(F32)
    tri = jnp.concatenate(
        [
            jnp.concatenate([strict, strict_t], axis=1),
            jnp.concatenate([weak, weak_t], axis=1),
            jnp.concatenate([strict_t, strict], axis=1),
        ],
        axis=0,
    ).astype(jnp.bfloat16)
    rows16 = iota((16, SPAN), 0)
    used = rows16 < 2 * heads
    rate = hp_ref[:, 1:2]

    def block(b, carry):
        bias_sum, log_sum, skip_sum = carry
        sl = pl.ds(pl.multiple_of(b * SPAN, SPAN), SPAN)
        dinner = din_s[b]
        both = jnp.concatenate(
            [jnp.where(lower, dinner, 0.0), jnp.where(lower, 0.0, dinner)], axis=0
        )
        dc_s[:, sl] = dc_s[:, sl] + dot3(spread(b_ref[:, sl], state), both)
        db = dot3(c_ref[:, sl], both, NT)
        db_s[0:state, sl] = db_s[0:state, sl] + db[0:state, 0:SPAN]
        db_s[state:, sl] = db_s[state:, sl] + db[state:, SPAN:]
        g = jnp.where(used, g_s[:, sl], 0.0)
        c = jnp.where(used, cv_s[:, sl], 0.0)
        v = jnp.where(used, v_s[:, sl], 0.0)
        steps = step_ref[:, sl]
        sums = exact_dot(jnp.concatenate([g, -c, v], axis=1), tri)
        dlog = jnp.where(rows16 < heads, sums[:, 0:SPAN], sums[:, SPAN:])
        dlog = dlog + jnp.where(used, tq_s[b], 0.0)
        pre = pre_ref[:, sl] + hp_ref[:, 0:1]
        small = steps < 1e-30
        ratio = jnp.where(small, 1.0, sigmoid(pre) / jnp.where(small, 1.0, steps))
        dpre = (c + v) * ratio - rate * dlog * sigmoid(pre)
        ddt_ref[:, sl] = dpre
        skip = jnp.where(rows16 < heads, dd_s[:, sl], 0.0)
        return bias_sum + dpre, log_sum - rate * dlog * steps, skip_sum + skip

    zeros16 = jnp.zeros((16, SPAN), F32)
    bias_sum, log_sum, skip = lax.fori_loop(0, blocks, block, (zeros16, zeros16, zeros16))
    dhp_ref[:, 0:1] = jnp.sum(bias_sum, axis=1, keepdims=True)
    dhp_ref[:, 1:2] = jnp.sum(log_sum, axis=1, keepdims=True)
    dhp_ref[:, 2:3] = jnp.sum(skip, axis=1, keepdims=True)


def conv_back(du, v, taps):
    count = taps.shape[1]
    dv = taps[:, count - 1 : count] * du
    sums = [jnp.sum(du * v, axis=1, keepdims=True)]
    for j in range(count - 2, -1, -1):
        moved = shift_left(du, count - 1 - j)
        dv = dv + taps[:, j : j + 1] * moved
        sums.append(jnp.sum(moved * v, axis=1, keepdims=True))
    return dv, sums[::-1]


def conv_x_back(xin_ref, cx_ref, dx_act_ref, dxc_s, dxin_ref, dcx_ref, start, count):
    def group(i, _):
        rows = pl.ds(pl.multiple_of(start + i * 8, 8), 8)
        dv, sums = conv_back(dxc_s[rows, :] * dx_act_ref[rows, :], xin_ref[rows, :], cx_ref[rows, :])
        dxin_ref[rows, :] = dv
        for j, item in enumerate(sums):
            dcx_ref[rows, j : j + 1] = item
        return 0

    lax.fori_loop(0, count // 8, group, 0, unroll=2)


def conv_bc_back(bc_ref, cbc_ref, dbc_act_ref, db_s, dc_s, dbc_ref, dcbc_ref):
    state = db_s.shape[0] // 2

    def group(i, _, src, grad, grad_row, shift):
        rows = pl.ds(pl.multiple_of(src * state + i * 8, 8), 8)
        from_rows = pl.ds(pl.multiple_of(grad_row + i * 8, 8), 8)
        d = grad[from_rows, :]
        if shift == 1:
            d = shift_left(d, 1)
        if shift == -1:
            d = shift_right(d, 1)
        dv, sums = conv_back(d * dbc_act_ref[rows, :], bc_ref[rows, :], cbc_ref[rows, :])
        dbc_ref[rows, :] = dv
        for j, item in enumerate(sums):
            dcbc_ref[rows, j : j + 1] = item
        return 0

    for src, grad, row, shift in ((0, db_s, 0, 0), (1, dc_s, 0, 1), (2, db_s, state, 0), (3, dc_s, state, -1)):
        lax.fori_loop(
            0,
            state // 8,
            functools.partial(group, src=src, grad=grad, grad_row=row, shift=shift),
            0,
            unroll=2,
        )


def pairs_of(heads):
    return [tuple(range(h, min(h + 2, heads))) for h in range(0, heads, 2)]


def bwd_kernel(
    heads,
    proj_ref,
    y_ref,
    xc_ref,
    dx_act_ref,
    b_ref,
    c_ref,
    dbc_act_ref,
    step_ref,
    cum_ref,
    cumex_ref,
    hcat_ref,
    inner_ref,
    don_ref,
    rms_ref,
    coef_ref,
    og_ref,
    cx_ref,
    cbc_ref,
    hp_ref,
    dproj_ref,
    dcx_ref,
    dcbc_ref,
    dhp_ref,
    dog_ref,
    dy_s,
    dxc_s,
    dh_s,
    db_s,
    dc_s,
    din_s,
    g_s,
    cv_s,
    v_s,
    dd_s,
    tq_s,
):
    chans, state = y_ref.shape[0], b_ref.shape[0] // 2
    z_ref, xin_ref, bc_ref, pre_ref = pieces(proj_ref, chans, state)
    dz_ref, dxin_ref, dbc_ref, ddt_ref = pieces(dproj_ref, chans, state)
    gate_back(z_ref, y_ref, don_ref, rms_ref[...], coef_ref[...], og_ref, dy_s, dz_ref, dog_ref)
    for chosen in pairs_of(heads):
        back_intra(
            xc_ref, c_ref, inner_ref, step_ref, cum_ref, cumex_ref, hcat_ref, hp_ref, dy_s, dxc_s, dh_s, dc_s,
            din_s, g_s, cv_s, dd_s, chosen, heads, lambda b: None,
        )
        back_states(cum_ref, hcat_ref, dh_s, tq_s, state, chosen, heads)
        back_inter(xc_ref, b_ref, step_ref, cum_ref, dxc_s, dh_s, db_s, v_s, chosen, heads, lambda b: None)
    conv_x_back(xin_ref, cx_ref, dx_act_ref, dxc_s, dxin_ref, dcx_ref, 0, chans)
    back_logs(
        b_ref, c_ref, pre_ref, step_ref, hp_ref, ddt_ref, dhp_ref, db_s, dc_s, din_s, g_s, cv_s, v_s, dd_s, tq_s, heads
    )
    conv_bc_back(bc_ref, cbc_ref, dbc_act_ref, db_s, dc_s, dbc_ref, dcbc_ref)


def call(kernel, out_shapes, scratch, flops):
    return pl.pallas_call(
        kernel,
        out_shape=[jax.ShapeDtypeStruct(shape, F32) for shape in out_shapes],
        scratch_shapes=[pltpu.VMEM(shape, F32) for shape in scratch],
        compiler_params=pltpu.CompilerParams(vmem_limit_bytes=56 * 1024 * 1024),
        cost_estimate=pl.CostEstimate(flops=flops, bytes_accessed=20_000_000, transcendentals=0),
    )


def run_fwd(proj, live, cx, cbc, hp, heads):
    tokens = proj.shape[1]
    chans, n4 = cx.shape[0], cbc.shape[0]
    blocks = tokens // SPAN
    full, half, rows = (chans, tokens), (n4 // 2, tokens), (16, tokens)
    return call(
        functools.partial(fwd_kernel, heads),
        [full, full, full, half, half, (n4, tokens), rows, rows, rows, (blocks, chans, n4 // 2), (blocks, SPAN, SPAN), full, (1, tokens)],
        [(blocks, chans, n4 // 2)],
        2_000_000_000,
    )(proj, live, cx, cbc, hp)


def run_bwd(proj, kept, don, rms, coef, og, cx, cbc, hp, heads):
    tokens = proj.shape[1]
    chans, n4 = cx.shape[0], cbc.shape[0]
    blocks = tokens // SPAN
    full, half, rows = (chans, tokens), (n4 // 2, tokens), (16, tokens)
    return call(
        functools.partial(bwd_kernel, heads),
        [proj.shape, (chans, 4), (n4, 4), (16, 3), (chans, 1)],
        [full, full, (blocks, chans, n4 // 2), half, half, (blocks, SPAN, SPAN), rows, rows, rows, rows, (blocks, 16, SPAN)],
        4_000_000_000,
    )(proj, *kept, don, rms, coef, og, cx, cbc, hp)


def square_sum(arrays):
    total = jnp.float32(0.0)
    for item in arrays:
        total = total + jnp.sum(item * item)
    return total


def pad_rows(v):
    return jnp.concatenate([v, jnp.zeros((16 - v.shape[0],) + v.shape[1:], v.dtype)], axis=0)


def local(
    hidden_in,
    out_cot,
    lengths,
    norm_gain,
    w_zx,
    w_bc,
    w_dt,
    conv_x,
    conv_bc,
    head_params,
    out_gain,
    w_out,
    left_statistic_gate,
    stat_right_zx,
    stat_left_out,
    stat_right_out,
    inverse_root_left_gate,
    inverse_root_right_gate,
    root_left_out,
    root_right_out,
):
    rows, chans = w_zx.shape[1], w_zx.shape[2]
    heads = w_dt.shape[1]
    n4 = w_bc.shape[1]
    own_rows, width = hidden_in.shape
    narrow_id, wide_id = lax.axis_index("narrow"), lax.axis_index("wide")

    full_in = lax.all_gather(hidden_in, "narrow", axis=0, tiled=True)
    full_gain = lax.all_gather(norm_gain, "narrow", axis=0, tiled=True)
    dt_cols = jnp.transpose(w_dt, (0, 2, 1)).reshape(rows, 2 * heads)
    own_w = jnp.concatenate(
        [w_zx[0], w_zx[1], w_bc, dt_cols, jnp.zeros((rows, 16 - 2 * heads), F32)], axis=1
    )
    w_in = lax.all_gather(own_w, "wide", axis=0, tiled=True)
    wide_out = lax.all_gather(w_out, "wide", axis=1, tiled=True)

    tokens = full_in.shape[0]
    live = (jnp.arange(tokens) < lengths[0]).astype(F32)
    row_start = narrow_id * own_rows
    live_own = lax.dynamic_slice_in_dim(live, row_start, own_rows, 0)
    dbranch = lax.all_gather(live_own[:, None] * out_cot, "narrow", axis=0, tiled=True)

    inv_rms = lax.rsqrt(jnp.mean(full_in * full_in, axis=-1) + 1e-05)
    normed = full_in * inv_rms[:, None] * full_gain
    proj = dot(w_in, normed, TT)
    cx, cbc = conv_x.T, conv_bc.T
    hp = jnp.concatenate(
        [
            pad_rows(head_params[0:2].reshape(2 * heads, 1)),
            pad_rows(jnp.exp(head_params[2:4]).reshape(2 * heads, 1)),
            pad_rows(head_params[4].reshape(heads, 1)),
        ],
        axis=1,
    )
    *kept, gated, squares = run_fwd(proj, live[None, :], cx, cbc, hp, heads)
    donorm = dot(wide_out, dbranch, NT)
    inner = jnp.sum(gated * (donorm * out_gain[:, None]), axis=0, keepdims=True)
    stats = lax.psum(jnp.concatenate([squares, inner], axis=0), "narrow")
    inner_total = chans * lax.axis_size("narrow")
    rms = lax.rsqrt(stats[0:1] / inner_total + 1e-05)
    coef = rms**3 * stats[1:2] / inner_total
    onorm = gated * rms * out_gain[:, None]
    branch = lax.psum_scatter(dot(onorm, wide_out, TN), "narrow", scatter_dimension=0, tiled=True)
    block_out = hidden_in + live_own[:, None] * branch
    g_out = lax.psum(dot(onorm, dbranch), "wide")

    dproj, d_cx, d_cbc, d_hp, d_og = run_bwd(
        proj, kept, donorm, rms, coef, out_gain[:, None], cx, cbc, hp, heads
    )
    d_normed = dot(dproj, w_in, TT)
    d_w = dot(normed, dproj, TT)
    dnormed = lax.psum_scatter(d_normed, "narrow", scatter_dimension=0, tiled=True)
    own_inv = lax.dynamic_slice_in_dim(inv_rms, row_start, own_rows, 0)[:, None]
    total_dot = jnp.sum(hidden_in * full_gain * dnormed, axis=1, keepdims=True)
    in_grad = out_cot + (
        own_inv * full_gain * dnormed - hidden_in * (own_inv**3 * total_dot / width)
    )
    d_gain = jnp.sum(hidden_in * own_inv * dnormed, axis=0)

    g_zx = lax.psum(d_w[:, 0 : 2 * chans], "wide")
    g_dt, g_cx, g_hp, g_og = lax.psum((d_w[:, 2 * chans + n4 :], d_cx, d_hp, d_og), "wide")
    g_bc, g_cbc, g_gain = lax.psum(
        (d_w[:, 2 * chans : 2 * chans + n4], d_cbc, d_gain), ("wide", "narrow")
    )
    shard = norm_gain.shape[0]
    g_ng = lax.dynamic_slice_in_dim(g_gain, narrow_id * shard, shard, 0)
    g_dt = jnp.transpose(g_dt[:, 0 : 2 * heads].reshape(width, 2, heads), (0, 2, 1))
    g_cx, g_cbc, g_og = g_cx.T, g_cbc.T, g_og[:, 0]
    g_head = jnp.concatenate(
        [
            g_hp[0 : 2 * heads, 0].reshape(2, heads),
            g_hp[0 : 2 * heads, 1].reshape(2, heads),
            g_hp[0:heads, 2].reshape(1, heads),
        ],
        axis=0,
    )
    local_squares = square_sum((g_zx, g_out, g_dt, g_cx, g_head, g_og, g_ng))
    total_squares = lax.psum(local_squares, "narrow") + square_sum((g_bc, g_cbc))
    clip_norm = jnp.sqrt(total_squares)
    factor = 1.0 / jnp.maximum(clip_norm, 1.0)
    c_zx, c_out, c_bc, c_dt = g_zx * factor, g_out * factor, g_bc * factor, g_dt * factor
    c_cx, c_cbc, c_head, c_og, c_ng = (
        g_cx * factor,
        g_cbc * factor,
        g_head * factor,
        g_og * factor,
        g_ng * factor,
    )
    halves = (c_zx[:, 0:chans], c_zx[:, chans:])
    own_zx = lax.dynamic_slice_in_dim(c_zx, wide_id * rows, rows, 0)
    own_halves = (own_zx[:, 0:chans], own_zx[:, chans:])
    left_zx = jnp.stack(
        [
            0.5 * left_statistic_gate[m, 0] + 0.5 * dot(own_halves[m], halves[m], NT)
            for m in range(2)
        ]
    )[:, None]
    right_zx = jnp.stack(
        [0.5 * stat_right_zx[m] + 0.5 * dot(halves[m], halves[m], TN) for m in range(2)]
    )
    new_zx = jnp.stack(
        [
            w_zx[m]
            - 0.5
            * dot(dot(inverse_root_left_gate[m, 0], halves[m]), inverse_root_right_gate[m])
            for m in range(2)
        ]
    )
    cols = w_out.shape[1]
    own_out = lax.dynamic_slice_in_dim(c_out, wide_id * cols, cols, 1)
    left_out = 0.5 * stat_left_out + 0.5 * dot(c_out, c_out, NT)
    right_out = 0.5 * stat_right_out + 0.5 * dot(own_out, c_out, TN)[None]
    new_out = w_out - 0.5 * dot(dot(root_left_out, c_out), root_right_out[0], NT)
    own_bc = lax.dynamic_slice_in_dim(c_bc, wide_id * rows, rows, 0)
    own_dt = lax.dynamic_slice_in_dim(c_dt, wide_id * rows, rows, 0)
    rate = 10.0
    return (
        block_out,
        in_grad,
        clip_norm,
        jnp.stack(own_halves),
        new_zx,
        left_zx,
        right_zx,
        own_out,
        new_out,
        left_out,
        right_out,
        own_bc,
        w_bc - rate * own_bc,
        own_dt,
        w_dt - rate * own_dt,
        c_cx,
        conv_x - rate * c_cx,
        c_cbc,
        conv_bc - rate * c_cbc,
        c_head,
        head_params - rate * c_head,
        c_og,
        out_gain - rate * c_og,
        c_ng,
        norm_gain - rate * c_ng,
    )


MESH = pl.DeviceIdType.MESH
MIB = 1024 * 1024


class Place:
    def __init__(self, wide):
        self.wide = wide
        self.depth = wide // 2
        self.w, self.n = lax.axis_index("wide"), lax.axis_index("narrow")
        self.z, self.x = self.w // 2, self.w % 2
        self.y, self.c = self.n // 2, self.n % 2
        self.core = (self.w, self.y * 2 + 1 - self.c)
        self.row = (self.w, (1 - self.y) * 2 + self.c)
        self.corner = (self.w, (1 - self.y) * 2 + 1 - self.c)
        self.across = (self.z * 2 + 1 - self.x, self.n)

    def group(self):
        return [self.core, self.row, self.corner]

    def along(self, k):
        return ((self.z + k) % self.depth) * 2 + self.x, self.n

    def others(self, k):
        return (self.w + k) % self.wide, self.n


class Links:
    def __init__(self, send, recv):
        self.send, self.recv, self.count, self.started = send, recv, 0, []

    def plan(self, src, dst, device):
        i = self.count
        self.count = i + 1
        item = pltpu.make_async_remote_copy(
            src_ref=src,
            dst_ref=dst,
            send_sem=self.send.at[i],
            recv_sem=self.recv.at[i],
            device_id=device,
            device_id_type=MESH,
        )
        self.started.append(item)
        return item

    def copy(self, src, dst, device):
        item = self.plan(src, dst, device)
        item.start()
        return item

    def release(self, items):
        for item in items:
            item.wait_send()
        self.started = [item for item in self.started if all(item is not done for done in items)]

    def drain(self):
        self.release(list(self.started))


def arrived(copies):
    for item in copies:
        item.wait_recv()


def begin(copies):
    for item in copies:
        item.start()


def greet(devices):
    barrier = pltpu.get_barrier_semaphore()
    for device in devices:
        pl.semaphore_signal(barrier, inc=1, device_id=device, device_id_type=MESH)
    return lambda: pl.semaphore_wait(barrier, len(devices))


def as_row(col):
    return jnp.transpose(jnp.broadcast_to(col, (col.shape[0], 128)))[0:1]


def as_col(row):
    return jnp.transpose(jnp.broadcast_to(row, (128, 128)))[:, 0:1]


def flat(v):
    return v.reshape(-1, v.shape[-1])


class Piece:
    def __init__(self, here, links, part, x_rx, z_rx, full, square):
        self.here, self.part, self.x_rx, self.z_rx = here, part, x_rx, z_rx
        self.full, self.square = full, square
        steps = range(1, here.depth)
        place, column = full.at[here.z, here.x], full.at[:, here.x]
        self.first = links.plan(part.at[:, 1 - here.x], x_rx, here.across)
        self.second = [
            links.plan(x_rx.at[(here.z + k) % here.depth], z_rx.at[k - 1], here.along(k)) for k in steps
        ]
        self.third = [links.plan(place, place, here.along(k)) for k in steps]
        self.fourth = links.plan(column, column, here.across)
        self.holding = [self.first]

    def start(self):
        self.first.start()

    def fold(self):
        self.first.wait_recv()
        for k in range(self.here.depth):
            self.x_rx[k] = self.x_rx[k] + self.part[k, self.here.x]
        begin(self.second)

    def own(self):
        arrived(self.second)
        total = self.x_rx[self.here.z]
        for k in range(1, self.here.depth):
            total = total + self.z_rx[k - 1]
        self.full[self.here.z, self.here.x] = total
        begin(self.third)
        self.square[...] = jnp.broadcast_to(total_square(total), self.square.shape)

    def spread(self):
        arrived(self.third)
        self.fourth.start()

    def finish(self):
        self.fourth.wait_recv()


class CrossPiece:
    def __init__(self, here, links, part, z_rx, x_rx, full, square):
        self.here, self.part, self.z_rx, self.x_rx = here, part, z_rx, x_rx
        self.full, self.square = full, square
        steps = range(1, here.depth)
        mine, pair = full.at[here.z, here.x], full.at[here.z]
        self.first = [
            links.plan(part.at[(here.z + k) % here.depth], z_rx.at[k - 1], here.along(k)) for k in steps
        ]
        self.second = links.plan(part.at[here.z, 1 - here.x], x_rx, here.across)
        self.third = links.plan(mine, mine, here.across)
        self.fourth = [links.plan(pair, pair, here.along(k)) for k in steps]
        self.holding = [*self.first, self.second]

    def start(self):
        begin(self.first)

    def fold(self):
        arrived(self.first)
        total = self.part[self.here.z]
        for k in range(1, self.here.depth):
            total = total + self.z_rx[k - 1]
        self.part[self.here.z] = total
        self.second.start()

    def own(self):
        self.second.wait_recv()
        total = self.part[self.here.z, self.here.x] + self.x_rx[...]
        self.full[self.here.z, self.here.x] = total
        self.third.start()
        self.square[...] = jnp.broadcast_to(total_square(total), self.square.shape)

    def spread(self):
        self.third.wait_recv()
        begin(self.fourth)

    def finish(self):
        arrived(self.fourth)


def total_square(v):
    return jnp.sum(jnp.sum(v * v, axis=0, keepdims=True), axis=1, keepdims=True)


def layer_kernel(
    wide,
    heads,
    shard,
    inner_total,
    length_ref,
    hidden_ref,
    cot_ref,
    gain_ref,
    w_ref,
    wout_ref,
    bcw_ref,
    dtw_ref,
    cx_in,
    cbc_in,
    hp_in,
    og_in,
    block_ref,
    grad_ref,
    gfull,
    bc_own,
    dt_own,
    sv_sum,
    norm_ref,
    hq,
    cq,
    wz_g,
    wx_g,
    wo_g,
    bc_g,
    dt_g,
    gain_g,
    dtt,
    gain_col,
    gain_row,
    turn_s,
    cx_ref,
    cbc_ref,
    hp_ref,
    og_ref,
    live_ref,
    inv_ref,
    proj,
    y_s,
    xc,
    dx_act,
    b_s,
    c_s,
    dbc_act,
    step_s,
    cum_s,
    cumex_s,
    hcat,
    inner_s,
    don,
    onorm,
    dy_s,
    dh_s,
    db_s,
    dc_s,
    din_s,
    g_s,
    cv_s,
    v_s,
    dd_s,
    tq_s,
    cols_s,
    dcbc_s,
    dhp_s,
    dog_s,
    dgain_s,
    stat_own,
    stat_g,
    part,
    x_rx,
    z_rx,
    zz_rx,
    xx_rx,
    core_rx,
    row_rx,
    gbc,
    bc_core,
    bc_row,
    bc_mine,
    bc_rx,
    gdt,
    dt_rx,
    shared_g,
    sv_g,
    norm_n,
    norm_w,
    square_s,
    hq_hi,
    hq_lo,
    wt_hi,
    wt_lo,
    send,
    recv,
    stat_send,
    stat_recv,
):
    here = Place(wide)
    links = Links(send, recv)
    w, n, z, x, y, c, depth = here.w, here.n, here.z, here.x, here.y, here.c, here.depth
    group = here.group()
    far = [here.others(k) for k in range(1, wide)]
    own_rows, width = hidden_ref.shape
    chans, tokens = y_s.shape
    state = b_s.shape[0] // 2
    blocks = tokens // SPAN
    parts = tokens // own_rows
    thirds = chans // 128
    z_ref, x_ref, bc_ref, pre_ref = pieces(proj, chans, state)
    met = greet(group + far)
    jobs = []
    crossing = (2 * thirds - 1, 2 * thirds)
    for i in range(3 * thirds):
        source = part.at[i if i < 2 * thirds else i - thirds]
        k = sum(1 for other in crossing if other < i)
        if i in crossing:
            jobs.append(CrossPiece(here, links, source, zz_rx.at[k], xx_rx.at[k], gfull.at[i], square_s.at[i]))
        else:
            jobs.append(Piece(here, links, source, x_rx.at[i - k], z_rx.at[i - k], gfull.at[i], square_s.at[i]))
    z_jobs, x_jobs, o_jobs = jobs[0:thirds], jobs[thirds : 2 * thirds], jobs[2 * thirds :]

    half = bcw_ref.shape[0] // 2
    wx_g[z, x] = w_ref[1]
    bc_g[z, x, c] = bcw_ref[pl.ds(pl.multiple_of(c * half, 8), half), :]
    dt_g[z, x] = jnp.zeros(dt_g.shape[2:], F32)
    for h in range(heads):
        for i in range(2):
            row = i * heads + h
            dt_g[z, x, row : row + 1, 0 : dtw_ref.shape[2]] = dtw_ref[h, i : i + 1, :]
    line = gain_ref[...].reshape(1, shard)
    gain_g[n] = jnp.zeros(gain_g.shape[1:], F32)
    for i in range((shard + 127) // 128):
        size = min(128, shard - 128 * i)
        gain_g[n, i : i + 1, 0:size] = line[:, 128 * i : 128 * i + size]
    squares = jnp.zeros((1, own_rows), F32)
    for i in range(width // 128):
        turned = jnp.transpose(hidden_ref[:, i * 128 : (i + 1) * 128])
        squares = squares + jnp.sum(turned * turned, axis=0, keepdims=True)
        hq[n, i * 128 : (i + 1) * 128, :] = turned
    inv_ref[...] = lax.rsqrt(squares / width + 1e-05)
    for i in range(width // 128):
        hq[n, i * 128 : (i + 1) * 128, :] = hq[n, i * 128 : (i + 1) * 128, :] * inv_ref[...]
    met()

    def along(ref):
        return [links.copy(ref, ref, here.along(k)) for k in range(1, depth)]

    def exchange(ref):
        return [links.copy(ref, ref, here.row), links.copy(ref, ref, here.core)]

    class Relay:
        def __init__(self, *views):
            self.views = views
            self.direct = [along(view(z)) for view in views]
            self.passed = []

        def begin(self):
            self.passed = [links.copy(view(z), view(z), here.across) for view in self.views]

        def forward(self, steps=tuple(range(1, depth))):
            for k in steps:
                source = (z + depth - k) % depth
                for view, copies in zip(self.views, self.direct):
                    copies[k - 1].wait_recv()
                    self.passed.append(links.copy(view(source), view(source), here.across))

        def wait(self):
            arrived(self.passed)

    split = chans - 128

    class Cross:
        def __init__(self, ref):
            self.mine, self.pair = ref.at[z, x, :, split:], ref.at[z, :, :, split:]

        def begin(self):
            self.across = links.copy(self.mine, self.mine, here.across)

        def forward(self):
            self.across.wait_recv()
            self.sent = along(self.pair)

        def wait(self):
            arrived(self.sent)

    h_copies = exchange(hq.at[n])
    gain_copies = [links.copy(gain_g.at[n], gain_g.at[n], device) for device in group]
    early = Relay(lambda i: bc_g.at[i, x, c], lambda i: dt_g.at[i, x])
    early.begin()
    first_cross, second_cross, third_cross = Cross(wx_g), Cross(wz_g), Cross(wo_g)
    first_cross.begin()
    first = Relay(lambda i: wx_g.at[i, x, :, 0:split])
    first.begin()

    wz_g[z, x] = w_ref[0]
    wo_g[z, x] = wout_ref[...]
    live_ref[...] = jnp.where(iota((1, tokens), 1) < length_ref[0], 1.0, 0.0)
    live_own = live_ref[:, pl.ds(pl.multiple_of(n * own_rows, 128), own_rows)]
    for i in range(width // 128):
        cq[n, i * 128 : (i + 1) * 128, :] = jnp.transpose(cot_ref[:, i * 128 : (i + 1) * 128]) * live_own
    turn_s[...] = jnp.zeros_like(turn_s)
    for ref, out in ((cx_in, cx_ref), (cbc_in, cbc_ref)):
        for i in range(ref.shape[1] // 128):
            turn_s[0:4, :] = ref[:, i * 128 : (i + 1) * 128]
            out[i * 128 : (i + 1) * 128, :] = jnp.transpose(turn_s[...])[:, 0:4]
    turn_s[...] = jnp.zeros_like(turn_s)
    turn_s[0:1, 0:heads] = hp_in[0:1, :]
    turn_s[0:1, heads : 2 * heads] = hp_in[1:2, :]
    turn_s[1:2, 0:heads] = jnp.exp(hp_in[2:3, :])
    turn_s[1:2, heads : 2 * heads] = jnp.exp(hp_in[3:4, :])
    turn_s[2:3, 0:heads] = hp_in[4:5, :]
    hp_ref[...] = jnp.transpose(turn_s[...])[0:16, 0:3]
    og_line = og_in[...].reshape(1, chans)
    for i in range(thirds):
        og_ref[i * 128 : (i + 1) * 128, :] = as_col(og_line[:, i * 128 : (i + 1) * 128])
    cols_s[...] = jnp.zeros_like(cols_s)
    dcbc_s[...] = jnp.zeros_like(dcbc_s)
    dhp_s[...] = jnp.zeros_like(dhp_s)

    def cut(q):
        hq_hi[q], hq_lo[q] = halves(hq[q])

    cut(n)
    h_copies[1].wait_recv()
    cut(here.core[1])
    first_cross.forward()
    early.forward()
    first.forward()
    second_cross.begin()
    second = Relay(lambda i: wz_g.at[i, x, :, 0:split])
    h_copies[0].wait_recv()
    other = here.row[1]
    h_far = links.copy(hq.at[other], hq.at[other], here.core)
    c_copies = exchange(cq.at[n])
    arrived(gain_copies)
    for q in range(parts):
        turned = jnp.transpose(jnp.concatenate([gain_g[q], jnp.zeros((120, 128), F32)], axis=0))
        for i in range((shard + 127) // 128):
            size = min(128, shard - 128 * i)
            start = shard * q + 128 * i
            gain_col[start : start + size, :] = turned[0:size, i : i + 1]
    for i in range(width // 128):
        gain_row[:, i * 128 : (i + 1) * 128] = as_row(gain_col[i * 128 : (i + 1) * 128, :])

    def turn(ref, row, scale=True):
        for i in range(ref.shape[-1] // 128):
            cols = flat(ref[..., i * 128 : (i + 1) * 128])
            if scale:
                cols = cols * gain_col[...]
            for dst, value in zip((wt_hi, wt_lo), halves(jnp.transpose(cols))):
                dst[row + i * 128 : row + (i + 1) * 128, :] = value

    def quarter(q):
        return pl.ds(pl.multiple_of(q * own_rows, 128), own_rows)

    def each_quarter(body):
        def step(q, _):
            body(q)
            return 0

        lax.fori_loop(0, parts, step, 0)

    def rows_of(start, stop):
        return wt_hi[start:stop, :], wt_lo[start:stop, :]

    def project(out_ref, weights):
        def body(q):
            out_ref[:, quarter(q)] = product(weights(), (hq_hi[q], hq_lo[q]))

        each_quarter(body)

    early.wait()
    bc_core_copy = links.copy(bc_g.at[:, :, c], bc_g.at[:, :, c], here.core)
    lanes = width // wide
    for i in range(wide):
        dtt[:, i * lanes : (i + 1) * lanes] = dt_g[i // 2, i % 2][:, 0:lanes]
    last = 2 * chans + 4 * state
    wt_hi[last:, :], wt_lo[last:, :] = halves(dtt[...] * gain_row[...])
    bc_core_copy.wait_recv()
    turn(bc_g, 2 * chans)
    first.wait()
    first_cross.wait()
    second.begin()
    second.forward((1,))
    second_cross.forward()
    turn(wx_g, chans)
    second.forward((2,))
    h_far.wait_recv()
    cut(here.row[1])
    cut(here.corner[1])
    project(proj.at[chans:], lambda: rows_of(chans, last + 16))
    second.forward((3,))
    third_cross.begin()
    third = Relay(lambda i: wo_g.at[i, x, :, 0:split])
    third.begin()
    c_copies[0].wait_recv()
    c_far = links.copy(cq.at[other], cq.at[other], here.core)
    convolve(x_ref, bc_ref, live_ref, cx_ref, cbc_ref, xc, dx_act, b_s, c_s, dbc_act)
    step_sizes(pre_ref, hp_ref, step_s, cum_s, cumex_s, heads)
    states(xc, b_s, step_s, cum_s, dh_s, hcat, heads)
    second.wait()
    second_cross.wait()
    turn(wz_g, 0)
    project(z_ref, lambda: rows_of(0, chans))
    third.forward()
    third_cross.forward()

    def stat_copy(j, b):
        return pltpu.make_async_remote_copy(
            src_ref=stat_own.at[b],
            dst_ref=stat_g.at[n, b],
            send_sem=stat_send.at[j, b],
            recv_sem=stat_recv.at[j, b],
            device_id=group[j],
            device_id_type=MESH,
        )

    def tell(b, row):
        stats = jnp.broadcast_to(row, (8, SPAN))
        stat_own[b] = stats
        stat_g[n, b] = stats
        for j in range(3):
            stat_copy(j, b).start()

    def told(b):
        for j in range(3):
            stat_copy(j, b).wait_recv()
        total = stat_g[0, b]
        for q in range(1, parts):
            total = total + stat_g[q, b]
        return total[0:1]

    def emit(b, sl, h, rows, gated, sums):
        onorm[rows, sl] = gated
        row = jnp.sum(gated * gated, axis=0, keepdims=True)
        row = row if sums is None else row + sums
        if h == heads - 1:
            tell(b, row)
        return row

    outputs(z_ref, xc, b_s, c_s, step_s, cum_s, cumex_s, hcat, hp_ref, y_s, inner_s, heads, emit)
    rms = jnp.concatenate(
        [lax.rsqrt(told(b) / inner_total + 1e-05) for b in range(blocks)], axis=1
    )

    def scale_rows(i, _):
        rows = pl.ds(pl.multiple_of(i * 8, 8), 8)
        onorm[rows, :] = onorm[rows, :] * rms * og_ref[rows, :]
        return 0

    lax.fori_loop(0, chans // 8, scale_rows, 0, unroll=2)
    c_copies[1].wait_recv()
    c_far.wait_recv()

    def weight_grad(put, right, left=lambda q: (hq_hi[q], hq_lo[q])):
        def body(q):
            put(q, product(left(q), halves(right(q)), NT))

        each_quarter(body)

    block_shape = part.shape[1:]

    def add_to(start, count):
        def put(q, value):
            for i in range(count):
                ref = part.at[start + i]
                piece = value[:, i * 128 : (i + 1) * 128].reshape(block_shape)
                ref[...] = jnp.where(q == 0, piece, ref[...] + piece)

        return put

    def scaled(i):
        part[i] = (flat(part[i]) * gain_col[...]).reshape(block_shape)

    part[...] = jnp.zeros_like(part)
    for start, stop in ((0, 1), (1, thirds)):
        rows = slice(start * 128, stop * 128)
        weight_grad(
            add_to(thirds + start, stop - start),
            lambda q, rows=rows: onorm[rows, quarter(q)],
            lambda q: halves(cq[q]),
        )
        for job in o_jobs[start:stop]:
            job.start()
    third.wait()
    third_cross.wait()
    turn(wo_g, 0, False)

    def donorm(q):
        don[:, quarter(q)] = product(rows_of(0, chans), halves(cq[q]))

    each_quarter(donorm)

    def inner_sums(b, _):
        sl = pl.ds(pl.multiple_of(b * SPAN, SPAN), SPAN)
        gate = z_ref[:, sl]
        gated = y_s[:, sl] * (gate * sigmoid(gate))
        tell(blocks + b, jnp.sum(gated * (don[:, sl] * og_ref[...]), axis=0, keepdims=True))
        return 0

    lax.fori_loop(0, blocks, inner_sums, 0)

    links.release(c_copies + [c_far])

    class Return:
        def __init__(self, rx, row_rx, compute, steps=((), (), (), ())):
            self.rx, self.row_rx = rx, row_rx
            first = links.count
            self.cores = [links.plan(cq.at[k * 2 + 1 - c], rx.at[k], here.core) for k in range(2)]
            self.last = links.plan(rx.at[1 - y], row_rx, here.row)

            def body(k, _):
                q = (k % 2) * 2 + (c + 1 + k // 2) % 2
                cq[q] = compute(q)

                @pl.when(k < 2)
                def _():
                    pltpu.make_async_remote_copy(
                        src_ref=cq.at[q],
                        dst_ref=rx.at[k % 2],
                        send_sem=links.send.at[first + k % 2],
                        recv_sem=links.recv.at[first + k % 2],
                        device_id=here.core,
                        device_id_type=MESH,
                    ).start()

                for at, items in enumerate(steps):

                    @pl.when(k == at)
                    def _(items=items):
                        for step in items:
                            step()

                return 0

            lax.fori_loop(0, 4, body, 0)

        def fold(self):
            arrived(self.cores)
            for k in range(2):
                self.rx[k] = self.rx[k] + cq[k * 2 + c]
            self.last.start()

        def total(self):
            self.last.wait_recv()
            return self.rx[y] + self.row_rx[...]

    o0, o1, o2 = o_jobs
    z0, z1, z2 = z_jobs
    x0, x1, x2 = x_jobs
    branch = Return(core_rx.at[0], row_rx.at[0], lambda q: dot3(flat(wo_g[...]), onorm[:, quarter(q)]))
    told_inner = jnp.concatenate([told(blocks + b) for b in range(blocks)], axis=1)
    coef = rms**3 * told_inner / inner_total
    gate_back(z_ref, y_s, don, rms, coef, og_ref, dy_s, z_ref, dog_s)
    o0.fold()
    o1.fold()
    weight_grad(add_to(0, thirds), lambda q: z_ref[:, quarter(q)])
    for i, job in enumerate(z_jobs):
        scaled(i)
        job.start()

    def x_grad(i):
        links.release(o_jobs[i].holding)
        part[thirds + i] = jnp.zeros(block_shape, F32)
        weight_grad(add_to(thirds + i, 1), lambda q: x_ref[i * 128 : (i + 1) * 128, quarter(q)])
        scaled(thirds + i)

    within = [
        {3: [o2.fold, o1.own], 5: [o0.own]},
        {1: [o1.spread], 3: [branch.fold], 5: [o2.spread, z1.fold]},
        {5: [z0.spread]},
    ]
    between = [{7: [o2.own]}, {3: [z0.own]}, {}]
    after_states = [(), (), (x0.fold, z2.own)]
    after_conv = [(z0.fold,), (), ()]
    after_grad = [(), (z2.fold, z1.own, o0.spread), (z1.spread,)]

    def run(steps):
        for step in steps:
            step()

    def ticks(plan):
        def tick(b):
            for at, steps in plan.items():

                @pl.when(b == at)
                def _(steps=steps):
                    for step in steps:
                        step()

        return tick

    for i, chosen in enumerate(pairs_of(heads)):
        back_intra(
            xc, c_s, inner_s, step_s, cum_s, cumex_s, hcat, hp_ref, dy_s, y_s, dh_s, dc_s,
            din_s, g_s, cv_s, dd_s, chosen, heads, ticks(within[i]),
        )
        back_states(cum_s, hcat, dh_s, tq_s, state, chosen, heads)
        run(after_states[i])
        back_inter(xc, b_s, step_s, cum_s, y_s, dh_s, db_s, v_s, chosen, heads, ticks(between[i]))
        conv_x_back(x_ref, cx_ref, dx_act, y_s, x_ref, cols_s, i * 128, 128)
        run(after_conv[i])
        x_grad(i)
        x_jobs[i].start()
        run(after_grad[i])

    back_logs(
        b_s, c_s, pre_ref, step_s, hp_ref, pre_ref, dhp_s, db_s, dc_s, din_s, g_s, cv_s, v_s, dd_s, tq_s, heads
    )
    conv_bc_back(bc_ref, cbc_ref, dbc_act, db_s, dc_s, bc_ref, dcbc_s)
    gbc_shape = gbc.shape

    def add_bc(q, value):
        gbc[...] = jnp.where(q == 0, value.reshape(gbc_shape), gbc[...] + value.reshape(gbc_shape))

    gbc[...] = jnp.zeros_like(gbc)
    weight_grad(add_bc, lambda q: bc_ref[:, quarter(q)])
    gbc[...] = (flat(gbc[...]) * gain_col[...]).reshape(gbc_shape)
    bc_first = links.copy(gbc.at[:, :, 1 - c], bc_core, here.core)
    dt_grad = jnp.zeros((16, width), F32)
    for q in range(parts):
        step = halves(pre_ref[:, q * own_rows : (q + 1) * own_rows])
        dt_grad = dt_grad + product(step, (hq_hi[q], hq_lo[q]), NT)
    dt_grad = dt_grad * gain_row[...]
    gdt[...] = jnp.zeros_like(gdt)
    for i in range(wide):
        gdt[i, :, 0:lanes] = dt_grad[:, i * lanes : (i + 1) * lanes]
    dt_rx[w] = gdt[w]
    dt_copies = [links.copy(gdt.at[device[0]], dt_rx.at[w], device) for device in far]
    dgain_s[...] = jnp.zeros_like(dgain_s)
    bc_first.wait_recv()
    for k in range(2):
        bc_core[:, k] = bc_core[:, k] + gbc[:, k, c]
    for k in range(wide):
        bc_mine[k] = bc_core[k, 1 - y]
    bc_second = links.copy(bc_mine, bc_row, here.row)

    links.release(branch.cores)

    for k in range(parts):
        pieces_of = []
        for ref, start in ((wz_g, 0), (wx_g, chans), (bc_g, 2 * chans)):
            a, b = max(k * own_rows, start), min((k + 1) * own_rows, start + ref.shape[-1])
            if a < b:
                pieces_of.append(flat(ref[..., a - start : b - start]))
        hq_hi[k], hq_lo[k] = halves(jnp.concatenate(pieces_of, axis=1))

    def normed_back(q):
        sl = quarter(q)

        def add(k, value):
            rows = pl.ds(pl.multiple_of(k * own_rows, 8), own_rows)
            return value + product((hq_hi[k], hq_lo[k]), halves(proj[rows, sl]))

        value = lax.fori_loop(0, parts, add, dot3(dtt[...], pre_ref[:, sl], TN))
        dgain_s[...] = dgain_s[...] + jnp.sum(value * hq[q], axis=1, keepdims=True)
        return value

    back = Return(core_rx.at[1], row_rx.at[1], normed_back, ([], [x0.own], [], [x1.fold, z2.spread]))
    back.fold()
    small = 128
    shared_g[n] = jnp.zeros(shared_g.shape[1:], F32)
    for i in range(4 * state // 128):
        sl = slice(i * 128, (i + 1) * 128)
        shared_g[n, 0:4, sl] = jnp.transpose(dcbc_s[sl, :])[0:4]
    for i in range(width // 128):
        shared_g[n, 8 + i : 9 + i, 0:128] = as_row(dgain_s[i * 128 : (i + 1) * 128, :])
    shared_copies = [links.copy(shared_g.at[n], shared_g.at[n], device) for device in group]
    bc_second.wait_recv()
    links.release([bc_second])
    for k in range(wide):
        bc_mine[k] = bc_core[k, y] + bc_row[k]
    bc_rx[w] = bc_mine[w]
    bc_copies = [links.copy(bc_mine.at[device[0]], bc_rx.at[w], device) for device in far]
    sv_g[w] = jnp.zeros(sv_g.shape[1:], F32)
    for i in range(thirds):
        sl = slice(i * 128, (i + 1) * 128)
        sv_g[w, 0:4, sl] = jnp.transpose(cols_s[sl, :])[0:4]
        sv_g[w, 4:5, sl] = as_row(dog_s[sl, :])
    sv_g[w, :, chans : chans + small] = dhp_s[...]
    x2.fold()
    arrived(shared_copies)
    total = shared_g[0]
    for q in range(1, parts):
        total = total + shared_g[q]
    sv_g[w, :, chans + small :] = total
    sv_copies = [links.copy(sv_g.at[w], sv_g.at[w], device) for device in far]

    x0.spread()
    x1.own()
    arrived(bc_copies)
    own = bc_rx[0]
    for k in range(1, wide):
        own = own + bc_rx[k]
    bc_own[n] = own
    bc_group = [links.copy(bc_own.at[n], bc_own.at[n], device) for device in group]
    squares = total_square(own)
    arrived(dt_copies)
    own = dt_rx[0]
    for k in range(1, wide):
        own = own + dt_rx[k]
    dt_own[...] = own
    squares = squares + total_square(own)
    arrived(sv_copies)
    own = sv_g[0]
    for k in range(1, wide):
        own = own + sv_g[k]
    sv_sum[...] = own
    x2.own()
    for i in range(3 * thirds):
        squares = squares + square_s[i][:, 0:1]
    once = jnp.where(w == 0, 1.0, 0.0)
    squares = squares + once * total_square(own[:, 0 : chans + small])
    squares = squares + jnp.where(n == 0, once, 0.0) * total_square(own[:, chans + small :])
    norm_n[n] = jnp.broadcast_to(squares, (8, 128))
    norm_copies = [links.copy(norm_n.at[n], norm_n.at[n], device) for device in group]

    x1.spread()

    block = branch.total() * live_ref[:, pl.ds(pl.multiple_of(n * own_rows, 128), own_rows)]
    for i in range(width // 128):
        sl = slice(i * 128, (i + 1) * 128)
        block_ref[:, sl] = hidden_ref[:, sl] + jnp.transpose(block[sl, :])
    arrived(norm_copies)
    norm_w[w] = norm_n[0] + norm_n[1] + norm_n[2] + norm_n[3]
    wide_copies = [links.copy(norm_w.at[w], norm_w.at[w], device) for device in far]
    x2.spread()
    dn = back.total() * gain_col[...]
    dots = jnp.sum(dn * hq[n], axis=0, keepdims=True) / width
    for i in range(width // 128):
        sl = slice(i * 128, (i + 1) * 128)
        value = inv_ref[...] * (dn[sl] - hq[n, sl, :] * dots)
        grad_ref[:, sl] = cot_ref[:, sl] + jnp.transpose(value)
    arrived(wide_copies)
    total = norm_w[0]
    for k in range(1, wide):
        total = total + norm_w[k]
    norm_ref[...] = jnp.sqrt(total)
    for job in jobs:
        job.finish()
    arrived(bc_group)
    links.drain()

    def sent(b, _):
        for j in range(3):
            stat_copy(j, b).wait_send()
        return 0

    lax.fori_loop(0, 2 * blocks, sent, 0)


def run_layer(lengths, hidden, cot, gain, w_zx, w_out, w_bc, dtw, cx, cbc, hp, og, heads, shard, wide, narrow):
    own_rows, width = hidden.shape
    tokens = own_rows * narrow
    chans, n4 = cx.shape[1], cbc.shape[1]
    rows = w_zx.shape[1]
    depth, blocks, half, thirds = wide // 2, tokens // SPAN, n4 // 2, chans // 128
    full, bc2, small = (chans, tokens), (half, tokens), (16, tokens)
    quarters = (narrow, width, own_rows)
    weights = (depth, 2, rows, chans)
    piece = (3 * thirds, depth, 2, rows, 128)
    quarter = (width // wide // 4, n4)
    sums = (16, chans + 128 + 256)
    shapes = [
        hidden.shape,
        hidden.shape,
        piece,
        (4,) + quarter,
        (16, 128),
        sums,
        (8, 128),
    ]
    scratch = [
        quarters,
        quarters,
        weights,
        weights,
        weights,
        (depth, 2, 2, rows // 2, n4),
        (depth, 2, 16, 128),
        (narrow, 8, 128),
        (16, width),
        (width, 1),
        (1, width),
        (128, 128),
        (chans, 4),
        (n4, 4),
        (16, 3),
        (chans, 1),
        (1, tokens),
        (1, own_rows),
        (2 * chans + n4 + 16, tokens),
        full,
        full,
        full,
        bc2,
        bc2,
        (n4, tokens),
        small,
        small,
        small,
        (blocks, chans, half),
        (blocks, SPAN, SPAN),
        full,
        full,
        full,
        (blocks, chans, half),
        bc2,
        bc2,
        (blocks, SPAN, SPAN),
        small,
        small,
        small,
        small,
        (blocks, 16, SPAN),
        (chans, 128),
        (n4, 128),
        (16, 128),
        (chans, 1),
        (width, 1),
        (2 * blocks, 8, 128),
        (narrow, 2 * blocks, 8, 128),
        (2 * thirds,) + piece[1:],
        (3 * thirds - 2, depth, rows, 128),
        (3 * thirds - 2, depth - 1, rows, 128),
        (2, depth - 1, 2, rows, 128),
        (2, rows, 128),
        (2, 2, width, own_rows),
        (2, width, own_rows),
        (wide, 2, 2) + quarter,
        (wide, 2) + quarter,
        (wide,) + quarter,
        (wide,) + quarter,
        (wide,) + quarter,
        (wide, 16, 128),
        (wide, 16, 128),
        (narrow, 16, 256),
        (wide,) + sums,
        (narrow, 8, 128),
        (wide, 8, 128),
        (3 * thirds, 1, 128),
    ]
    lows = [quarters] * 2 + [(2 * chans + n4 + 16, width)] * 2
    copies = 200
    operands = (lengths, hidden, cot, gain, w_zx, w_out, w_bc, dtw, cx, cbc, hp, og)
    return pl.pallas_call(
        functools.partial(layer_kernel, wide, heads, shard, chans * narrow),
        out_shape=[jax.ShapeDtypeStruct(shape, F32) for shape in shapes],
        in_specs=[pl.BlockSpec(memory_space=pltpu.SMEM)]
        + [pl.BlockSpec(memory_space=pltpu.VMEM)] * (len(operands) - 1),
        scratch_shapes=[pltpu.VMEM(shape, F32) for shape in scratch]
        + [pltpu.VMEM(shape, jnp.bfloat16) for shape in lows]
        + [
            pltpu.SemaphoreType.DMA((copies,)),
            pltpu.SemaphoreType.DMA((copies,)),
            pltpu.SemaphoreType.DMA((3, 2 * blocks)),
            pltpu.SemaphoreType.DMA((3, 2 * blocks)),
        ],
        compiler_params=pltpu.CompilerParams(
            vmem_limit_bytes=62 * MIB, collective_id=0, has_side_effects=True
        ),
        cost_estimate=pl.CostEstimate(flops=20_000_000_000, bytes_accessed=20_000_000, transcendentals=0),
    )(*operands)


def finish_kernel(
    wide,
    narrow,
    gfull,
    bc_own,
    dt_own,
    sv,
    norm_ref,
    block_in,
    grad_in,
    stat_l,
    stat_r,
    stat_lo,
    stat_ro,
    root_l,
    root_r,
    root_lo,
    root_ro,
    w_ref,
    wout_ref,
    bcw_ref,
    dtw_ref,
    cx_ref,
    cbc_ref,
    hp_ref,
    og_ref,
    gain_ref,
    block_out,
    in_grad,
    clip,
    g_zx,
    new_zx,
    new_l,
    new_r,
    g_out,
    new_out,
    new_lo,
    new_ro,
    g_bc,
    new_bc,
    g_dt,
    new_dt,
    g_cx,
    new_cx,
    g_cbc,
    new_cbc,
    g_hp,
    new_hp,
    g_og,
    new_og,
    g_ng,
    new_ng,
    g_s,
    l_s,
    r_s,
    lo_s,
    ro_s,
    rl_s,
    rr_s,
    rlo_s,
    rro_s,
    in_sem,
    out_sem,
):
    rate = 10.0
    chans = w_ref.shape[2]
    thirds = chans // 128
    place = lax.axis_index("wide")
    z, x = place // 2, place % 2
    factor = 1.0 / jnp.maximum(norm_ref[0:1, 0:1], 1.0)
    fetches, results = [], []

    def fetch(src, dst):
        item = pltpu.make_async_copy(src, dst, in_sem.at[len(fetches)])
        item.start()
        fetches.append(item)
        return item

    def result(src, dst):
        item = pltpu.make_async_copy(src, dst, out_sem.at[len(results)])
        item.start()
        results.append(item)

    waits = []
    for m in (2, 0, 1):
        gs = g_s.at[m * thirds : (m + 1) * thirds]
        whole_m = fetch(gfull.at[m * thirds : (m + 1) * thirds], gs)
        if m == 2:
            others = [(root_ro, rro_s), (root_lo, rlo_s), (stat_ro, ro_s), (stat_lo, lo_s)]
        else:
            others = [(root_l.at[m], rl_s.at[m]), (root_r.at[m], rr_s.at[m])]
            others += [(stat_l.at[m], l_s.at[m]), (stat_r.at[m], r_s.at[m])]
        waits.append([whole_m] + [fetch(*pair) for pair in others])
    block_out[...] = block_in[...]
    in_grad[...] = grad_in[...]
    clip[...] = norm_ref[0:1, 0:1]

    def both(m):
        for item in waits[(1, 2, 0)[m]]:
            item.wait()
        parts = [flat(g_s[m * thirds + i]) for i in range(thirds)]
        mine = [g_s[m * thirds + i, z, x] for i in range(thirds)]
        return jnp.concatenate(mine, axis=1) * factor, halves(jnp.concatenate(parts, axis=1) * factor)

    own, full = both(2)
    g_out[...] = own
    ro_s[...] = 0.5 * ro_s[...] + 0.5 * product(halves(own), full, NT)
    result(ro_s, new_ro)
    lo_s[...] = 0.5 * lo_s[...] + 0.5 * product(full, full, TN)
    result(lo_s, new_lo)
    new_out[...] = wout_ref[...] - 0.5 * dot3(product(halves(rro_s[...]), full), rlo_s[...], NT)
    for m in range(2):
        own, full = both(m)
        g_zx[m] = own
        l_s[m] = 0.5 * l_s[m] + 0.5 * product(halves(own), full, NT)
        result(l_s.at[m], new_l.at[m])
        r_s[m] = 0.5 * r_s[m] + 0.5 * product(full, full, TN)
        result(r_s.at[m], new_r.at[m])
        new_zx[m] = w_ref[m] - 0.5 * dot3(product(halves(rl_s[m]), full), rr_s[m])

    grad = flat(bc_own[...]) * factor
    g_bc[...] = grad
    new_bc[...] = bcw_ref[...] - rate * grad
    heads, _, rows = dtw_ref.shape
    for h in range(heads):
        for i in range(2):
            row = i * heads + h
            grad = dt_own[row : row + 1, 0:rows] * factor
            g_dt[h, i : i + 1, :] = grad
            new_dt[h, i : i + 1, :] = dtw_ref[h, i : i + 1, :] - rate * grad
    sums = sv[...] * factor
    grad = sums[0:4, 0:chans]
    g_cx[...] = grad
    new_cx[...] = cx_ref[...] - rate * grad
    grad = sums[4:5, 0:chans]
    g_og[...] = grad.reshape(chans)
    new_og[...] = og_ref[...] - rate * g_og[...]
    n4 = cbc_ref.shape[1]
    last = chans + 128
    grad = sums[0:4, last : last + n4]
    g_cbc[...] = grad
    new_cbc[...] = cbc_ref[...] - rate * grad
    turned = jnp.transpose(
        jnp.concatenate([sums[:, chans:last], jnp.zeros((112, 128), F32)], axis=0)
    )
    for i, (row, start) in enumerate(((0, 0), (0, heads), (1, 0), (1, heads), (2, 0))):
        grad = turned[row : row + 1, start : start + heads]
        g_hp[i : i + 1, :] = grad
        new_hp[i : i + 1, :] = hp_ref[i : i + 1, :] - rate * grad
    shard = gain_ref.shape[0]
    count = narrow * shard // 128
    line = jnp.concatenate([sums[8 + i : 9 + i, last : last + 128] for i in range(count)], axis=1)
    grad = jnp.zeros((1, shard), F32)
    for q in range(narrow):
        piece = line[:, q * shard : (q + 1) * shard]
        grad = jnp.where(lax.axis_index("narrow") == q, piece, grad)
    g_ng[...] = grad.reshape(shard)
    new_ng[...] = gain_ref[...] - rate * g_ng[...]
    for item in results:
        item.wait()


def run_finish(partials, stats, roots, params, tokens_shape, wide, narrow):
    stat_l, stat_r, stat_lo, stat_ro = stats
    w_zx, w_out, w_bc, w_dt, cx, cbc, hp, og, gain = params
    like = [w_zx, w_zx, stat_l, stat_r, w_out, w_out, stat_lo, stat_ro]
    like += [item for item in (w_bc, w_dt, cx, cbc, hp, og, gain) for _ in range(2)]
    shapes = [tokens_shape, tokens_shape, (1, 1)] + [item.shape for item in like]
    far, near = pl.BlockSpec(memory_space=pl.ANY), pl.BlockSpec(memory_space=pltpu.VMEM)
    gfull = partials[0]
    kept = [gfull, stat_l, stat_r, stat_lo, stat_ro, *roots]
    return pl.pallas_call(
        functools.partial(finish_kernel, wide, narrow),
        out_shape=[jax.ShapeDtypeStruct(shape, F32) for shape in shapes],
        in_specs=[far] + [near] * 6 + [far] * 8 + [near] * len(params),
        out_specs=[near] * 5 + [far] * 2 + [near] * 2 + [far] * 2 + [near] * (len(shapes) - 11),
        scratch_shapes=[pltpu.VMEM(item.shape, F32) for item in kept]
        + [pltpu.SemaphoreType.DMA((15,)), pltpu.SemaphoreType.DMA((6,))],
        compiler_params=pltpu.CompilerParams(vmem_limit_bytes=56 * MIB),
        cost_estimate=pl.CostEstimate(flops=4_000_000_000, bytes_accessed=20_000_000, transcendentals=0),
    )(*partials, *stats, *roots, *params)


def fast_local(
    wide,
    narrow,
    hidden_in,
    out_cot,
    lengths,
    norm_gain,
    w_zx,
    w_bc,
    w_dt,
    conv_x,
    conv_bc,
    head_params,
    out_gain,
    w_out,
    left_statistic_gate,
    stat_right_zx,
    stat_left_out,
    stat_right_out,
    inverse_root_left_gate,
    inverse_root_right_gate,
    root_left_out,
    root_right_out,
):
    heads, shard = w_dt.shape[1], norm_gain.shape[0]
    out_rows, dt_rows = w_out.T, jnp.transpose(w_dt, (1, 2, 0))
    block, grad, *partials = run_layer(
        lengths,
        hidden_in,
        out_cot,
        norm_gain,
        w_zx,
        out_rows,
        w_bc,
        dt_rows,
        conv_x,
        conv_bc,
        head_params,
        out_gain,
        heads,
        shard,
        wide,
        narrow,
    )
    (
        block_out,
        in_grad,
        clip,
        g_zx,
        new_zx,
        new_l,
        new_r,
        g_out,
        new_out,
        new_lo,
        new_ro,
        g_bc,
        new_bc,
        g_dt,
        new_dt,
        *rest,
    ) = run_finish(
        (*partials, block, grad),
        (left_statistic_gate[:, 0], stat_right_zx, stat_left_out, stat_right_out[0]),
        (inverse_root_left_gate[:, 0], inverse_root_right_gate, root_left_out, root_right_out[0]),
        (w_zx, out_rows, w_bc, dt_rows, conv_x, conv_bc, head_params, out_gain, norm_gain),
        hidden_in.shape,
        wide,
        narrow,
    )
    return (
        block_out,
        in_grad,
        clip.reshape(()),
        g_zx,
        new_zx,
        new_l[:, None],
        new_r,
        g_out.T,
        new_out.T,
        new_lo,
        new_ro[None],
        g_bc,
        new_bc,
        jnp.transpose(g_dt, (2, 0, 1)),
        jnp.transpose(new_dt, (2, 0, 1)),
        *rest,
    )


def solution(mesh):
    wide, narrow = mesh.shape["wide"], mesh.shape["narrow"]
    body = functools.partial(fast_local, wide, narrow) if (wide, narrow) == (8, 4) else local
    return jax.shard_map(
        body,
        mesh=mesh,
        in_specs=(
            P(("wide", "narrow"), None),
            P(("wide", "narrow"), None),
            P("wide"),
            P("narrow"),
            P(None, "wide", "narrow"),
            P("wide", None),
            P("wide", "narrow", None),
            P(None, "narrow"),
            P(),
            P(None, "narrow"),
            P("narrow"),
            P("narrow", "wide"),
            P(None, "narrow", "wide", None),
            P(None, "narrow", None),
            P("narrow", None),
            P("narrow", "wide", None),
            P(None, "narrow", "wide", None),
            P(None, "narrow", None),
            P("narrow", None),
            P("narrow", "wide", None),
        ),
        out_specs=(
            P(("wide", "narrow"), None),
            P(("wide", "narrow"), None),
            P(),
            P(None, "wide", "narrow"),
            P(None, "wide", "narrow"),
            P(None, "narrow", "wide", None),
            P(None, "narrow", None),
            P("narrow", "wide"),
            P("narrow", "wide"),
            P("narrow", None),
            P("narrow", "wide", None),
            P("wide", None),
            P("wide", None),
            P("wide", "narrow", None),
            P("wide", "narrow", None),
            P(None, "narrow"),
            P(None, "narrow"),
            P(),
            P(),
            P(None, "narrow"),
            P(None, "narrow"),
            P("narrow"),
            P("narrow"),
            P("narrow"),
            P("narrow"),
        ),
        check_vma=False,
    )
```

```python
import functools

import jax
import jax.numpy as jnp
from jax import lax
from jax.experimental import pallas as pl
from jax.experimental.pallas import tpu as pltpu
from jax.sharding import PartitionSpec as P

SPAN = 128
WIDTH = 64
HIGH = lax.Precision.HIGH
F32 = jnp.float32
NN = (((1,), (0,)), ((), ()))
NT = (((1,), (1,)), ((), ()))
TN = (((0,), (0,)), ((), ()))
TT = (((0,), (1,)), ((), ()))


def dot(a, b, dims=NN):
    return lax.dot_general(a, b, dims, precision=HIGH, preferred_element_type=F32)


def halves(v):
    hi = v.astype(jnp.bfloat16)
    return hi, (v - hi.astype(F32)).astype(jnp.bfloat16)


def product(a, b, dims=NN):
    (ah, al), (bh, bl) = a, b
    (left,), (right,) = dims[0]
    rows, depth = ah.shape[1 - left], ah.shape[left]

    def times(u, v):
        return lax.dot_general(u, v, dims, preferred_element_type=F32)

    if depth < 128:
        return times(
            jnp.concatenate([ah, al, ah], axis=left), jnp.concatenate([bh, bh, bl], axis=right)
        )
    if depth == 128:
        top = jnp.concatenate([ah, ah], axis=left)
        low = jnp.concatenate([al, jnp.zeros_like(al)], axis=left)
        out = times(jnp.concatenate([top, low], axis=1 - left), jnp.concatenate([bh, bl], axis=right))
        return out[0:rows] + out[rows:]
    out = times(jnp.concatenate([ah, al], axis=1 - left), bh)
    return out[0:rows] + out[rows:] + times(ah, bl)


def dot3(a, b, dims=NN):
    return product(halves(a), halves(b), dims)


def sigmoid(v):
    return 1.0 / (1.0 + jnp.exp(-v))


def split3(v):
    hi = v.astype(jnp.bfloat16)
    rest = v - hi.astype(F32)
    mid = rest.astype(jnp.bfloat16)
    lo = (rest - mid.astype(F32)).astype(jnp.bfloat16)
    return jnp.concatenate([hi, mid, lo], axis=0)


def exact_dot(v, ones):
    rows = v.shape[0]
    out = lax.dot_general(split3(v), ones, NN, preferred_element_type=F32)
    return out[0:rows] + out[rows : 2 * rows] + out[2 * rows : 3 * rows]


def iota(shape, axis):
    return lax.broadcasted_iota(jnp.int32, shape, axis)


def shift_right(v, count):
    return jnp.where(iota(v.shape, 1) >= count, pltpu.roll(v, count, axis=1), 0.0)


def shift_left(v, count):
    length = v.shape[1]
    return jnp.where(iota(v.shape, 1) < length - count, pltpu.roll(v, length - count, axis=1), 0.0)


def conv_rows(v, taps):
    count = taps.shape[1]
    total = taps[:, count - 1 : count] * v
    for j in range(count - 1):
        total = total + taps[:, j : j + 1] * shift_right(v, count - 1 - j)
    return total


def pieces(ref, chans, state):
    bc = 2 * chans
    dt = bc + 4 * state
    return ref.at[0:chans], ref.at[chans:bc], ref.at[bc:dt], ref.at[dt : dt + 16]


def convolve(x_ref, bc_ref, live_ref, cx_ref, cbc_ref, xc_ref, dx_act_ref, b_ref, c_ref, dbc_act_ref):
    chans, tokens = xc_ref.shape
    state = c_ref.shape[0] // 2
    live = live_ref[...]

    def conv_x_rows(i, _):
        rows = pl.ds(pl.multiple_of(i * 8, 8), 8)
        u = conv_rows(x_ref[rows, :], cx_ref[rows, :])
        s = sigmoid(u)
        xc_ref[rows, :] = u * s * live
        dx_act_ref[rows, :] = (s + u * s * (1.0 - s)) * live
        return 0

    lax.fori_loop(0, chans // 8, conv_x_rows, 0, unroll=2)

    def conv_bc_rows(i, _, src, dst, dst_row, shift):
        rows = pl.ds(pl.multiple_of(src * state + i * 8, 8), 8)
        out = pl.ds(pl.multiple_of(dst_row + i * 8, 8), 8)
        u = conv_rows(bc_ref[rows, :], cbc_ref[rows, :])
        s = sigmoid(u)
        dbc_act_ref[rows, :] = s + u * s * (1.0 - s)
        v = u * s
        if shift == 1:
            v = shift_right(v, 1)
        if shift == -1:
            v = shift_left(v, 1)
        dst[out, :] = v
        return 0

    for src, dst, row, shift in ((0, b_ref, 0, 0), (1, c_ref, 0, 1), (2, b_ref, state, 0), (3, c_ref, state, -1)):
        lax.fori_loop(
            0,
            state // 8,
            functools.partial(conv_bc_rows, src=src, dst=dst, dst_row=row, shift=shift),
            0,
            unroll=2,
        )


def step_sizes(pre_ref, hp_ref, step_ref, cum_ref, cumex_ref, heads):
    blocks = pre_ref.shape[1] // SPAN
    pre = pre_ref[...] + hp_ref[:, 0:1]
    steps = jnp.maximum(pre, 0.0) + jnp.log1p(jnp.exp(-jnp.abs(pre)))
    step_ref[...] = steps
    logs = -hp_ref[:, 1:2] * steps
    rows16 = iota((16, SPAN), 0)
    lane16 = iota((16, SPAN), 1)
    row_q = iota((SPAN, SPAN), 0)
    lane_q = iota((SPAN, SPAN), 1)
    upto = (row_q <= lane_q).astype(F32).astype(jnp.bfloat16)
    downto = (row_q >= lane_q).astype(F32).astype(jnp.bfloat16)
    both = jnp.concatenate([upto, downto], axis=1)
    for b in range(blocks):
        sums = exact_dot(logs[:, b * SPAN : (b + 1) * SPAN], both)
        cum = jnp.where(rows16 < heads, sums[:, 0:SPAN], sums[:, SPAN : 2 * SPAN])
        ex_f = jnp.where(lane16 >= 1, pltpu.roll(cum, 1, axis=1), 0.0)
        ex_r = jnp.where(lane16 < SPAN - 1, pltpu.roll(cum, SPAN - 1, axis=1), 0.0)
        cum_ref[:, b * SPAN : (b + 1) * SPAN] = cum
        cumex_ref[:, b * SPAN : (b + 1) * SPAN] = jnp.where(rows16 < heads, ex_f, ex_r)


def states(xc_ref, b_ref, step_ref, cum_ref, sloc_ref, hcat_ref, heads):
    blocks = xc_ref.shape[1] // SPAN
    state = b_ref.shape[0] // 2

    def local_states(b, _):
        sl = pl.ds(pl.multiple_of(b * SPAN, SPAN), SPAN)
        bcat = spread(b_ref[:, sl], state)
        tail = tails(cum_ref[:, sl], step_ref[:, sl], heads)
        left = tailed(xc_ref[:, sl], tail, range(heads), heads)
        sloc_ref[b] = dot3(left, bcat, NT)
        return 0

    lax.fori_loop(0, blocks, local_states, 0)

    lane_h = iota((WIDTH, 2 * state), 1)
    for h in range(heads):
        rows = slice(h * WIDTH, (h + 1) * WIDTH)
        carry = jnp.zeros((WIDTH, 2 * state), F32)
        for i in range(blocks):
            r = blocks - 1 - i
            hcat_ref[i, rows, 0:state] = carry[:, 0:state]
            hcat_ref[r, rows, state : 2 * state] = carry[:, state : 2 * state]
            tot_f = jnp.exp(cum_ref[h : h + 1, (i + 1) * SPAN - 1 : (i + 1) * SPAN])
            tot_r = jnp.exp(cum_ref[heads + h : heads + h + 1, r * SPAN : r * SPAN + 1])
            factor = jnp.where(lane_h < state, tot_f, tot_r)
            piece = jnp.where(lane_h < state, sloc_ref[i, rows, :], sloc_ref[r, rows, :])
            carry = carry * factor + piece


def outputs(z_ref, xc_ref, b_ref, c_ref, step_ref, cum_ref, cumex_ref, hcat_ref, hp_ref, y_ref, inner_ref, heads, emit):
    blocks = xc_ref.shape[1] // SPAN
    state = b_ref.shape[0] // 2
    row_q = iota((SPAN, SPAN), 0)
    lane_q = iota((SPAN, SPAN), 1)
    lower = row_q < lane_q
    diag = row_q == lane_q

    def block(b, _):
        sl = pl.ds(pl.multiple_of(b * SPAN, SPAN), SPAN)
        bb, cc = b_ref[:, sl], c_ref[:, sl]
        inner = jnp.where(
            lower, dot3(bb[0:state], cc[0:state], TN), dot3(bb[state:], cc[state:], TN)
        )
        inner_ref[b] = inner
        cum, steps, cumex = cum_ref[:, sl], step_ref[:, sl], cumex_ref[:, sl]
        scale = jnp.exp(cumex)
        cols = columns(cum, steps)
        sums = None
        entering = dot3(hcat_ref[b], spread(cc, state))
        x_parts = halves(xc_ref[:, sl])
        for h in range(heads):
            rows = slice(h * WIDTH, (h + 1) * WIDTH)
            decay = decays(cols, cumex, lower, diag, h, heads)
            mt = jnp.where(diag, hp_ref[h : h + 1, 2:3], inner * decay)
            y = product((x_parts[0][rows], x_parts[1][rows]), halves(mt))
            y = y + entering[rows, 0:SPAN] * scale[h : h + 1]
            y = y + entering[rows, SPAN:] * scale[heads + h : heads + h + 1]
            z = z_ref[rows, sl]
            y_ref[rows, sl] = y
            sums = emit(b, sl, h, rows, y * (z * sigmoid(z)), sums)
        return 0

    lax.fori_loop(0, blocks, block, 0)


def fwd_kernel(
    heads,
    proj_ref,
    live_ref,
    cx_ref,
    cbc_ref,
    hp_ref,
    y_ref,
    xc_ref,
    dx_act_ref,
    b_ref,
    c_ref,
    dbc_act_ref,
    step_ref,
    cum_ref,
    cumex_ref,
    hcat_ref,
    inner_ref,
    gated_ref,
    sq_ref,
    sloc_ref,
):
    z_ref, x_ref, bc_ref, pre_ref = pieces(proj_ref, xc_ref.shape[0], c_ref.shape[0] // 2)
    convolve(x_ref, bc_ref, live_ref, cx_ref, cbc_ref, xc_ref, dx_act_ref, b_ref, c_ref, dbc_act_ref)
    step_sizes(pre_ref, hp_ref, step_ref, cum_ref, cumex_ref, heads)
    states(xc_ref, b_ref, step_ref, cum_ref, sloc_ref, hcat_ref, heads)

    def emit(b, sl, h, rows, gated, total):
        gated_ref[rows, sl] = gated
        part = jnp.sum(gated * gated, axis=0, keepdims=True)
        total = part if total is None else total + part
        if h == heads - 1:
            sq_ref[:, sl] = total
        return total

    outputs(z_ref, xc_ref, b_ref, c_ref, step_ref, cum_ref, cumex_ref, hcat_ref, hp_ref, y_ref, inner_ref, heads, emit)


def spread(bb, state):
    zero = jnp.zeros((state, SPAN), F32)
    top = jnp.concatenate([bb[0:state], zero], axis=1)
    low = jnp.concatenate([zero, bb[state:]], axis=1)
    return jnp.concatenate([top, low], axis=0)


def tails(cum, steps, heads):
    rows = iota((16, SPAN), 0)
    last = jnp.where(rows[:, 0:1] < heads, cum[:, SPAN - 1 : SPAN], cum[:, 0:1])
    return jnp.exp(last - cum) * steps


def tailed(xc, tail, chosen, heads):
    parts = []
    for i, h in enumerate(chosen):
        x = xc[i * WIDTH : (i + 1) * WIDTH]
        parts.append(
            jnp.concatenate([x * tail[h : h + 1], x * tail[heads + h : heads + h + 1]], axis=1)
        )
    return jnp.concatenate(parts, axis=0)


def columns(cum, steps):
    pad = jnp.zeros((SPAN - 32, SPAN), F32)
    return jnp.transpose(jnp.concatenate([cum, steps, pad], axis=0))


def decays(cols, cumex, lower, diag, h, heads):
    f, r = h, heads + h
    arg = jnp.where(
        lower, cumex[f : f + 1] - cols[:, f : f + 1], cumex[r : r + 1] - cols[:, r : r + 1]
    )
    step = jnp.where(lower, cols[:, 16 + f : 17 + f], cols[:, 16 + r : 17 + r])
    return jnp.where(diag, 0.0, jnp.exp(arg) * step)


def gate_back(z_ref, y_ref, don_ref, rms, coef, og_ref, dy_ref, dz_ref, dog_ref, onorm_ref=None):
    chans = y_ref.shape[0]

    def gate_rows(i, _):
        rows = pl.ds(pl.multiple_of(i * 8, 8), 8)
        z, y, don, og = z_ref[rows, :], y_ref[rows, :], don_ref[rows, :], og_ref[rows, :]
        s = sigmoid(z)
        act = z * s
        gated = y * act
        normed = rms * don
        dog_ref[rows, 0:1] = jnp.sum(gated * normed, axis=1, keepdims=True)
        dgated = normed * og - gated * coef
        dy_ref[rows, :] = dgated * act
        dz_ref[rows, :] = dgated * y * (s + act * (1.0 - s))
        if onorm_ref is not None:
            onorm_ref[rows, :] = gated * rms * og
        return 0

    lax.fori_loop(0, chans // 8, gate_rows, 0, unroll=2)


def back_intra(xc_ref, c_ref, inner_ref, step_ref, cum_ref, cumex_ref, hcat_ref, hp_ref, dy_s, dxc_s, dh_s, dc_s, din_s, g_s, cv_s, dd_s, chosen, heads, tick):
    blocks = xc_ref.shape[1] // SPAN
    state = c_ref.shape[0] // 2
    lower = iota((SPAN, SPAN), 0) < iota((SPAN, SPAN), 1)
    diag = iota((SPAN, SPAN), 0) == iota((SPAN, SPAN), 1)
    first = chosen[0] == 0

    def block(b, put):
        sl = pl.ds(pl.multiple_of(b * SPAN, SPAN), SPAN)
        cc = c_ref[:, sl]
        inner = inner_ref[b]
        cumex = cumex_ref[:, sl]
        scale = jnp.exp(cumex)
        cols = columns(cum_ref[:, sl], step_ref[:, sl])
        dinner = jnp.zeros((SPAN, SPAN), F32) if first else din_s[b]
        dcc = jnp.zeros((2 * state, SPAN), F32) if first else dc_s[:, sl]
        for h in chosen:
            f, r = h, heads + h
            rows = slice(h * WIDTH, (h + 1) * WIDTH)
            decay = decays(cols, cumex, lower, diag, h, heads)
            mt = inner * decay
            e_f, e_r = scale[f : f + 1], scale[r : r + 1]
            ce = jnp.concatenate([cc[0:state] * e_f, cc[state:] * e_r], axis=0)
            x = xc_ref[rows, sl]
            dy = dy_s[rows, sl]
            dy_parts = halves(dy)
            left = jnp.concatenate([x, hcat_ref[b, rows, :]], axis=1)
            back = product(halves(left), dy_parts, TN)
            dmt, dce = back[0:SPAN], back[SPAN:]
            dinner = dinner + dmt * decay
            w = dmt * mt
            over_f = jnp.sum(jnp.where(lower, w, 0.0), axis=0, keepdims=True)
            over_r = jnp.sum(jnp.where(lower, 0.0, w), axis=0, keepdims=True)
            prod = dce * ce
            put(g_s, (slice(f, f + 1), sl), over_f + jnp.sum(prod[0:state], axis=0, keepdims=True))
            put(g_s, (slice(r, r + 1), sl), over_r + jnp.sum(prod[state:], axis=0, keepdims=True))
            dcc = dcc + jnp.concatenate([dce[0:state] * e_f, dce[state:] * e_r], axis=0)
            right = jnp.concatenate(
                [jnp.where(lower, mt, 0.0), jnp.where(lower, 0.0, mt), ce], axis=0
            )
            out = product(dy_parts, halves(right), NT)
            dx_f, dx_r = out[:, 0:SPAN], out[:, SPAN : 2 * SPAN]
            put(dh_s, (b, rows, slice(None)), out[:, 2 * SPAN :])
            put(cv_s, (slice(f, f + 1), sl), jnp.sum(x * dx_f, axis=0, keepdims=True))
            put(cv_s, (slice(r, r + 1), sl), jnp.sum(x * dx_r, axis=0, keepdims=True))
            put(dd_s, (slice(h, h + 1), sl), jnp.sum(x * dy, axis=0, keepdims=True))
            put(dxc_s, (rows, sl), dx_f + dx_r + hp_ref[h : h + 1, 2:3] * dy)
        put(din_s, (b,), dinner)
        put(dc_s, (slice(None), sl), dcc)

    two_at_a_time(blocks, block, tick)


def two_at_a_time(blocks, block, tick):
    def body(i, _):
        stores = []
        for b in (2 * i, 2 * i + 1):
            block(b, lambda ref, at, value: stores.append((ref, at, value)))
        for ref, at, value in stores:
            ref[at] = value
        tick(2 * i)
        tick(2 * i + 1)
        return 0

    lax.fori_loop(0, blocks // 2, body, 0)


def back_states(cum_ref, hcat_ref, dh_s, tq_s, state, chosen, heads):
    blocks = hcat_ref.shape[0]
    lane_h = iota((WIDTH, 2 * state), 1)
    lane_1 = iota((1, 2 * state), 1)
    for h in chosen:
        rows = slice(h * WIDTH, (h + 1) * WIDTH)
        carry = jnp.zeros((WIDTH, 2 * state), F32)
        for i in range(blocks):
            f = blocks - 1 - i
            tot_f = jnp.exp(cum_ref[h : h + 1, (f + 1) * SPAN - 1 : (f + 1) * SPAN])
            tot_r = jnp.exp(cum_ref[heads + h : heads + h + 1, i * SPAN : i * SPAN + 1])
            factor = jnp.where(lane_h < state, tot_f, tot_r)
            direct = jnp.where(lane_h < state, dh_s[f, rows, :], dh_s[i, rows, :])
            kept = jnp.where(lane_h < state, hcat_ref[f, rows, :], hcat_ref[i, rows, :])
            scaled = carry * factor
            dots = jnp.sum(scaled * kept, axis=0, keepdims=True)
            q_f = jnp.sum(jnp.where(lane_1 < state, dots, 0.0), axis=1, keepdims=True)
            q_r = jnp.sum(jnp.where(lane_1 < state, 0.0, dots), axis=1, keepdims=True)
            tq_s[f, h : h + 1, :] = jnp.broadcast_to(q_f, (1, SPAN))
            tq_s[i, heads + h : heads + h + 1, :] = jnp.broadcast_to(q_r, (1, SPAN))
            dh_s[f, rows, 0:state] = carry[:, 0:state]
            dh_s[i, rows, state:] = carry[:, state:]
            carry = scaled + direct


def back_inter(xc_ref, b_ref, step_ref, cum_ref, dxc_s, dh_s, db_s, v_s, chosen, heads, tick):
    blocks = xc_ref.shape[1] // SPAN
    state = b_ref.shape[0] // 2
    first = chosen[0] == 0
    group = slice(chosen[0] * WIDTH, (chosen[-1] + 1) * WIDTH)

    def block(b, put):
        sl = pl.ds(pl.multiple_of(b * SPAN, SPAN), SPAN)
        bcat = spread(b_ref[:, sl], state)
        tail = tails(cum_ref[:, sl], step_ref[:, sl], heads)
        xc = xc_ref[group, sl]
        dxc = dxc_s[group, sl]
        dsl = halves(dh_s[b, group, :])
        dleft = product(dsl, halves(bcat))
        dbs = product(dsl, halves(tailed(xc, tail, chosen, heads)), TN)
        db = jnp.concatenate([dbs[0:state, 0:SPAN], dbs[state:, SPAN:]], axis=0)
        put(db_s, (slice(None), sl), db if first else db_s[:, sl] + db)
        parts = []
        for i, h in enumerate(chosen):
            f, r = h, heads + h
            part = slice(i * WIDTH, (i + 1) * WIDTH)
            tx_f = dleft[part, 0:SPAN] * tail[f : f + 1]
            tx_r = dleft[part, SPAN:] * tail[r : r + 1]
            put(v_s, (slice(f, f + 1), sl), jnp.sum(xc[part] * tx_f, axis=0, keepdims=True))
            put(v_s, (slice(r, r + 1), sl), jnp.sum(xc[part] * tx_r, axis=0, keepdims=True))
            parts.append(dxc[part] + tx_f + tx_r)
        put(dxc_s, (group, sl), jnp.concatenate(parts, axis=0))

    two_at_a_time(blocks, block, tick)


def back_logs(b_ref, c_ref, pre_ref, step_ref, hp_ref, ddt_ref, dhp_ref, db_s, dc_s, din_s, g_s, cv_s, v_s, dd_s, tq_s, heads):
    blocks = pre_ref.shape[1] // SPAN
    state = b_ref.shape[0] // 2
    row_q = iota((SPAN, SPAN), 0)
    lane_q = iota((SPAN, SPAN), 1)
    lower = row_q < lane_q
    strict = (row_q > lane_q).astype(F32)
    weak = (row_q >= lane_q).astype(F32)
    strict_t = (row_q < lane_q).astype(F32)
    weak_t = (row_q <= lane_q).astype(F32)
    tri = jnp.concatenate(
        [
            jnp.concatenate([strict, strict_t], axis=1),
            jnp.concatenate([weak, weak_t], axis=1),
            jnp.concatenate([strict_t, strict], axis=1),
        ],
        axis=0,
    ).astype(jnp.bfloat16)
    rows16 = iota((16, SPAN), 0)
    used = rows16 < 2 * heads
    rate = hp_ref[:, 1:2]

    def block(b, carry):
        bias_sum, log_sum, skip_sum = carry
        sl = pl.ds(pl.multiple_of(b * SPAN, SPAN), SPAN)
        dinner = din_s[b]
        both = jnp.concatenate(
            [jnp.where(lower, dinner, 0.0), jnp.where(lower, 0.0, dinner)], axis=0
        )
        dc_s[:, sl] = dc_s[:, sl] + dot3(spread(b_ref[:, sl], state), both)
        db = dot3(c_ref[:, sl], both, NT)
        db_s[0:state, sl] = db_s[0:state, sl] + db[0:state, 0:SPAN]
        db_s[state:, sl] = db_s[state:, sl] + db[state:, SPAN:]
        g = jnp.where(used, g_s[:, sl], 0.0)
        c = jnp.where(used, cv_s[:, sl], 0.0)
        v = jnp.where(used, v_s[:, sl], 0.0)
        steps = step_ref[:, sl]
        sums = exact_dot(jnp.concatenate([g, -c, v], axis=1), tri)
        dlog = jnp.where(rows16 < heads, sums[:, 0:SPAN], sums[:, SPAN:])
        dlog = dlog + jnp.where(used, tq_s[b], 0.0)
        pre = pre_ref[:, sl] + hp_ref[:, 0:1]
        small = steps < 1e-30
        ratio = jnp.where(small, 1.0, sigmoid(pre) / jnp.where(small, 1.0, steps))
        dpre = (c + v) * ratio - rate * dlog * sigmoid(pre)
        ddt_ref[:, sl] = dpre
        skip = jnp.where(rows16 < heads, dd_s[:, sl], 0.0)
        return bias_sum + dpre, log_sum - rate * dlog * steps, skip_sum + skip

    zeros16 = jnp.zeros((16, SPAN), F32)
    bias_sum, log_sum, skip = lax.fori_loop(0, blocks, block, (zeros16, zeros16, zeros16))
    dhp_ref[:, 0:1] = jnp.sum(bias_sum, axis=1, keepdims=True)
    dhp_ref[:, 1:2] = jnp.sum(log_sum, axis=1, keepdims=True)
    dhp_ref[:, 2:3] = jnp.sum(skip, axis=1, keepdims=True)


def conv_back(du, v, taps):
    count = taps.shape[1]
    dv = taps[:, count - 1 : count] * du
    sums = [jnp.sum(du * v, axis=1, keepdims=True)]
    for j in range(count - 2, -1, -1):
        moved = shift_left(du, count - 1 - j)
        dv = dv + taps[:, j : j + 1] * moved
        sums.append(jnp.sum(moved * v, axis=1, keepdims=True))
    return dv, sums[::-1]


def conv_x_back(xin_ref, cx_ref, dx_act_ref, dxc_s, dxin_ref, dcx_ref, start, count):
    def group(i, _):
        rows = pl.ds(pl.multiple_of(start + i * 8, 8), 8)
        dv, sums = conv_back(dxc_s[rows, :] * dx_act_ref[rows, :], xin_ref[rows, :], cx_ref[rows, :])
        dxin_ref[rows, :] = dv
        for j, item in enumerate(sums):
            dcx_ref[rows, j : j + 1] = item
        return 0

    lax.fori_loop(0, count // 8, group, 0, unroll=2)


def conv_bc_back(bc_ref, cbc_ref, dbc_act_ref, db_s, dc_s, dbc_ref, dcbc_ref):
    state = db_s.shape[0] // 2

    def group(i, _, src, grad, grad_row, shift):
        rows = pl.ds(pl.multiple_of(src * state + i * 8, 8), 8)
        from_rows = pl.ds(pl.multiple_of(grad_row + i * 8, 8), 8)
        d = grad[from_rows, :]
        if shift == 1:
            d = shift_left(d, 1)
        if shift == -1:
            d = shift_right(d, 1)
        dv, sums = conv_back(d * dbc_act_ref[rows, :], bc_ref[rows, :], cbc_ref[rows, :])
        dbc_ref[rows, :] = dv
        for j, item in enumerate(sums):
            dcbc_ref[rows, j : j + 1] = item
        return 0

    for src, grad, row, shift in ((0, db_s, 0, 0), (1, dc_s, 0, 1), (2, db_s, state, 0), (3, dc_s, state, -1)):
        lax.fori_loop(
            0,
            state // 8,
            functools.partial(group, src=src, grad=grad, grad_row=row, shift=shift),
            0,
            unroll=2,
        )


def pairs_of(heads):
    return [tuple(range(h, min(h + 2, heads))) for h in range(0, heads, 2)]


def bwd_kernel(
    heads,
    proj_ref,
    y_ref,
    xc_ref,
    dx_act_ref,
    b_ref,
    c_ref,
    dbc_act_ref,
    step_ref,
    cum_ref,
    cumex_ref,
    hcat_ref,
    inner_ref,
    don_ref,
    rms_ref,
    coef_ref,
    og_ref,
    cx_ref,
    cbc_ref,
    hp_ref,
    dproj_ref,
    dcx_ref,
    dcbc_ref,
    dhp_ref,
    dog_ref,
    dy_s,
    dxc_s,
    dh_s,
    db_s,
    dc_s,
    din_s,
    g_s,
    cv_s,
    v_s,
    dd_s,
    tq_s,
):
    chans, state = y_ref.shape[0], b_ref.shape[0] // 2
    z_ref, xin_ref, bc_ref, pre_ref = pieces(proj_ref, chans, state)
    dz_ref, dxin_ref, dbc_ref, ddt_ref = pieces(dproj_ref, chans, state)
    gate_back(z_ref, y_ref, don_ref, rms_ref[...], coef_ref[...], og_ref, dy_s, dz_ref, dog_ref)
    for chosen in pairs_of(heads):
        back_intra(
            xc_ref, c_ref, inner_ref, step_ref, cum_ref, cumex_ref, hcat_ref, hp_ref, dy_s, dxc_s, dh_s, dc_s,
            din_s, g_s, cv_s, dd_s, chosen, heads, lambda b: None,
        )
        back_states(cum_ref, hcat_ref, dh_s, tq_s, state, chosen, heads)
        back_inter(xc_ref, b_ref, step_ref, cum_ref, dxc_s, dh_s, db_s, v_s, chosen, heads, lambda b: None)
    conv_x_back(xin_ref, cx_ref, dx_act_ref, dxc_s, dxin_ref, dcx_ref, 0, chans)
    back_logs(
        b_ref, c_ref, pre_ref, step_ref, hp_ref, ddt_ref, dhp_ref, db_s, dc_s, din_s, g_s, cv_s, v_s, dd_s, tq_s, heads
    )
    conv_bc_back(bc_ref, cbc_ref, dbc_act_ref, db_s, dc_s, dbc_ref, dcbc_ref)


def call(kernel, out_shapes, scratch, flops):
    return pl.pallas_call(
        kernel,
        out_shape=[jax.ShapeDtypeStruct(shape, F32) for shape in out_shapes],
        scratch_shapes=[pltpu.VMEM(shape, F32) for shape in scratch],
        compiler_params=pltpu.CompilerParams(vmem_limit_bytes=56 * 1024 * 1024),
        cost_estimate=pl.CostEstimate(flops=flops, bytes_accessed=20_000_000, transcendentals=0),
    )


def run_fwd(proj, live, cx, cbc, hp, heads):
    tokens = proj.shape[1]
    chans, n4 = cx.shape[0], cbc.shape[0]
    blocks = tokens // SPAN
    full, half, rows = (chans, tokens), (n4 // 2, tokens), (16, tokens)
    return call(
        functools.partial(fwd_kernel, heads),
        [full, full, full, half, half, (n4, tokens), rows, rows, rows, (blocks, chans, n4 // 2), (blocks, SPAN, SPAN), full, (1, tokens)],
        [(blocks, chans, n4 // 2)],
        2_000_000_000,
    )(proj, live, cx, cbc, hp)


def run_bwd(proj, kept, don, rms, coef, og, cx, cbc, hp, heads):
    tokens = proj.shape[1]
    chans, n4 = cx.shape[0], cbc.shape[0]
    blocks = tokens // SPAN
    full, half, rows = (chans, tokens), (n4 // 2, tokens), (16, tokens)
    return call(
        functools.partial(bwd_kernel, heads),
        [proj.shape, (chans, 4), (n4, 4), (16, 3), (chans, 1)],
        [full, full, (blocks, chans, n4 // 2), half, half, (blocks, SPAN, SPAN), rows, rows, rows, rows, (blocks, 16, SPAN)],
        4_000_000_000,
    )(proj, *kept, don, rms, coef, og, cx, cbc, hp)


def square_sum(arrays):
    total = jnp.float32(0.0)
    for item in arrays:
        total = total + jnp.sum(item * item)
    return total


def pad_rows(v):
    return jnp.concatenate([v, jnp.zeros((16 - v.shape[0],) + v.shape[1:], v.dtype)], axis=0)


def local(
    hidden_in,
    out_cot,
    lengths,
    norm_gain,
    w_zx,
    w_bc,
    w_dt,
    conv_x,
    conv_bc,
    head_params,
    out_gain,
    w_out,
    left_statistic_gate,
    stat_right_zx,
    stat_left_out,
    stat_right_out,
    inverse_root_left_gate,
    inverse_root_right_gate,
    root_left_out,
    root_right_out,
):
    rows, chans = w_zx.shape[1], w_zx.shape[2]
    heads = w_dt.shape[1]
    n4 = w_bc.shape[1]
    own_rows, width = hidden_in.shape
    narrow_id, wide_id = lax.axis_index("narrow"), lax.axis_index("wide")

    full_in = lax.all_gather(hidden_in, "narrow", axis=0, tiled=True)
    full_gain = lax.all_gather(norm_gain, "narrow", axis=0, tiled=True)
    dt_cols = jnp.transpose(w_dt, (0, 2, 1)).reshape(rows, 2 * heads)
    own_w = jnp.concatenate(
        [w_zx[0], w_zx[1], w_bc, dt_cols, jnp.zeros((rows, 16 - 2 * heads), F32)], axis=1
    )
    w_in = lax.all_gather(own_w, "wide", axis=0, tiled=True)
    wide_out = lax.all_gather(w_out, "wide", axis=1, tiled=True)

    tokens = full_in.shape[0]
    live = (jnp.arange(tokens) < lengths[0]).astype(F32)
    row_start = narrow_id * own_rows
    live_own = lax.dynamic_slice_in_dim(live, row_start, own_rows, 0)
    dbranch = lax.all_gather(live_own[:, None] * out_cot, "narrow", axis=0, tiled=True)

    inv_rms = lax.rsqrt(jnp.mean(full_in * full_in, axis=-1) + 1e-05)
    normed = full_in * inv_rms[:, None] * full_gain
    proj = dot(w_in, normed, TT)
    cx, cbc = conv_x.T, conv_bc.T
    hp = jnp.concatenate(
        [
            pad_rows(head_params[0:2].reshape(2 * heads, 1)),
            pad_rows(jnp.exp(head_params[2:4]).reshape(2 * heads, 1)),
            pad_rows(head_params[4].reshape(heads, 1)),
        ],
        axis=1,
    )
    *kept, gated, squares = run_fwd(proj, live[None, :], cx, cbc, hp, heads)
    donorm = dot(wide_out, dbranch, NT)
    inner = jnp.sum(gated * (donorm * out_gain[:, None]), axis=0, keepdims=True)
    stats = lax.psum(jnp.concatenate([squares, inner], axis=0), "narrow")
    inner_total = chans * lax.axis_size("narrow")
    rms = lax.rsqrt(stats[0:1] / inner_total + 1e-05)
    coef = rms**3 * stats[1:2] / inner_total
    onorm = gated * rms * out_gain[:, None]
    branch = lax.psum_scatter(dot(onorm, wide_out, TN), "narrow", scatter_dimension=0, tiled=True)
    block_out = hidden_in + live_own[:, None] * branch
    g_out = lax.psum(dot(onorm, dbranch), "wide")

    dproj, d_cx, d_cbc, d_hp, d_og = run_bwd(
        proj, kept, donorm, rms, coef, out_gain[:, None], cx, cbc, hp, heads
    )
    d_normed = dot(dproj, w_in, TT)
    d_w = dot(normed, dproj, TT)
    dnormed = lax.psum_scatter(d_normed, "narrow", scatter_dimension=0, tiled=True)
    own_inv = lax.dynamic_slice_in_dim(inv_rms, row_start, own_rows, 0)[:, None]
    total_dot = jnp.sum(hidden_in * full_gain * dnormed, axis=1, keepdims=True)
    in_grad = out_cot + (
        own_inv * full_gain * dnormed - hidden_in * (own_inv**3 * total_dot / width)
    )
    d_gain = jnp.sum(hidden_in * own_inv * dnormed, axis=0)

    g_zx = lax.psum(d_w[:, 0 : 2 * chans], "wide")
    g_dt, g_cx, g_hp, g_og = lax.psum((d_w[:, 2 * chans + n4 :], d_cx, d_hp, d_og), "wide")
    g_bc, g_cbc, g_gain = lax.psum(
        (d_w[:, 2 * chans : 2 * chans + n4], d_cbc, d_gain), ("wide", "narrow")
    )
    shard = norm_gain.shape[0]
    g_ng = lax.dynamic_slice_in_dim(g_gain, narrow_id * shard, shard, 0)
    g_dt = jnp.transpose(g_dt[:, 0 : 2 * heads].reshape(width, 2, heads), (0, 2, 1))
    g_cx, g_cbc, g_og = g_cx.T, g_cbc.T, g_og[:, 0]
    g_head = jnp.concatenate(
        [
            g_hp[0 : 2 * heads, 0].reshape(2, heads),
            g_hp[0 : 2 * heads, 1].reshape(2, heads),
            g_hp[0:heads, 2].reshape(1, heads),
        ],
        axis=0,
    )
    local_squares = square_sum((g_zx, g_out, g_dt, g_cx, g_head, g_og, g_ng))
    total_squares = lax.psum(local_squares, "narrow") + square_sum((g_bc, g_cbc))
    clip_norm = jnp.sqrt(total_squares)
    factor = 1.0 / jnp.maximum(clip_norm, 1.0)
    c_zx, c_out, c_bc, c_dt = g_zx * factor, g_out * factor, g_bc * factor, g_dt * factor
    c_cx, c_cbc, c_head, c_og, c_ng = (
        g_cx * factor,
        g_cbc * factor,
        g_head * factor,
        g_og * factor,
        g_ng * factor,
    )
    halves = (c_zx[:, 0:chans], c_zx[:, chans:])
    own_zx = lax.dynamic_slice_in_dim(c_zx, wide_id * rows, rows, 0)
    own_halves = (own_zx[:, 0:chans], own_zx[:, chans:])
    left_zx = jnp.stack(
        [
            0.5 * left_statistic_gate[m, 0] + 0.5 * dot(own_halves[m], halves[m], NT)
            for m in range(2)
        ]
    )[:, None]
    right_zx = jnp.stack(
        [0.5 * stat_right_zx[m] + 0.5 * dot(halves[m], halves[m], TN) for m in range(2)]
    )
    new_zx = jnp.stack(
        [
            w_zx[m]
            - 0.5
            * dot(dot(inverse_root_left_gate[m, 0], halves[m]), inverse_root_right_gate[m])
            for m in range(2)
        ]
    )
    cols = w_out.shape[1]
    own_out = lax.dynamic_slice_in_dim(c_out, wide_id * cols, cols, 1)
    left_out = 0.5 * stat_left_out + 0.5 * dot(c_out, c_out, NT)
    right_out = 0.5 * stat_right_out + 0.5 * dot(own_out, c_out, TN)[None]
    new_out = w_out - 0.5 * dot(dot(root_left_out, c_out), root_right_out[0], NT)
    own_bc = lax.dynamic_slice_in_dim(c_bc, wide_id * rows, rows, 0)
    own_dt = lax.dynamic_slice_in_dim(c_dt, wide_id * rows, rows, 0)
    rate = 10.0
    return (
        block_out,
        in_grad,
        clip_norm,
        jnp.stack(own_halves),
        new_zx,
        left_zx,
        right_zx,
        own_out,
        new_out,
        left_out,
        right_out,
        own_bc,
        w_bc - rate * own_bc,
        own_dt,
        w_dt - rate * own_dt,
        c_cx,
        conv_x - rate * c_cx,
        c_cbc,
        conv_bc - rate * c_cbc,
        c_head,
        head_params - rate * c_head,
        c_og,
        out_gain - rate * c_og,
        c_ng,
        norm_gain - rate * c_ng,
    )


MESH = pl.DeviceIdType.MESH
MIB = 1024 * 1024


class Place:
    def __init__(self, wide):
        self.wide = wide
        self.depth = wide // 2
        self.w, self.n = lax.axis_index("wide"), lax.axis_index("narrow")
        self.z, self.x = self.w // 2, self.w % 2
        self.y, self.c = self.n // 2, self.n % 2
        self.core = (self.w, self.y * 2 + 1 - self.c)
        self.row = (self.w, (1 - self.y) * 2 + self.c)
        self.corner = (self.w, (1 - self.y) * 2 + 1 - self.c)
        self.across = (self.z * 2 + 1 - self.x, self.n)

    def group(self):
        return [self.core, self.row, self.corner]

    def along(self, k):
        return ((self.z + k) % self.depth) * 2 + self.x, self.n

    def others(self, k):
        return (self.w + k) % self.wide, self.n


class Links:
    def __init__(self, send, recv):
        self.send, self.recv, self.count, self.started = send, recv, 0, []

    def plan(self, src, dst, device):
        i = self.count
        self.count = i + 1
        item = pltpu.make_async_remote_copy(
            src_ref=src,
            dst_ref=dst,
            send_sem=self.send.at[i],
            recv_sem=self.recv.at[i],
            device_id=device,
            device_id_type=MESH,
        )
        self.started.append(item)
        return item

    def copy(self, src, dst, device):
        item = self.plan(src, dst, device)
        item.start()
        return item

    def release(self, items):
        for item in items:
            item.wait_send()
        self.started = [item for item in self.started if all(item is not done for done in items)]

    def drain(self):
        self.release(list(self.started))


def arrived(copies):
    for item in copies:
        item.wait_recv()


def begin(copies):
    for item in copies:
        item.start()


def greet(devices):
    barrier = pltpu.get_barrier_semaphore()
    for device in devices:
        pl.semaphore_signal(barrier, inc=1, device_id=device, device_id_type=MESH)
    return lambda: pl.semaphore_wait(barrier, len(devices))


def as_row(col):
    return jnp.transpose(jnp.broadcast_to(col, (col.shape[0], 128)))[0:1]


def as_col(row):
    return jnp.transpose(jnp.broadcast_to(row, (128, 128)))[:, 0:1]


def flat(v):
    return v.reshape(-1, v.shape[-1])


class Piece:
    def __init__(self, here, links, part, x_rx, z_rx, full, square):
        self.here, self.part, self.x_rx, self.z_rx = here, part, x_rx, z_rx
        self.full, self.square = full, square
        steps = range(1, here.depth)
        place, column = full.at[here.z, here.x], full.at[:, here.x]
        self.first = links.plan(part.at[:, 1 - here.x], x_rx, here.across)
        self.second = [
            links.plan(x_rx.at[(here.z + k) % here.depth], z_rx.at[k - 1], here.along(k)) for k in steps
        ]
        self.third = [links.plan(place, place, here.along(k)) for k in steps]
        self.fourth = links.plan(column, column, here.across)
        self.holding = [self.first]

    def start(self):
        self.first.start()

    def fold(self):
        self.first.wait_recv()
        for k in range(self.here.depth):
            self.x_rx[k] = self.x_rx[k] + self.part[k, self.here.x]
        begin(self.second)

    def own(self):
        arrived(self.second)
        total = self.x_rx[self.here.z]
        for k in range(1, self.here.depth):
            total = total + self.z_rx[k - 1]
        self.full[self.here.z, self.here.x] = total
        begin(self.third)
        self.square[...] = jnp.broadcast_to(total_square(total), self.square.shape)

    def spread(self):
        arrived(self.third)
        self.fourth.start()

    def finish(self):
        self.fourth.wait_recv()


class CrossPiece:
    def __init__(self, here, links, part, z_rx, x_rx, full, square):
        self.here, self.part, self.z_rx, self.x_rx = here, part, z_rx, x_rx
        self.full, self.square = full, square
        steps = range(1, here.depth)
        mine, pair = full.at[here.z, here.x], full.at[here.z]
        self.first = [
            links.plan(part.at[(here.z + k) % here.depth], z_rx.at[k - 1], here.along(k)) for k in steps
        ]
        self.second = links.plan(part.at[here.z, 1 - here.x], x_rx, here.across)
        self.third = links.plan(mine, mine, here.across)
        self.fourth = [links.plan(pair, pair, here.along(k)) for k in steps]
        self.holding = [*self.first, self.second]

    def start(self):
        begin(self.first)

    def fold(self):
        arrived(self.first)
        total = self.part[self.here.z]
        for k in range(1, self.here.depth):
            total = total + self.z_rx[k - 1]
        self.part[self.here.z] = total
        self.second.start()

    def own(self):
        self.second.wait_recv()
        total = self.part[self.here.z, self.here.x] + self.x_rx[...]
        self.full[self.here.z, self.here.x] = total
        self.third.start()
        self.square[...] = jnp.broadcast_to(total_square(total), self.square.shape)

    def spread(self):
        self.third.wait_recv()
        begin(self.fourth)

    def finish(self):
        arrived(self.fourth)


def total_square(v):
    return jnp.sum(jnp.sum(v * v, axis=0, keepdims=True), axis=1, keepdims=True)


def layer_kernel(
    wide,
    heads,
    shard,
    inner_total,
    length_ref,
    hidden_ref,
    cot_ref,
    gain_ref,
    w_ref,
    wout_ref,
    bcw_ref,
    dtw_ref,
    cx_in,
    cbc_in,
    hp_in,
    og_in,
    block_ref,
    grad_ref,
    gfull,
    bc_own,
    dt_own,
    sv_sum,
    norm_ref,
    hq,
    cq,
    wz_g,
    wx_g,
    wo_g,
    bc_g,
    dt_g,
    gain_g,
    dtt,
    gain_col,
    gain_row,
    turn_s,
    cx_ref,
    cbc_ref,
    hp_ref,
    og_ref,
    live_ref,
    inv_ref,
    proj,
    y_s,
    xc,
    dx_act,
    b_s,
    c_s,
    dbc_act,
    step_s,
    cum_s,
    cumex_s,
    hcat,
    inner_s,
    don,
    onorm,
    dy_s,
    dh_s,
    db_s,
    dc_s,
    din_s,
    g_s,
    cv_s,
    v_s,
    dd_s,
    tq_s,
    cols_s,
    dcbc_s,
    dhp_s,
    dog_s,
    dgain_s,
    stat_own,
    stat_g,
    part,
    x_rx,
    z_rx,
    zz_rx,
    xx_rx,
    core_rx,
    row_rx,
    gbc,
    bc_core,
    bc_row,
    bc_mine,
    bc_rx,
    gdt,
    dt_rx,
    shared_g,
    sv_g,
    norm_n,
    norm_w,
    square_s,
    hq_hi,
    hq_lo,
    wt_hi,
    wt_lo,
    send,
    recv,
    stat_send,
    stat_recv,
):
    here = Place(wide)
    links = Links(send, recv)
    w, n, z, x, y, c, depth = here.w, here.n, here.z, here.x, here.y, here.c, here.depth
    group = here.group()
    far = [here.others(k) for k in range(1, wide)]
    own_rows, width = hidden_ref.shape
    chans, tokens = y_s.shape
    state = b_s.shape[0] // 2
    blocks = tokens // SPAN
    parts = tokens // own_rows
    thirds = chans // 128
    z_ref, x_ref, bc_ref, pre_ref = pieces(proj, chans, state)
    met = greet(group + far)
    jobs = []
    crossing = (2 * thirds - 1, 2 * thirds)
    for i in range(3 * thirds):
        source = part.at[i if i < 2 * thirds else i - thirds]
        k = sum(1 for other in crossing if other < i)
        if i in crossing:
            jobs.append(CrossPiece(here, links, source, zz_rx.at[k], xx_rx.at[k], gfull.at[i], square_s.at[i]))
        else:
            jobs.append(Piece(here, links, source, x_rx.at[i - k], z_rx.at[i - k], gfull.at[i], square_s.at[i]))
    z_jobs, x_jobs, o_jobs = jobs[0:thirds], jobs[thirds : 2 * thirds], jobs[2 * thirds :]

    half = bcw_ref.shape[0] // 2
    wx_g[z, x] = w_ref[1]
    bc_g[z, x, c] = bcw_ref[pl.ds(pl.multiple_of(c * half, 8), half), :]
    dt_g[z, x] = jnp.zeros(dt_g.shape[2:], F32)
    for h in range(heads):
        for i in range(2):
            row = i * heads + h
            dt_g[z, x, row : row + 1, 0 : dtw_ref.shape[2]] = dtw_ref[h, i : i + 1, :]
    line = gain_ref[...].reshape(1, shard)
    gain_g[n] = jnp.zeros(gain_g.shape[1:], F32)
    for i in range((shard + 127) // 128):
        size = min(128, shard - 128 * i)
        gain_g[n, i : i + 1, 0:size] = line[:, 128 * i : 128 * i + size]
    squares = jnp.zeros((1, own_rows), F32)
    for i in range(width // 128):
        turned = jnp.transpose(hidden_ref[:, i * 128 : (i + 1) * 128])
        squares = squares + jnp.sum(turned * turned, axis=0, keepdims=True)
        hq[n, i * 128 : (i + 1) * 128, :] = turned
    inv_ref[...] = lax.rsqrt(squares / width + 1e-05)
    for i in range(width // 128):
        hq[n, i * 128 : (i + 1) * 128, :] = hq[n, i * 128 : (i + 1) * 128, :] * inv_ref[...]
    met()

    def along(ref):
        return [links.copy(ref, ref, here.along(k)) for k in range(1, depth)]

    def exchange(ref):
        return [links.copy(ref, ref, here.row), links.copy(ref, ref, here.core)]

    class Relay:
        def __init__(self, *views):
            self.views = views
            self.direct = [along(view(z)) for view in views]
            self.passed = []

        def begin(self):
            self.passed = [links.copy(view(z), view(z), here.across) for view in self.views]

        def forward(self, steps=tuple(range(1, depth))):
            for k in steps:
                source = (z + depth - k) % depth
                for view, copies in zip(self.views, self.direct):
                    copies[k - 1].wait_recv()
                    self.passed.append(links.copy(view(source), view(source), here.across))

        def wait(self):
            arrived(self.passed)

    split = chans - 128

    class Cross:
        def __init__(self, ref):
            self.mine, self.pair = ref.at[z, x, :, split:], ref.at[z, :, :, split:]

        def begin(self):
            self.across = links.copy(self.mine, self.mine, here.across)

        def forward(self):
            self.across.wait_recv()
            self.sent = along(self.pair)

        def wait(self):
            arrived(self.sent)

    h_copies = exchange(hq.at[n])
    gain_copies = [links.copy(gain_g.at[n], gain_g.at[n], device) for device in group]
    early = Relay(lambda i: bc_g.at[i, x, c], lambda i: dt_g.at[i, x])
    early.begin()
    first_cross, second_cross, third_cross = Cross(wx_g), Cross(wz_g), Cross(wo_g)
    first_cross.begin()
    first = Relay(lambda i: wx_g.at[i, x, :, 0:split])
    first.begin()

    wz_g[z, x] = w_ref[0]
    wo_g[z, x] = wout_ref[...]
    live_ref[...] = jnp.where(iota((1, tokens), 1) < length_ref[0], 1.0, 0.0)
    live_own = live_ref[:, pl.ds(pl.multiple_of(n * own_rows, 128), own_rows)]
    for i in range(width // 128):
        cq[n, i * 128 : (i + 1) * 128, :] = jnp.transpose(cot_ref[:, i * 128 : (i + 1) * 128]) * live_own
    turn_s[...] = jnp.zeros_like(turn_s)
    for ref, out in ((cx_in, cx_ref), (cbc_in, cbc_ref)):
        for i in range(ref.shape[1] // 128):
            turn_s[0:4, :] = ref[:, i * 128 : (i + 1) * 128]
            out[i * 128 : (i + 1) * 128, :] = jnp.transpose(turn_s[...])[:, 0:4]
    turn_s[...] = jnp.zeros_like(turn_s)
    turn_s[0:1, 0:heads] = hp_in[0:1, :]
    turn_s[0:1, heads : 2 * heads] = hp_in[1:2, :]
    turn_s[1:2, 0:heads] = jnp.exp(hp_in[2:3, :])
    turn_s[1:2, heads : 2 * heads] = jnp.exp(hp_in[3:4, :])
    turn_s[2:3, 0:heads] = hp_in[4:5, :]
    hp_ref[...] = jnp.transpose(turn_s[...])[0:16, 0:3]
    og_line = og_in[...].reshape(1, chans)
    for i in range(thirds):
        og_ref[i * 128 : (i + 1) * 128, :] = as_col(og_line[:, i * 128 : (i + 1) * 128])
    cols_s[...] = jnp.zeros_like(cols_s)
    dcbc_s[...] = jnp.zeros_like(dcbc_s)
    dhp_s[...] = jnp.zeros_like(dhp_s)

    def cut(q):
        hq_hi[q], hq_lo[q] = halves(hq[q])

    cut(n)
    h_copies[1].wait_recv()
    cut(here.core[1])
    first_cross.forward()
    early.forward()
    first.forward()
    second_cross.begin()
    second = Relay(lambda i: wz_g.at[i, x, :, 0:split])
    h_copies[0].wait_recv()
    other = here.row[1]
    h_far = links.copy(hq.at[other], hq.at[other], here.core)
    c_copies = exchange(cq.at[n])
    arrived(gain_copies)
    for q in range(parts):
        turned = jnp.transpose(jnp.concatenate([gain_g[q], jnp.zeros((120, 128), F32)], axis=0))
        for i in range((shard + 127) // 128):
            size = min(128, shard - 128 * i)
            start = shard * q + 128 * i
            gain_col[start : start + size, :] = turned[0:size, i : i + 1]
    for i in range(width // 128):
        gain_row[:, i * 128 : (i + 1) * 128] = as_row(gain_col[i * 128 : (i + 1) * 128, :])

    def turn(ref, row, scale=True):
        for i in range(ref.shape[-1] // 128):
            cols = flat(ref[..., i * 128 : (i + 1) * 128])
            if scale:
                cols = cols * gain_col[...]
            for dst, value in zip((wt_hi, wt_lo), halves(jnp.transpose(cols))):
                dst[row + i * 128 : row + (i + 1) * 128, :] = value

    def quarter(q):
        return pl.ds(pl.multiple_of(q * own_rows, 128), own_rows)

    def each_quarter(body):
        def step(q, _):
            body(q)
            return 0

        lax.fori_loop(0, parts, step, 0)

    def rows_of(start, stop):
        return wt_hi[start:stop, :], wt_lo[start:stop, :]

    def project(out_ref, weights):
        def body(q):
            out_ref[:, quarter(q)] = product(weights(), (hq_hi[q], hq_lo[q]))

        each_quarter(body)

    early.wait()
    bc_core_copy = links.copy(bc_g.at[:, :, c], bc_g.at[:, :, c], here.core)
    lanes = width // wide
    for i in range(wide):
        dtt[:, i * lanes : (i + 1) * lanes] = dt_g[i // 2, i % 2][:, 0:lanes]
    last = 2 * chans + 4 * state
    wt_hi[last:, :], wt_lo[last:, :] = halves(dtt[...] * gain_row[...])
    bc_core_copy.wait_recv()
    turn(bc_g, 2 * chans)
    first.wait()
    first_cross.wait()
    second.begin()
    second.forward((1,))
    second_cross.forward()
    turn(wx_g, chans)
    second.forward((2,))
    h_far.wait_recv()
    cut(here.row[1])
    cut(here.corner[1])
    project(proj.at[chans:], lambda: rows_of(chans, last + 16))
    second.forward((3,))
    third_cross.begin()
    third = Relay(lambda i: wo_g.at[i, x, :, 0:split])
    third.begin()
    c_copies[0].wait_recv()
    c_far = links.copy(cq.at[other], cq.at[other], here.core)
    convolve(x_ref, bc_ref, live_ref, cx_ref, cbc_ref, xc, dx_act, b_s, c_s, dbc_act)
    step_sizes(pre_ref, hp_ref, step_s, cum_s, cumex_s, heads)
    states(xc, b_s, step_s, cum_s, dh_s, hcat, heads)
    second.wait()
    second_cross.wait()
    turn(wz_g, 0)
    project(z_ref, lambda: rows_of(0, chans))
    third.forward()
    third_cross.forward()

    def stat_copy(j, b):
        return pltpu.make_async_remote_copy(
            src_ref=stat_own.at[b],
            dst_ref=stat_g.at[n, b],
            send_sem=stat_send.at[j, b],
            recv_sem=stat_recv.at[j, b],
            device_id=group[j],
            device_id_type=MESH,
        )

    def tell(b, row):
        stats = jnp.broadcast_to(row, (8, SPAN))
        stat_own[b] = stats
        stat_g[n, b] = stats
        for j in range(3):
            stat_copy(j, b).start()

    def told(b):
        for j in range(3):
            stat_copy(j, b).wait_recv()
        total = stat_g[0, b]
        for q in range(1, parts):
            total = total + stat_g[q, b]
        return total[0:1]

    def emit(b, sl, h, rows, gated, sums):
        onorm[rows, sl] = gated
        row = jnp.sum(gated * gated, axis=0, keepdims=True)
        row = row if sums is None else row + sums
        if h == heads - 1:
            tell(b, row)
        return row

    outputs(z_ref, xc, b_s, c_s, step_s, cum_s, cumex_s, hcat, hp_ref, y_s, inner_s, heads, emit)
    rms = jnp.concatenate(
        [lax.rsqrt(told(b) / inner_total + 1e-05) for b in range(blocks)], axis=1
    )

    def scale_rows(i, _):
        rows = pl.ds(pl.multiple_of(i * 8, 8), 8)
        onorm[rows, :] = onorm[rows, :] * rms * og_ref[rows, :]
        return 0

    lax.fori_loop(0, chans // 8, scale_rows, 0, unroll=2)
    c_copies[1].wait_recv()
    c_far.wait_recv()

    def weight_grad(put, right, left=lambda q: (hq_hi[q], hq_lo[q])):
        def body(q):
            put(q, product(left(q), halves(right(q)), NT))

        each_quarter(body)

    block_shape = part.shape[1:]

    def add_to(start, count):
        def put(q, value):
            for i in range(count):
                ref = part.at[start + i]
                piece = value[:, i * 128 : (i + 1) * 128].reshape(block_shape)
                ref[...] = jnp.where(q == 0, piece, ref[...] + piece)

        return put

    def scaled(i):
        part[i] = (flat(part[i]) * gain_col[...]).reshape(block_shape)

    part[...] = jnp.zeros_like(part)
    for start, stop in ((0, 1), (1, thirds)):
        rows = slice(start * 128, stop * 128)
        weight_grad(
            add_to(thirds + start, stop - start),
            lambda q, rows=rows: onorm[rows, quarter(q)],
            lambda q: halves(cq[q]),
        )
        for job in o_jobs[start:stop]:
            job.start()
    third.wait()
    third_cross.wait()
    turn(wo_g, 0, False)

    def donorm(q):
        don[:, quarter(q)] = product(rows_of(0, chans), halves(cq[q]))

    each_quarter(donorm)

    def inner_sums(b, _):
        sl = pl.ds(pl.multiple_of(b * SPAN, SPAN), SPAN)
        gate = z_ref[:, sl]
        gated = y_s[:, sl] * (gate * sigmoid(gate))
        tell(blocks + b, jnp.sum(gated * (don[:, sl] * og_ref[...]), axis=0, keepdims=True))
        return 0

    lax.fori_loop(0, blocks, inner_sums, 0)

    links.release(c_copies + [c_far])

    class Return:
        def __init__(self, rx, row_rx, compute, steps=((), (), (), ())):
            self.rx, self.row_rx = rx, row_rx
            near, away = y * 2, (1 - y) * 2
            self.cores = [
                links.plan(cq.at[away + 1 - c], rx.at[0], here.core),
                links.plan(cq.at[near + 1 - c], rx.at[1], here.core),
            ]
            self.last = links.plan(cq.at[away + c], row_rx, here.row)

            def body(k, _):
                row = 1 - y + (k // 2) * (2 * y - 1)
                q = row * 2 + 1 - c + (k % 2) * (2 * c - 1)
                cq[q] = compute(q)

                @pl.when(k == 0)
                def _():
                    self.cores[0].start()

                @pl.when(k == 2)
                def _():
                    self.cores[1].start()
                    self.cores[0].wait_recv()
                    cq[away + c] = cq[away + c] + rx[0]
                    self.last.start()

                for at, items in enumerate(steps):

                    @pl.when(k == at)
                    def _(items=items):
                        for step in items:
                            step()

                return 0

            lax.fori_loop(0, 4, body, 0)

        def fold(self):
            self.cores[1].wait_recv()
            self.rx[1] = self.rx[1] + cq[y * 2 + c]

        def total(self):
            self.last.wait_recv()
            return self.rx[1] + self.row_rx[...]

    o0, o1, o2 = o_jobs
    z0, z1, z2 = z_jobs
    x0, x1, x2 = x_jobs
    branch = Return(core_rx.at[0], row_rx.at[0], lambda q: dot3(flat(wo_g[...]), onorm[:, quarter(q)]))
    told_inner = jnp.concatenate([told(blocks + b) for b in range(blocks)], axis=1)
    coef = rms**3 * told_inner / inner_total
    gate_back(z_ref, y_s, don, rms, coef, og_ref, dy_s, z_ref, dog_s)
    o0.fold()
    o1.fold()
    weight_grad(add_to(0, thirds), lambda q: z_ref[:, quarter(q)])
    for i, job in enumerate(z_jobs):
        scaled(i)
        job.start()

    def x_grad(i):
        links.release(o_jobs[i].holding)
        part[thirds + i] = jnp.zeros(block_shape, F32)
        weight_grad(add_to(thirds + i, 1), lambda q: x_ref[i * 128 : (i + 1) * 128, quarter(q)])
        scaled(thirds + i)

    within = [
        {3: [o2.fold, o1.own], 5: [o0.own]},
        {1: [o1.spread], 3: [branch.fold], 5: [o2.spread, z1.fold]},
        {5: [z0.spread]},
    ]
    between = [{7: [o2.own]}, {3: [z0.own]}, {}]
    after_states = [(), (), (x0.fold, z2.own)]
    after_conv = [(z0.fold,), (), ()]
    after_grad = [(), (z2.fold, z1.own, o0.spread), (z1.spread,)]

    def run(steps):
        for step in steps:
            step()

    def ticks(plan):
        def tick(b):
            for at, steps in plan.items():

                @pl.when(b == at)
                def _(steps=steps):
                    for step in steps:
                        step()

        return tick

    for i, chosen in enumerate(pairs_of(heads)):
        back_intra(
            xc, c_s, inner_s, step_s, cum_s, cumex_s, hcat, hp_ref, dy_s, y_s, dh_s, dc_s,
            din_s, g_s, cv_s, dd_s, chosen, heads, ticks(within[i]),
        )
        back_states(cum_s, hcat, dh_s, tq_s, state, chosen, heads)
        run(after_states[i])
        back_inter(xc, b_s, step_s, cum_s, y_s, dh_s, db_s, v_s, chosen, heads, ticks(between[i]))
        conv_x_back(x_ref, cx_ref, dx_act, y_s, x_ref, cols_s, i * 128, 128)
        run(after_conv[i])
        x_grad(i)
        x_jobs[i].start()
        run(after_grad[i])

    back_logs(
        b_s, c_s, pre_ref, step_s, hp_ref, pre_ref, dhp_s, db_s, dc_s, din_s, g_s, cv_s, v_s, dd_s, tq_s, heads
    )
    conv_bc_back(bc_ref, cbc_ref, dbc_act, db_s, dc_s, bc_ref, dcbc_s)
    gbc_shape = gbc.shape

    def add_bc(q, value):
        gbc[...] = jnp.where(q == 0, value.reshape(gbc_shape), gbc[...] + value.reshape(gbc_shape))

    gbc[...] = jnp.zeros_like(gbc)
    weight_grad(add_bc, lambda q: bc_ref[:, quarter(q)])
    gbc[...] = (flat(gbc[...]) * gain_col[...]).reshape(gbc_shape)
    bc_first = links.copy(gbc.at[:, :, 1 - c], bc_core, here.core)
    dt_grad = jnp.zeros((16, width), F32)
    for q in range(parts):
        step = halves(pre_ref[:, q * own_rows : (q + 1) * own_rows])
        dt_grad = dt_grad + product(step, (hq_hi[q], hq_lo[q]), NT)
    dt_grad = dt_grad * gain_row[...]
    gdt[...] = jnp.zeros_like(gdt)
    for i in range(wide):
        gdt[i, :, 0:lanes] = dt_grad[:, i * lanes : (i + 1) * lanes]
    dt_rx[w] = gdt[w]
    dt_copies = [links.copy(gdt.at[device[0]], dt_rx.at[w], device) for device in far]
    dgain_s[...] = jnp.zeros_like(dgain_s)
    bc_first.wait_recv()
    for k in range(2):
        bc_core[:, k] = bc_core[:, k] + gbc[:, k, c]
    for k in range(wide):
        bc_mine[k] = bc_core[k, 1 - y]
    bc_second = links.copy(bc_mine, bc_row, here.row)

    links.release(branch.cores + [branch.last])

    for k in range(parts):
        pieces_of = []
        for ref, start in ((wz_g, 0), (wx_g, chans), (bc_g, 2 * chans)):
            a, b = max(k * own_rows, start), min((k + 1) * own_rows, start + ref.shape[-1])
            if a < b:
                pieces_of.append(flat(ref[..., a - start : b - start]))
        hq_hi[k], hq_lo[k] = halves(jnp.concatenate(pieces_of, axis=1))

    def normed_back(q):
        sl = quarter(q)

        def add(k, value):
            rows = pl.ds(pl.multiple_of(k * own_rows, 8), own_rows)
            return value + product((hq_hi[k], hq_lo[k]), halves(proj[rows, sl]))

        value = lax.fori_loop(0, parts, add, dot3(dtt[...], pre_ref[:, sl], TN))
        dgain_s[...] = dgain_s[...] + jnp.sum(value * hq[q], axis=1, keepdims=True)
        return value

    back = Return(core_rx.at[1], row_rx.at[1], normed_back, ([], [x0.own], [], [x1.fold, z2.spread]))
    back.fold()
    small = 128
    shared_g[n] = jnp.zeros(shared_g.shape[1:], F32)
    for i in range(4 * state // 128):
        sl = slice(i * 128, (i + 1) * 128)
        shared_g[n, 0:4, sl] = jnp.transpose(dcbc_s[sl, :])[0:4]
    for i in range(width // 128):
        shared_g[n, 8 + i : 9 + i, 0:128] = as_row(dgain_s[i * 128 : (i + 1) * 128, :])
    shared_copies = [links.copy(shared_g.at[n], shared_g.at[n], device) for device in group]
    bc_second.wait_recv()
    links.release([bc_second])
    for k in range(wide):
        bc_mine[k] = bc_core[k, y] + bc_row[k]
    bc_rx[w] = bc_mine[w]
    bc_copies = [links.copy(bc_mine.at[device[0]], bc_rx.at[w], device) for device in far]
    sv_g[w] = jnp.zeros(sv_g.shape[1:], F32)
    for i in range(thirds):
        sl = slice(i * 128, (i + 1) * 128)
        sv_g[w, 0:4, sl] = jnp.transpose(cols_s[sl, :])[0:4]
        sv_g[w, 4:5, sl] = as_row(dog_s[sl, :])
    sv_g[w, :, chans : chans + small] = dhp_s[...]
    x2.fold()
    arrived(shared_copies)
    total = shared_g[0]
    for q in range(1, parts):
        total = total + shared_g[q]
    sv_g[w, :, chans + small :] = total
    sv_copies = [links.copy(sv_g.at[w], sv_g.at[w], device) for device in far]

    x0.spread()
    x1.own()
    arrived(bc_copies)
    own = bc_rx[0]
    for k in range(1, wide):
        own = own + bc_rx[k]
    bc_own[n] = own
    bc_group = [links.copy(bc_own.at[n], bc_own.at[n], device) for device in group]
    squares = total_square(own)
    arrived(dt_copies)
    own = dt_rx[0]
    for k in range(1, wide):
        own = own + dt_rx[k]
    dt_own[...] = own
    squares = squares + total_square(own)
    arrived(sv_copies)
    own = sv_g[0]
    for k in range(1, wide):
        own = own + sv_g[k]
    sv_sum[...] = own
    x2.own()
    for i in range(3 * thirds):
        squares = squares + square_s[i][:, 0:1]
    once = jnp.where(w == 0, 1.0, 0.0)
    squares = squares + once * total_square(own[:, 0 : chans + small])
    squares = squares + jnp.where(n == 0, once, 0.0) * total_square(own[:, chans + small :])
    norm_n[n] = jnp.broadcast_to(squares, (8, 128))
    norm_copies = [links.copy(norm_n.at[n], norm_n.at[n], device) for device in group]

    x1.spread()

    block = branch.total() * live_ref[:, pl.ds(pl.multiple_of(n * own_rows, 128), own_rows)]
    for i in range(width // 128):
        sl = slice(i * 128, (i + 1) * 128)
        block_ref[:, sl] = hidden_ref[:, sl] + jnp.transpose(block[sl, :])
    arrived(norm_copies)
    norm_w[w] = norm_n[0] + norm_n[1] + norm_n[2] + norm_n[3]
    wide_copies = [links.copy(norm_w.at[w], norm_w.at[w], device) for device in far]
    x2.spread()
    dn = back.total() * gain_col[...]
    dots = jnp.sum(dn * hq[n], axis=0, keepdims=True) / width
    for i in range(width // 128):
        sl = slice(i * 128, (i + 1) * 128)
        value = inv_ref[...] * (dn[sl] - hq[n, sl, :] * dots)
        grad_ref[:, sl] = cot_ref[:, sl] + jnp.transpose(value)
    arrived(wide_copies)
    total = norm_w[0]
    for k in range(1, wide):
        total = total + norm_w[k]
    norm_ref[...] = jnp.sqrt(total)
    for job in jobs:
        job.finish()
    arrived(bc_group)
    links.drain()

    def sent(b, _):
        for j in range(3):
            stat_copy(j, b).wait_send()
        return 0

    lax.fori_loop(0, 2 * blocks, sent, 0)


def run_layer(lengths, hidden, cot, gain, w_zx, w_out, w_bc, dtw, cx, cbc, hp, og, heads, shard, wide, narrow):
    own_rows, width = hidden.shape
    tokens = own_rows * narrow
    chans, n4 = cx.shape[1], cbc.shape[1]
    rows = w_zx.shape[1]
    depth, blocks, half, thirds = wide // 2, tokens // SPAN, n4 // 2, chans // 128
    full, bc2, small = (chans, tokens), (half, tokens), (16, tokens)
    quarters = (narrow, width, own_rows)
    weights = (depth, 2, rows, chans)
    piece = (3 * thirds, depth, 2, rows, 128)
    quarter = (width // wide // 4, n4)
    sums = (16, chans + 128 + 256)
    shapes = [
        hidden.shape,
        hidden.shape,
        piece,
        (4,) + quarter,
        (16, 128),
        sums,
        (8, 128),
    ]
    scratch = [
        quarters,
        quarters,
        weights,
        weights,
        weights,
        (depth, 2, 2, rows // 2, n4),
        (depth, 2, 16, 128),
        (narrow, 8, 128),
        (16, width),
        (width, 1),
        (1, width),
        (128, 128),
        (chans, 4),
        (n4, 4),
        (16, 3),
        (chans, 1),
        (1, tokens),
        (1, own_rows),
        (2 * chans + n4 + 16, tokens),
        full,
        full,
        full,
        bc2,
        bc2,
        (n4, tokens),
        small,
        small,
        small,
        (blocks, chans, half),
        (blocks, SPAN, SPAN),
        full,
        full,
        full,
        (blocks, chans, half),
        bc2,
        bc2,
        (blocks, SPAN, SPAN),
        small,
        small,
        small,
        small,
        (blocks, 16, SPAN),
        (chans, 128),
        (n4, 128),
        (16, 128),
        (chans, 1),
        (width, 1),
        (2 * blocks, 8, 128),
        (narrow, 2 * blocks, 8, 128),
        (2 * thirds,) + piece[1:],
        (3 * thirds - 2, depth, rows, 128),
        (3 * thirds - 2, depth - 1, rows, 128),
        (2, depth - 1, 2, rows, 128),
        (2, rows, 128),
        (2, 2, width, own_rows),
        (2, width, own_rows),
        (wide, 2, 2) + quarter,
        (wide, 2) + quarter,
        (wide,) + quarter,
        (wide,) + quarter,
        (wide,) + quarter,
        (wide, 16, 128),
        (wide, 16, 128),
        (narrow, 16, 256),
        (wide,) + sums,
        (narrow, 8, 128),
        (wide, 8, 128),
        (3 * thirds, 1, 128),
    ]
    lows = [quarters] * 2 + [(2 * chans + n4 + 16, width)] * 2
    copies = 200
    operands = (lengths, hidden, cot, gain, w_zx, w_out, w_bc, dtw, cx, cbc, hp, og)
    return pl.pallas_call(
        functools.partial(layer_kernel, wide, heads, shard, chans * narrow),
        out_shape=[jax.ShapeDtypeStruct(shape, F32) for shape in shapes],
        in_specs=[pl.BlockSpec(memory_space=pltpu.SMEM)]
        + [pl.BlockSpec(memory_space=pltpu.VMEM)] * (len(operands) - 1),
        scratch_shapes=[pltpu.VMEM(shape, F32) for shape in scratch]
        + [pltpu.VMEM(shape, jnp.bfloat16) for shape in lows]
        + [
            pltpu.SemaphoreType.DMA((copies,)),
            pltpu.SemaphoreType.DMA((copies,)),
            pltpu.SemaphoreType.DMA((3, 2 * blocks)),
            pltpu.SemaphoreType.DMA((3, 2 * blocks)),
        ],
        compiler_params=pltpu.CompilerParams(
            vmem_limit_bytes=62 * MIB, collective_id=0, has_side_effects=True
        ),
        cost_estimate=pl.CostEstimate(flops=20_000_000_000, bytes_accessed=20_000_000, transcendentals=0),
    )(*operands)


def finish_kernel(
    wide,
    narrow,
    gfull,
    bc_own,
    dt_own,
    sv,
    norm_ref,
    block_in,
    grad_in,
    stat_l,
    stat_r,
    stat_lo,
    stat_ro,
    root_l,
    root_r,
    root_lo,
    root_ro,
    w_ref,
    wout_ref,
    bcw_ref,
    dtw_ref,
    cx_ref,
    cbc_ref,
    hp_ref,
    og_ref,
    gain_ref,
    block_out,
    in_grad,
    clip,
    g_zx,
    new_zx,
    new_l,
    new_r,
    g_out,
    new_out,
    new_lo,
    new_ro,
    g_bc,
    new_bc,
    g_dt,
    new_dt,
    g_cx,
    new_cx,
    g_cbc,
    new_cbc,
    g_hp,
    new_hp,
    g_og,
    new_og,
    g_ng,
    new_ng,
    g_s,
    l_s,
    r_s,
    lo_s,
    ro_s,
    rl_s,
    rr_s,
    rlo_s,
    rro_s,
    in_sem,
    out_sem,
):
    rate = 10.0
    chans = w_ref.shape[2]
    thirds = chans // 128
    place = lax.axis_index("wide")
    z, x = place // 2, place % 2
    factor = 1.0 / jnp.maximum(norm_ref[0:1, 0:1], 1.0)
    fetches, results = [], []

    def fetch(src, dst):
        item = pltpu.make_async_copy(src, dst, in_sem.at[len(fetches)])
        item.start()
        fetches.append(item)
        return item

    def result(src, dst):
        item = pltpu.make_async_copy(src, dst, out_sem.at[len(results)])
        item.start()
        results.append(item)

    waits = []
    for m in (2, 0, 1):
        gs = g_s.at[m * thirds : (m + 1) * thirds]
        whole_m = fetch(gfull.at[m * thirds : (m + 1) * thirds], gs)
        if m == 2:
            others = [(root_ro, rro_s), (root_lo, rlo_s), (stat_ro, ro_s), (stat_lo, lo_s)]
        else:
            others = [(root_l.at[m], rl_s.at[m]), (root_r.at[m], rr_s.at[m])]
            others += [(stat_l.at[m], l_s.at[m]), (stat_r.at[m], r_s.at[m])]
        waits.append([whole_m] + [fetch(*pair) for pair in others])
    block_out[...] = block_in[...]
    in_grad[...] = grad_in[...]
    clip[...] = norm_ref[0:1, 0:1]

    def both(m):
        for item in waits[(1, 2, 0)[m]]:
            item.wait()
        parts = [flat(g_s[m * thirds + i]) for i in range(thirds)]
        mine = [g_s[m * thirds + i, z, x] for i in range(thirds)]
        parts = [item * factor for item in parts]
        turned = jnp.concatenate([jnp.transpose(item) for item in parts], axis=0)
        return jnp.concatenate(mine, axis=1) * factor, halves(jnp.concatenate(parts, axis=1)), halves(turned)

    own, full, turned = both(2)
    g_out[...] = own
    ro_s[...] = 0.5 * ro_s[...] + 0.5 * product(halves(own), full, NT)
    result(ro_s, new_ro)
    lo_s[...] = 0.5 * lo_s[...] + 0.5 * product(turned, full)
    result(lo_s, new_lo)
    new_out[...] = wout_ref[...] - 0.5 * dot3(product(halves(rro_s[...]), full), rlo_s[...], NT)
    for m in range(2):
        own, full, turned = both(m)
        g_zx[m] = own
        l_s[m] = 0.5 * l_s[m] + 0.5 * product(halves(own), full, NT)
        result(l_s.at[m], new_l.at[m])
        r_s[m] = 0.5 * r_s[m] + 0.5 * product(turned, full)
        result(r_s.at[m], new_r.at[m])
        new_zx[m] = w_ref[m] - 0.5 * dot3(product(halves(rl_s[m]), full), rr_s[m])

    grad = flat(bc_own[...]) * factor
    g_bc[...] = grad
    new_bc[...] = bcw_ref[...] - rate * grad
    heads, _, rows = dtw_ref.shape
    for h in range(heads):
        for i in range(2):
            row = i * heads + h
            grad = dt_own[row : row + 1, 0:rows] * factor
            g_dt[h, i : i + 1, :] = grad
            new_dt[h, i : i + 1, :] = dtw_ref[h, i : i + 1, :] - rate * grad
    sums = sv[...] * factor
    grad = sums[0:4, 0:chans]
    g_cx[...] = grad
    new_cx[...] = cx_ref[...] - rate * grad
    grad = sums[4:5, 0:chans]
    g_og[...] = grad.reshape(chans)
    new_og[...] = og_ref[...] - rate * g_og[...]
    n4 = cbc_ref.shape[1]
    last = chans + 128
    grad = sums[0:4, last : last + n4]
    g_cbc[...] = grad
    new_cbc[...] = cbc_ref[...] - rate * grad
    turned = jnp.transpose(
        jnp.concatenate([sums[:, chans:last], jnp.zeros((112, 128), F32)], axis=0)
    )
    for i, (row, start) in enumerate(((0, 0), (0, heads), (1, 0), (1, heads), (2, 0))):
        grad = turned[row : row + 1, start : start + heads]
        g_hp[i : i + 1, :] = grad
        new_hp[i : i + 1, :] = hp_ref[i : i + 1, :] - rate * grad
    shard = gain_ref.shape[0]
    count = narrow * shard // 128
    line = jnp.concatenate([sums[8 + i : 9 + i, last : last + 128] for i in range(count)], axis=1)
    grad = jnp.zeros((1, shard), F32)
    for q in range(narrow):
        piece = line[:, q * shard : (q + 1) * shard]
        grad = jnp.where(lax.axis_index("narrow") == q, piece, grad)
    g_ng[...] = grad.reshape(shard)
    new_ng[...] = gain_ref[...] - rate * g_ng[...]
    for item in results:
        item.wait()


def run_finish(partials, stats, roots, params, tokens_shape, wide, narrow):
    stat_l, stat_r, stat_lo, stat_ro = stats
    w_zx, w_out, w_bc, w_dt, cx, cbc, hp, og, gain = params
    like = [w_zx, w_zx, stat_l, stat_r, w_out, w_out, stat_lo, stat_ro]
    like += [item for item in (w_bc, w_dt, cx, cbc, hp, og, gain) for _ in range(2)]
    shapes = [tokens_shape, tokens_shape, (1, 1)] + [item.shape for item in like]
    far, near = pl.BlockSpec(memory_space=pl.ANY), pl.BlockSpec(memory_space=pltpu.VMEM)
    gfull = partials[0]
    kept = [gfull, stat_l, stat_r, stat_lo, stat_ro, *roots]
    return pl.pallas_call(
        functools.partial(finish_kernel, wide, narrow),
        out_shape=[jax.ShapeDtypeStruct(shape, F32) for shape in shapes],
        in_specs=[far] + [near] * 6 + [far] * 8 + [near] * len(params),
        out_specs=[near] * 5 + [far] * 2 + [near] * 2 + [far] * 2 + [near] * (len(shapes) - 11),
        scratch_shapes=[pltpu.VMEM(item.shape, F32) for item in kept]
        + [pltpu.SemaphoreType.DMA((15,)), pltpu.SemaphoreType.DMA((6,))],
        compiler_params=pltpu.CompilerParams(vmem_limit_bytes=56 * MIB),
        cost_estimate=pl.CostEstimate(flops=4_000_000_000, bytes_accessed=20_000_000, transcendentals=0),
    )(*partials, *stats, *roots, *params)


def fast_local(
    wide,
    narrow,
    hidden_in,
    out_cot,
    lengths,
    norm_gain,
    w_zx,
    w_bc,
    w_dt,
    conv_x,
    conv_bc,
    head_params,
    out_gain,
    w_out,
    left_statistic_gate,
    stat_right_zx,
    stat_left_out,
    stat_right_out,
    inverse_root_left_gate,
    inverse_root_right_gate,
    root_left_out,
    root_right_out,
):
    heads, shard = w_dt.shape[1], norm_gain.shape[0]
    out_rows, dt_rows = w_out.T, jnp.transpose(w_dt, (1, 2, 0))
    block, grad, *partials = run_layer(
        lengths,
        hidden_in,
        out_cot,
        norm_gain,
        w_zx,
        out_rows,
        w_bc,
        dt_rows,
        conv_x,
        conv_bc,
        head_params,
        out_gain,
        heads,
        shard,
        wide,
        narrow,
    )
    (
        block_out,
        in_grad,
        clip,
        g_zx,
        new_zx,
        new_l,
        new_r,
        g_out,
        new_out,
        new_lo,
        new_ro,
        g_bc,
        new_bc,
        g_dt,
        new_dt,
        *rest,
    ) = run_finish(
        (*partials, block, grad),
        (left_statistic_gate[:, 0], stat_right_zx, stat_left_out, stat_right_out[0]),
        (inverse_root_left_gate[:, 0], inverse_root_right_gate, root_left_out, root_right_out[0]),
        (w_zx, out_rows, w_bc, dt_rows, conv_x, conv_bc, head_params, out_gain, norm_gain),
        hidden_in.shape,
        wide,
        narrow,
    )
    return (
        block_out,
        in_grad,
        clip.reshape(()),
        g_zx,
        new_zx,
        new_l[:, None],
        new_r,
        g_out.T,
        new_out.T,
        new_lo,
        new_ro[None],
        g_bc,
        new_bc,
        jnp.transpose(g_dt, (2, 0, 1)),
        jnp.transpose(new_dt, (2, 0, 1)),
        *rest,
    )


def solution(mesh):
    wide, narrow = mesh.shape["wide"], mesh.shape["narrow"]
    body = functools.partial(fast_local, wide, narrow) if (wide, narrow) == (8, 4) else local
    return jax.shard_map(
        body,
        mesh=mesh,
        in_specs=(
            P(("wide", "narrow"), None),
            P(("wide", "narrow"), None),
            P("wide"),
            P("narrow"),
            P(None, "wide", "narrow"),
            P("wide", None),
            P("wide", "narrow", None),
            P(None, "narrow"),
            P(),
            P(None, "narrow"),
            P("narrow"),
            P("narrow", "wide"),
            P(None, "narrow", "wide", None),
            P(None, "narrow", None),
            P("narrow", None),
            P("narrow", "wide", None),
            P(None, "narrow", "wide", None),
            P(None, "narrow", None),
            P("narrow", None),
            P("narrow", "wide", None),
        ),
        out_specs=(
            P(("wide", "narrow"), None),
            P(("wide", "narrow"), None),
            P(),
            P(None, "wide", "narrow"),
            P(None, "wide", "narrow"),
            P(None, "narrow", "wide", None),
            P(None, "narrow", None),
            P("narrow", "wide"),
            P("narrow", "wide"),
            P("narrow", None),
            P("narrow", "wide", None),
            P("wide", None),
            P("wide", None),
            P("wide", "narrow", None),
            P("wide", "narrow", None),
            P(None, "narrow"),
            P(None, "narrow"),
            P(),
            P(),
            P(None, "narrow"),
            P(None, "narrow"),
            P("narrow"),
            P("narrow"),
            P("narrow"),
            P("narrow"),
        ),
        check_vma=False,
    )
```

```python
import functools

import jax
import jax.numpy as jnp
from jax import lax
from jax.experimental import pallas as pl
from jax.experimental.pallas import tpu as pltpu
from jax.sharding import PartitionSpec as P

SPAN = 128
WIDTH = 64
HIGH = lax.Precision.HIGH
F32 = jnp.float32
NN = (((1,), (0,)), ((), ()))
NT = (((1,), (1,)), ((), ()))
TN = (((0,), (0,)), ((), ()))
TT = (((0,), (1,)), ((), ()))


def dot(a, b, dims=NN):
    return lax.dot_general(a, b, dims, precision=HIGH, preferred_element_type=F32)


def halves(v):
    hi = v.astype(jnp.bfloat16)
    return hi, (v - hi.astype(F32)).astype(jnp.bfloat16)


def product(a, b, dims=NN):
    (ah, al), (bh, bl) = a, b
    (left,), (right,) = dims[0]
    rows, depth = ah.shape[1 - left], ah.shape[left]

    def times(u, v):
        return lax.dot_general(u, v, dims, preferred_element_type=F32)

    if depth < 128:
        return times(
            jnp.concatenate([ah, al, ah], axis=left), jnp.concatenate([bh, bh, bl], axis=right)
        )
    if depth == 128:
        top = jnp.concatenate([ah, ah], axis=left)
        low = jnp.concatenate([al, jnp.zeros_like(al)], axis=left)
        out = times(jnp.concatenate([top, low], axis=1 - left), jnp.concatenate([bh, bl], axis=right))
        return out[0:rows] + out[rows:]
    out = times(jnp.concatenate([ah, al], axis=1 - left), bh)
    return out[0:rows] + out[rows:] + times(ah, bl)


def dot3(a, b, dims=NN):
    return product(halves(a), halves(b), dims)


def sigmoid(v):
    return 1.0 / (1.0 + jnp.exp(-v))


def split3(v):
    hi = v.astype(jnp.bfloat16)
    rest = v - hi.astype(F32)
    mid = rest.astype(jnp.bfloat16)
    lo = (rest - mid.astype(F32)).astype(jnp.bfloat16)
    return jnp.concatenate([hi, mid, lo], axis=0)


def exact_dot(v, ones):
    rows = v.shape[0]
    out = lax.dot_general(split3(v), ones, NN, preferred_element_type=F32)
    return out[0:rows] + out[rows : 2 * rows] + out[2 * rows : 3 * rows]


def iota(shape, axis):
    return lax.broadcasted_iota(jnp.int32, shape, axis)


def shift_right(v, count):
    return jnp.where(iota(v.shape, 1) >= count, pltpu.roll(v, count, axis=1), 0.0)


def shift_left(v, count):
    length = v.shape[1]
    return jnp.where(iota(v.shape, 1) < length - count, pltpu.roll(v, length - count, axis=1), 0.0)


def conv_rows(v, taps):
    count = taps.shape[1]
    total = taps[:, count - 1 : count] * v
    for j in range(count - 1):
        total = total + taps[:, j : j + 1] * shift_right(v, count - 1 - j)
    return total


def pieces(ref, chans, state):
    bc = 2 * chans
    dt = bc + 4 * state
    return ref.at[0:chans], ref.at[chans:bc], ref.at[bc:dt], ref.at[dt : dt + 16]


def convolve(x_ref, bc_ref, live_ref, cx_ref, cbc_ref, xc_ref, dx_act_ref, b_ref, c_ref, dbc_act_ref):
    chans, tokens = xc_ref.shape
    state = c_ref.shape[0] // 2
    live = live_ref[...]

    def conv_x_rows(i, _):
        rows = pl.ds(pl.multiple_of(i * 8, 8), 8)
        u = conv_rows(x_ref[rows, :], cx_ref[rows, :])
        s = sigmoid(u)
        xc_ref[rows, :] = u * s * live
        dx_act_ref[rows, :] = (s + u * s * (1.0 - s)) * live
        return 0

    lax.fori_loop(0, chans // 8, conv_x_rows, 0, unroll=2)

    def conv_bc_rows(i, _, src, dst, dst_row, shift):
        rows = pl.ds(pl.multiple_of(src * state + i * 8, 8), 8)
        out = pl.ds(pl.multiple_of(dst_row + i * 8, 8), 8)
        u = conv_rows(bc_ref[rows, :], cbc_ref[rows, :])
        s = sigmoid(u)
        dbc_act_ref[rows, :] = s + u * s * (1.0 - s)
        v = u * s
        if shift == 1:
            v = shift_right(v, 1)
        if shift == -1:
            v = shift_left(v, 1)
        dst[out, :] = v
        return 0

    for src, dst, row, shift in ((0, b_ref, 0, 0), (1, c_ref, 0, 1), (2, b_ref, state, 0), (3, c_ref, state, -1)):
        lax.fori_loop(
            0,
            state // 8,
            functools.partial(conv_bc_rows, src=src, dst=dst, dst_row=row, shift=shift),
            0,
            unroll=2,
        )


def step_sizes(pre_ref, hp_ref, step_ref, cum_ref, cumex_ref, heads):
    blocks = pre_ref.shape[1] // SPAN
    pre = pre_ref[...] + hp_ref[:, 0:1]
    steps = jnp.maximum(pre, 0.0) + jnp.log1p(jnp.exp(-jnp.abs(pre)))
    step_ref[...] = steps
    logs = -hp_ref[:, 1:2] * steps
    rows16 = iota((16, SPAN), 0)
    lane16 = iota((16, SPAN), 1)
    row_q = iota((SPAN, SPAN), 0)
    lane_q = iota((SPAN, SPAN), 1)
    upto = (row_q <= lane_q).astype(F32).astype(jnp.bfloat16)
    downto = (row_q >= lane_q).astype(F32).astype(jnp.bfloat16)
    both = jnp.concatenate([upto, downto], axis=1)
    for b in range(blocks):
        sums = exact_dot(logs[:, b * SPAN : (b + 1) * SPAN], both)
        cum = jnp.where(rows16 < heads, sums[:, 0:SPAN], sums[:, SPAN : 2 * SPAN])
        ex_f = jnp.where(lane16 >= 1, pltpu.roll(cum, 1, axis=1), 0.0)
        ex_r = jnp.where(lane16 < SPAN - 1, pltpu.roll(cum, SPAN - 1, axis=1), 0.0)
        cum_ref[:, b * SPAN : (b + 1) * SPAN] = cum
        cumex_ref[:, b * SPAN : (b + 1) * SPAN] = jnp.where(rows16 < heads, ex_f, ex_r)


def states(xc_ref, b_ref, step_ref, cum_ref, sloc_ref, hcat_ref, heads):
    blocks = xc_ref.shape[1] // SPAN
    state = b_ref.shape[0] // 2

    def local_states(b, _):
        sl = pl.ds(pl.multiple_of(b * SPAN, SPAN), SPAN)
        bcat = spread(b_ref[:, sl], state)
        tail = tails(cum_ref[:, sl], step_ref[:, sl], heads)
        left = tailed(xc_ref[:, sl], tail, range(heads), heads)
        sloc_ref[b] = dot3(left, bcat, NT)
        return 0

    lax.fori_loop(0, blocks, local_states, 0)

    lane_h = iota((WIDTH, 2 * state), 1)
    for h in range(heads):
        rows = slice(h * WIDTH, (h + 1) * WIDTH)
        carry = jnp.zeros((WIDTH, 2 * state), F32)
        for i in range(blocks):
            r = blocks - 1 - i
            hcat_ref[i, rows, 0:state] = carry[:, 0:state]
            hcat_ref[r, rows, state : 2 * state] = carry[:, state : 2 * state]
            tot_f = jnp.exp(cum_ref[h : h + 1, (i + 1) * SPAN - 1 : (i + 1) * SPAN])
            tot_r = jnp.exp(cum_ref[heads + h : heads + h + 1, r * SPAN : r * SPAN + 1])
            factor = jnp.where(lane_h < state, tot_f, tot_r)
            piece = jnp.where(lane_h < state, sloc_ref[i, rows, :], sloc_ref[r, rows, :])
            carry = carry * factor + piece


def outputs(z_ref, xc_ref, b_ref, c_ref, step_ref, cum_ref, cumex_ref, hcat_ref, hp_ref, y_ref, inner_ref, heads, emit):
    blocks = xc_ref.shape[1] // SPAN
    state = b_ref.shape[0] // 2
    row_q = iota((SPAN, SPAN), 0)
    lane_q = iota((SPAN, SPAN), 1)
    lower = row_q < lane_q
    diag = row_q == lane_q

    def block(b, _):
        sl = pl.ds(pl.multiple_of(b * SPAN, SPAN), SPAN)
        bb, cc = b_ref[:, sl], c_ref[:, sl]
        inner = jnp.where(
            lower, dot3(bb[0:state], cc[0:state], TN), dot3(bb[state:], cc[state:], TN)
        )
        inner_ref[b] = inner
        cum, steps, cumex = cum_ref[:, sl], step_ref[:, sl], cumex_ref[:, sl]
        scale = jnp.exp(cumex)
        cols = columns(cum, steps)
        sums = None
        entering = dot3(hcat_ref[b], spread(cc, state))
        x_parts = halves(xc_ref[:, sl])
        for h in range(heads):
            rows = slice(h * WIDTH, (h + 1) * WIDTH)
            decay = decays(cols, cumex, lower, diag, h, heads)
            mt = jnp.where(diag, hp_ref[h : h + 1, 2:3], inner * decay)
            y = product((x_parts[0][rows], x_parts[1][rows]), halves(mt))
            y = y + entering[rows, 0:SPAN] * scale[h : h + 1]
            y = y + entering[rows, SPAN:] * scale[heads + h : heads + h + 1]
            z = z_ref[rows, sl]
            y_ref[rows, sl] = y
            sums = emit(b, sl, h, rows, y * (z * sigmoid(z)), sums)
        return 0

    lax.fori_loop(0, blocks, block, 0)


def fwd_kernel(
    heads,
    proj_ref,
    live_ref,
    cx_ref,
    cbc_ref,
    hp_ref,
    y_ref,
    xc_ref,
    dx_act_ref,
    b_ref,
    c_ref,
    dbc_act_ref,
    step_ref,
    cum_ref,
    cumex_ref,
    hcat_ref,
    inner_ref,
    gated_ref,
    sq_ref,
    sloc_ref,
):
    z_ref, x_ref, bc_ref, pre_ref = pieces(proj_ref, xc_ref.shape[0], c_ref.shape[0] // 2)
    convolve(x_ref, bc_ref, live_ref, cx_ref, cbc_ref, xc_ref, dx_act_ref, b_ref, c_ref, dbc_act_ref)
    step_sizes(pre_ref, hp_ref, step_ref, cum_ref, cumex_ref, heads)
    states(xc_ref, b_ref, step_ref, cum_ref, sloc_ref, hcat_ref, heads)

    def emit(b, sl, h, rows, gated, total):
        gated_ref[rows, sl] = gated
        part = jnp.sum(gated * gated, axis=0, keepdims=True)
        total = part if total is None else total + part
        if h == heads - 1:
            sq_ref[:, sl] = total
        return total

    outputs(z_ref, xc_ref, b_ref, c_ref, step_ref, cum_ref, cumex_ref, hcat_ref, hp_ref, y_ref, inner_ref, heads, emit)


def spread(bb, state):
    zero = jnp.zeros((state, SPAN), F32)
    top = jnp.concatenate([bb[0:state], zero], axis=1)
    low = jnp.concatenate([zero, bb[state:]], axis=1)
    return jnp.concatenate([top, low], axis=0)


def tails(cum, steps, heads):
    rows = iota((16, SPAN), 0)
    last = jnp.where(rows[:, 0:1] < heads, cum[:, SPAN - 1 : SPAN], cum[:, 0:1])
    return jnp.exp(last - cum) * steps


def tailed(xc, tail, chosen, heads):
    parts = []
    for i, h in enumerate(chosen):
        x = xc[i * WIDTH : (i + 1) * WIDTH]
        parts.append(
            jnp.concatenate([x * tail[h : h + 1], x * tail[heads + h : heads + h + 1]], axis=1)
        )
    return jnp.concatenate(parts, axis=0)


def columns(cum, steps):
    pad = jnp.zeros((SPAN - 32, SPAN), F32)
    return jnp.transpose(jnp.concatenate([cum, steps, pad], axis=0))


def decays(cols, cumex, lower, diag, h, heads):
    f, r = h, heads + h
    arg = jnp.where(
        lower, cumex[f : f + 1] - cols[:, f : f + 1], cumex[r : r + 1] - cols[:, r : r + 1]
    )
    step = jnp.where(lower, cols[:, 16 + f : 17 + f], cols[:, 16 + r : 17 + r])
    return jnp.where(diag, 0.0, jnp.exp(arg) * step)


def gate_back(z_ref, y_ref, don_ref, rms, coef, og_ref, dy_ref, dz_ref, dog_ref, onorm_ref=None):
    chans = y_ref.shape[0]

    def gate_rows(i, _):
        rows = pl.ds(pl.multiple_of(i * 8, 8), 8)
        z, y, don, og = z_ref[rows, :], y_ref[rows, :], don_ref[rows, :], og_ref[rows, :]
        s = sigmoid(z)
        act = z * s
        gated = y * act
        normed = rms * don
        dog_ref[rows, 0:1] = jnp.sum(gated * normed, axis=1, keepdims=True)
        dgated = normed * og - gated * coef
        dy_ref[rows, :] = dgated * act
        dz_ref[rows, :] = dgated * y * (s + act * (1.0 - s))
        if onorm_ref is not None:
            onorm_ref[rows, :] = gated * rms * og
        return 0

    lax.fori_loop(0, chans // 8, gate_rows, 0, unroll=2)


def back_intra(xc_ref, c_ref, inner_ref, step_ref, cum_ref, cumex_ref, hcat_ref, hp_ref, dy_s, dxc_s, dh_s, dc_s, din_s, g_s, cv_s, dd_s, chosen, heads, tick):
    blocks = xc_ref.shape[1] // SPAN
    state = c_ref.shape[0] // 2
    lower = iota((SPAN, SPAN), 0) < iota((SPAN, SPAN), 1)
    diag = iota((SPAN, SPAN), 0) == iota((SPAN, SPAN), 1)
    first = chosen[0] == 0

    def block(b, put):
        sl = pl.ds(pl.multiple_of(b * SPAN, SPAN), SPAN)
        cc = c_ref[:, sl]
        inner = inner_ref[b]
        cumex = cumex_ref[:, sl]
        scale = jnp.exp(cumex)
        cols = columns(cum_ref[:, sl], step_ref[:, sl])
        dinner = jnp.zeros((SPAN, SPAN), F32) if first else din_s[b]
        dcc = jnp.zeros((2 * state, SPAN), F32) if first else dc_s[:, sl]
        for h in chosen:
            f, r = h, heads + h
            rows = slice(h * WIDTH, (h + 1) * WIDTH)
            decay = decays(cols, cumex, lower, diag, h, heads)
            mt = inner * decay
            e_f, e_r = scale[f : f + 1], scale[r : r + 1]
            ce = jnp.concatenate([cc[0:state] * e_f, cc[state:] * e_r], axis=0)
            x = xc_ref[rows, sl]
            dy = dy_s[rows, sl]
            dy_parts = halves(dy)
            left = jnp.concatenate([x, hcat_ref[b, rows, :]], axis=1)
            back = product(halves(left), dy_parts, TN)
            dmt, dce = back[0:SPAN], back[SPAN:]
            dinner = dinner + dmt * decay
            w = dmt * mt
            over_f = jnp.sum(jnp.where(lower, w, 0.0), axis=0, keepdims=True)
            over_r = jnp.sum(jnp.where(lower, 0.0, w), axis=0, keepdims=True)
            prod = dce * ce
            put(g_s, (slice(f, f + 1), sl), over_f + jnp.sum(prod[0:state], axis=0, keepdims=True))
            put(g_s, (slice(r, r + 1), sl), over_r + jnp.sum(prod[state:], axis=0, keepdims=True))
            dcc = dcc + jnp.concatenate([dce[0:state] * e_f, dce[state:] * e_r], axis=0)
            right = jnp.concatenate(
                [jnp.where(lower, mt, 0.0), jnp.where(lower, 0.0, mt), ce], axis=0
            )
            out = product(dy_parts, halves(right), NT)
            dx_f, dx_r = out[:, 0:SPAN], out[:, SPAN : 2 * SPAN]
            put(dh_s, (b, rows, slice(None)), out[:, 2 * SPAN :])
            put(cv_s, (slice(f, f + 1), sl), jnp.sum(x * dx_f, axis=0, keepdims=True))
            put(cv_s, (slice(r, r + 1), sl), jnp.sum(x * dx_r, axis=0, keepdims=True))
            put(dd_s, (slice(h, h + 1), sl), jnp.sum(x * dy, axis=0, keepdims=True))
            put(dxc_s, (rows, sl), dx_f + dx_r + hp_ref[h : h + 1, 2:3] * dy)
        put(din_s, (b,), dinner)
        put(dc_s, (slice(None), sl), dcc)

    two_at_a_time(blocks, block, tick)


def two_at_a_time(blocks, block, tick):
    def body(i, _):
        stores = []
        for b in (2 * i, 2 * i + 1):
            block(b, lambda ref, at, value: stores.append((ref, at, value)))
        for ref, at, value in stores:
            ref[at] = value
        tick(2 * i)
        tick(2 * i + 1)
        return 0

    lax.fori_loop(0, blocks // 2, body, 0)


def back_states(cum_ref, hcat_ref, dh_s, tq_s, state, chosen, heads):
    blocks = hcat_ref.shape[0]
    lane_h = iota((WIDTH, 2 * state), 1)
    lane_1 = iota((1, 2 * state), 1)
    for h in chosen:
        rows = slice(h * WIDTH, (h + 1) * WIDTH)
        carry = jnp.zeros((WIDTH, 2 * state), F32)
        for i in range(blocks):
            f = blocks - 1 - i
            tot_f = jnp.exp(cum_ref[h : h + 1, (f + 1) * SPAN - 1 : (f + 1) * SPAN])
            tot_r = jnp.exp(cum_ref[heads + h : heads + h + 1, i * SPAN : i * SPAN + 1])
            factor = jnp.where(lane_h < state, tot_f, tot_r)
            direct = jnp.where(lane_h < state, dh_s[f, rows, :], dh_s[i, rows, :])
            kept = jnp.where(lane_h < state, hcat_ref[f, rows, :], hcat_ref[i, rows, :])
            scaled = carry * factor
            dots = jnp.sum(scaled * kept, axis=0, keepdims=True)
            q_f = jnp.sum(jnp.where(lane_1 < state, dots, 0.0), axis=1, keepdims=True)
            q_r = jnp.sum(jnp.where(lane_1 < state, 0.0, dots), axis=1, keepdims=True)
            tq_s[f, h : h + 1, :] = jnp.broadcast_to(q_f, (1, SPAN))
            tq_s[i, heads + h : heads + h + 1, :] = jnp.broadcast_to(q_r, (1, SPAN))
            dh_s[f, rows, 0:state] = carry[:, 0:state]
            dh_s[i, rows, state:] = carry[:, state:]
            carry = scaled + direct


def back_inter(xc_ref, b_ref, step_ref, cum_ref, dxc_s, dh_s, db_s, v_s, chosen, heads, tick):
    blocks = xc_ref.shape[1] // SPAN
    state = b_ref.shape[0] // 2
    first = chosen[0] == 0
    group = slice(chosen[0] * WIDTH, (chosen[-1] + 1) * WIDTH)

    def block(b, put):
        sl = pl.ds(pl.multiple_of(b * SPAN, SPAN), SPAN)
        bcat = spread(b_ref[:, sl], state)
        tail = tails(cum_ref[:, sl], step_ref[:, sl], heads)
        xc = xc_ref[group, sl]
        dxc = dxc_s[group, sl]
        dsl = halves(dh_s[b, group, :])
        dleft = product(dsl, halves(bcat))
        dbs = product(dsl, halves(tailed(xc, tail, chosen, heads)), TN)
        db = jnp.concatenate([dbs[0:state, 0:SPAN], dbs[state:, SPAN:]], axis=0)
        put(db_s, (slice(None), sl), db if first else db_s[:, sl] + db)
        parts = []
        for i, h in enumerate(chosen):
            f, r = h, heads + h
            part = slice(i * WIDTH, (i + 1) * WIDTH)
            tx_f = dleft[part, 0:SPAN] * tail[f : f + 1]
            tx_r = dleft[part, SPAN:] * tail[r : r + 1]
            put(v_s, (slice(f, f + 1), sl), jnp.sum(xc[part] * tx_f, axis=0, keepdims=True))
            put(v_s, (slice(r, r + 1), sl), jnp.sum(xc[part] * tx_r, axis=0, keepdims=True))
            parts.append(dxc[part] + tx_f + tx_r)
        put(dxc_s, (group, sl), jnp.concatenate(parts, axis=0))

    two_at_a_time(blocks, block, tick)


def back_logs(b_ref, c_ref, pre_ref, step_ref, hp_ref, ddt_ref, dhp_ref, db_s, dc_s, din_s, g_s, cv_s, v_s, dd_s, tq_s, heads):
    blocks = pre_ref.shape[1] // SPAN
    state = b_ref.shape[0] // 2
    row_q = iota((SPAN, SPAN), 0)
    lane_q = iota((SPAN, SPAN), 1)
    lower = row_q < lane_q
    strict = (row_q > lane_q).astype(F32)
    weak = (row_q >= lane_q).astype(F32)
    strict_t = (row_q < lane_q).astype(F32)
    weak_t = (row_q <= lane_q).astype(F32)
    tri = jnp.concatenate(
        [
            jnp.concatenate([strict, strict_t], axis=1),
            jnp.concatenate([weak, weak_t], axis=1),
            jnp.concatenate([strict_t, strict], axis=1),
        ],
        axis=0,
    ).astype(jnp.bfloat16)
    rows16 = iota((16, SPAN), 0)
    used = rows16 < 2 * heads
    rate = hp_ref[:, 1:2]

    def block(b, carry):
        bias_sum, log_sum, skip_sum = carry
        sl = pl.ds(pl.multiple_of(b * SPAN, SPAN), SPAN)
        dinner = din_s[b]
        both = jnp.concatenate(
            [jnp.where(lower, dinner, 0.0), jnp.where(lower, 0.0, dinner)], axis=0
        )
        dc_s[:, sl] = dc_s[:, sl] + dot3(spread(b_ref[:, sl], state), both)
        db = dot3(c_ref[:, sl], both, NT)
        db_s[0:state, sl] = db_s[0:state, sl] + db[0:state, 0:SPAN]
        db_s[state:, sl] = db_s[state:, sl] + db[state:, SPAN:]
        g = jnp.where(used, g_s[:, sl], 0.0)
        c = jnp.where(used, cv_s[:, sl], 0.0)
        v = jnp.where(used, v_s[:, sl], 0.0)
        steps = step_ref[:, sl]
        sums = exact_dot(jnp.concatenate([g, -c, v], axis=1), tri)
        dlog = jnp.where(rows16 < heads, sums[:, 0:SPAN], sums[:, SPAN:])
        dlog = dlog + jnp.where(used, tq_s[b], 0.0)
        pre = pre_ref[:, sl] + hp_ref[:, 0:1]
        small = steps < 1e-30
        ratio = jnp.where(small, 1.0, sigmoid(pre) / jnp.where(small, 1.0, steps))
        dpre = (c + v) * ratio - rate * dlog * sigmoid(pre)
        ddt_ref[:, sl] = dpre
        skip = jnp.where(rows16 < heads, dd_s[:, sl], 0.0)
        return bias_sum + dpre, log_sum - rate * dlog * steps, skip_sum + skip

    zeros16 = jnp.zeros((16, SPAN), F32)
    bias_sum, log_sum, skip = lax.fori_loop(0, blocks, block, (zeros16, zeros16, zeros16))
    dhp_ref[:, 0:1] = jnp.sum(bias_sum, axis=1, keepdims=True)
    dhp_ref[:, 1:2] = jnp.sum(log_sum, axis=1, keepdims=True)
    dhp_ref[:, 2:3] = jnp.sum(skip, axis=1, keepdims=True)


def conv_back(du, v, taps):
    count = taps.shape[1]
    dv = taps[:, count - 1 : count] * du
    sums = [jnp.sum(du * v, axis=1, keepdims=True)]
    for j in range(count - 2, -1, -1):
        moved = shift_left(du, count - 1 - j)
        dv = dv + taps[:, j : j + 1] * moved
        sums.append(jnp.sum(moved * v, axis=1, keepdims=True))
    return dv, sums[::-1]


def conv_x_back(xin_ref, cx_ref, dx_act_ref, dxc_s, dxin_ref, dcx_ref, start, count):
    def group(i, _):
        rows = pl.ds(pl.multiple_of(start + i * 8, 8), 8)
        dv, sums = conv_back(dxc_s[rows, :] * dx_act_ref[rows, :], xin_ref[rows, :], cx_ref[rows, :])
        dxin_ref[rows, :] = dv
        for j, item in enumerate(sums):
            dcx_ref[rows, j : j + 1] = item
        return 0

    lax.fori_loop(0, count // 8, group, 0, unroll=2)


def conv_bc_back(bc_ref, cbc_ref, dbc_act_ref, db_s, dc_s, dbc_ref, dcbc_ref):
    state = db_s.shape[0] // 2

    def group(i, _, src, grad, grad_row, shift):
        rows = pl.ds(pl.multiple_of(src * state + i * 8, 8), 8)
        from_rows = pl.ds(pl.multiple_of(grad_row + i * 8, 8), 8)
        d = grad[from_rows, :]
        if shift == 1:
            d = shift_left(d, 1)
        if shift == -1:
            d = shift_right(d, 1)
        dv, sums = conv_back(d * dbc_act_ref[rows, :], bc_ref[rows, :], cbc_ref[rows, :])
        dbc_ref[rows, :] = dv
        for j, item in enumerate(sums):
            dcbc_ref[rows, j : j + 1] = item
        return 0

    for src, grad, row, shift in ((0, db_s, 0, 0), (1, dc_s, 0, 1), (2, db_s, state, 0), (3, dc_s, state, -1)):
        lax.fori_loop(
            0,
            state // 8,
            functools.partial(group, src=src, grad=grad, grad_row=row, shift=shift),
            0,
            unroll=2,
        )


def pairs_of(heads):
    return [tuple(range(h, min(h + 2, heads))) for h in range(0, heads, 2)]


def bwd_kernel(
    heads,
    proj_ref,
    y_ref,
    xc_ref,
    dx_act_ref,
    b_ref,
    c_ref,
    dbc_act_ref,
    step_ref,
    cum_ref,
    cumex_ref,
    hcat_ref,
    inner_ref,
    don_ref,
    rms_ref,
    coef_ref,
    og_ref,
    cx_ref,
    cbc_ref,
    hp_ref,
    dproj_ref,
    dcx_ref,
    dcbc_ref,
    dhp_ref,
    dog_ref,
    dy_s,
    dxc_s,
    dh_s,
    db_s,
    dc_s,
    din_s,
    g_s,
    cv_s,
    v_s,
    dd_s,
    tq_s,
):
    chans, state = y_ref.shape[0], b_ref.shape[0] // 2
    z_ref, xin_ref, bc_ref, pre_ref = pieces(proj_ref, chans, state)
    dz_ref, dxin_ref, dbc_ref, ddt_ref = pieces(dproj_ref, chans, state)
    gate_back(z_ref, y_ref, don_ref, rms_ref[...], coef_ref[...], og_ref, dy_s, dz_ref, dog_ref)
    for chosen in pairs_of(heads):
        back_intra(
            xc_ref, c_ref, inner_ref, step_ref, cum_ref, cumex_ref, hcat_ref, hp_ref, dy_s, dxc_s, dh_s, dc_s,
            din_s, g_s, cv_s, dd_s, chosen, heads, lambda b: None,
        )
        back_states(cum_ref, hcat_ref, dh_s, tq_s, state, chosen, heads)
        back_inter(xc_ref, b_ref, step_ref, cum_ref, dxc_s, dh_s, db_s, v_s, chosen, heads, lambda b: None)
    conv_x_back(xin_ref, cx_ref, dx_act_ref, dxc_s, dxin_ref, dcx_ref, 0, chans)
    back_logs(
        b_ref, c_ref, pre_ref, step_ref, hp_ref, ddt_ref, dhp_ref, db_s, dc_s, din_s, g_s, cv_s, v_s, dd_s, tq_s, heads
    )
    conv_bc_back(bc_ref, cbc_ref, dbc_act_ref, db_s, dc_s, dbc_ref, dcbc_ref)


def call(kernel, out_shapes, scratch, flops):
    return pl.pallas_call(
        kernel,
        out_shape=[jax.ShapeDtypeStruct(shape, F32) for shape in out_shapes],
        scratch_shapes=[pltpu.VMEM(shape, F32) for shape in scratch],
        compiler_params=pltpu.CompilerParams(vmem_limit_bytes=56 * 1024 * 1024),
        cost_estimate=pl.CostEstimate(flops=flops, bytes_accessed=20_000_000, transcendentals=0),
    )


def run_fwd(proj, live, cx, cbc, hp, heads):
    tokens = proj.shape[1]
    chans, n4 = cx.shape[0], cbc.shape[0]
    blocks = tokens // SPAN
    full, half, rows = (chans, tokens), (n4 // 2, tokens), (16, tokens)
    return call(
        functools.partial(fwd_kernel, heads),
        [full, full, full, half, half, (n4, tokens), rows, rows, rows, (blocks, chans, n4 // 2), (blocks, SPAN, SPAN), full, (1, tokens)],
        [(blocks, chans, n4 // 2)],
        2_000_000_000,
    )(proj, live, cx, cbc, hp)


def run_bwd(proj, kept, don, rms, coef, og, cx, cbc, hp, heads):
    tokens = proj.shape[1]
    chans, n4 = cx.shape[0], cbc.shape[0]
    blocks = tokens // SPAN
    full, half, rows = (chans, tokens), (n4 // 2, tokens), (16, tokens)
    return call(
        functools.partial(bwd_kernel, heads),
        [proj.shape, (chans, 4), (n4, 4), (16, 3), (chans, 1)],
        [full, full, (blocks, chans, n4 // 2), half, half, (blocks, SPAN, SPAN), rows, rows, rows, rows, (blocks, 16, SPAN)],
        4_000_000_000,
    )(proj, *kept, don, rms, coef, og, cx, cbc, hp)


def square_sum(arrays):
    total = jnp.float32(0.0)
    for item in arrays:
        total = total + jnp.sum(item * item)
    return total


def pad_rows(v):
    return jnp.concatenate([v, jnp.zeros((16 - v.shape[0],) + v.shape[1:], v.dtype)], axis=0)


def local(
    hidden_in,
    out_cot,
    lengths,
    norm_gain,
    w_zx,
    w_bc,
    w_dt,
    conv_x,
    conv_bc,
    head_params,
    out_gain,
    w_out,
    left_statistic_gate,
    stat_right_zx,
    stat_left_out,
    stat_right_out,
    inverse_root_left_gate,
    inverse_root_right_gate,
    root_left_out,
    root_right_out,
):
    rows, chans = w_zx.shape[1], w_zx.shape[2]
    heads = w_dt.shape[1]
    n4 = w_bc.shape[1]
    own_rows, width = hidden_in.shape
    narrow_id, wide_id = lax.axis_index("narrow"), lax.axis_index("wide")

    full_in = lax.all_gather(hidden_in, "narrow", axis=0, tiled=True)
    full_gain = lax.all_gather(norm_gain, "narrow", axis=0, tiled=True)
    dt_cols = jnp.transpose(w_dt, (0, 2, 1)).reshape(rows, 2 * heads)
    own_w = jnp.concatenate(
        [w_zx[0], w_zx[1], w_bc, dt_cols, jnp.zeros((rows, 16 - 2 * heads), F32)], axis=1
    )
    w_in = lax.all_gather(own_w, "wide", axis=0, tiled=True)
    wide_out = lax.all_gather(w_out, "wide", axis=1, tiled=True)

    tokens = full_in.shape[0]
    live = (jnp.arange(tokens) < lengths[0]).astype(F32)
    row_start = narrow_id * own_rows
    live_own = lax.dynamic_slice_in_dim(live, row_start, own_rows, 0)
    dbranch = lax.all_gather(live_own[:, None] * out_cot, "narrow", axis=0, tiled=True)

    inv_rms = lax.rsqrt(jnp.mean(full_in * full_in, axis=-1) + 1e-05)
    normed = full_in * inv_rms[:, None] * full_gain
    proj = dot(w_in, normed, TT)
    cx, cbc = conv_x.T, conv_bc.T
    hp = jnp.concatenate(
        [
            pad_rows(head_params[0:2].reshape(2 * heads, 1)),
            pad_rows(jnp.exp(head_params[2:4]).reshape(2 * heads, 1)),
            pad_rows(head_params[4].reshape(heads, 1)),
        ],
        axis=1,
    )
    *kept, gated, squares = run_fwd(proj, live[None, :], cx, cbc, hp, heads)
    donorm = dot(wide_out, dbranch, NT)
    inner = jnp.sum(gated * (donorm * out_gain[:, None]), axis=0, keepdims=True)
    stats = lax.psum(jnp.concatenate([squares, inner], axis=0), "narrow")
    inner_total = chans * lax.axis_size("narrow")
    rms = lax.rsqrt(stats[0:1] / inner_total + 1e-05)
    coef = rms**3 * stats[1:2] / inner_total
    onorm = gated * rms * out_gain[:, None]
    branch = lax.psum_scatter(dot(onorm, wide_out, TN), "narrow", scatter_dimension=0, tiled=True)
    block_out = hidden_in + live_own[:, None] * branch
    g_out = lax.psum(dot(onorm, dbranch), "wide")

    dproj, d_cx, d_cbc, d_hp, d_og = run_bwd(
        proj, kept, donorm, rms, coef, out_gain[:, None], cx, cbc, hp, heads
    )
    d_normed = dot(dproj, w_in, TT)
    d_w = dot(normed, dproj, TT)
    dnormed = lax.psum_scatter(d_normed, "narrow", scatter_dimension=0, tiled=True)
    own_inv = lax.dynamic_slice_in_dim(inv_rms, row_start, own_rows, 0)[:, None]
    total_dot = jnp.sum(hidden_in * full_gain * dnormed, axis=1, keepdims=True)
    in_grad = out_cot + (
        own_inv * full_gain * dnormed - hidden_in * (own_inv**3 * total_dot / width)
    )
    d_gain = jnp.sum(hidden_in * own_inv * dnormed, axis=0)

    g_zx = lax.psum(d_w[:, 0 : 2 * chans], "wide")
    g_dt, g_cx, g_hp, g_og = lax.psum((d_w[:, 2 * chans + n4 :], d_cx, d_hp, d_og), "wide")
    g_bc, g_cbc, g_gain = lax.psum(
        (d_w[:, 2 * chans : 2 * chans + n4], d_cbc, d_gain), ("wide", "narrow")
    )
    shard = norm_gain.shape[0]
    g_ng = lax.dynamic_slice_in_dim(g_gain, narrow_id * shard, shard, 0)
    g_dt = jnp.transpose(g_dt[:, 0 : 2 * heads].reshape(width, 2, heads), (0, 2, 1))
    g_cx, g_cbc, g_og = g_cx.T, g_cbc.T, g_og[:, 0]
    g_head = jnp.concatenate(
        [
            g_hp[0 : 2 * heads, 0].reshape(2, heads),
            g_hp[0 : 2 * heads, 1].reshape(2, heads),
            g_hp[0:heads, 2].reshape(1, heads),
        ],
        axis=0,
    )
    local_squares = square_sum((g_zx, g_out, g_dt, g_cx, g_head, g_og, g_ng))
    total_squares = lax.psum(local_squares, "narrow") + square_sum((g_bc, g_cbc))
    clip_norm = jnp.sqrt(total_squares)
    factor = 1.0 / jnp.maximum(clip_norm, 1.0)
    c_zx, c_out, c_bc, c_dt = g_zx * factor, g_out * factor, g_bc * factor, g_dt * factor
    c_cx, c_cbc, c_head, c_og, c_ng = (
        g_cx * factor,
        g_cbc * factor,
        g_head * factor,
        g_og * factor,
        g_ng * factor,
    )
    halves = (c_zx[:, 0:chans], c_zx[:, chans:])
    own_zx = lax.dynamic_slice_in_dim(c_zx, wide_id * rows, rows, 0)
    own_halves = (own_zx[:, 0:chans], own_zx[:, chans:])
    left_zx = jnp.stack(
        [
            0.5 * left_statistic_gate[m, 0] + 0.5 * dot(own_halves[m], halves[m], NT)
            for m in range(2)
        ]
    )[:, None]
    right_zx = jnp.stack(
        [0.5 * stat_right_zx[m] + 0.5 * dot(halves[m], halves[m], TN) for m in range(2)]
    )
    new_zx = jnp.stack(
        [
            w_zx[m]
            - 0.5
            * dot(dot(inverse_root_left_gate[m, 0], halves[m]), inverse_root_right_gate[m])
            for m in range(2)
        ]
    )
    cols = w_out.shape[1]
    own_out = lax.dynamic_slice_in_dim(c_out, wide_id * cols, cols, 1)
    left_out = 0.5 * stat_left_out + 0.5 * dot(c_out, c_out, NT)
    right_out = 0.5 * stat_right_out + 0.5 * dot(own_out, c_out, TN)[None]
    new_out = w_out - 0.5 * dot(dot(root_left_out, c_out), root_right_out[0], NT)
    own_bc = lax.dynamic_slice_in_dim(c_bc, wide_id * rows, rows, 0)
    own_dt = lax.dynamic_slice_in_dim(c_dt, wide_id * rows, rows, 0)
    rate = 10.0
    return (
        block_out,
        in_grad,
        clip_norm,
        jnp.stack(own_halves),
        new_zx,
        left_zx,
        right_zx,
        own_out,
        new_out,
        left_out,
        right_out,
        own_bc,
        w_bc - rate * own_bc,
        own_dt,
        w_dt - rate * own_dt,
        c_cx,
        conv_x - rate * c_cx,
        c_cbc,
        conv_bc - rate * c_cbc,
        c_head,
        head_params - rate * c_head,
        c_og,
        out_gain - rate * c_og,
        c_ng,
        norm_gain - rate * c_ng,
    )


MESH = pl.DeviceIdType.MESH
MIB = 1024 * 1024


class Place:
    def __init__(self, wide):
        self.wide = wide
        self.depth = wide // 2
        self.w, self.n = lax.axis_index("wide"), lax.axis_index("narrow")
        self.z, self.x = self.w // 2, self.w % 2
        self.y, self.c = self.n // 2, self.n % 2
        self.core = (self.w, self.y * 2 + 1 - self.c)
        self.row = (self.w, (1 - self.y) * 2 + self.c)
        self.corner = (self.w, (1 - self.y) * 2 + 1 - self.c)
        self.across = (self.z * 2 + 1 - self.x, self.n)

    def group(self):
        return [self.core, self.row, self.corner]

    def along(self, k):
        return ((self.z + k) % self.depth) * 2 + self.x, self.n

    def others(self, k):
        return (self.w + k) % self.wide, self.n


class Links:
    def __init__(self, send, recv):
        self.send, self.recv, self.count, self.started = send, recv, 0, []

    def plan(self, src, dst, device):
        i = self.count
        self.count = i + 1
        item = pltpu.make_async_remote_copy(
            src_ref=src,
            dst_ref=dst,
            send_sem=self.send.at[i],
            recv_sem=self.recv.at[i],
            device_id=device,
            device_id_type=MESH,
        )
        self.started.append(item)
        return item

    def copy(self, src, dst, device):
        item = self.plan(src, dst, device)
        item.start()
        return item

    def release(self, items):
        for item in items:
            item.wait_send()
        self.started = [item for item in self.started if all(item is not done for done in items)]

    def drain(self):
        self.release(list(self.started))


def arrived(copies):
    for item in copies:
        item.wait_recv()


def begin(copies):
    for item in copies:
        item.start()


def greet(devices):
    barrier = pltpu.get_barrier_semaphore()
    for device in devices:
        pl.semaphore_signal(barrier, inc=1, device_id=device, device_id_type=MESH)
    return lambda: pl.semaphore_wait(barrier, len(devices))


def as_row(col):
    return jnp.transpose(jnp.broadcast_to(col, (col.shape[0], 128)))[0:1]


def as_col(row):
    return jnp.transpose(jnp.broadcast_to(row, (128, 128)))[:, 0:1]


def flat(v):
    return v.reshape(-1, v.shape[-1])


class Piece:
    def __init__(self, here, links, part, x_rx, z_rx, full, square):
        self.here, self.part, self.x_rx, self.z_rx = here, part, x_rx, z_rx
        self.full, self.square = full, square
        steps = range(1, here.depth)
        place, column = full.at[here.z, here.x], full.at[:, here.x]
        self.first = links.plan(part.at[:, 1 - here.x], x_rx, here.across)
        self.second = [
            links.plan(x_rx.at[(here.z + k) % here.depth], z_rx.at[k - 1], here.along(k)) for k in steps
        ]
        self.third = [links.plan(place, place, here.along(k)) for k in steps]
        self.fourth = links.plan(column, column, here.across)
        self.holding = [self.first]

    def start(self):
        self.first.start()

    def fold(self):
        self.first.wait_recv()
        for k in range(self.here.depth):
            self.x_rx[k] = self.x_rx[k] + self.part[k, self.here.x]
        begin(self.second)

    def own(self):
        arrived(self.second)
        total = self.x_rx[self.here.z]
        for k in range(1, self.here.depth):
            total = total + self.z_rx[k - 1]
        self.full[self.here.z, self.here.x] = total
        begin(self.third)
        self.square[...] = jnp.broadcast_to(total_square(total), self.square.shape)

    def spread(self):
        arrived(self.third)
        self.fourth.start()

    def finish(self):
        self.fourth.wait_recv()


class CrossPiece:
    def __init__(self, here, links, part, z_rx, x_rx, full, square):
        self.here, self.part, self.z_rx, self.x_rx = here, part, z_rx, x_rx
        self.full, self.square = full, square
        steps = range(1, here.depth)
        mine, pair = full.at[here.z, here.x], full.at[here.z]
        self.first = [
            links.plan(part.at[(here.z + k) % here.depth], z_rx.at[k - 1], here.along(k)) for k in steps
        ]
        self.second = links.plan(part.at[here.z, 1 - here.x], x_rx, here.across)
        self.third = links.plan(mine, mine, here.across)
        self.fourth = [links.plan(pair, pair, here.along(k)) for k in steps]
        self.holding = [*self.first, self.second]

    def start(self):
        begin(self.first)

    def fold(self):
        arrived(self.first)
        total = self.part[self.here.z]
        for k in range(1, self.here.depth):
            total = total + self.z_rx[k - 1]
        self.part[self.here.z] = total
        self.second.start()

    def own(self):
        self.second.wait_recv()
        total = self.part[self.here.z, self.here.x] + self.x_rx[...]
        self.full[self.here.z, self.here.x] = total
        self.third.start()
        self.square[...] = jnp.broadcast_to(total_square(total), self.square.shape)

    def spread(self):
        self.third.wait_recv()
        begin(self.fourth)

    def finish(self):
        arrived(self.fourth)


def total_square(v):
    return jnp.sum(jnp.sum(v * v, axis=0, keepdims=True), axis=1, keepdims=True)


def layer_kernel(
    wide,
    heads,
    shard,
    inner_total,
    length_ref,
    hidden_ref,
    cot_ref,
    gain_ref,
    w_ref,
    wout_ref,
    bcw_ref,
    dtw_ref,
    cx_in,
    cbc_in,
    hp_in,
    og_in,
    block_ref,
    grad_ref,
    gfull,
    bc_own,
    dt_own,
    sv_sum,
    norm_ref,
    hq,
    cq,
    wz_g,
    wx_g,
    wo_g,
    bc_g,
    dt_g,
    gain_g,
    dtt,
    gain_col,
    gain_row,
    turn_s,
    cx_ref,
    cbc_ref,
    hp_ref,
    og_ref,
    live_ref,
    inv_ref,
    proj,
    y_s,
    xc,
    dx_act,
    b_s,
    c_s,
    dbc_act,
    step_s,
    cum_s,
    cumex_s,
    hcat,
    inner_s,
    don,
    onorm,
    dy_s,
    dh_s,
    db_s,
    dc_s,
    din_s,
    g_s,
    cv_s,
    v_s,
    dd_s,
    tq_s,
    cols_s,
    dcbc_s,
    dhp_s,
    dog_s,
    dgain_s,
    stat_own,
    stat_g,
    part,
    x_rx,
    z_rx,
    zz_rx,
    xx_rx,
    core_rx,
    row_rx,
    gbc,
    bc_core,
    bc_row,
    bc_mine,
    bc_rx,
    gdt,
    dt_rx,
    shared_g,
    sv_g,
    sw_g,
    norm_n,
    norm_w,
    square_s,
    hq_hi,
    hq_lo,
    wt_hi,
    wt_lo,
    send,
    recv,
    stat_send,
    stat_recv,
):
    here = Place(wide)
    links = Links(send, recv)
    w, n, z, x, y, c, depth = here.w, here.n, here.z, here.x, here.y, here.c, here.depth
    group = here.group()
    far = [here.others(k) for k in range(1, wide)]
    own_rows, width = hidden_ref.shape
    chans, tokens = y_s.shape
    state = b_s.shape[0] // 2
    blocks = tokens // SPAN
    parts = tokens // own_rows
    thirds = chans // 128
    z_ref, x_ref, bc_ref, pre_ref = pieces(proj, chans, state)
    met = greet(group + far)
    jobs = []
    crossing = (2 * thirds - 1, 2 * thirds)
    for i in range(3 * thirds):
        source = part.at[i if i < 2 * thirds else i - thirds]
        k = sum(1 for other in crossing if other < i)
        if i in crossing:
            jobs.append(CrossPiece(here, links, source, zz_rx.at[k], xx_rx.at[k], gfull.at[i], square_s.at[i]))
        else:
            jobs.append(Piece(here, links, source, x_rx.at[i - k], z_rx.at[i - k], gfull.at[i], square_s.at[i]))
    z_jobs, x_jobs, o_jobs = jobs[0:thirds], jobs[thirds : 2 * thirds], jobs[2 * thirds :]

    half = bcw_ref.shape[0] // 2
    wx_g[z, x] = w_ref[1]
    bc_g[z, x, c] = bcw_ref[pl.ds(pl.multiple_of(c * half, 8), half), :]
    dt_g[z, x] = jnp.zeros(dt_g.shape[2:], F32)
    for h in range(heads):
        for i in range(2):
            row = i * heads + h
            dt_g[z, x, row : row + 1, 0 : dtw_ref.shape[2]] = dtw_ref[h, i : i + 1, :]
    line = gain_ref[...].reshape(1, shard)
    gain_g[n] = jnp.zeros(gain_g.shape[1:], F32)
    for i in range((shard + 127) // 128):
        size = min(128, shard - 128 * i)
        gain_g[n, i : i + 1, 0:size] = line[:, 128 * i : 128 * i + size]
    squares = jnp.zeros((1, own_rows), F32)
    for i in range(width // 128):
        turned = jnp.transpose(hidden_ref[:, i * 128 : (i + 1) * 128])
        squares = squares + jnp.sum(turned * turned, axis=0, keepdims=True)
        hq[n, i * 128 : (i + 1) * 128, :] = turned
    inv_ref[...] = lax.rsqrt(squares / width + 1e-05)
    for i in range(width // 128):
        hq[n, i * 128 : (i + 1) * 128, :] = hq[n, i * 128 : (i + 1) * 128, :] * inv_ref[...]
    met()

    def along(ref):
        return [links.copy(ref, ref, here.along(k)) for k in range(1, depth)]

    def exchange(ref):
        return [links.copy(ref, ref, here.row), links.copy(ref, ref, here.core)]

    class Relay:
        def __init__(self, *views):
            self.views = views
            self.direct = [along(view(z)) for view in views]
            self.passed = []

        def begin(self):
            self.passed = [links.copy(view(z), view(z), here.across) for view in self.views]

        def forward(self, steps=tuple(range(1, depth))):
            for k in steps:
                source = (z + depth - k) % depth
                for view, copies in zip(self.views, self.direct):
                    copies[k - 1].wait_recv()
                    self.passed.append(links.copy(view(source), view(source), here.across))

        def wait(self):
            arrived(self.passed)

    split = chans - 128

    class Cross:
        def __init__(self, ref):
            self.mine, self.pair = ref.at[z, x, :, split:], ref.at[z, :, :, split:]

        def begin(self):
            self.across = links.copy(self.mine, self.mine, here.across)

        def forward(self):
            self.across.wait_recv()
            self.sent = along(self.pair)

        def wait(self):
            arrived(self.sent)

    h_copies = exchange(hq.at[n])
    gain_copies = [links.copy(gain_g.at[n], gain_g.at[n], device) for device in group]
    early = Relay(lambda i: bc_g.at[i, x, c], lambda i: dt_g.at[i, x])
    early.begin()
    first_cross, second_cross, third_cross = Cross(wx_g), Cross(wz_g), Cross(wo_g)
    first_cross.begin()
    first = Relay(lambda i: wx_g.at[i, x, :, 0:split])
    first.begin()

    wz_g[z, x] = w_ref[0]
    wo_g[z, x] = wout_ref[...]
    live_ref[...] = jnp.where(iota((1, tokens), 1) < length_ref[0], 1.0, 0.0)
    live_own = live_ref[:, pl.ds(pl.multiple_of(n * own_rows, 128), own_rows)]
    for i in range(width // 128):
        cq[n, i * 128 : (i + 1) * 128, :] = jnp.transpose(cot_ref[:, i * 128 : (i + 1) * 128]) * live_own
    turn_s[...] = jnp.zeros_like(turn_s)
    for ref, out in ((cx_in, cx_ref), (cbc_in, cbc_ref)):
        for i in range(ref.shape[1] // 128):
            turn_s[0:4, :] = ref[:, i * 128 : (i + 1) * 128]
            out[i * 128 : (i + 1) * 128, :] = jnp.transpose(turn_s[...])[:, 0:4]
    turn_s[...] = jnp.zeros_like(turn_s)
    turn_s[0:1, 0:heads] = hp_in[0:1, :]
    turn_s[0:1, heads : 2 * heads] = hp_in[1:2, :]
    turn_s[1:2, 0:heads] = jnp.exp(hp_in[2:3, :])
    turn_s[1:2, heads : 2 * heads] = jnp.exp(hp_in[3:4, :])
    turn_s[2:3, 0:heads] = hp_in[4:5, :]
    hp_ref[...] = jnp.transpose(turn_s[...])[0:16, 0:3]
    og_line = og_in[...].reshape(1, chans)
    for i in range(thirds):
        og_ref[i * 128 : (i + 1) * 128, :] = as_col(og_line[:, i * 128 : (i + 1) * 128])
    cols_s[...] = jnp.zeros_like(cols_s)
    dcbc_s[...] = jnp.zeros_like(dcbc_s)
    dhp_s[...] = jnp.zeros_like(dhp_s)

    def cut(q):
        hq_hi[q], hq_lo[q] = halves(hq[q])

    cut(n)
    h_copies[1].wait_recv()
    cut(here.core[1])
    first_cross.forward()
    early.forward()
    first.forward()
    second_cross.begin()
    second = Relay(lambda i: wz_g.at[i, x, :, 0:split])
    h_copies[0].wait_recv()
    other = here.row[1]
    h_far = links.copy(hq.at[other], hq.at[other], here.core)
    c_copies = exchange(cq.at[n])
    arrived(gain_copies)
    for q in range(parts):
        turned = jnp.transpose(jnp.concatenate([gain_g[q], jnp.zeros((120, 128), F32)], axis=0))
        for i in range((shard + 127) // 128):
            size = min(128, shard - 128 * i)
            start = shard * q + 128 * i
            gain_col[start : start + size, :] = turned[0:size, i : i + 1]
    for i in range(width // 128):
        gain_row[:, i * 128 : (i + 1) * 128] = as_row(gain_col[i * 128 : (i + 1) * 128, :])

    def turn(ref, row, scale=True):
        for i in range(ref.shape[-1] // 128):
            cols = flat(ref[..., i * 128 : (i + 1) * 128])
            if scale:
                cols = cols * gain_col[...]
            for dst, value in zip((wt_hi, wt_lo), halves(jnp.transpose(cols))):
                dst[row + i * 128 : row + (i + 1) * 128, :] = value

    def quarter(q):
        return pl.ds(pl.multiple_of(q * own_rows, 128), own_rows)

    def each_quarter(body):
        def step(q, _):
            body(q)
            return 0

        lax.fori_loop(0, parts, step, 0)

    def rows_of(start, stop):
        return wt_hi[start:stop, :], wt_lo[start:stop, :]

    def project(out_ref, weights):
        def body(q):
            out_ref[:, quarter(q)] = product(weights(), (hq_hi[q], hq_lo[q]))

        each_quarter(body)

    early.wait()
    bc_core_copy = links.copy(bc_g.at[:, :, c], bc_g.at[:, :, c], here.core)
    lanes = width // wide
    for i in range(wide):
        dtt[:, i * lanes : (i + 1) * lanes] = dt_g[i // 2, i % 2][:, 0:lanes]
    last = 2 * chans + 4 * state
    wt_hi[last:, :], wt_lo[last:, :] = halves(dtt[...] * gain_row[...])
    bc_core_copy.wait_recv()
    turn(bc_g, 2 * chans)
    first.wait()
    first_cross.wait()
    second.begin()
    second.forward((1,))
    second_cross.forward()
    turn(wx_g, chans)
    second.forward((2,))
    h_far.wait_recv()
    cut(here.row[1])
    cut(here.corner[1])
    project(proj.at[chans:], lambda: rows_of(chans, last + 16))
    second.forward((3,))
    third_cross.begin()
    third = Relay(lambda i: wo_g.at[i, x, :, 0:split])
    third.begin()
    c_copies[0].wait_recv()
    c_far = links.copy(cq.at[other], cq.at[other], here.core)
    convolve(x_ref, bc_ref, live_ref, cx_ref, cbc_ref, xc, dx_act, b_s, c_s, dbc_act)
    step_sizes(pre_ref, hp_ref, step_s, cum_s, cumex_s, heads)
    states(xc, b_s, step_s, cum_s, dh_s, hcat, heads)
    second.wait()
    second_cross.wait()
    turn(wz_g, 0)
    project(z_ref, lambda: rows_of(0, chans))
    third.forward()
    third_cross.forward()

    def stat_copy(j, b):
        return pltpu.make_async_remote_copy(
            src_ref=stat_own.at[b],
            dst_ref=stat_g.at[n, b],
            send_sem=stat_send.at[j, b],
            recv_sem=stat_recv.at[j, b],
            device_id=group[j],
            device_id_type=MESH,
        )

    def tell(b, row):
        stats = jnp.broadcast_to(row, (8, SPAN))
        stat_own[b] = stats
        stat_g[n, b] = stats
        for j in range(3):
            stat_copy(j, b).start()

    def told(b):
        for j in range(3):
            stat_copy(j, b).wait_recv()
        total = stat_g[0, b]
        for q in range(1, parts):
            total = total + stat_g[q, b]
        return total[0:1]

    def emit(b, sl, h, rows, gated, sums):
        onorm[rows, sl] = gated
        row = jnp.sum(gated * gated, axis=0, keepdims=True)
        row = row if sums is None else row + sums
        if h == heads - 1:
            tell(b, row)
        return row

    outputs(z_ref, xc, b_s, c_s, step_s, cum_s, cumex_s, hcat, hp_ref, y_s, inner_s, heads, emit)
    rms = jnp.concatenate(
        [lax.rsqrt(told(b) / inner_total + 1e-05) for b in range(blocks)], axis=1
    )

    def scale_rows(i, _):
        rows = pl.ds(pl.multiple_of(i * 8, 8), 8)
        onorm[rows, :] = onorm[rows, :] * rms * og_ref[rows, :]
        return 0

    lax.fori_loop(0, chans // 8, scale_rows, 0, unroll=2)
    c_copies[1].wait_recv()
    c_far.wait_recv()

    def weight_grad(put, right, left=lambda q: (hq_hi[q], hq_lo[q])):
        def body(q):
            put(q, product(left(q), halves(right(q)), NT))

        each_quarter(body)

    block_shape = part.shape[1:]

    def add_to(start, count):
        def put(q, value):
            for i in range(count):
                ref = part.at[start + i]
                piece = value[:, i * 128 : (i + 1) * 128].reshape(block_shape)
                ref[...] = jnp.where(q == 0, piece, ref[...] + piece)

        return put

    def scaled(i):
        part[i] = (flat(part[i]) * gain_col[...]).reshape(block_shape)

    part[...] = jnp.zeros_like(part)
    for start, stop in ((0, 1), (1, thirds)):
        rows = slice(start * 128, stop * 128)
        weight_grad(
            add_to(thirds + start, stop - start),
            lambda q, rows=rows: onorm[rows, quarter(q)],
            lambda q: halves(cq[q]),
        )
        for job in o_jobs[start:stop]:
            job.start()
    third.wait()
    third_cross.wait()
    turn(wo_g, 0, False)

    def donorm(q):
        don[:, quarter(q)] = product(rows_of(0, chans), halves(cq[q]))

    each_quarter(donorm)

    def inner_sums(b, _):
        sl = pl.ds(pl.multiple_of(b * SPAN, SPAN), SPAN)
        gate = z_ref[:, sl]
        gated = y_s[:, sl] * (gate * sigmoid(gate))
        tell(blocks + b, jnp.sum(gated * (don[:, sl] * og_ref[...]), axis=0, keepdims=True))
        return 0

    lax.fori_loop(0, blocks, inner_sums, 0)

    links.release(c_copies + [c_far])

    class Return:
        def __init__(self, rx, row_rx, compute, steps=((), (), (), ())):
            self.rx, self.row_rx = rx, row_rx
            near, away = y * 2, (1 - y) * 2
            self.cores = [
                links.plan(cq.at[away + 1 - c], rx.at[0], here.core),
                links.plan(cq.at[near + 1 - c], rx.at[1], here.core),
            ]
            self.last = links.plan(cq.at[away + c], row_rx, here.row)

            def body(k, _):
                row = 1 - y + (k // 2) * (2 * y - 1)
                q = row * 2 + 1 - c + (k % 2) * (2 * c - 1)
                cq[q] = compute(q)

                @pl.when(k == 0)
                def _():
                    self.cores[0].start()

                @pl.when(k == 2)
                def _():
                    self.cores[1].start()
                    self.cores[0].wait_recv()
                    cq[away + c] = cq[away + c] + rx[0]
                    self.last.start()

                for at, items in enumerate(steps):

                    @pl.when(k == at)
                    def _(items=items):
                        for step in items:
                            step()

                return 0

            lax.fori_loop(0, 4, body, 0)

        def fold(self):
            self.cores[1].wait_recv()
            self.rx[1] = self.rx[1] + cq[y * 2 + c]

        def total(self):
            self.last.wait_recv()
            return self.rx[1] + self.row_rx[...]

    o0, o1, o2 = o_jobs
    z0, z1, z2 = z_jobs
    x0, x1, x2 = x_jobs
    branch = Return(core_rx.at[0], row_rx.at[0], lambda q: dot3(flat(wo_g[...]), onorm[:, quarter(q)]))
    told_inner = jnp.concatenate([told(blocks + b) for b in range(blocks)], axis=1)
    coef = rms**3 * told_inner / inner_total
    gate_back(z_ref, y_s, don, rms, coef, og_ref, dy_s, z_ref, dog_s)
    o0.fold()
    o1.fold()
    weight_grad(add_to(0, thirds), lambda q: z_ref[:, quarter(q)])
    for i, job in enumerate(z_jobs):
        scaled(i)
        job.start()

    def x_grad(i):
        links.release(o_jobs[i].holding)
        part[thirds + i] = jnp.zeros(block_shape, F32)
        weight_grad(add_to(thirds + i, 1), lambda q: x_ref[i * 128 : (i + 1) * 128, quarter(q)])
        scaled(thirds + i)

    within = [
        {3: [o2.fold, o1.own], 5: [o0.own]},
        {1: [o1.spread], 3: [branch.fold], 5: [o2.spread, z1.fold]},
        {5: [z0.spread]},
    ]
    between = [{7: [o2.own]}, {3: [z0.own]}, {}]
    after_states = [(), (), (x0.fold, z2.own)]
    after_conv = [(z0.fold,), (), ()]
    after_grad = [(), (z2.fold, z1.own, o0.spread), (z1.spread,)]

    def run(steps):
        for step in steps:
            step()

    def ticks(plan):
        def tick(b):
            for at, steps in plan.items():

                @pl.when(b == at)
                def _(steps=steps):
                    for step in steps:
                        step()

        return tick

    for i, chosen in enumerate(pairs_of(heads)):
        back_intra(
            xc, c_s, inner_s, step_s, cum_s, cumex_s, hcat, hp_ref, dy_s, y_s, dh_s, dc_s,
            din_s, g_s, cv_s, dd_s, chosen, heads, ticks(within[i]),
        )
        back_states(cum_s, hcat, dh_s, tq_s, state, chosen, heads)
        run(after_states[i])
        back_inter(xc, b_s, step_s, cum_s, y_s, dh_s, db_s, v_s, chosen, heads, ticks(between[i]))
        conv_x_back(x_ref, cx_ref, dx_act, y_s, x_ref, cols_s, i * 128, 128)
        run(after_conv[i])
        x_grad(i)
        x_jobs[i].start()
        run(after_grad[i])

    back_logs(
        b_s, c_s, pre_ref, step_s, hp_ref, pre_ref, dhp_s, db_s, dc_s, din_s, g_s, cv_s, v_s, dd_s, tq_s, heads
    )
    x0.own()
    conv_bc_back(bc_ref, cbc_ref, dbc_act, db_s, dc_s, bc_ref, dcbc_s)
    x1.fold()
    small = 128
    sv_g[w] = jnp.zeros(sv_g.shape[1:], F32)
    for i in range(thirds):
        sl = slice(i * 128, (i + 1) * 128)
        sv_g[w, 0:4, sl] = jnp.transpose(cols_s[sl, :])[0:4]
        sv_g[w, 4:5, sl] = as_row(dog_s[sl, :])
    sv_g[w, :, chans : chans + small] = dhp_s[...]
    sv_copies = [links.copy(sv_g.at[w], sv_g.at[w], device) for device in far]
    gbc_shape = gbc.shape

    def add_bc(q, value):
        gbc[...] = jnp.where(q == 0, value.reshape(gbc_shape), gbc[...] + value.reshape(gbc_shape))

    gbc[...] = jnp.zeros_like(gbc)
    weight_grad(add_bc, lambda q: bc_ref[:, quarter(q)])
    gbc[...] = (flat(gbc[...]) * gain_col[...]).reshape(gbc_shape)
    bc_first = links.copy(gbc.at[:, :, 1 - c], bc_core, here.core)
    x2.fold()
    z2.spread()
    dt_grad = jnp.zeros((16, width), F32)
    for q in range(parts):
        step = halves(pre_ref[:, q * own_rows : (q + 1) * own_rows])
        dt_grad = dt_grad + product(step, (hq_hi[q], hq_lo[q]), NT)
    dt_grad = dt_grad * gain_row[...]
    gdt[...] = jnp.zeros_like(gdt)
    for i in range(wide):
        gdt[i, :, 0:lanes] = dt_grad[:, i * lanes : (i + 1) * lanes]
    dt_rx[w] = gdt[w]
    dt_copies = [links.copy(gdt.at[device[0]], dt_rx.at[w], device) for device in far]
    x0.spread()
    dgain_s[...] = jnp.zeros_like(dgain_s)
    bc_first.wait_recv()
    for k in range(2):
        bc_core[:, k] = bc_core[:, k] + gbc[:, k, c]
    for k in range(wide):
        bc_mine[k] = bc_core[k, 1 - y]
    bc_second = links.copy(bc_mine, bc_row, here.row)

    links.release(branch.cores + [branch.last])

    for k in range(parts):
        pieces_of = []
        for ref, start in ((wz_g, 0), (wx_g, chans), (bc_g, 2 * chans)):
            a, b = max(k * own_rows, start), min((k + 1) * own_rows, start + ref.shape[-1])
            if a < b:
                pieces_of.append(flat(ref[..., a - start : b - start]))
        hq_hi[k], hq_lo[k] = halves(jnp.concatenate(pieces_of, axis=1))

    def normed_back(q):
        sl = quarter(q)

        def add(k, value):
            rows = pl.ds(pl.multiple_of(k * own_rows, 8), own_rows)
            return value + product((hq_hi[k], hq_lo[k]), halves(proj[rows, sl]))

        value = lax.fori_loop(0, parts, add, dot3(dtt[...], pre_ref[:, sl], TN))
        dgain_s[...] = dgain_s[...] + jnp.sum(value * hq[q], axis=1, keepdims=True)
        return value

    back = Return(core_rx.at[1], row_rx.at[1], normed_back, ([x1.own], [x2.own], [x1.spread], [x2.spread]))
    shared_g[n] = jnp.zeros(shared_g.shape[1:], F32)
    for i in range(4 * state // 128):
        sl = slice(i * 128, (i + 1) * 128)
        shared_g[n, 0:4, sl] = jnp.transpose(dcbc_s[sl, :])[0:4]
    for i in range(width // 128):
        shared_g[n, 8 + i : 9 + i, 0:128] = as_row(dgain_s[i * 128 : (i + 1) * 128, :])
    shared_copies = [links.copy(shared_g.at[n], shared_g.at[n], device) for device in group]
    bc_second.wait_recv()
    links.release([bc_second])
    for k in range(wide):
        bc_mine[k] = bc_core[k, y] + bc_row[k]
    bc_rx[w] = bc_mine[w]
    bc_copies = [links.copy(bc_mine.at[device[0]], bc_rx.at[w], device) for device in far]
    back.fold()
    arrived(dt_copies)
    own = dt_rx[0]
    for k in range(1, wide):
        own = own + dt_rx[k]
    dt_own[...] = own
    squares = total_square(own)
    arrived(sv_copies)
    own = sv_g[0]
    for k in range(1, wide):
        own = own + sv_g[k]
    sv_sum[:, 0 : chans + small] = own
    squares = squares + jnp.where(w == 0, 1.0, 0.0) * total_square(own)
    for i in range(3 * thirds):
        squares = squares + square_s[i][:, 0:1]
    arrived(shared_copies)
    total = shared_g[0]
    for q in range(1, parts):
        total = total + shared_g[q]
    sw_g[w] = total
    sw_copies = [links.copy(sw_g.at[w], sw_g.at[w], device) for device in far]
    arrived(bc_copies)
    own = bc_rx[0]
    for k in range(1, wide):
        own = own + bc_rx[k]
    bc_own[n] = own
    bc_group = [links.copy(bc_own.at[n], bc_own.at[n], device) for device in group]
    squares = squares + total_square(own)
    norm_n[n] = jnp.broadcast_to(squares, (8, 128))
    norm_copies = [links.copy(norm_n.at[n], norm_n.at[n], device) for device in group]

    block = branch.total() * live_ref[:, pl.ds(pl.multiple_of(n * own_rows, 128), own_rows)]
    for i in range(width // 128):
        sl = slice(i * 128, (i + 1) * 128)
        block_ref[:, sl] = hidden_ref[:, sl] + jnp.transpose(block[sl, :])
    arrived(norm_copies)
    norm_w[w] = norm_n[0] + norm_n[1] + norm_n[2] + norm_n[3]
    wide_copies = [links.copy(norm_w.at[w], norm_w.at[w], device) for device in far]
    dn = back.total() * gain_col[...]
    dots = jnp.sum(dn * hq[n], axis=0, keepdims=True) / width
    for i in range(width // 128):
        sl = slice(i * 128, (i + 1) * 128)
        value = inv_ref[...] * (dn[sl] - hq[n, sl, :] * dots)
        grad_ref[:, sl] = cot_ref[:, sl] + jnp.transpose(value)
    arrived(sw_copies)
    shared = sw_g[0]
    for k in range(1, wide):
        shared = shared + sw_g[k]
    sv_sum[:, chans + small :] = shared
    arrived(wide_copies)
    total = norm_w[0]
    for k in range(1, wide):
        total = total + norm_w[k]
    total = total + total_square(shared)
    norm_ref[...] = jnp.sqrt(total)
    for job in jobs:
        job.finish()
    arrived(bc_group)
    links.drain()

    def sent(b, _):
        for j in range(3):
            stat_copy(j, b).wait_send()
        return 0

    lax.fori_loop(0, 2 * blocks, sent, 0)


def run_layer(lengths, hidden, cot, gain, w_zx, w_out, w_bc, dtw, cx, cbc, hp, og, heads, shard, wide, narrow):
    own_rows, width = hidden.shape
    tokens = own_rows * narrow
    chans, n4 = cx.shape[1], cbc.shape[1]
    rows = w_zx.shape[1]
    depth, blocks, half, thirds = wide // 2, tokens // SPAN, n4 // 2, chans // 128
    full, bc2, small = (chans, tokens), (half, tokens), (16, tokens)
    quarters = (narrow, width, own_rows)
    weights = (depth, 2, rows, chans)
    piece = (3 * thirds, depth, 2, rows, 128)
    quarter = (width // wide // 4, n4)
    sums = (16, chans + 128 + 256)
    shapes = [
        hidden.shape,
        hidden.shape,
        piece,
        (4,) + quarter,
        (16, 128),
        sums,
        (8, 128),
    ]
    scratch = [
        quarters,
        quarters,
        weights,
        weights,
        weights,
        (depth, 2, 2, rows // 2, n4),
        (depth, 2, 16, 128),
        (narrow, 8, 128),
        (16, width),
        (width, 1),
        (1, width),
        (128, 128),
        (chans, 4),
        (n4, 4),
        (16, 3),
        (chans, 1),
        (1, tokens),
        (1, own_rows),
        (2 * chans + n4 + 16, tokens),
        full,
        full,
        full,
        bc2,
        bc2,
        (n4, tokens),
        small,
        small,
        small,
        (blocks, chans, half),
        (blocks, SPAN, SPAN),
        full,
        full,
        full,
        (blocks, chans, half),
        bc2,
        bc2,
        (blocks, SPAN, SPAN),
        small,
        small,
        small,
        small,
        (blocks, 16, SPAN),
        (chans, 128),
        (n4, 128),
        (16, 128),
        (chans, 1),
        (width, 1),
        (2 * blocks, 8, 128),
        (narrow, 2 * blocks, 8, 128),
        (2 * thirds,) + piece[1:],
        (3 * thirds - 2, depth, rows, 128),
        (3 * thirds - 2, depth - 1, rows, 128),
        (2, depth - 1, 2, rows, 128),
        (2, rows, 128),
        (2, 2, width, own_rows),
        (2, width, own_rows),
        (wide, 2, 2) + quarter,
        (wide, 2) + quarter,
        (wide,) + quarter,
        (wide,) + quarter,
        (wide,) + quarter,
        (wide, 16, 128),
        (wide, 16, 128),
        (narrow, 16, 256),
        (wide, 16, chans + 128),
        (wide, 16, 256),
        (narrow, 8, 128),
        (wide, 8, 128),
        (3 * thirds, 1, 128),
    ]
    lows = [quarters] * 2 + [(2 * chans + n4 + 16, width)] * 2
    copies = 200
    operands = (lengths, hidden, cot, gain, w_zx, w_out, w_bc, dtw, cx, cbc, hp, og)
    return pl.pallas_call(
        functools.partial(layer_kernel, wide, heads, shard, chans * narrow),
        out_shape=[jax.ShapeDtypeStruct(shape, F32) for shape in shapes],
        in_specs=[pl.BlockSpec(memory_space=pltpu.SMEM)]
        + [pl.BlockSpec(memory_space=pltpu.VMEM)] * (len(operands) - 1),
        scratch_shapes=[pltpu.VMEM(shape, F32) for shape in scratch]
        + [pltpu.VMEM(shape, jnp.bfloat16) for shape in lows]
        + [
            pltpu.SemaphoreType.DMA((copies,)),
            pltpu.SemaphoreType.DMA((copies,)),
            pltpu.SemaphoreType.DMA((3, 2 * blocks)),
            pltpu.SemaphoreType.DMA((3, 2 * blocks)),
        ],
        compiler_params=pltpu.CompilerParams(
            vmem_limit_bytes=62 * MIB, collective_id=0, has_side_effects=True
        ),
        cost_estimate=pl.CostEstimate(flops=20_000_000_000, bytes_accessed=20_000_000, transcendentals=0),
    )(*operands)


def finish_kernel(
    wide,
    narrow,
    gfull,
    bc_own,
    dt_own,
    sv,
    norm_ref,
    block_in,
    grad_in,
    stat_l,
    stat_r,
    stat_lo,
    stat_ro,
    root_l,
    root_r,
    root_lo,
    root_ro,
    w_ref,
    wout_ref,
    bcw_ref,
    dtw_ref,
    cx_ref,
    cbc_ref,
    hp_ref,
    og_ref,
    gain_ref,
    block_out,
    in_grad,
    clip,
    g_zx,
    new_zx,
    new_l,
    new_r,
    g_out,
    new_out,
    new_lo,
    new_ro,
    g_bc,
    new_bc,
    g_dt,
    new_dt,
    g_cx,
    new_cx,
    g_cbc,
    new_cbc,
    g_hp,
    new_hp,
    g_og,
    new_og,
    g_ng,
    new_ng,
    g_s,
    l_s,
    r_s,
    lo_s,
    ro_s,
    rl_s,
    rr_s,
    rlo_s,
    rro_s,
    in_sem,
    out_sem,
):
    rate = 10.0
    chans = w_ref.shape[2]
    thirds = chans // 128
    place = lax.axis_index("wide")
    z, x = place // 2, place % 2
    factor = 1.0 / jnp.maximum(norm_ref[0:1, 0:1], 1.0)
    fetches, results = [], []

    def fetch(src, dst):
        item = pltpu.make_async_copy(src, dst, in_sem.at[len(fetches)])
        item.start()
        fetches.append(item)
        return item

    def result(src, dst):
        item = pltpu.make_async_copy(src, dst, out_sem.at[len(results)])
        item.start()
        results.append(item)

    waits = []
    for m in (2, 0, 1):
        gs = g_s.at[m * thirds : (m + 1) * thirds]
        whole_m = fetch(gfull.at[m * thirds : (m + 1) * thirds], gs)
        if m == 2:
            others = [(root_ro, rro_s), (root_lo, rlo_s), (stat_ro, ro_s), (stat_lo, lo_s)]
        else:
            others = [(root_l.at[m], rl_s.at[m]), (root_r.at[m], rr_s.at[m])]
            others += [(stat_l.at[m], l_s.at[m]), (stat_r.at[m], r_s.at[m])]
        waits.append([whole_m] + [fetch(*pair) for pair in others])
    block_out[...] = block_in[...]
    in_grad[...] = grad_in[...]
    clip[...] = norm_ref[0:1, 0:1]

    def both(m):
        for item in waits[(1, 2, 0)[m]]:
            item.wait()
        parts = [flat(g_s[m * thirds + i]) for i in range(thirds)]
        mine = [g_s[m * thirds + i, z, x] for i in range(thirds)]
        parts = [item * factor for item in parts]
        turned = jnp.concatenate([jnp.transpose(item) for item in parts], axis=0)
        return jnp.concatenate(mine, axis=1) * factor, halves(jnp.concatenate(parts, axis=1)), halves(turned)

    own, full, turned = both(2)
    g_out[...] = own
    ro_s[...] = 0.5 * ro_s[...] + 0.5 * product(halves(own), full, NT)
    result(ro_s, new_ro)
    lo_s[...] = 0.5 * lo_s[...] + 0.5 * product(turned, full)
    result(lo_s, new_lo)
    new_out[...] = wout_ref[...] - 0.5 * dot3(product(halves(rro_s[...]), full), rlo_s[...], NT)
    for m in range(2):
        own, full, turned = both(m)
        g_zx[m] = own
        l_s[m] = 0.5 * l_s[m] + 0.5 * product(halves(own), full, NT)
        result(l_s.at[m], new_l.at[m])
        r_s[m] = 0.5 * r_s[m] + 0.5 * product(turned, full)
        result(r_s.at[m], new_r.at[m])
        new_zx[m] = w_ref[m] - 0.5 * dot3(product(halves(rl_s[m]), full), rr_s[m])

    grad = flat(bc_own[...]) * factor
    g_bc[...] = grad
    new_bc[...] = bcw_ref[...] - rate * grad
    heads, _, rows = dtw_ref.shape
    for h in range(heads):
        for i in range(2):
            row = i * heads + h
            grad = dt_own[row : row + 1, 0:rows] * factor
            g_dt[h, i : i + 1, :] = grad
            new_dt[h, i : i + 1, :] = dtw_ref[h, i : i + 1, :] - rate * grad
    sums = sv[...] * factor
    grad = sums[0:4, 0:chans]
    g_cx[...] = grad
    new_cx[...] = cx_ref[...] - rate * grad
    grad = sums[4:5, 0:chans]
    g_og[...] = grad.reshape(chans)
    new_og[...] = og_ref[...] - rate * g_og[...]
    n4 = cbc_ref.shape[1]
    last = chans + 128
    grad = sums[0:4, last : last + n4]
    g_cbc[...] = grad
    new_cbc[...] = cbc_ref[...] - rate * grad
    turned = jnp.transpose(
        jnp.concatenate([sums[:, chans:last], jnp.zeros((112, 128), F32)], axis=0)
    )
    for i, (row, start) in enumerate(((0, 0), (0, heads), (1, 0), (1, heads), (2, 0))):
        grad = turned[row : row + 1, start : start + heads]
        g_hp[i : i + 1, :] = grad
        new_hp[i : i + 1, :] = hp_ref[i : i + 1, :] - rate * grad
    shard = gain_ref.shape[0]
    count = narrow * shard // 128
    line = jnp.concatenate([sums[8 + i : 9 + i, last : last + 128] for i in range(count)], axis=1)
    grad = jnp.zeros((1, shard), F32)
    for q in range(narrow):
        piece = line[:, q * shard : (q + 1) * shard]
        grad = jnp.where(lax.axis_index("narrow") == q, piece, grad)
    g_ng[...] = grad.reshape(shard)
    new_ng[...] = gain_ref[...] - rate * g_ng[...]
    for item in results:
        item.wait()


def run_finish(partials, stats, roots, params, tokens_shape, wide, narrow):
    stat_l, stat_r, stat_lo, stat_ro = stats
    w_zx, w_out, w_bc, w_dt, cx, cbc, hp, og, gain = params
    like = [w_zx, w_zx, stat_l, stat_r, w_out, w_out, stat_lo, stat_ro]
    like += [item for item in (w_bc, w_dt, cx, cbc, hp, og, gain) for _ in range(2)]
    shapes = [tokens_shape, tokens_shape, (1, 1)] + [item.shape for item in like]
    far, near = pl.BlockSpec(memory_space=pl.ANY), pl.BlockSpec(memory_space=pltpu.VMEM)
    gfull = partials[0]
    kept = [gfull, stat_l, stat_r, stat_lo, stat_ro, *roots]
    return pl.pallas_call(
        functools.partial(finish_kernel, wide, narrow),
        out_shape=[jax.ShapeDtypeStruct(shape, F32) for shape in shapes],
        in_specs=[far] + [near] * 6 + [far] * 8 + [near] * len(params),
        out_specs=[near] * 5 + [far] * 2 + [near] * 2 + [far] * 2 + [near] * (len(shapes) - 11),
        scratch_shapes=[pltpu.VMEM(item.shape, F32) for item in kept]
        + [pltpu.SemaphoreType.DMA((15,)), pltpu.SemaphoreType.DMA((6,))],
        compiler_params=pltpu.CompilerParams(vmem_limit_bytes=56 * MIB),
        cost_estimate=pl.CostEstimate(flops=4_000_000_000, bytes_accessed=20_000_000, transcendentals=0),
    )(*partials, *stats, *roots, *params)


def fast_local(
    wide,
    narrow,
    hidden_in,
    out_cot,
    lengths,
    norm_gain,
    w_zx,
    w_bc,
    w_dt,
    conv_x,
    conv_bc,
    head_params,
    out_gain,
    w_out,
    left_statistic_gate,
    stat_right_zx,
    stat_left_out,
    stat_right_out,
    inverse_root_left_gate,
    inverse_root_right_gate,
    root_left_out,
    root_right_out,
):
    heads, shard = w_dt.shape[1], norm_gain.shape[0]
    out_rows, dt_rows = w_out.T, jnp.transpose(w_dt, (1, 2, 0))
    block, grad, *partials = run_layer(
        lengths,
        hidden_in,
        out_cot,
        norm_gain,
        w_zx,
        out_rows,
        w_bc,
        dt_rows,
        conv_x,
        conv_bc,
        head_params,
        out_gain,
        heads,
        shard,
        wide,
        narrow,
    )
    (
        block_out,
        in_grad,
        clip,
        g_zx,
        new_zx,
        new_l,
        new_r,
        g_out,
        new_out,
        new_lo,
        new_ro,
        g_bc,
        new_bc,
        g_dt,
        new_dt,
        *rest,
    ) = run_finish(
        (*partials, block, grad),
        (left_statistic_gate[:, 0], stat_right_zx, stat_left_out, stat_right_out[0]),
        (inverse_root_left_gate[:, 0], inverse_root_right_gate, root_left_out, root_right_out[0]),
        (w_zx, out_rows, w_bc, dt_rows, conv_x, conv_bc, head_params, out_gain, norm_gain),
        hidden_in.shape,
        wide,
        narrow,
    )
    return (
        block_out,
        in_grad,
        clip.reshape(()),
        g_zx,
        new_zx,
        new_l[:, None],
        new_r,
        g_out.T,
        new_out.T,
        new_lo,
        new_ro[None],
        g_bc,
        new_bc,
        jnp.transpose(g_dt, (2, 0, 1)),
        jnp.transpose(new_dt, (2, 0, 1)),
        *rest,
    )


def solution(mesh):
    wide, narrow = mesh.shape["wide"], mesh.shape["narrow"]
    body = functools.partial(fast_local, wide, narrow) if (wide, narrow) == (8, 4) else local
    return jax.shard_map(
        body,
        mesh=mesh,
        in_specs=(
            P(("wide", "narrow"), None),
            P(("wide", "narrow"), None),
            P("wide"),
            P("narrow"),
            P(None, "wide", "narrow"),
            P("wide", None),
            P("wide", "narrow", None),
            P(None, "narrow"),
            P(),
            P(None, "narrow"),
            P("narrow"),
            P("narrow", "wide"),
            P(None, "narrow", "wide", None),
            P(None, "narrow", None),
            P("narrow", None),
            P("narrow", "wide", None),
            P(None, "narrow", "wide", None),
            P(None, "narrow", None),
            P("narrow", None),
            P("narrow", "wide", None),
        ),
        out_specs=(
            P(("wide", "narrow"), None),
            P(("wide", "narrow"), None),
            P(),
            P(None, "wide", "narrow"),
            P(None, "wide", "narrow"),
            P(None, "narrow", "wide", None),
            P(None, "narrow", None),
            P("narrow", "wide"),
            P("narrow", "wide"),
            P("narrow", None),
            P("narrow", "wide", None),
            P("wide", None),
            P("wide", None),
            P("wide", "narrow", None),
            P("wide", "narrow", None),
            P(None, "narrow"),
            P(None, "narrow"),
            P(),
            P(),
            P(None, "narrow"),
            P(None, "narrow"),
            P("narrow"),
            P("narrow"),
            P("narrow"),
            P("narrow"),
        ),
        check_vma=False,
    )
```
